32 devices in a mesh: dp: 8 (over z, y), expert: 4 (over x, core).
Axes of the slice: x: 2, y: 2, z: 4, core: 2. Of those that a mesh axis runs over, the one named last changes fastest.
Arguments:
- tokens: bfloat16 [12288, 1536], P(('dp', 'expert')), may hold values from -6 to 6
- cotangent: bfloat16 [12288, 1536], P(('dp', 'expert')), may hold values from -6 to 6
- lengths: int32 [32], P(('dp', 'expert')), may hold values from 96 to 384, as said below
- routes: int32 [12288, 8], P(('dp', 'expert')), may hold values from 0 to 39, as said below
- slots: int32 [12288, 8], P(('dp', 'expert')), may hold values from 0 to 151, as said below
- first_gain: bfloat16 [1536], P(('dp', 'expert')), may hold values from 0.5 to 1.5
- qkv_weight: bfloat16 [1536, 2560], P(('dp', 'expert')), may hold values from -0.4375 to 0.4375
- out_weight: bfloat16 [1536, 1536], P(None, ('dp', 'expert')), may hold values from -2.5 to 2.5
- second_gain: bfloat16 [1536], P(('dp', 'expert')), may hold values from 0.5 to 1.5
- router_weight: bfloat16 [1536, 40], P(('dp', 'expert')), may hold values from -0.078125 to 0.078125
- gate_up_weight: bfloat16 [40, 1536, 1024], P('expert', 'dp'), may hold values from -0.15625 to 0.15625
- down_weight: bfloat16 [40, 512, 1536], P('expert', None, 'dp'), may hold values from -4 to 4
Outputs:
- output: bfloat16 [12288, 1536], P(('dp', 'expert'))
- input_grad: float32 [12288, 1536], P(('dp', 'expert'))
- first_gain_grad: float32 [1536], P(('dp', 'expert'))
- qkv_grad: float32 [1536, 2560], P(('dp', 'expert'))
- out_grad: float32 [1536, 1536], P(None, ('dp', 'expert'))
- second_gain_grad: float32 [1536], P(('dp', 'expert'))
- router_grad: float32 [1536, 40], P(('dp', 'expert'))
- gate_up_grad: float32 [40, 1536, 1024], P('expert', 'dp')
- down_grad: float32 [40, 512, 1536], P('expert', None, 'dp')
The draws below stay inside these ranges and needn't reach their ends.
Inputs may be any that keep to these rules, and one draw needn't show every extreme that they name: `lengths`: in every draw one sequence has exactly 384 valid tokens. `routes`: A token's 8 experts are distinct. Among the rows of one device no expert is named more than 152 times; in every draw, for each index of dp, some expert is named exactly 152 times by every one of the 4 devices of that index. `slots`: for one device and one expert, the places of the rows naming it are distinct and run from 0 to that expert's count of rows less one.
All inputs are finite; a program needn't handle non-finite values.
Results may differ from the reference program's by a relative error of at most 0.017.
Values may be sent and summed in bfloat16 or wider, within the bound.
No kernel may reach another device: no remote copies, remote signals or barrier semaphores. Data moves between devices by JAX's collectives and lax.ppermute only.
A program may use at most 320 MiB of HBM per device.

```python
import jax
import jax.numpy as jnp
from jax import lax

D = 1536
QUERY_HEADS = 24
KEY_VALUE_HEADS = 8
HEAD_SIZE = 64
FF = 512
EXPERTS = 40
TOP = 8
TOKENS_PER_SEQ = 384
SEQUENCE_COUNT = 32
TOKENS = 12288
QKV = 2560
CAP = 152
N_EXPERT = 4


def route_table(key):
    total = TOKENS_PER_SEQ * TOP
    base = total // EXPERTS
    extra = total % EXPERTS
    widest = base + (1 if extra > 0 else 0)
    spread = CAP - widest
    index = jnp.arange(EXPERTS)
    base_load = base + (index < extra).astype(jnp.int32)

    def one_block(block_tile):
        block_key = jax.random.fold_in(key, block_tile)
        key_spread, key_label, key_order = jax.random.split(block_key, 3)
        paired = jax.random.randint(key_spread, (EXPERTS // 2,), 0, spread + 1)
        paired = paired.at[0].set(spread)
        delta = jnp.stack([paired, -paired], axis=1).reshape(EXPERTS)
        loads = base_load + delta
        ends = jnp.cumsum(loads)
        starts = ends - loads
        group_key = jax.random.fold_in(jax.random.fold_in(key, 1048576), block_tile // N_EXPERT)
        favoured = jax.random.randint(group_key, (), 0, EXPERTS)
        labels = jax.random.permutation(key_label, EXPERTS)
        place = jnp.argmax(labels == favoured)
        labels = labels.at[place].set(labels[0]).at[0].set(favoured)
        order = jax.random.permutation(key_order, TOKENS_PER_SEQ)
        position = order[:, None] + TOKENS_PER_SEQ * jnp.arange(TOP)[None, :]
        run = jnp.sum((position[:, :, None] >= ends[None, None, :]).astype(jnp.int32), axis=-1)
        return (labels[run], position - starts[run])
    route_blocks, slot_blocks = jax.vmap(one_block)(jnp.arange(SEQUENCE_COUNT))
    return (route_blocks.reshape(TOKENS, TOP).astype(jnp.int32), slot_blocks.reshape(TOKENS, TOP).astype(jnp.int32))


def draw_routes(key, part):
    return route_table(key)[0]


def draw_slots(key, part):
    return route_table(key)[1]


def draw_lengths(key, part):
    key = jax.random.fold_in(key, 5)
    key_length, key_pick = jax.random.split(key)
    drawn = jax.random.randint(key_length, (SEQUENCE_COUNT,), TOKENS_PER_SEQ // 4, TOKENS_PER_SEQ + 1)
    picked = jax.random.randint(key_pick, (), 0, SEQUENCE_COUNT)
    return drawn.at[picked].set(TOKENS_PER_SEQ).astype(jnp.int32)


def with_spikes(values, rng, source, target, blocks, factor):
    def block_of(axis_at):
        return (jnp.arange(values.shape[axis_at]) // (values.shape[axis_at] // blocks)).reshape((-1,) + (1,) * (values.ndim - 1 - axis_at))

    first = jax.random.permutation(rng, blocks)[block_of(target)]
    other_side = (block_of(target) + blocks // 2) % blocks
    return jnp.where((block_of(source) == first) | (block_of(source) == other_side), factor * values, values)


def block_scale(stream_key, dims, cuts, smallest, high):
    factor_of = 1.0
    for axis_at, blocks in cuts:
        draws = jax.random.uniform(jax.random.fold_in(jax.random.fold_in(stream_key, 6), axis_at), (blocks,), jnp.float32, smallest / len(cuts), high / len(cuts))
        factor_of = factor_of * jnp.repeat(jnp.exp(draws), dims[axis_at] // blocks).reshape((-1,) + (1,) * (len(dims) - 1 - axis_at))
    return factor_of


def scatter_about(rng, extent, scale, bound, cuts=(), kind=jnp.bfloat16):
    values = jax.random.normal(rng, extent, jnp.float32) * scale
    if len(cuts) > 0:
        values = block_scale(rng, extent, cuts, -0.22, 0.18) * values
    return jnp.clip(values, min=-bound, max=bound).astype(kind)


def bell_draw_with(rng, extent, deviation, most, cuts, heavy, kind=jnp.bfloat16):
    entries = deviation * jax.random.normal(rng, extent, jnp.float32)
    if cuts:
        entries = entries * block_scale(rng, extent, cuts, -0.22, 0.18)
    return jnp.clip(with_spikes(entries, jax.random.fold_in(rng, 3), *heavy), -most, most).astype(kind)


def setup_inputs(seed: int = 0) -> dict:
    arg_keys = jax.random.split(jax.random.key(seed), 13)
    return {
        "tokens": scatter_about(arg_keys[0], (TOKENS, D), 1.0, 6.0, ((0, 32),)),
        "cotangent": bell_draw_with(arg_keys[1], (TOKENS, D), 1.0, 6.0, ((0, 32),), (0, 1, 32, 2.75)),
        "lengths": draw_lengths(jax.random.fold_in(arg_keys[12], 71), 0),
        "routes": draw_routes(jax.random.fold_in(arg_keys[12], 71), 0),
        "slots": draw_slots(jax.random.fold_in(arg_keys[12], 71), 0),
        "first_gain": jnp.clip(1.0 + 0.1 * jax.random.normal(arg_keys[5], (D,), jnp.float32), 0.5, 1.5).astype(jnp.bfloat16),
        "qkv_weight": scatter_about(arg_keys[6], (D, QKV), (D // 8) ** -0.5, 0.4375, ((0, 32),)),
        "out_weight": scatter_about(arg_keys[7], (QUERY_HEADS * HEAD_SIZE, D), (D // 256) ** -0.5, 2.5, ((1, 32),)),
        "second_gain": jnp.clip(1.0 + 0.1 * jax.random.normal(arg_keys[8], (D,), jnp.float32), 0.5, 1.5).astype(jnp.bfloat16),
        "router_weight": scatter_about(arg_keys[9], (D, EXPERTS), (4 * D) ** -0.5, 0.078125, ((0, 32),)),
        "gate_up_weight": scatter_about(arg_keys[10], (EXPERTS, D, 2 * FF), D ** -0.5, 0.15625, ((0, 4), (1, 8))),
        "down_weight": scatter_about(arg_keys[11], (EXPERTS, FF, D), (max(FF // 256, 1)) ** -0.5, 4.0, ((0, 4), (2, 8))),
    }


@jax.custom_vjp
def lower_half(v):
    return lax.optimization_barrier(v.astype(jnp.bfloat16)).astype(jnp.float32)

@jax.custom_vjp
def low_back(v):
    return v

def low_keep(v):
    return (lower_half(v), None)

def low_pass(kept, grad):
    return (grad,)

def back_keep(v):
    return (v, None)

def back_low(kept, grad):
    return (lower_half(grad),)
lower_half.defvjp(low_keep, low_pass)
low_back.defvjp(back_keep, back_low)
epsilon = 1e-06
residual_scale = 0.22
score_scale = 0.015625
rope_base = 10000.0
masked_score = -1e+30
highest = lax.Precision.HIGHEST

def matmul(left, right):
    return jnp.dot(left, right, precision=highest, preferred_element_type=jnp.float32)

def normalize(value_rows, gain):
    inverse = lax.rsqrt(lax.optimization_barrier(jnp.mean(value_rows * value_rows, axis=-1, keepdims=True)) + epsilon)
    return value_rows * inverse * gain

def rope_tables():
    half = HEAD_SIZE // 2
    freqs = jnp.power(rope_base, -2.0 * jnp.arange(half, dtype=jnp.float32) / HEAD_SIZE)
    angles = jnp.arange(TOKENS_PER_SEQ, dtype=jnp.float32)[:, None] * freqs[None, :]
    cosine_table = jnp.concatenate([jnp.cos(angles), jnp.cos(angles)], axis=-1)
    sine_table = jnp.concatenate([jnp.sin(angles), jnp.sin(angles)], axis=-1)
    return (cosine_table, sine_table)

def rotate_pairs(value_rows, cosine_table, sine_table):
    half = HEAD_SIZE // 2
    turned = jnp.concatenate([-value_rows[..., half:], value_rows[..., :half]], axis=-1)
    return value_rows * cosine_table[:, None, :] + turned * sine_table[:, None, :]

def attend(inputs):
    query_rows, keys, value_rows, length = inputs
    query_group = QUERY_HEADS // KEY_VALUE_HEADS
    grouped_queries = query_rows.reshape(TOKENS_PER_SEQ, KEY_VALUE_HEADS, query_group, HEAD_SIZE)
    scores = jnp.einsum('qhgd,khd->hgqk', grouped_queries, keys, precision=highest, preferred_element_type=jnp.float32) * score_scale
    positions = jnp.arange(TOKENS_PER_SEQ)
    allowed = (positions[None, :] <= positions[:, None]) & (positions[None, :] < length)
    scores = low_back(jnp.where(allowed, scores, masked_score))
    peak = lax.optimization_barrier(jnp.max(scores, axis=-1, keepdims=True))
    exponent = jnp.exp(scores - peak)
    weights = exponent / lax.optimization_barrier(jnp.sum(exponent, axis=-1, keepdims=True))
    mixed = jnp.einsum('hgqk,khd->qhgd', lower_half(weights), value_rows, precision=highest, preferred_element_type=jnp.float32)
    return mixed.reshape(TOKENS_PER_SEQ, QUERY_HEADS * HEAD_SIZE)

def experts_one(inputs, gate_up_all, down_all):
    hidden_two, routes_seq, slots_seq, gates_seq = inputs
    copies = low_back(jnp.broadcast_to(hidden_two[:, None, :], (TOKENS_PER_SEQ, TOP, D)))
    buffer = jnp.zeros((EXPERTS, CAP, D), jnp.float32).at[routes_seq, slots_seq].set(copies)
    gate_up = low_back(jnp.einsum('ecd,edf->ecf', buffer, gate_up_all, precision=highest, preferred_element_type=jnp.float32))
    hidden = lower_half(jax.nn.silu(gate_up[..., :FF]) * gate_up[..., FF:])
    produced = low_back(lower_half(jnp.einsum('ecf,efd->ecd', hidden, down_all, precision=highest, preferred_element_type=jnp.float32)))
    picked = produced[routes_seq, slots_seq]
    return lax.optimization_barrier(jnp.sum(gates_seq[..., None] * picked, axis=1))

def layer(inputs, lengths, routes, slots, first_gain, qkv_weight, out_weight, second_gain, router_weight, gate_up_weight, down_weight):
    hidden_one = lower_half(normalize(inputs, first_gain))
    projected_rows = low_back(matmul(hidden_one.reshape(TOKENS, D), qkv_weight)).reshape(SEQUENCE_COUNT, TOKENS_PER_SEQ, QKV)
    query_width_total = QUERY_HEADS * HEAD_SIZE
    key_width_total = KEY_VALUE_HEADS * HEAD_SIZE
    cosine_table, sine_table = rope_tables()

    def turn_query(block_tile):
        return rotate_pairs(block_tile.reshape(TOKENS_PER_SEQ, QUERY_HEADS, HEAD_SIZE), cosine_table, sine_table)

    def turn_key(block_tile):
        return rotate_pairs(block_tile.reshape(TOKENS_PER_SEQ, KEY_VALUE_HEADS, HEAD_SIZE), cosine_table, sine_table)
    query_rows = lower_half(jax.vmap(turn_query)(projected_rows[..., :query_width_total]))
    keys = lower_half(jax.vmap(turn_key)(projected_rows[..., query_width_total:query_width_total + key_width_total]))
    value_rows = lower_half(projected_rows[..., query_width_total + key_width_total:].reshape(SEQUENCE_COUNT, TOKENS_PER_SEQ, KEY_VALUE_HEADS, HEAD_SIZE))
    mixed = lax.map(jax.checkpoint(attend), (query_rows, keys, value_rows, lengths))
    mixed = low_back(lower_half(mixed))
    branch = low_back(matmul(mixed.reshape(TOKENS, QUERY_HEADS * HEAD_SIZE), out_weight)).reshape(SEQUENCE_COUNT, TOKENS_PER_SEQ, D)
    middle = inputs + residual_scale * branch
    hidden_two = lower_half(normalize(middle, second_gain))
    logits = low_back(matmul(hidden_two.reshape(TOKENS, D), router_weight)).reshape(SEQUENCE_COUNT, TOKENS_PER_SEQ, EXPERTS)
    chosen = jnp.take_along_axis(logits, routes, axis=-1)
    gates = jax.nn.softmax(chosen, axis=-1)

    def moe_step(carry, pieces):
        return (carry, jax.checkpoint(experts_one)(pieces, gate_up_weight, down_weight))
    _, mixture = lax.scan(moe_step, None, (hidden_two, routes, slots, gates))
    return middle + residual_scale * mixture

def reference(tokens, cotangent, lengths, routes, slots, first_gain, qkv_weight, out_weight, second_gain, router_weight, gate_up_weight, down_weight):
    inputs = tokens.astype(jnp.float32).reshape(SEQUENCE_COUNT, TOKENS_PER_SEQ, D)
    routes_seq = routes.reshape(SEQUENCE_COUNT, TOKENS_PER_SEQ, TOP).astype(jnp.int32)
    slots_seq = slots.reshape(SEQUENCE_COUNT, TOKENS_PER_SEQ, TOP).astype(jnp.int32)
    lengths_seq = lengths.astype(jnp.int32)

    def forward(inputs, first_gain, qkv_weight, out_weight, second_gain, router_weight, gate_up_weight, down_weight):
        return layer(inputs, lengths_seq, routes_seq, slots_seq, first_gain, qkv_weight, out_weight, second_gain, router_weight, gate_up_weight, down_weight)
    primals = (inputs, first_gain.astype(jnp.float32), qkv_weight.astype(jnp.float32), out_weight.astype(jnp.float32), second_gain.astype(jnp.float32), router_weight.astype(jnp.float32), gate_up_weight.astype(jnp.float32), down_weight.astype(jnp.float32))
    result, pullback = jax.vjp(forward, *primals)
    grads = pullback(cotangent.astype(jnp.float32).reshape(SEQUENCE_COUNT, TOKENS_PER_SEQ, D))
    return (result.reshape(TOKENS, D).astype(jnp.bfloat16), grads[0].reshape(TOKENS, D), grads[1], grads[2], grads[3], grads[4], grads[5], grads[6], grads[7])
```

```python
import jax
import jax.numpy as jnp
from jax import lax
from jax.sharding import PartitionSpec as P

QUERY_HEADS = 24
KEY_VALUE_HEADS = 8
HEAD_SIZE = 64
FF = 512
EXPERTS = 40
TOP = 8
CAP = 152


epsilon = 1e-06
residual_scale = 0.22
score_scale = 0.015625
rope_base = 10000.0
masked_score = -1e30


def rope_tables(length):
    half = HEAD_SIZE // 2
    freqs = jnp.power(rope_base, -2.0 * jnp.arange(half, dtype=jnp.float32) / HEAD_SIZE)
    angles = jnp.arange(length, dtype=jnp.float32)[:, None] * freqs[None, :]
    cosine_table = jnp.concatenate([jnp.cos(angles), jnp.cos(angles)], axis=-1)
    sine_table = jnp.concatenate([jnp.sin(angles), jnp.sin(angles)], axis=-1)
    return (cosine_table, sine_table)


def rotate_half(value_rows):
    half = value_rows.shape[-1] // 2
    return jnp.concatenate([-value_rows[..., half:], value_rows[..., :half]], axis=-1)


def rotate_pairs(value_rows, cosine_table, sine_table):
    return value_rows * cosine_table[:, None, :] + rotate_half(value_rows) * sine_table[:, None, :]


def unrotate(grads, cosine_table, sine_table):
    return grads * cosine_table[:, None, :] - rotate_half(grads * sine_table[:, None, :])


def rms_inverse(value_rows):
    return lax.rsqrt(jnp.mean(value_rows * value_rows, axis=-1, keepdims=True) + epsilon)


def norm_backward(grad_normed, normal, inverse, gain):
    gain_term = jnp.sum(grad_normed * normal, axis=0)
    scaled = grad_normed * gain
    grad_input = inverse * (scaled - normal * jnp.mean(scaled * normal, axis=-1, keepdims=True))
    return (gain_term, grad_input)


def contract_rows(left, right):
    return lax.dot_general(
        left, right, (((0,), (0,)), ((), ())), preferred_element_type=jnp.float32
    )


def multiply_transposed(left, right):
    return lax.dot_general(
        left, right, (((1,), (1,)), ((), ())), preferred_element_type=jnp.float32
    )


def fetch_expert(gate_up_shard, down_shard):
    return (
        lax.all_gather(gate_up_shard, "dp", axis=0, tiled=True),
        lax.all_gather(down_shard, "dp", axis=1, tiled=True),
    )


def gate_values(hidden_rows, router_full, route_rows):
    logits = jnp.dot(hidden_rows, router_full, preferred_element_type=jnp.float32)
    chosen_mask = route_rows[:, :, None] == jnp.arange(EXPERTS)[None, None, :]
    chosen = jnp.sum(jnp.where(chosen_mask, logits[:, None, :], 0.0), axis=-1)
    return (chosen_mask, jax.nn.softmax(chosen, axis=-1))


def general_body(
    tokens,
    cotangent,
    lengths,
    routes,
    slots,
    first_gain,
    qkv_weight,
    out_weight,
    second_gain,
    router_weight,
    gate_up_weight,
    down_weight,
):
    sequence_length = tokens.shape[0]
    width = tokens.shape[1]
    query_group = QUERY_HEADS // KEY_VALUE_HEADS
    length = lengths[0]
    gathered = (
        lax.all_gather(first_gain, ("dp", "expert"), axis=0, tiled=True),
        lax.all_gather(qkv_weight, ("dp", "expert"), axis=0, tiled=True),
        lax.all_gather(out_weight, ("dp", "expert"), axis=1, tiled=True),
        lax.all_gather(second_gain, ("dp", "expert"), axis=0, tiled=True),
        lax.all_gather(router_weight, ("dp", "expert"), axis=0, tiled=True),
    )
    gain_one, qkv_full, out_full, gain_two, router_full = gathered
    inputs = tokens.astype(jnp.float32)
    inverse_one = rms_inverse(inputs)
    normal_one = inputs * inverse_one
    hidden_one = (normal_one * gain_one.astype(jnp.float32)).astype(jnp.bfloat16)
    projected_rows = jnp.dot(hidden_one, qkv_full, preferred_element_type=jnp.float32)
    cosine_table, sine_table = rope_tables(sequence_length)
    query_width_total = QUERY_HEADS * HEAD_SIZE
    key_width_total = KEY_VALUE_HEADS * HEAD_SIZE
    query_rows = rotate_pairs(
        projected_rows[:, :query_width_total].reshape(sequence_length, QUERY_HEADS, HEAD_SIZE),
        cosine_table,
        sine_table,
    ).astype(jnp.bfloat16)
    keys = rotate_pairs(
        projected_rows[:, query_width_total : query_width_total + key_width_total].reshape(
            sequence_length, KEY_VALUE_HEADS, HEAD_SIZE
        ),
        cosine_table,
        sine_table,
    ).astype(jnp.bfloat16)
    value_rows = (
        projected_rows[:, query_width_total + key_width_total :]
        .reshape(sequence_length, KEY_VALUE_HEADS, HEAD_SIZE)
        .astype(jnp.bfloat16)
    )
    row_index = jnp.arange(sequence_length)[:, None]
    column_index = jnp.arange(sequence_length)[None, :]
    allowed = (column_index <= row_index) & (column_index < length)

    def head_scores(head):
        head_query = lax.dynamic_slice_in_dim(query_rows, head * query_group, query_group, 1)
        head_key = lax.dynamic_index_in_dim(keys, head, 1, keepdims=False)
        head_value = lax.dynamic_index_in_dim(value_rows, head, 1, keepdims=False)
        scores = (
            jnp.einsum("qgd,kd->gqk", head_query, head_key, preferred_element_type=jnp.float32)
            * score_scale
        )
        return (head_query, head_key, head_value, jnp.where(allowed[None], scores, masked_score))

    def attention_head_forward(head):
        head_query, head_key, head_value, scores = head_scores(head)
        peak = jnp.max(scores, axis=-1, keepdims=True)
        exponent = jnp.exp(scores - peak)
        total = jnp.sum(exponent, axis=-1, keepdims=True)
        weights = (exponent / total).astype(jnp.bfloat16)
        head_mixed = jnp.einsum(
            "gqk,kd->qgd", weights, head_value, preferred_element_type=jnp.float32
        ).astype(jnp.bfloat16)
        return (head_mixed, (peak + jnp.log(total))[..., 0])

    mixed_head_output, log_sum_totals = lax.map(attention_head_forward, jnp.arange(KEY_VALUE_HEADS))
    mixed = mixed_head_output.transpose(1, 0, 2, 3).reshape(
        sequence_length, QUERY_HEADS * HEAD_SIZE
    )
    branch = jnp.dot(mixed, out_full, preferred_element_type=jnp.float32)
    middle = inputs + residual_scale * branch
    inverse_two = rms_inverse(middle)
    normal_two = middle * inverse_two
    hidden_two = (normal_two * gain_two.astype(jnp.float32)).astype(jnp.bfloat16)
    chosen_mask, gates = gate_values(hidden_two, router_full, routes)
    grad_out = cotangent.astype(jnp.float32)
    grad_mixture = residual_scale * grad_out

    def expert_forward(carry, pieces):
        rows, gate_up_shard, down_shard = pieces
        gate_up_full, down_full = fetch_expert(gate_up_shard, down_shard)
        gate_up = jnp.dot(rows, gate_up_full, preferred_element_type=jnp.float32)
        hidden = (jax.nn.silu(gate_up[:, :FF]) * gate_up[:, FF:]).astype(jnp.bfloat16)
        return (
            carry,
            jnp.dot(hidden, down_full, preferred_element_type=jnp.float32).astype(jnp.bfloat16),
        )

    copies = jnp.broadcast_to(hidden_two[:, None, :], (sequence_length, TOP, width))
    outgoing = jnp.zeros((EXPERTS, CAP, width), jnp.bfloat16).at[routes, slots].set(copies)
    received = lax.all_to_all(outgoing, "expert", split_axis=0, concat_axis=1, tiled=True)
    _, produced = lax.scan(expert_forward, None, (received, gate_up_weight, down_weight))
    returned = lax.all_to_all(produced, "expert", split_axis=1, concat_axis=0, tiled=True)
    expert_rows = returned[routes, slots].astype(jnp.float32)
    mixture = jnp.sum(gates[:, :, None] * expert_rows, axis=1)
    grad_gates = jnp.sum(expert_rows * grad_mixture[:, None, :], axis=-1)
    grad_rows = (gates[:, :, None] * grad_mixture[:, None, :]).astype(jnp.bfloat16)
    outgoing_grad = jnp.zeros((EXPERTS, CAP, width), jnp.bfloat16).at[routes, slots].set(grad_rows)
    grad_received = lax.all_to_all(outgoing_grad, "expert", split_axis=0, concat_axis=1, tiled=True)
    output = (middle + residual_scale * mixture).astype(jnp.bfloat16)
    again = (
        lax.all_gather(first_gain, ("dp", "expert"), axis=0, tiled=True),
        lax.all_gather(qkv_weight, ("dp", "expert"), axis=0, tiled=True),
        lax.all_gather(out_weight, ("dp", "expert"), axis=1, tiled=True),
        lax.all_gather(second_gain, ("dp", "expert"), axis=0, tiled=True),
        lax.all_gather(router_weight, ("dp", "expert"), axis=0, tiled=True),
    )
    gain_back, qkv_back, output_gradient, gain_two_back, router_back = again
    grad_chosen = gates * (grad_gates - jnp.sum(gates * grad_gates, axis=-1, keepdims=True))
    grad_logits = jnp.sum(jnp.where(chosen_mask, grad_chosen[:, :, None], 0.0), axis=1).astype(
        jnp.bfloat16
    )

    def expert_backward(carry, pieces):
        rows, grad_produced, gate_up_shard, down_shard = pieces
        gate_up_full, down_full = fetch_expert(gate_up_shard, down_shard)
        gate_up = jnp.dot(rows, gate_up_full, preferred_element_type=jnp.float32)
        gate = gate_up[:, :FF]
        upper = gate_up[:, FF:]
        sigmoid = jax.nn.sigmoid(gate)
        swish = gate * sigmoid
        hidden = (swish * upper).astype(jnp.bfloat16)
        grad_hidden = multiply_transposed(grad_produced, down_full)
        grad_gate_up = jnp.concatenate(
            [grad_hidden * upper * sigmoid * (1.0 + gate * (1.0 - sigmoid)), grad_hidden * swish],
            axis=-1,
        ).astype(jnp.bfloat16)
        grad_copy = multiply_transposed(grad_gate_up, gate_up_full).astype(jnp.bfloat16)
        gate_up_part = lax.psum_scatter(
            contract_rows(rows, grad_gate_up).astype(jnp.bfloat16),
            "dp",
            scatter_dimension=0,
            tiled=True,
        ).astype(jnp.float32)
        down_part = lax.psum_scatter(
            contract_rows(grad_produced, hidden).astype(jnp.bfloat16),
            "dp",
            scatter_dimension=0,
            tiled=True,
        ).astype(jnp.float32)
        return (carry, (grad_copy, gate_up_part, down_part.T))

    _, (grad_copies, gate_up_grads, down_grads) = lax.scan(
        expert_backward, None, (received, grad_received, gate_up_weight, down_weight)
    )
    grad_back = lax.all_to_all(grad_copies, "expert", split_axis=1, concat_axis=0, tiled=True)
    copy_sum = jnp.sum(grad_back[routes, slots].astype(jnp.float32), axis=1)
    grad_hidden_two = copy_sum + multiply_transposed(grad_logits, router_back)
    router_term = contract_rows(hidden_two, grad_logits)
    second_term, grad_norm_two = norm_backward(
        grad_hidden_two, normal_two, inverse_two, gain_two_back.astype(jnp.float32)
    )
    grad_middle = grad_out + grad_norm_two
    branch_gradient = (residual_scale * grad_middle).astype(jnp.bfloat16)
    out_term = contract_rows(mixed, branch_gradient)
    grad_mixed = (
        multiply_transposed(branch_gradient, output_gradient)
        .astype(jnp.bfloat16)
        .reshape(sequence_length, KEY_VALUE_HEADS, query_group, HEAD_SIZE)
    )

    def attention_head_backward(head):
        head_query, head_key, head_value, scores = head_scores(head)
        head_grad = lax.dynamic_index_in_dim(grad_mixed, head, 1, keepdims=False)
        head_total = lax.dynamic_index_in_dim(log_sum_totals, head, 0, keepdims=False)
        probs = jnp.exp(scores - head_total[..., None])
        grad_weights = jnp.einsum(
            "qgd,kd->gqk", head_grad, head_value, preferred_element_type=jnp.float32
        )
        grad_scores = (
            probs * (grad_weights - jnp.sum(probs * grad_weights, axis=-1, keepdims=True))
        ).astype(jnp.bfloat16)
        grad_query = (
            jnp.einsum("gqk,kd->qgd", grad_scores, head_key, preferred_element_type=jnp.float32)
            * score_scale
        )
        grad_key = (
            jnp.einsum("gqk,qgd->kd", grad_scores, head_query, preferred_element_type=jnp.float32)
            * score_scale
        )
        grad_value = jnp.einsum(
            "gqk,qgd->kd", probs.astype(jnp.bfloat16), head_grad, preferred_element_type=jnp.float32
        )
        return (grad_query, grad_key, grad_value)

    query_head_rows, key_head_rows, value_head_rows = lax.map(
        attention_head_backward, jnp.arange(KEY_VALUE_HEADS)
    )
    grad_query = unrotate(
        query_head_rows.transpose(1, 0, 2, 3).reshape(sequence_length, QUERY_HEADS, HEAD_SIZE),
        cosine_table,
        sine_table,
    )
    grad_key = unrotate(key_head_rows.transpose(1, 0, 2), cosine_table, sine_table)
    grad_value = value_head_rows.transpose(1, 0, 2)
    grad_projected = jnp.concatenate(
        [
            grad_query.reshape(sequence_length, query_width_total),
            grad_key.reshape(sequence_length, key_width_total),
            grad_value.reshape(sequence_length, key_width_total),
        ],
        axis=-1,
    ).astype(jnp.bfloat16)
    qkv_term = contract_rows(hidden_one, grad_projected)
    grad_hidden_one = multiply_transposed(grad_projected, qkv_back)
    first_term, grad_norm_one = norm_backward(
        grad_hidden_one, normal_one, inverse_one, gain_back.astype(jnp.float32)
    )
    grad_input = grad_middle + grad_norm_one
    summed = (
        lax.psum_scatter(first_term, ("dp", "expert"), scatter_dimension=0, tiled=True),
        lax.psum_scatter(qkv_term, ("dp", "expert"), scatter_dimension=0, tiled=True),
        lax.psum_scatter(out_term, ("dp", "expert"), scatter_dimension=1, tiled=True),
        lax.psum_scatter(second_term, ("dp", "expert"), scatter_dimension=0, tiled=True),
        lax.psum_scatter(router_term, ("dp", "expert"), scatter_dimension=0, tiled=True),
    )
    return (
        output,
        grad_input,
        summed[0],
        summed[1],
        summed[2],
        summed[3],
        summed[4],
        gate_up_grads,
        down_grads,
    )


WIDE = 160
Z_SIZE, Y_SIZE, X_SIZE, C_SIZE = 4, 2, 2, 2
MESH_AXES = ("dp", "expert")


def device_index(z, y, x, c):
    return ((z * Y_SIZE + y) * X_SIZE + x) * C_SIZE + c


def device_pairs(target):
    pairs = []
    for z in range(Z_SIZE):
        for y in range(Y_SIZE):
            for x in range(X_SIZE):
                for c in range(C_SIZE):
                    to = target(z, y, x, c)
                    if to is not None:
                        pairs.append((device_index(z, y, x, c), device_index(*to)))
    return pairs


PAIRS_X = device_pairs(lambda z, y, x, c: (z, y, 1 - x, c))
PAIRS_Y = device_pairs(lambda z, y, x, c: (z, 1 - y, x, c))
PAIRS_C = device_pairs(lambda z, y, x, c: (z, y, x, 1 - c))


def pairs_shift(step):
    return device_pairs(lambda z, y, x, c: ((z + step) % Z_SIZE, y, x, c))


def pairs_up(first):
    return device_pairs(
        lambda z, y, x, c: (z + 1, y, x, c) if first <= z < Z_SIZE - 1 else None
    )


def pairs_up_below(last):
    return device_pairs(lambda z, y, x, c: (z + 1, y, x, c) if z <= last else None)


def pairs_down(last):
    return device_pairs(lambda z, y, x, c: (z - 1, y, x, c) if 1 <= z <= last else None)


def pairs_down_above(first):
    return device_pairs(lambda z, y, x, c: (z - 1, y, x, c) if z >= first else None)


def move(value, pairs):
    return lax.ppermute(value, MESH_AXES, pairs)


def line_gather(block, z):
    ups, downs = [None], [None]
    up = down = block
    for step in range(1, Z_SIZE):
        up = move(up, pairs_up(step - 1))
        down = move(down, pairs_down(Z_SIZE - step))
        ups.append(up)
        downs.append(down)
    blocks = [block] + [
        jnp.where(z >= s, ups[s], downs[Z_SIZE - s]) for s in range(1, Z_SIZE)
    ]
    return [(part, move(part, PAIRS_C)) for part in blocks]


def line_scatter(parts):
    low = jnp.bfloat16
    terms = [own + move(other.astype(low), PAIRS_C).astype(jnp.float32) for own, other in parts]

    def sent(value, pairs):
        return move(value.astype(low), pairs).astype(jnp.float32)

    up = terms[2] + sent(terms[1], pairs_up_below(0))
    down = terms[2] + sent(terms[3], pairs_down_above(3))
    up = terms[3] + sent(up, pairs_up_below(1))
    down = terms[1] + sent(down, pairs_down_above(2))
    return terms[0] + sent(up, pairs_up_below(2)) + sent(down, pairs_down_above(1))


def half_order(z_to):
    first = 10 * (z_to // 2)
    if z_to % 2 == 0:
        return [first, first + 1, first + 2, first + 3, first + 4]
    return [first + 6, first + 7, first + 8, first + 9, first + 5]


HALF_ORDER = [half_order(z_to) for z_to in range(Z_SIZE)]
HALF_PLACE = [0] * (Z_SIZE * 5)
for order_z in range(Z_SIZE):
    for order_q in range(5):
        HALF_PLACE[HALF_ORDER[order_z][order_q]] = order_z * 5 + order_q
UNIT_HALVES = ((0, 2), (2, 4), (4, 5))


def shift_exchange(chunks, z):
    own = lax.dynamic_index_in_dim(chunks, z, 0, keepdims=True)
    result = lax.dynamic_update_slice_in_dim(jnp.zeros_like(chunks), own, z, 0)
    for step in range(1, Z_SIZE):
        chunk = lax.dynamic_index_in_dim(chunks, (z + step) % Z_SIZE, 0, keepdims=True)
        got = move(chunk, pairs_shift(step))
        result = lax.dynamic_update_slice_in_dim(result, got, (z + Z_SIZE - step) % Z_SIZE, 0)
    return result


def gather_weights(gate_up_weight, down_weight, z):
    experts, rows = gate_up_weight.shape[0], gate_up_weight.shape[1]
    gate, upper = gate_up_weight[..., :FF], gate_up_weight[..., FF:]
    down_t = down_weight.transpose(0, 2, 1)
    half = FF // 2
    halves = jnp.concatenate(
        [part.reshape(experts, rows, 2, half) for part in (gate, upper, down_t)], axis=-1
    ).transpose(0, 2, 1, 3).reshape(2 * experts, rows, 3 * half)
    chunks = jnp.stack(
        [jnp.stack([halves[q] for q in HALF_ORDER[z_to]]) for z_to in range(Z_SIZE)]
    )
    mine = shift_exchange(chunks, z)
    mine = mine.transpose(1, 0, 2, 3).reshape(5, Z_SIZE * rows, 3 * half)
    own_units, other_units = [], []
    middle = Z_SIZE * rows // 2
    for first, last in UNIT_HALVES:
        piece = mine[first:last]
        from_y = move(piece, PAIRS_Y)
        from_x = move(piece, PAIRS_X)
        far_a = move(from_y[:, :middle], PAIRS_X)
        far_b = move(from_x[:, middle:], PAIRS_Y)
        own_units.append(jnp.concatenate([piece, from_y], axis=1))
        other_units.append(jnp.concatenate([from_x, far_a, far_b], axis=1))
    return other_units + own_units


def scatter_grads(other_grads, own_grads, z, rows):
    span = Z_SIZE * rows
    middle = span // 2
    low = jnp.bfloat16
    full = jnp.float32
    sums = []
    for other, own in zip(other_grads, own_grads):
        via_x = move(other[:, span : span + middle], PAIRS_X)
        via_y = move(other[:, span + middle :], PAIRS_Y)
        to_x = jnp.concatenate(
            [
                other[:, :middle],
                (other[:, middle:span].astype(full) + via_y.astype(full)).astype(low),
            ],
            axis=1,
        )
        to_y = jnp.concatenate(
            [
                (own[:, span : span + middle].astype(full) + via_x.astype(full)).astype(low),
                own[:, span + middle :],
            ],
            axis=1,
        )
        got_x = move(to_x, PAIRS_X)
        got_y = move(to_y, PAIRS_Y)
        sums.append(
            (own[:, :span].astype(full) + got_x.astype(full) + got_y.astype(full)).astype(low)
        )
    total = jnp.concatenate(sums, axis=0)
    chunks = total.reshape(5, Z_SIZE, rows, total.shape[-1]).transpose(1, 0, 2, 3)
    back = shift_exchange(chunks, z).reshape(Z_SIZE * 5, rows, total.shape[-1])
    return jnp.stack([back[HALF_PLACE[q]] for q in range(Z_SIZE * 5)]).astype(full)


def swap_features(value, y, rows):
    lead = value.shape[:-1]
    parts = value.reshape(*lead, Z_SIZE, Y_SIZE, rows)
    first = jnp.where(y == 0, parts[..., 0, :], parts[..., 1, :])
    second = jnp.where(y == 0, parts[..., 1, :], parts[..., 0, :])
    return jnp.concatenate(
        [first.reshape(*lead, Z_SIZE * rows), second.reshape(*lead, Z_SIZE * rows)], axis=-1
    )


def unswap_features(value, y, rows):
    lead = value.shape[:-1]
    first = value[..., : Z_SIZE * rows].reshape(*lead, Z_SIZE, rows)
    second = value[..., Z_SIZE * rows :].reshape(*lead, Z_SIZE, rows)
    even = jnp.where(y == 0, first, second)
    odd = jnp.where(y == 0, second, first)
    return jnp.stack([even, odd], axis=-2).reshape(*lead, Z_SIZE * Y_SIZE * rows)


def dense_gates(logits, chosen):
    peak = jnp.max(jnp.where(chosen, logits, -jnp.inf), axis=-1, keepdims=True)
    exponent = jnp.where(chosen, jnp.exp(logits - peak), 0.0)
    return exponent / jnp.sum(exponent, axis=-1, keepdims=True)


def expert_unit(weights, slot_rows, gate_rows, rows_in, grads_in):
    half = FF // 2
    low = jnp.bfloat16
    full = jnp.float32
    sources, length = slot_rows.shape
    width = rows_in.shape[-1]
    pick = slot_rows[:, None, :] == jnp.arange(WIDE, dtype=jnp.int32)[None, :, None]
    one_hot = pick.astype(low)
    picked = jnp.einsum("ist,itd->isd", one_hot, rows_in, preferred_element_type=full)
    picked = picked.astype(low).reshape(sources * WIDE, width)
    dys = jnp.einsum("ist,itd->isd", one_hot, grads_in, preferred_element_type=full)
    dys = dys.reshape(sources * WIDE, width)
    gate_of = jnp.sum(jnp.where(pick, gate_rows[:, None, :], 0.0), axis=-1).reshape(-1, 1)
    grad_rows = (residual_scale * gate_of * dys).astype(low)
    dys = dys.astype(low)
    produced = jnp.zeros((sources * WIDE, width), full)
    grad_copy = jnp.zeros((sources * WIDE, width), full)
    grad_gate = jnp.zeros((sources * WIDE,), full)
    grads = []
    for part in range(weights.shape[0]):
        gate_up_w = weights[part, :, : 2 * half]
        down_t = weights[part, :, 2 * half :]
        gate_up = jnp.dot(picked, gate_up_w, preferred_element_type=full)
        gate = gate_up[:, :half]
        upper = gate_up[:, half:]
        sigmoid = jax.nn.sigmoid(gate)
        swish = gate * sigmoid
        hidden_full = swish * upper
        hidden = hidden_full.astype(low)
        produced = produced + multiply_transposed(hidden, down_t)
        grad_plain = residual_scale * jnp.dot(dys, down_t, preferred_element_type=full)
        grad_gate = grad_gate + jnp.sum(hidden.astype(full) * grad_plain, axis=-1)
        grad_hidden = grad_plain * gate_of
        grad_gate_up = jnp.concatenate(
            [grad_hidden * upper * sigmoid * (1.0 + gate * (1.0 - sigmoid)), grad_hidden * swish],
            axis=-1,
        ).astype(low)
        grad_copy = grad_copy + multiply_transposed(grad_gate_up, gate_up_w)
        grads.append(
            jnp.concatenate(
                [contract_rows(picked, grad_gate_up), contract_rows(grad_rows, hidden)], axis=-1
            ).astype(low)
        )
    produced = (produced * gate_of).astype(low).reshape(sources, WIDE, width)
    grad_copy = grad_copy.astype(low).reshape(sources, WIDE, width)
    grad_gate = jnp.sum(jnp.where(pick, grad_gate.reshape(sources, WIDE, 1), 0.0), axis=1)
    return one_hot, produced, grad_copy, grad_gate, jnp.stack(grads)


def body(
    tokens,
    cotangent,
    lengths,
    routes,
    slots,
    first_gain,
    qkv_weight,
    out_weight,
    second_gain,
    router_weight,
    gate_up_weight,
    down_weight,
):
    low = jnp.bfloat16
    full = jnp.float32
    dp_index = lax.axis_index("dp")
    expert_index = lax.axis_index("expert")
    z, y = dp_index // Y_SIZE, dp_index % Y_SIZE
    x, c = expert_index // C_SIZE, expert_index % C_SIZE
    sequence_length = tokens.shape[0]
    width = tokens.shape[1]
    rows = gate_up_weight.shape[1]
    query_group = QUERY_HEADS // KEY_VALUE_HEADS
    query_width_total = QUERY_HEADS * HEAD_SIZE
    key_width_total = KEY_VALUE_HEADS * HEAD_SIZE
    length = lengths[0]

    chosen_by = routes[None, :, :] == jnp.arange(EXPERTS, dtype=jnp.int32)[:, None, None]
    slot_table = jnp.sum(jnp.where(chosen_by, slots[None, :, :] + 1, 0), axis=-1) - 1
    slot_tables = lax.all_gather(slot_table, MESH_AXES, axis=0, tiled=False)

    small = jnp.concatenate(
        [router_weight, first_gain[:, None], second_gain[:, None]], axis=1
    )
    small = jnp.pad(small, ((0, 0), (0, 128 - small.shape[1])))
    first_pack = lax.all_gather(
        jnp.concatenate([qkv_weight, small], axis=1), MESH_AXES, axis=0, tiled=True
    )
    out_t = lax.all_gather(out_weight.T, MESH_AXES, axis=0, tiled=True)
    qkv_full = first_pack[:, : qkv_weight.shape[1]]
    small_full = first_pack[:, qkv_weight.shape[1] :]
    router_full = small_full[:, :EXPERTS]
    gain_one = small_full[:, EXPERTS].astype(full)
    gain_two = small_full[:, EXPERTS + 1].astype(full)

    inputs = tokens.astype(full)
    inverse_one = rms_inverse(inputs)
    normal_one = inputs * inverse_one
    hidden_one = (normal_one * gain_one).astype(low)
    projected_rows = jnp.dot(hidden_one, qkv_full, preferred_element_type=full)
    cosine_table, sine_table = rope_tables(sequence_length)
    query_rows = rotate_pairs(
        projected_rows[:, :query_width_total].reshape(sequence_length, QUERY_HEADS, HEAD_SIZE),
        cosine_table,
        sine_table,
    ).astype(low)
    keys = rotate_pairs(
        projected_rows[:, query_width_total : query_width_total + key_width_total].reshape(
            sequence_length, KEY_VALUE_HEADS, HEAD_SIZE
        ),
        cosine_table,
        sine_table,
    ).astype(low)
    value_rows = (
        projected_rows[:, query_width_total + key_width_total :]
        .reshape(sequence_length, KEY_VALUE_HEADS, HEAD_SIZE)
        .astype(low)
    )
    row_index = jnp.arange(sequence_length)[:, None]
    column_index = jnp.arange(sequence_length)[None, :]
    allowed = (column_index <= row_index) & (column_index < length)

    def head_scores(head):
        head_query = lax.dynamic_slice_in_dim(query_rows, head * query_group, query_group, 1)
        head_key = lax.dynamic_index_in_dim(keys, head, 1, keepdims=False)
        head_value = lax.dynamic_index_in_dim(value_rows, head, 1, keepdims=False)
        scores = (
            jnp.einsum("qgd,kd->gqk", head_query, head_key, preferred_element_type=full)
            * score_scale
        )
        return (head_query, head_key, head_value, jnp.where(allowed[None], scores, masked_score))

    def attention_head_forward(head):
        head_query, head_key, head_value, scores = head_scores(head)
        peak = jnp.max(scores, axis=-1, keepdims=True)
        exponent = jnp.exp(scores - peak)
        total = jnp.sum(exponent, axis=-1, keepdims=True)
        weights = (exponent / total).astype(low)
        head_mixed = jnp.einsum(
            "gqk,kd->qgd", weights, head_value, preferred_element_type=full
        ).astype(low)
        return (head_mixed, (peak + jnp.log(total))[..., 0])

    mixed_head_output, log_sum_totals = lax.map(attention_head_forward, jnp.arange(KEY_VALUE_HEADS))
    mixed = mixed_head_output.transpose(1, 0, 2, 3).reshape(
        sequence_length, QUERY_HEADS * HEAD_SIZE
    )
    branch = multiply_transposed(mixed, out_t)
    middle = inputs + residual_scale * branch
    inverse_two = rms_inverse(middle)
    normal_two = middle * inverse_two
    hidden_two = (normal_two * gain_two).astype(low)
    grad_out = cotangent.astype(full)

    grad_blocks = line_gather(swap_features(cotangent, y, rows), z)
    row_blocks = line_gather(swap_features(hidden_two, y, rows), z)
    grads_in = jnp.stack([part for pair in grad_blocks for part in pair])
    rows_in = jnp.stack([part for pair in row_blocks for part in pair])
    sources = [
        device_index((z + Z_SIZE - s) % Z_SIZE, y, x, c if k == 0 else 1 - c)
        for s in range(Z_SIZE)
        for k in range(C_SIZE)
    ]
    slots_in = jnp.stack(
        [lax.dynamic_index_in_dim(slot_tables, source, 0, keepdims=False) for source in sources]
    )
    router_t = router_full.T
    logits_in = jnp.einsum(
        "ed,itd->iet", swap_features(router_t, y, rows), rows_in, preferred_element_type=full
    )
    chosen_in = slots_in >= 0
    peak_in = jnp.max(jnp.where(chosen_in, logits_in, -jnp.inf), axis=1, keepdims=True)
    exponent_in = jnp.where(chosen_in, jnp.exp(logits_in - peak_in), 0.0)
    gates_in = exponent_in / jnp.sum(exponent_in, axis=1, keepdims=True)

    units = gather_weights(gate_up_weight, down_weight, z)
    even = z % 2 == 0
    ids = []
    for group in (1 - x, x):
        base = EXPERTS // (X_SIZE * C_SIZE) * (group * C_SIZE + c) + 5 * (z // 2)
        ids += [base + jnp.where(even, 0, 3), base + jnp.where(even, 1, 4), base + 2]
    hots, outs, copies, gate_grads, weight_grads = [], [], [], [], []
    for unit, expert in zip(units, ids):
        hot, produced, grad_copy, grad_gate, grads = expert_unit(
            unit,
            lax.dynamic_index_in_dim(slots_in, expert, 1, keepdims=False),
            lax.dynamic_index_in_dim(gates_in, expert, 1, keepdims=False),
            rows_in,
            grads_in,
        )
        hots.append(hot)
        outs.append(produced)
        copies.append(grad_copy)
        gate_grads.append(grad_gate)
        weight_grads.append(grads)
    hot_all = jnp.concatenate(hots, axis=1)
    copy_parts = jnp.einsum(
        "ist,isd->itd", hot_all, jnp.concatenate(copies, axis=1), preferred_element_type=full
    )
    out_parts = jnp.einsum(
        "ist,isd->itd", hot_all, jnp.concatenate(outs, axis=1), preferred_element_type=full
    )
    expert_iota = jnp.arange(64, dtype=jnp.int32)[None, None, :]
    gate_parts = sum(
        jnp.where(expert_iota == expert, grad_gate[:, :, None], 0.0)
        for expert, grad_gate in zip(ids, gate_grads)
    )
    gate_high = gate_parts.astype(low).astype(full)
    copy_parts = jnp.concatenate([copy_parts, gate_high, gate_parts - gate_high], axis=-1)
    pairs_of = lambda parts: [(parts[2 * s], parts[2 * s + 1]) for s in range(Z_SIZE)]
    copy_sum = line_scatter(pairs_of(copy_parts))
    mixture = unswap_features(line_scatter(pairs_of(out_parts)), y, rows)
    output = (middle + residual_scale * mixture).astype(low)
    grad_gates = copy_sum[:, width : width + EXPERTS] + copy_sum[:, width + 64 : width + 64 + EXPERTS]
    copy_sum = unswap_features(copy_sum[:, :width], y, rows)

    chosen = (slot_table >= 0).T
    gates = dense_gates(jnp.dot(hidden_two, router_full, preferred_element_type=full), chosen)
    grad_logits = (
        gates * (grad_gates - jnp.sum(gates * grad_gates, axis=-1, keepdims=True))
    ).astype(low)
    grad_hidden_two = copy_sum + multiply_transposed(grad_logits, router_full)
    router_term = contract_rows(hidden_two, grad_logits)
    second_term, grad_norm_two = norm_backward(
        grad_hidden_two, normal_two, inverse_two, gain_two
    )
    grad_middle = grad_out + grad_norm_two
    branch_gradient = (residual_scale * grad_middle).astype(low)
    out_term = contract_rows(branch_gradient, mixed)
    grad_mixed = (
        jnp.dot(branch_gradient, out_t, preferred_element_type=full)
        .astype(low)
        .reshape(sequence_length, KEY_VALUE_HEADS, query_group, HEAD_SIZE)
    )

    def attention_head_backward(head):
        head_query, head_key, head_value, scores = head_scores(head)
        head_grad = lax.dynamic_index_in_dim(grad_mixed, head, 1, keepdims=False)
        head_total = lax.dynamic_index_in_dim(log_sum_totals, head, 0, keepdims=False)
        probs = jnp.exp(scores - head_total[..., None])
        grad_weights = jnp.einsum(
            "qgd,kd->gqk", head_grad, head_value, preferred_element_type=full
        )
        grad_scores = (
            probs * (grad_weights - jnp.sum(probs * grad_weights, axis=-1, keepdims=True))
        ).astype(low)
        grad_query = (
            jnp.einsum("gqk,kd->qgd", grad_scores, head_key, preferred_element_type=full)
            * score_scale
        )
        grad_key = (
            jnp.einsum("gqk,qgd->kd", grad_scores, head_query, preferred_element_type=full)
            * score_scale
        )
        grad_value = jnp.einsum(
            "gqk,qgd->kd", probs.astype(low), head_grad, preferred_element_type=full
        )
        return (grad_query, grad_key, grad_value)

    query_head_rows, key_head_rows, value_head_rows = lax.map(
        attention_head_backward, jnp.arange(KEY_VALUE_HEADS)
    )
    grad_query = unrotate(
        query_head_rows.transpose(1, 0, 2, 3).reshape(sequence_length, QUERY_HEADS, HEAD_SIZE),
        cosine_table,
        sine_table,
    )
    grad_key = unrotate(key_head_rows.transpose(1, 0, 2), cosine_table, sine_table)
    grad_value = value_head_rows.transpose(1, 0, 2)
    grad_projected = jnp.concatenate(
        [
            grad_query.reshape(sequence_length, query_width_total),
            grad_key.reshape(sequence_length, key_width_total),
            grad_value.reshape(sequence_length, key_width_total),
        ],
        axis=-1,
    ).astype(low)
    qkv_term = contract_rows(hidden_one, grad_projected)
    grad_hidden_one = multiply_transposed(grad_projected, qkv_full)
    first_term, grad_norm_one = norm_backward(
        grad_hidden_one, normal_one, inverse_one, gain_one
    )
    grad_input = grad_middle + grad_norm_one

    weight_sums = scatter_grads(weight_grads[:3], weight_grads[3:], z, rows)
    weight_sums = weight_sums.reshape(EXPERTS // (X_SIZE * C_SIZE), 2, rows, 3 * FF // 2)
    parts = [
        weight_sums[..., i * FF // 2 : (i + 1) * FF // 2].transpose(0, 2, 1, 3).reshape(-1, rows, FF)
        for i in range(3)
    ]
    gate_up_grads = jnp.concatenate(parts[:2], axis=-1)
    down_grads = parts[2].transpose(0, 2, 1)

    small_term = jnp.concatenate(
        [router_term, first_term[:, None], second_term[:, None]], axis=1
    )
    small_sum = lax.psum_scatter(small_term, MESH_AXES, scatter_dimension=0, tiled=True)
    out_sum = lax.psum_scatter(out_term.astype(low), MESH_AXES, scatter_dimension=0, tiled=True)
    qkv_sum = lax.psum_scatter(qkv_term.astype(low), MESH_AXES, scatter_dimension=0, tiled=True)
    return (
        output,
        grad_input,
        small_sum[:, EXPERTS],
        qkv_sum.astype(full),
        out_sum.astype(full).T,
        small_sum[:, EXPERTS + 1],
        small_sum[:, :EXPERTS],
        gate_up_grads,
        down_grads,
    )


def solution(mesh):
    in_specs = (
        P(("dp", "expert"), None),
        P(("dp", "expert"), None),
        P(("dp", "expert")),
        P(("dp", "expert"), None),
        P(("dp", "expert"), None),
        P(("dp", "expert")),
        P(("dp", "expert"), None),
        P(None, ("dp", "expert")),
        P(("dp", "expert")),
        P(("dp", "expert"), None),
        P("expert", "dp", None),
        P("expert", None, "dp"),
    )
    out_specs = (
        P(("dp", "expert"), None),
        P(("dp", "expert"), None),
        P(("dp", "expert")),
        P(("dp", "expert"), None),
        P(None, ("dp", "expert")),
        P(("dp", "expert")),
        P(("dp", "expert"), None),
        P("expert", "dp", None),
        P("expert", None, "dp"),
    )
    fits = mesh.shape["dp"] == Z_SIZE * Y_SIZE and mesh.shape["expert"] == X_SIZE * C_SIZE
    chosen = body if fits else general_body
    return jax.shard_map(chosen, mesh=mesh, in_specs=in_specs, out_specs=out_specs, check_vma=False)
```

```python
import functools

import jax
import jax.numpy as jnp
from jax import lax
from jax.experimental import pallas as pl
from jax.experimental.pallas import tpu as pltpu
from jax.sharding import PartitionSpec as P

QUERY_HEADS = 24
KEY_VALUE_HEADS = 8
HEAD_SIZE = 64
FF = 512
EXPERTS = 40
TOP = 8
CAP = 152


epsilon = 1e-06
residual_scale = 0.22
score_scale = 0.015625
rope_base = 10000.0
masked_score = -1e30


def rope_tables(length):
    half = HEAD_SIZE // 2
    freqs = jnp.power(rope_base, -2.0 * jnp.arange(half, dtype=jnp.float32) / HEAD_SIZE)
    angles = jnp.arange(length, dtype=jnp.float32)[:, None] * freqs[None, :]
    cosine_table = jnp.concatenate([jnp.cos(angles), jnp.cos(angles)], axis=-1)
    sine_table = jnp.concatenate([jnp.sin(angles), jnp.sin(angles)], axis=-1)
    return (cosine_table, sine_table)


def rotate_half(value_rows):
    half = value_rows.shape[-1] // 2
    return jnp.concatenate([-value_rows[..., half:], value_rows[..., :half]], axis=-1)


def rotate_pairs(value_rows, cosine_table, sine_table):
    return value_rows * cosine_table[:, None, :] + rotate_half(value_rows) * sine_table[:, None, :]


def unrotate(grads, cosine_table, sine_table):
    return grads * cosine_table[:, None, :] - rotate_half(grads * sine_table[:, None, :])


def rms_inverse(value_rows):
    return lax.rsqrt(jnp.mean(value_rows * value_rows, axis=-1, keepdims=True) + epsilon)


def norm_backward(grad_normed, normal, inverse, gain):
    gain_term = jnp.sum(grad_normed * normal, axis=0)
    scaled = grad_normed * gain
    grad_input = inverse * (scaled - normal * jnp.mean(scaled * normal, axis=-1, keepdims=True))
    return (gain_term, grad_input)


def contract_rows(left, right):
    return lax.dot_general(
        left, right, (((0,), (0,)), ((), ())), preferred_element_type=jnp.float32
    )


def multiply_transposed(left, right):
    return lax.dot_general(
        left, right, (((1,), (1,)), ((), ())), preferred_element_type=jnp.float32
    )


def fetch_expert(gate_up_shard, down_shard):
    return (
        lax.all_gather(gate_up_shard, "dp", axis=0, tiled=True),
        lax.all_gather(down_shard, "dp", axis=1, tiled=True),
    )


def gate_values(hidden_rows, router_full, route_rows):
    logits = jnp.dot(hidden_rows, router_full, preferred_element_type=jnp.float32)
    chosen_mask = route_rows[:, :, None] == jnp.arange(EXPERTS)[None, None, :]
    chosen = jnp.sum(jnp.where(chosen_mask, logits[:, None, :], 0.0), axis=-1)
    return (chosen_mask, jax.nn.softmax(chosen, axis=-1))


def general_body(
    tokens,
    cotangent,
    lengths,
    routes,
    slots,
    first_gain,
    qkv_weight,
    out_weight,
    second_gain,
    router_weight,
    gate_up_weight,
    down_weight,
):
    sequence_length = tokens.shape[0]
    width = tokens.shape[1]
    query_group = QUERY_HEADS // KEY_VALUE_HEADS
    length = lengths[0]
    gathered = (
        lax.all_gather(first_gain, ("dp", "expert"), axis=0, tiled=True),
        lax.all_gather(qkv_weight, ("dp", "expert"), axis=0, tiled=True),
        lax.all_gather(out_weight, ("dp", "expert"), axis=1, tiled=True),
        lax.all_gather(second_gain, ("dp", "expert"), axis=0, tiled=True),
        lax.all_gather(router_weight, ("dp", "expert"), axis=0, tiled=True),
    )
    gain_one, qkv_full, out_full, gain_two, router_full = gathered
    inputs = tokens.astype(jnp.float32)
    inverse_one = rms_inverse(inputs)
    normal_one = inputs * inverse_one
    hidden_one = (normal_one * gain_one.astype(jnp.float32)).astype(jnp.bfloat16)
    projected_rows = jnp.dot(hidden_one, qkv_full, preferred_element_type=jnp.float32)
    cosine_table, sine_table = rope_tables(sequence_length)
    query_width_total = QUERY_HEADS * HEAD_SIZE
    key_width_total = KEY_VALUE_HEADS * HEAD_SIZE
    query_rows = rotate_pairs(
        projected_rows[:, :query_width_total].reshape(sequence_length, QUERY_HEADS, HEAD_SIZE),
        cosine_table,
        sine_table,
    ).astype(jnp.bfloat16)
    keys = rotate_pairs(
        projected_rows[:, query_width_total : query_width_total + key_width_total].reshape(
            sequence_length, KEY_VALUE_HEADS, HEAD_SIZE
        ),
        cosine_table,
        sine_table,
    ).astype(jnp.bfloat16)
    value_rows = (
        projected_rows[:, query_width_total + key_width_total :]
        .reshape(sequence_length, KEY_VALUE_HEADS, HEAD_SIZE)
        .astype(jnp.bfloat16)
    )
    row_index = jnp.arange(sequence_length)[:, None]
    column_index = jnp.arange(sequence_length)[None, :]
    allowed = (column_index <= row_index) & (column_index < length)

    def head_scores(head):
        head_query = lax.dynamic_slice_in_dim(query_rows, head * query_group, query_group, 1)
        head_key = lax.dynamic_index_in_dim(keys, head, 1, keepdims=False)
        head_value = lax.dynamic_index_in_dim(value_rows, head, 1, keepdims=False)
        scores = (
            jnp.einsum("qgd,kd->gqk", head_query, head_key, preferred_element_type=jnp.float32)
            * score_scale
        )
        return (head_query, head_key, head_value, jnp.where(allowed[None], scores, masked_score))

    def attention_head_forward(head):
        head_query, head_key, head_value, scores = head_scores(head)
        peak = jnp.max(scores, axis=-1, keepdims=True)
        exponent = jnp.exp(scores - peak)
        total = jnp.sum(exponent, axis=-1, keepdims=True)
        weights = (exponent / total).astype(jnp.bfloat16)
        head_mixed = jnp.einsum(
            "gqk,kd->qgd", weights, head_value, preferred_element_type=jnp.float32
        ).astype(jnp.bfloat16)
        return (head_mixed, (peak + jnp.log(total))[..., 0])

    mixed_head_output, log_sum_totals = lax.map(attention_head_forward, jnp.arange(KEY_VALUE_HEADS))
    mixed = mixed_head_output.transpose(1, 0, 2, 3).reshape(
        sequence_length, QUERY_HEADS * HEAD_SIZE
    )
    branch = jnp.dot(mixed, out_full, preferred_element_type=jnp.float32)
    middle = inputs + residual_scale * branch
    inverse_two = rms_inverse(middle)
    normal_two = middle * inverse_two
    hidden_two = (normal_two * gain_two.astype(jnp.float32)).astype(jnp.bfloat16)
    chosen_mask, gates = gate_values(hidden_two, router_full, routes)
    grad_out = cotangent.astype(jnp.float32)
    grad_mixture = residual_scale * grad_out

    def expert_forward(carry, pieces):
        rows, gate_up_shard, down_shard = pieces
        gate_up_full, down_full = fetch_expert(gate_up_shard, down_shard)
        gate_up = jnp.dot(rows, gate_up_full, preferred_element_type=jnp.float32)
        hidden = (jax.nn.silu(gate_up[:, :FF]) * gate_up[:, FF:]).astype(jnp.bfloat16)
        return (
            carry,
            jnp.dot(hidden, down_full, preferred_element_type=jnp.float32).astype(jnp.bfloat16),
        )

    copies = jnp.broadcast_to(hidden_two[:, None, :], (sequence_length, TOP, width))
    outgoing = jnp.zeros((EXPERTS, CAP, width), jnp.bfloat16).at[routes, slots].set(copies)
    received = lax.all_to_all(outgoing, "expert", split_axis=0, concat_axis=1, tiled=True)
    _, produced = lax.scan(expert_forward, None, (received, gate_up_weight, down_weight))
    returned = lax.all_to_all(produced, "expert", split_axis=1, concat_axis=0, tiled=True)
    expert_rows = returned[routes, slots].astype(jnp.float32)
    mixture = jnp.sum(gates[:, :, None] * expert_rows, axis=1)
    grad_gates = jnp.sum(expert_rows * grad_mixture[:, None, :], axis=-1)
    grad_rows = (gates[:, :, None] * grad_mixture[:, None, :]).astype(jnp.bfloat16)
    outgoing_grad = jnp.zeros((EXPERTS, CAP, width), jnp.bfloat16).at[routes, slots].set(grad_rows)
    grad_received = lax.all_to_all(outgoing_grad, "expert", split_axis=0, concat_axis=1, tiled=True)
    output = (middle + residual_scale * mixture).astype(jnp.bfloat16)
    again = (
        lax.all_gather(first_gain, ("dp", "expert"), axis=0, tiled=True),
        lax.all_gather(qkv_weight, ("dp", "expert"), axis=0, tiled=True),
        lax.all_gather(out_weight, ("dp", "expert"), axis=1, tiled=True),
        lax.all_gather(second_gain, ("dp", "expert"), axis=0, tiled=True),
        lax.all_gather(router_weight, ("dp", "expert"), axis=0, tiled=True),
    )
    gain_back, qkv_back, output_gradient, gain_two_back, router_back = again
    grad_chosen = gates * (grad_gates - jnp.sum(gates * grad_gates, axis=-1, keepdims=True))
    grad_logits = jnp.sum(jnp.where(chosen_mask, grad_chosen[:, :, None], 0.0), axis=1).astype(
        jnp.bfloat16
    )

    def expert_backward(carry, pieces):
        rows, grad_produced, gate_up_shard, down_shard = pieces
        gate_up_full, down_full = fetch_expert(gate_up_shard, down_shard)
        gate_up = jnp.dot(rows, gate_up_full, preferred_element_type=jnp.float32)
        gate = gate_up[:, :FF]
        upper = gate_up[:, FF:]
        sigmoid = jax.nn.sigmoid(gate)
        swish = gate * sigmoid
        hidden = (swish * upper).astype(jnp.bfloat16)
        grad_hidden = multiply_transposed(grad_produced, down_full)
        grad_gate_up = jnp.concatenate(
            [grad_hidden * upper * sigmoid * (1.0 + gate * (1.0 - sigmoid)), grad_hidden * swish],
            axis=-1,
        ).astype(jnp.bfloat16)
        grad_copy = multiply_transposed(grad_gate_up, gate_up_full).astype(jnp.bfloat16)
        gate_up_part = lax.psum_scatter(
            contract_rows(rows, grad_gate_up).astype(jnp.bfloat16),
            "dp",
            scatter_dimension=0,
            tiled=True,
        ).astype(jnp.float32)
        down_part = lax.psum_scatter(
            contract_rows(grad_produced, hidden).astype(jnp.bfloat16),
            "dp",
            scatter_dimension=0,
            tiled=True,
        ).astype(jnp.float32)
        return (carry, (grad_copy, gate_up_part, down_part.T))

    _, (grad_copies, gate_up_grads, down_grads) = lax.scan(
        expert_backward, None, (received, grad_received, gate_up_weight, down_weight)
    )
    grad_back = lax.all_to_all(grad_copies, "expert", split_axis=1, concat_axis=0, tiled=True)
    copy_sum = jnp.sum(grad_back[routes, slots].astype(jnp.float32), axis=1)
    grad_hidden_two = copy_sum + multiply_transposed(grad_logits, router_back)
    router_term = contract_rows(hidden_two, grad_logits)
    second_term, grad_norm_two = norm_backward(
        grad_hidden_two, normal_two, inverse_two, gain_two_back.astype(jnp.float32)
    )
    grad_middle = grad_out + grad_norm_two
    branch_gradient = (residual_scale * grad_middle).astype(jnp.bfloat16)
    out_term = contract_rows(mixed, branch_gradient)
    grad_mixed = (
        multiply_transposed(branch_gradient, output_gradient)
        .astype(jnp.bfloat16)
        .reshape(sequence_length, KEY_VALUE_HEADS, query_group, HEAD_SIZE)
    )

    def attention_head_backward(head):
        head_query, head_key, head_value, scores = head_scores(head)
        head_grad = lax.dynamic_index_in_dim(grad_mixed, head, 1, keepdims=False)
        head_total = lax.dynamic_index_in_dim(log_sum_totals, head, 0, keepdims=False)
        probs = jnp.exp(scores - head_total[..., None])
        grad_weights = jnp.einsum(
            "qgd,kd->gqk", head_grad, head_value, preferred_element_type=jnp.float32
        )
        grad_scores = (
            probs * (grad_weights - jnp.sum(probs * grad_weights, axis=-1, keepdims=True))
        ).astype(jnp.bfloat16)
        grad_query = (
            jnp.einsum("gqk,kd->qgd", grad_scores, head_key, preferred_element_type=jnp.float32)
            * score_scale
        )
        grad_key = (
            jnp.einsum("gqk,qgd->kd", grad_scores, head_query, preferred_element_type=jnp.float32)
            * score_scale
        )
        grad_value = jnp.einsum(
            "gqk,qgd->kd", probs.astype(jnp.bfloat16), head_grad, preferred_element_type=jnp.float32
        )
        return (grad_query, grad_key, grad_value)

    query_head_rows, key_head_rows, value_head_rows = lax.map(
        attention_head_backward, jnp.arange(KEY_VALUE_HEADS)
    )
    grad_query = unrotate(
        query_head_rows.transpose(1, 0, 2, 3).reshape(sequence_length, QUERY_HEADS, HEAD_SIZE),
        cosine_table,
        sine_table,
    )
    grad_key = unrotate(key_head_rows.transpose(1, 0, 2), cosine_table, sine_table)
    grad_value = value_head_rows.transpose(1, 0, 2)
    grad_projected = jnp.concatenate(
        [
            grad_query.reshape(sequence_length, query_width_total),
            grad_key.reshape(sequence_length, key_width_total),
            grad_value.reshape(sequence_length, key_width_total),
        ],
        axis=-1,
    ).astype(jnp.bfloat16)
    qkv_term = contract_rows(hidden_one, grad_projected)
    grad_hidden_one = multiply_transposed(grad_projected, qkv_back)
    first_term, grad_norm_one = norm_backward(
        grad_hidden_one, normal_one, inverse_one, gain_back.astype(jnp.float32)
    )
    grad_input = grad_middle + grad_norm_one
    summed = (
        lax.psum_scatter(first_term, ("dp", "expert"), scatter_dimension=0, tiled=True),
        lax.psum_scatter(qkv_term, ("dp", "expert"), scatter_dimension=0, tiled=True),
        lax.psum_scatter(out_term, ("dp", "expert"), scatter_dimension=1, tiled=True),
        lax.psum_scatter(second_term, ("dp", "expert"), scatter_dimension=0, tiled=True),
        lax.psum_scatter(router_term, ("dp", "expert"), scatter_dimension=0, tiled=True),
    )
    return (
        output,
        grad_input,
        summed[0],
        summed[1],
        summed[2],
        summed[3],
        summed[4],
        gate_up_grads,
        down_grads,
    )


WIDE = 160
Z_SIZE, Y_SIZE, X_SIZE, C_SIZE = 4, 2, 2, 2
MESH_AXES = ("dp", "expert")


def device_index(z, y, x, c):
    return ((z * Y_SIZE + y) * X_SIZE + x) * C_SIZE + c


def device_pairs(target):
    pairs = []
    for z in range(Z_SIZE):
        for y in range(Y_SIZE):
            for x in range(X_SIZE):
                for c in range(C_SIZE):
                    to = target(z, y, x, c)
                    if to is not None:
                        pairs.append((device_index(z, y, x, c), device_index(*to)))
    return pairs


PAIRS_X = device_pairs(lambda z, y, x, c: (z, y, 1 - x, c))
PAIRS_Y = device_pairs(lambda z, y, x, c: (z, 1 - y, x, c))
PAIRS_C = device_pairs(lambda z, y, x, c: (z, y, x, 1 - c))


def pairs_shift(step):
    return device_pairs(lambda z, y, x, c: ((z + step) % Z_SIZE, y, x, c))


def pairs_up(first):
    return device_pairs(
        lambda z, y, x, c: (z + 1, y, x, c) if first <= z < Z_SIZE - 1 else None
    )


def pairs_up_below(last):
    return device_pairs(lambda z, y, x, c: (z + 1, y, x, c) if z <= last else None)


def pairs_down(last):
    return device_pairs(lambda z, y, x, c: (z - 1, y, x, c) if 1 <= z <= last else None)


def pairs_down_above(first):
    return device_pairs(lambda z, y, x, c: (z - 1, y, x, c) if z >= first else None)


def tie_kernel(*refs):
    del refs


def tie(value, *after):
    any_spec = pl.BlockSpec(memory_space=pl.ANY)
    return pl.pallas_call(
        tie_kernel,
        in_specs=[any_spec] * (1 + len(after)),
        out_specs=any_spec,
        out_shape=jax.ShapeDtypeStruct(value.shape, value.dtype),
        input_output_aliases={0: 0},
        name="tie",
    )(value, *after)


def join_kernel(*refs):
    refs[-1][...] = jnp.zeros_like(refs[-1])


class Rounds:
    def __init__(self):
        self.token = None

    def gate(self, value):
        return value if self.token is None else tie(value, self.token)

    def after(self):
        return () if self.token is None else (self.token,)

    def close(self, *arrays):
        arrays = list(arrays) + list(self.after())
        self.token = pl.pallas_call(
            join_kernel,
            in_specs=[pl.BlockSpec(memory_space=pl.ANY)] * len(arrays),
            out_specs=pl.BlockSpec(memory_space=pltpu.VMEM),
            out_shape=jax.ShapeDtypeStruct((8, 128), jnp.float32),
            name="join",
        )(*arrays)


def move(value, pairs):
    return lax.ppermute(value, MESH_AXES, pairs)


def line_hop(step, up, down):
    return move(up, pairs_up(step - 1)), move(down, pairs_down(Z_SIZE - step))


def rows_kernel(info, own, u1, u2, u3, d1, d2, d3, *rest):
    other, out, sem = rest[:7], rest[7], rest[8]
    z = info[0]
    mine = (own, u1, u2, u3, d1, d2, d3)
    waits = []
    for k, parts in enumerate((other, mine)):
        ups, downs = parts[1:4], parts[4:7]
        target = out.at[k * Z_SIZE]
        first = pltpu.make_async_copy(parts[0], target, sem.at[k * Z_SIZE])
        first.start()
        waits.append(first)
        for s in range(1, Z_SIZE):
            target = out.at[k * Z_SIZE + s]
            below = pltpu.make_async_copy(ups[s - 1], target, sem.at[k * Z_SIZE + s])
            above = pltpu.make_async_copy(downs[Z_SIZE - s - 1], target, sem.at[k * Z_SIZE + s])
            pl.when(z >= s)(below.start)
            pl.when(z < s)(above.start)
            waits.append(below)
    for copy in waits:
        copy.wait()


def line_blocks(z, mine, other):
    any_spec = pl.BlockSpec(memory_space=pl.ANY)
    block = mine[0]
    return pl.pallas_call(
        rows_kernel,
        grid_spec=pltpu.PrefetchScalarGridSpec(
            num_scalar_prefetch=1,
            grid=(),
            in_specs=[any_spec] * 14,
            out_specs=pl.BlockSpec(memory_space=pltpu.VMEM),
            scratch_shapes=[pltpu.SemaphoreType.DMA((2 * Z_SIZE,))],
        ),
        out_shape=jax.ShapeDtypeStruct((2 * Z_SIZE, *block.shape), block.dtype),
        cost_estimate=pl.CostEstimate(
            flops=0, bytes_accessed=32 * block.size, transcendentals=0
        ),
        compiler_params=pltpu.CompilerParams(vmem_limit_bytes=32 * 1024 * 1024),
        name="line_blocks",
    )(z[None], *mine, *other)


def dense_kernel(info, *refs):
    pieces, out, sem = refs[:10], refs[10], refs[11]
    y, x, c = info[0], info[1], info[2]
    zs = Z_SIZE // 2
    copies = []
    for k in range(2):
        at_c = c if k == 0 else 1 - c
        block, from_x, from_y, far_a, far_b = pieces[5 * k : 5 * k + 5]
        targets = [
            (block, out.at[:, y, x, at_c]),
            (from_x, out.at[:, y, 1 - x, at_c]),
            (from_y, out.at[:, 1 - y, x, at_c]),
            (far_a, out.at[pl.ds(0, zs), 1 - y, 1 - x, at_c]),
            (far_b, out.at[pl.ds(zs, zs), 1 - y, 1 - x, at_c]),
        ]
        for piece, target in targets:
            copies.append(pltpu.make_async_copy(piece, target, sem.at[len(copies)]))
    for copy in copies:
        copy.start()
    for copy in copies:
        copy.wait()


def dense_assemble(place, mine, other):
    z, y, x, c = place
    any_spec = pl.BlockSpec(memory_space=pl.ANY)
    block = mine[0]
    rows, n = block.shape[1:]
    full = pl.pallas_call(
        dense_kernel,
        grid_spec=pltpu.PrefetchScalarGridSpec(
            num_scalar_prefetch=1,
            grid=(),
            in_specs=[any_spec] * 10,
            out_specs=pl.BlockSpec(memory_space=pltpu.VMEM),
            scratch_shapes=[pltpu.SemaphoreType.DMA((10,))],
        ),
        out_shape=jax.ShapeDtypeStruct((Z_SIZE, Y_SIZE, X_SIZE, C_SIZE, rows, n), block.dtype),
        cost_estimate=pl.CostEstimate(
            flops=0, bytes_accessed=32 * block.size, transcendentals=0
        ),
        compiler_params=pltpu.CompilerParams(vmem_limit_bytes=32 * 1024 * 1024),
        name="dense_assemble",
    )(jnp.stack([y, x, c]), *mine, *other)
    return full.reshape(-1, n)


def half_order(z_to):
    first = 10 * (z_to // 2)
    if z_to % 2 == 0:
        return [first, first + 1, first + 2, first + 3, first + 4]
    return [first + 6, first + 7, first + 8, first + 9, first + 5]


HALF_ORDER = [half_order(z_to) for z_to in range(Z_SIZE)]
HALF_PLACE = [0] * (Z_SIZE * 5)
for order_z in range(Z_SIZE):
    for order_q in range(5):
        HALF_PLACE[HALF_ORDER[order_z][order_q]] = order_z * 5 + order_q
UNIT_HALVES = ((0, 2), (2, 4), (4, 5))


def dense_gates(logits, chosen):
    peak = jnp.max(jnp.where(chosen, logits, -jnp.inf), axis=-1, keepdims=True)
    exponent = jnp.where(chosen, jnp.exp(logits - peak), 0.0)
    return exponent / jnp.sum(exponent, axis=-1, keepdims=True)


def mm(left, right):
    return jnp.dot(left, right, preferred_element_type=jnp.float32)


def weight_loads(pieces, w_s, sem, y):
    zs = Z_SIZE // 2
    count = len(pieces) // w_s.shape[0]
    copies = []
    for h in range(w_s.shape[0]):
        places = [w_s.at[h, :, y]]
        if count == 2:
            places.append(w_s.at[h, :, 1 - y])
        else:
            places += [w_s.at[h, pl.ds(0, zs), 1 - y], w_s.at[h, pl.ds(zs, zs), 1 - y]]
        for piece, place in zip(pieces[h * count : (h + 1) * count], places):
            copies.append(pltpu.make_async_copy(piece, place, sem.at[len(copies)]))
    return copies


def expert_forward_kernel(info, slots, gates, rows, *rest, count, waits):
    pieces = rest[:count]
    out, kept, gate_up_out, w_s, in_sem = rest[count + waits :]
    low = jnp.bfloat16
    step = pl.program_id(0)
    half = FF // 2
    halves = w_s.shape[0]
    loads = weight_loads(pieces, w_s, in_sem, info[0])

    @pl.when(step == 0)
    def _():
        for load in loads:
            load.start()

    group, length, width = rows.shape
    span = group * WIDE
    iota = lax.broadcasted_iota(jnp.int32, (WIDE, length), 0)
    gate_cols = []
    for j in range(group):
        pick = iota == slots[j]
        one_hot = jnp.where(pick, 1.0, 0.0).astype(low)
        gate_cols.append(jnp.sum(jnp.where(pick, gates[j], 0.0), axis=1, keepdims=True))
        kept[j * WIDE : (j + 1) * WIDE, :] = mm(one_hot, rows[j]).astype(low)
    gate_col = jnp.concatenate(gate_cols, axis=0)

    @pl.when(step == 0)
    def _():
        for load in loads:
            load.wait()

    produced = None
    for h in range(halves):
        gate_up_w = w_s[h, :, :, :, : 2 * half].reshape(width, 2 * half)
        down_t = w_s[h, :, :, :, 2 * half :].reshape(width, half)
        gate_up = mm(kept[...], gate_up_w)
        gate_up_out[:, 2 * h * half : 2 * (h + 1) * half] = gate_up
        gate = gate_up[:, :half]
        hidden = (gate * (1.0 / (1.0 + jnp.exp(-gate))) * gate_up[:, half:]).astype(low)
        term = multiply_transposed(hidden, down_t)
        produced = term if produced is None else produced + term
    out[...] = (produced * gate_col).astype(low).reshape(group, WIDE, width)


def expert_forward(place, halves, y, slots, gates, rows_in, pieces, buffer, after):
    sources, length, width = rows_in.shape
    _, rows, lanes = pieces[0].shape
    half = FF // 2
    low = jnp.bfloat16
    group = 2
    units = 2 * len(UNIT_HALVES)
    any_spec = pl.BlockSpec(memory_space=pl.ANY)
    row_spec = pl.BlockSpec((group, 1, length), lambda i, info: (i, 0, 0))
    waits = list(after)
    aliases = {}
    if buffer is not None:
        aliases = {4 + len(pieces): 0}
        waits = [buffer] + waits
    total = sources * WIDE
    span = group * WIDE
    return pl.pallas_call(
        functools.partial(expert_forward_kernel, count=len(pieces), waits=len(waits)),
        grid_spec=pltpu.PrefetchScalarGridSpec(
            num_scalar_prefetch=1,
            grid=(sources // group,),
            in_specs=[
                row_spec,
                row_spec,
                pl.BlockSpec((group, length, width), lambda i, info: (i, 0, 0)),
            ]
            + [any_spec] * (len(pieces) + len(waits)),
            out_specs=[
                pl.BlockSpec((group, WIDE, width), lambda i, info: (i, place, 0)),
                pl.BlockSpec((span, width), lambda i, info: (i, 0)),
                pl.BlockSpec((span, 2 * half * halves), lambda i, info: (i, 0)),
            ],
            scratch_shapes=[
                pltpu.VMEM((halves, Z_SIZE, Y_SIZE, rows, lanes), low),
                pltpu.SemaphoreType.DMA((6,)),
            ],
        ),
        out_shape=[
            jax.ShapeDtypeStruct((sources, units * WIDE, width), low),
            jax.ShapeDtypeStruct((total, width), low),
            jax.ShapeDtypeStruct((total, 2 * half * halves), jnp.float32),
        ],
        input_output_aliases=aliases,
        compiler_params=pltpu.CompilerParams(vmem_limit_bytes=48 * 1024 * 1024),
        cost_estimate=pl.CostEstimate(
            flops=2 * total * width * (3 * half * halves + length),
            bytes_accessed=2 * (sources * length * width + 2 * total * width)
            + 8 * total * half * halves
            + 2 * halves * width * lanes,
            transcendentals=total * half * halves,
        ),
        name="expert_forward",
    )(y, slots, gates, rows_in, *pieces, *waits)


def expert_back_kernel(info, slots, gates, dys, kept, gate_ups, *rest, count, waits):
    pieces = rest[:count]
    back, near_a_g, near_b_g, far_a_g, far_b_g = rest[count + waits : count + waits + 5]
    w_s, x_s, gd_s, dgu_s, hid_s, g_s, in_sem, out_sem = rest[count + waits + 5 :]
    low = jnp.bfloat16
    full = jnp.float32
    step = pl.program_id(0)
    y = info[0]
    expert = info[1]
    half = FF // 2
    zs = Z_SIZE // 2
    halves = w_s.shape[0]
    loads = weight_loads(pieces, w_s, in_sem, y)

    @pl.when(step == 0)
    def _():
        for load in loads:
            load.start()

    group, length, width = dys.shape
    span = group * WIDE
    here = pl.ds(pl.multiple_of(step * span, span), span)
    iota = lax.broadcasted_iota(jnp.int32, (WIDE, length), 0)
    gate_cols = []
    dy_parts = []
    for j in range(group):
        pick = iota == slots[j]
        one_hot = jnp.where(pick, 1.0, 0.0).astype(low)
        gate_col = jnp.sum(jnp.where(pick, gates[j], 0.0), axis=1, keepdims=True)
        at = pl.multiple_of(step * span + j * WIDE, WIDE)
        dy = mm(one_hot, dys[j])
        gd_s[pl.ds(at, WIDE), :] = (dy * (residual_scale * gate_col)).astype(low)
        dy_parts.append(dy.astype(low))
        gate_cols.append(gate_col)
    dy = jnp.concatenate(dy_parts, axis=0)
    gate_col = jnp.concatenate(gate_cols, axis=0)
    x_s[here, :] = kept[...]

    @pl.when(step == 0)
    def _():
        for load in loads:
            load.wait()

    grad_copy = None
    grad_gate = None
    for h in range(halves):
        gate_up_w = w_s[h, :, :, :, : 2 * half].reshape(width, 2 * half)
        down_t = w_s[h, :, :, :, 2 * half :].reshape(width, half)
        gate = gate_ups[:, 2 * h * half : (2 * h + 1) * half]
        upper = gate_ups[:, (2 * h + 1) * half : (2 * h + 2) * half]
        sigmoid = 1.0 / (1.0 + jnp.exp(-gate))
        swish = gate * sigmoid
        hidden = (swish * upper).astype(low)
        hid_s[here, h * half : (h + 1) * half] = hidden
        grad_plain = residual_scale * mm(dy, down_t)
        term = jnp.sum(hidden.astype(full) * grad_plain, axis=1, keepdims=True)
        grad_gate = term if grad_gate is None else grad_gate + term
        grad_hidden = grad_plain * gate_col
        dgu_s[here, 2 * h * half : (2 * h + 1) * half] = (
            grad_hidden * upper * sigmoid * (1.0 + gate * (1.0 - sigmoid))
        ).astype(low)
        dgu_s[here, (2 * h + 1) * half : (2 * h + 2) * half] = (grad_hidden * swish).astype(low)
        term = multiply_transposed(dgu_s[here, 2 * h * half : 2 * (h + 1) * half], gate_up_w)
        grad_copy = term if grad_copy is None else grad_copy + term
    back[:, :, :width] = grad_copy.astype(low).reshape(group, WIDE, width)
    lane = lax.broadcasted_iota(jnp.int32, (span, 128), 1)
    high = grad_gate.astype(low).astype(full)
    extra = jnp.where(lane == expert, high, 0.0) + jnp.where(
        lane == expert + 64, grad_gate - high, 0.0
    )
    back[:, :, width:] = extra.astype(low).reshape(group, WIDE, 128)

    @pl.when(step == pl.num_programs(0) - 1)
    def _():
        piece = width // Z_SIZE
        for h in range(halves):
            for zz in range(Z_SIZE):
                cols = slice(zz * piece, (zz + 1) * piece)
                got = contract_rows(x_s[:, cols], dgu_s[:, 2 * h * half : 2 * (h + 1) * half])
                g_s[h, zz, :, :, : 2 * half] = got.astype(low).reshape(2, piece // 2, 2 * half)
                got = contract_rows(gd_s[:, cols], hid_s[:, h * half : (h + 1) * half])
                g_s[h, zz, :, :, 2 * half :] = got.astype(low).reshape(2, piece // 2, half)
        stores = [
            (g_s.at[:, pl.ds(0, zs), y], near_a_g),
            (g_s.at[:, pl.ds(zs, zs), y], near_b_g),
            (g_s.at[:, pl.ds(0, zs), 1 - y], far_a_g),
            (g_s.at[:, pl.ds(zs, zs), 1 - y], far_b_g),
        ]
        stores = [pltpu.make_async_copy(a, b, out_sem.at[i]) for i, (a, b) in enumerate(stores)]
        for store in stores:
            store.start()
        for store in stores:
            store.wait()


def expert_backward(
    place, halves, info, slots, gates, grads_in, kept, gate_ups, pieces, buffer, after
):
    sources, length, width = grads_in.shape
    _, rows, lanes = pieces[0].shape
    half = FF // 2
    low = jnp.bfloat16
    group = 2
    units = 2 * len(UNIT_HALVES)
    any_spec = pl.BlockSpec(memory_space=pl.ANY)
    row_spec = pl.BlockSpec((group, 1, length), lambda i, info: (i, 0, 0))
    waits = list(after)
    aliases = {}
    if buffer is not None:
        aliases = {6 + len(pieces): 0}
        waits = [buffer] + waits
    total = sources * WIDE
    span = group * WIDE
    quarter = (halves, Z_SIZE // 2, rows, lanes)
    result = pl.pallas_call(
        functools.partial(expert_back_kernel, count=len(pieces), waits=len(waits)),
        grid_spec=pltpu.PrefetchScalarGridSpec(
            num_scalar_prefetch=1,
            grid=(sources // group,),
            in_specs=[
                row_spec,
                row_spec,
                pl.BlockSpec((group, length, width), lambda i, info: (i, 0, 0)),
                pl.BlockSpec((span, width), lambda i, info: (i, 0)),
                pl.BlockSpec((span, 2 * half * halves), lambda i, info: (i, 0)),
            ]
            + [any_spec] * (len(pieces) + len(waits)),
            out_specs=[
                pl.BlockSpec((group, WIDE, width + 128), lambda i, info: (i, place, 0)),
            ]
            + [any_spec] * 4,
            scratch_shapes=[
                pltpu.VMEM((halves, Z_SIZE, Y_SIZE, rows, lanes), low),
                pltpu.VMEM((total, width), low),
                pltpu.VMEM((total, width), low),
                pltpu.VMEM((total, 2 * half * halves), low),
                pltpu.VMEM((total, half * halves), low),
                pltpu.VMEM((halves, Z_SIZE, Y_SIZE, rows, lanes), low),
                pltpu.SemaphoreType.DMA((6,)),
                pltpu.SemaphoreType.DMA((4,)),
            ],
        ),
        out_shape=[jax.ShapeDtypeStruct((sources, units * WIDE, width + 128), low)]
        + [jax.ShapeDtypeStruct(quarter, low)] * 4,
        input_output_aliases=aliases,
        compiler_params=pltpu.CompilerParams(vmem_limit_bytes=60 * 1024 * 1024),
        cost_estimate=pl.CostEstimate(
            flops=2 * total * width * (6 * half * halves + length),
            bytes_accessed=2 * (sources * length * width + 2 * total * width)
            + 8 * total * half * halves
            + 4 * halves * width * lanes,
            transcendentals=total * half * halves,
        ),
        name="expert_backward",
    )(info, slots, gates, grads_in, kept, gate_ups, *pieces, *waits)
    return result[0], result[1:]


def turn_halves(value):
    lanes = value.shape[-1]
    lane = lax.broadcasted_iota(jnp.int32, value.shape, 1)
    ahead = pltpu.roll(value, lanes - HEAD_SIZE // 2, 1)
    behind = pltpu.roll(value, HEAD_SIZE // 2, 1)
    return jnp.where(lane % HEAD_SIZE < HEAD_SIZE // 2, -ahead, behind)


def heads_of(value, first, count):
    return jnp.concatenate(
        [value[:, (first + i) * HEAD_SIZE : (first + i + 1) * HEAD_SIZE] for i in range(count)],
        axis=0,
    )


ROW_BLOCK = 128
PAIR = 2
GROUP = QUERY_HEADS // KEY_VALUE_HEADS
QUERY_LANES = PAIR * GROUP * HEAD_SIZE
KEY_LANES = PAIR * HEAD_SIZE


def block_mask(block, length):
    shape = (ROW_BLOCK, (block + 1) * ROW_BLOCK)
    row = lax.broadcasted_iota(jnp.int32, shape, 0) + block * ROW_BLOCK
    column = lax.broadcasted_iota(jnp.int32, shape, 1)
    allowed = jnp.where((column <= row) & (column < length), 1, 0)
    return jnp.concatenate([allowed] * GROUP, axis=0) > 0


def attention_kernel(
    length, tokens, gain, wq, wk, wv, cosine, sine, *rest
):
    h1, q, k, v, mixed, lse, h_s, lse_s = rest[-8:]
    step = pl.program_id(0)
    low = jnp.bfloat16
    rows = tokens.shape[0]

    @pl.when(step == 0)
    def _():
        value = tokens[...].astype(jnp.float32)
        hidden = (value * rms_inverse(value) * gain[...]).astype(low)
        h_s[...] = hidden
        h1[...] = hidden

    lane = lax.broadcasted_iota(jnp.int32, (rows, 128), 1)
    cos = cosine[...]
    sin = sine[...]
    query = mm(h_s[...], wq[...])
    query = (query * cos + turn_halves(query) * sin).astype(low)
    key = mm(h_s[...], wk[...])
    key = (key * cos[:, :KEY_LANES] + turn_halves(key) * sin[:, :KEY_LANES]).astype(low)
    value = mm(h_s[...], wv[...]).astype(low)
    q[...] = query
    k[...] = key
    v[...] = value
    blocks = rows // ROW_BLOCK
    totals = [[] for _ in range(PAIR * GROUP)]
    masks = [block_mask(block, length[0]) for block in range(blocks)]
    outs = [[] for _ in range(PAIR * GROUP)]
    for head in range(PAIR):
        key_h = key[:, head * HEAD_SIZE : (head + 1) * HEAD_SIZE]
        value_h = value[:, head * HEAD_SIZE : (head + 1) * HEAD_SIZE]
        for block in range(blocks):
            keys = (block + 1) * ROW_BLOCK
            query_h = heads_of(
                query[block * ROW_BLOCK : (block + 1) * ROW_BLOCK], head * GROUP, GROUP
            )
            scores = multiply_transposed(query_h, key_h[:keys]) * score_scale
            scores = jnp.where(masks[block], scores, masked_score)
            peak = jnp.max(scores, axis=1, keepdims=True)
            exponent = jnp.exp(scores - peak)
            total = jnp.sum(exponent, axis=1, keepdims=True)
            weights = (exponent / total).astype(low)
            out = mm(weights, value_h[:keys]).astype(low)
            log_total = peak + jnp.log(total)
            for i in range(GROUP):
                part = slice(i * ROW_BLOCK, (i + 1) * ROW_BLOCK)
                outs[head * GROUP + i].append(out[part])
                totals[head * GROUP + i].append(log_total[part])
    mixed[...] = jnp.concatenate([jnp.concatenate(o, axis=0) for o in outs], axis=1)

    @pl.when(step == 0)
    def _():
        lse_s[...] = jnp.zeros_like(lse_s)

    kept = lse_s[...]
    for i in range(PAIR * GROUP):
        column = jnp.concatenate(totals[i], axis=0)
        kept = jnp.where(lane == step * PAIR * GROUP + i, column, kept)
    lse_s[...] = kept
    lse[...] = kept


def attention_forward(length, tokens, gain, weight, cosine, sine, after=()):
    rows, width = tokens.shape
    steps = KEY_VALUE_HEADS // PAIR
    low = jnp.bfloat16
    query_total = QUERY_HEADS * HEAD_SIZE
    key_total = KEY_VALUE_HEADS * HEAD_SIZE
    key_at = query_total // KEY_LANES
    value_at = key_at + steps
    whole = lambda shape: pl.BlockSpec(shape, lambda i, n: (0, 0))
    cols = lambda lanes, at: pl.BlockSpec((width, lanes), lambda i, n: (0, at + i))
    part = lambda lanes: pl.BlockSpec((rows, lanes), lambda i, n: (0, i))
    return pl.pallas_call(
        attention_kernel,
        grid_spec=pltpu.PrefetchScalarGridSpec(
            num_scalar_prefetch=1,
            grid=(steps,),
            in_specs=[
                whole((rows, width)),
                whole((1, width)),
                cols(QUERY_LANES, 0),
                cols(KEY_LANES, key_at),
                cols(KEY_LANES, value_at),
                whole((rows, QUERY_LANES)),
                whole((rows, QUERY_LANES)),
            ]
            + [pl.BlockSpec(memory_space=pl.ANY)] * len(after),
            out_specs=[
                whole((rows, width)),
                part(QUERY_LANES),
                part(KEY_LANES),
                part(KEY_LANES),
                part(QUERY_LANES),
                whole((rows, 128)),
            ],
            scratch_shapes=[pltpu.VMEM((rows, width), low), pltpu.VMEM((rows, 128), jnp.float32)],
        ),
        out_shape=[
            jax.ShapeDtypeStruct((rows, width), low),
            jax.ShapeDtypeStruct((rows, query_total), low),
            jax.ShapeDtypeStruct((rows, key_total), low),
            jax.ShapeDtypeStruct((rows, key_total), low),
            jax.ShapeDtypeStruct((rows, query_total), low),
            jax.ShapeDtypeStruct((rows, 128), jnp.float32),
        ],
        compiler_params=pltpu.CompilerParams(vmem_limit_bytes=48 * 1024 * 1024),
        cost_estimate=pl.CostEstimate(
            flops=2 * rows * width * (query_total + 2 * key_total)
            + 4 * QUERY_HEADS * rows * rows * HEAD_SIZE,
            bytes_accessed=2 * width * (query_total + 2 * key_total) + 10 * rows * width,
            transcendentals=QUERY_HEADS * rows * rows,
        ),
        name="attention_forward",
    )(length, tokens, gain, weight, weight, weight, cosine, sine, *after)


def attention_back_kernel(
    length, dbranch, wo, q, k, v, lse, h1, wq, wk, wv, cosine, sine, *rest, first
):
    grads, dh1, dh_s = rest[-3:]
    step = pl.program_id(0)
    low = jnp.bfloat16
    full = jnp.float32
    rows = dbranch.shape[0]
    blocks = rows // ROW_BLOCK
    dmixed = mm(dbranch[...], wo[...]).astype(low)
    lane = lax.broadcasted_iota(jnp.int32, (rows, 128), 1)
    kept = lse[...]
    query, key, value = q[...], k[...], v[...]
    columns = [
        jnp.sum(jnp.where(lane == (step + first) * PAIR * GROUP + i, kept, 0.0), axis=1, keepdims=True)
        for i in range(PAIR * GROUP)
    ]
    masks = [block_mask(block, length[0]) for block in range(blocks)]
    dq = [[] for _ in range(PAIR * GROUP)]
    dks, dvs = [], []
    for head in range(PAIR):
        key_h = key[:, head * HEAD_SIZE : (head + 1) * HEAD_SIZE]
        value_h = value[:, head * HEAD_SIZE : (head + 1) * HEAD_SIZE]
        dk = [None] * blocks
        dv = [None] * blocks
        for block in range(blocks):
            keys = (block + 1) * ROW_BLOCK
            at = slice(block * ROW_BLOCK, (block + 1) * ROW_BLOCK)
            query_h = heads_of(query[at], head * GROUP, GROUP)
            dmixed_h = heads_of(dmixed[at], head * GROUP, GROUP)
            log_total = jnp.concatenate(
                [columns[head * GROUP + i][at] for i in range(GROUP)], axis=0
            )
            scores = multiply_transposed(query_h, key_h[:keys]) * score_scale
            scores = jnp.where(masks[block], scores, masked_score)
            probs = jnp.exp(scores - log_total)
            dprobs = multiply_transposed(dmixed_h, value_h[:keys])
            delta = jnp.sum(probs * dprobs, axis=1, keepdims=True)
            dscores = (probs * (dprobs - delta)).astype(low)
            dquery = mm(dscores, key_h[:keys]) * score_scale
            dkey = contract_rows(dscores, query_h) * score_scale
            dvalue = contract_rows(probs.astype(low), dmixed_h)
            for i in range(GROUP):
                dq[head * GROUP + i].append(dquery[i * ROW_BLOCK : (i + 1) * ROW_BLOCK])
            for b in range(block + 1):
                part = slice(b * ROW_BLOCK, (b + 1) * ROW_BLOCK)
                dk[b] = dkey[part] if dk[b] is None else dk[b] + dkey[part]
                dv[b] = dvalue[part] if dv[b] is None else dv[b] + dvalue[part]
        dks.append(jnp.concatenate(dk, axis=0))
        dvs.append(jnp.concatenate(dv, axis=0))
    cos = cosine[...]
    sin = sine[...]
    dquery = jnp.concatenate([jnp.concatenate(o, axis=0) for o in dq], axis=1)
    dquery = (dquery * cos - turn_halves(dquery * sin)).astype(low)
    dkey = jnp.concatenate(dks, axis=1)
    dkey = (dkey * cos[:, :KEY_LANES] - turn_halves(dkey * sin[:, :KEY_LANES])).astype(low)
    dvalue = jnp.concatenate(dvs, axis=1).astype(low)
    hidden = h1[...]
    grads[:, :QUERY_LANES] = contract_rows(hidden, dquery).astype(low)
    both = contract_rows(hidden, jnp.concatenate([dkey, dvalue], axis=1)).astype(low)
    grads[:, QUERY_LANES:] = both
    term = (
        multiply_transposed(dquery, wq[...])
        + multiply_transposed(dkey, wk[...])
        + multiply_transposed(dvalue, wv[...])
    )

    @pl.when(step == 0)
    def _():
        dh_s[...] = term

    @pl.when(step > 0)
    def _():
        dh_s[...] += term

    @pl.when(step == pl.num_programs(0) - 1)
    def _():
        dh1[...] = dh_s[...]


def attention_backward(
    length, dbranch, out_t, q, k, v, lse, h1, weight, cosine, sine, first, steps, after=()
):
    rows, width = dbranch.shape
    pairs = KEY_VALUE_HEADS // PAIR
    low = jnp.bfloat16
    full = jnp.float32
    query_total = QUERY_HEADS * HEAD_SIZE
    key_total = KEY_VALUE_HEADS * HEAD_SIZE
    key_at = query_total // KEY_LANES
    value_at = key_at + pairs
    whole = lambda shape: pl.BlockSpec(shape, lambda i, n: (0, 0))
    cols = lambda lanes, at: pl.BlockSpec((width, lanes), lambda i, n: (0, at + first + i))
    part = lambda lanes: pl.BlockSpec((rows, lanes), lambda i, n: (0, first + i))
    lanes = QUERY_LANES + 2 * KEY_LANES
    return pl.pallas_call(
        functools.partial(attention_back_kernel, first=first),
        grid_spec=pltpu.PrefetchScalarGridSpec(
            num_scalar_prefetch=1,
            grid=(steps,),
            in_specs=[
                whole((rows, width)),
                cols(QUERY_LANES, 0),
                part(QUERY_LANES),
                part(KEY_LANES),
                part(KEY_LANES),
                whole((rows, 128)),
                whole((rows, width)),
                cols(QUERY_LANES, 0),
                cols(KEY_LANES, key_at),
                cols(KEY_LANES, value_at),
                whole((rows, QUERY_LANES)),
                whole((rows, QUERY_LANES)),
            ]
            + [pl.BlockSpec(memory_space=pl.ANY)] * len(after),
            out_specs=[pl.BlockSpec((width, lanes), lambda i, n: (0, i)), whole((rows, width))],
            scratch_shapes=[pltpu.VMEM((rows, width), full)],
        ),
        out_shape=[
            jax.ShapeDtypeStruct((width, steps * lanes), low),
            jax.ShapeDtypeStruct((rows, width), full),
        ],
        compiler_params=pltpu.CompilerParams(vmem_limit_bytes=48 * 1024 * 1024),
        cost_estimate=pl.CostEstimate(
            flops=4 * rows * width * (query_total + 2 * key_total)
            + 2 * rows * width * query_total
            + 10 * QUERY_HEADS * rows * rows * HEAD_SIZE,
            bytes_accessed=4 * width * (query_total + 2 * key_total) + 2 * width * width + 14 * rows * width,
            transcendentals=QUERY_HEADS * rows * rows,
        ),
        name="attention_backward",
    )(length, dbranch, out_t, q, k, v, lse, h1, weight, weight, weight, cosine, sine, *after)


def combine_kernel(slots, values, *rest):
    other, own, p_s = rest[-3:]
    step = pl.program_id(0)
    length = slots.shape[2]
    iota = lax.broadcasted_iota(jnp.int32, (WIDE, length), 0)
    for u in range(slots.shape[1]):
        pick = iota == slots[0, u : u + 1, :]
        p_s[u * WIDE : (u + 1) * WIDE, :] = jnp.where(pick, 1.0, 0.0).astype(jnp.bfloat16)
    result = contract_rows(p_s[...], values[0]).astype(jnp.bfloat16)

    @pl.when(step < Z_SIZE)
    def _():
        other[0] = result

    @pl.when(step >= Z_SIZE)
    def _():
        own[0] = result


def combine(slots, values, after=()):
    sources, units, length = slots.shape
    n = values.shape[-1]
    low = jnp.bfloat16
    return pl.pallas_call(
        combine_kernel,
        grid=(sources,),
        in_specs=[
            pl.BlockSpec((1, units, length), lambda i: (i, 0, 0)),
            pl.BlockSpec((1, units * WIDE, n), lambda i: (i, 0, 0)),
        ]
        + [pl.BlockSpec(memory_space=pl.ANY)] * len(after),
        out_specs=[
            pl.BlockSpec((1, length, n), lambda i: (jnp.minimum(i, Z_SIZE - 1), 0, 0)),
            pl.BlockSpec((1, length, n), lambda i: (jnp.maximum(i - Z_SIZE, 0), 0, 0)),
        ],
        out_shape=[jax.ShapeDtypeStruct((Z_SIZE, length, n), low)] * 2,
        scratch_shapes=[pltpu.VMEM((units * WIDE, length), low)],
        compiler_params=pltpu.CompilerParams(vmem_limit_bytes=60 * 1024 * 1024),
        cost_estimate=pl.CostEstimate(
            flops=2 * sources * units * WIDE * length * n,
            bytes_accessed=sources * (units * WIDE + length) * n * 2,
            transcendentals=0,
        ),
        name="combine",
    )(slots, values, *after)


def line_terms(own, moved):
    return [own[0].astype(jnp.float32) + moved[0].astype(jnp.float32)] + [
        plus(own[s], moved[s]).astype(jnp.bfloat16) for s in range(1, Z_SIZE)
    ]


def line_first(terms):
    return terms[1], terms[3]


def weight_chunks(gate_up_weight, down_weight):
    experts, rows = gate_up_weight.shape[0], gate_up_weight.shape[1]
    gate, upper = gate_up_weight[..., :FF], gate_up_weight[..., FF:]
    down_t = down_weight.transpose(0, 2, 1)
    half = FF // 2

    def one(q):
        cols = slice((q % 2) * half, (q % 2 + 1) * half)
        return jnp.concatenate([part[q // 2, :, cols] for part in (gate, upper, down_t)], axis=-1)

    return [
        jnp.stack([one(HALF_ORDER[z_to][j]) for z_to in range(Z_SIZE)]) for j in range(5)
    ]


def along_z(own, got, z):
    result = jnp.zeros((Z_SIZE, *own.shape), own.dtype)
    result = lax.dynamic_update_slice_in_dim(result, own[None], z, 0)
    for step in range(1, Z_SIZE):
        result = lax.dynamic_update_slice_in_dim(
            result, got[step - 1][None], (z + Z_SIZE - step) % Z_SIZE, 0
        )
    return result


def shift_sends(rounds, chunk, z, steps=(1, 2, 3), axis=0):
    return [
        move(
            rounds.gate(lax.dynamic_index_in_dim(chunk, (z + step) % Z_SIZE, axis, keepdims=False)),
            pairs_shift(step),
        )
        for step in steps
    ]


class DenseScatter:
    def __init__(self, rounds, term, place):
        self.rounds, self.place = rounds, place
        z, y, x, c = place
        rows, n = term.shape
        rows = rows // (Z_SIZE * Y_SIZE * X_SIZE * C_SIZE)
        blocks = term.reshape(Z_SIZE, Y_SIZE, X_SIZE, C_SIZE, rows, n)

        def block(at_y, at_x, at_c):
            got = lax.dynamic_slice(
                blocks, (0, at_y, at_x, at_c, 0, 0), (Z_SIZE, 1, 1, 1, rows, n)
            )
            return got.reshape(Z_SIZE, rows, n)

        order = [(y, x), (y, 1 - x), (1 - y, x), (1 - y, 1 - x)]
        self.mine = [block(at_y, at_x, c) for at_y, at_x in order]
        self.theirs = jnp.stack([block(at_y, at_x, 1 - c) for at_y, at_x in order])

    def cores(self):
        self.got = move(self.rounds.gate(self.theirs), PAIRS_C)
        return [self.got]

    def first(self):
        low = jnp.bfloat16
        zs = Z_SIZE // 2
        self.near, self.to_x, self.to_y, far = [
            plus(self.mine[i], self.got[i]) for i in range(4)
        ]
        gate = self.rounds.gate
        self.via_x = move(gate(far[:zs].astype(low)), PAIRS_X)
        self.via_y = move(gate(far[zs:].astype(low)), PAIRS_Y)
        self.x_a = move(gate(self.to_x[:zs].astype(low)), PAIRS_X)
        self.y_b = move(gate(self.to_y[zs:].astype(low)), PAIRS_Y)
        return [self.via_x, self.via_y, self.x_a, self.y_b]

    def second(self):
        low = jnp.bfloat16
        zs = Z_SIZE // 2
        gate = self.rounds.gate
        self.x_b = move(gate(plus(self.to_x[zs:], self.via_y).astype(low)), PAIRS_X)
        self.y_a = move(gate(plus(self.to_y[:zs], self.via_x).astype(low)), PAIRS_Y)
        return [self.x_b, self.y_a]

    def along(self):
        zs = Z_SIZE // 2
        z = self.place[0]
        total = jnp.concatenate(
            [
                plus(self.near[:zs], self.x_a) + self.y_a.astype(jnp.float32),
                plus(self.near[zs:], self.x_b) + self.y_b.astype(jnp.float32),
            ]
        ).astype(jnp.bfloat16)
        self.own = lax.dynamic_index_in_dim(total, z, 0, keepdims=False)
        self.parts = shift_sends(self.rounds, total, z)
        return self.parts

    def result(self):
        return plus(self.own, self.parts[0]) + plus(self.parts[1], self.parts[2])


def plus(a, b):
    return a.astype(jnp.float32) + b.astype(jnp.float32)


def ring_total(own, x_a, second):
    y_b, y_a, x_b = second
    return jnp.concatenate(
        [plus(own[0], x_a) + y_a.astype(jnp.float32), plus(own[1], x_b) + y_b.astype(jnp.float32)],
        axis=1,
    ).astype(jnp.bfloat16)


def body(
    tokens,
    cotangent,
    lengths,
    routes,
    slots,
    first_gain,
    qkv_weight,
    out_weight,
    second_gain,
    router_weight,
    gate_up_weight,
    down_weight,
):
    low = jnp.bfloat16
    full = jnp.float32
    dp_index = lax.axis_index("dp")
    expert_index = lax.axis_index("expert")
    z, y = dp_index // Y_SIZE, dp_index % Y_SIZE
    x, c = expert_index // C_SIZE, expert_index % C_SIZE
    sequence_length = tokens.shape[0]
    width = tokens.shape[1]
    rows = gate_up_weight.shape[1]

    chosen_by = routes[None, :, :] == jnp.arange(EXPERTS, dtype=jnp.int32)[:, None, None]
    slot_table = jnp.sum(jnp.where(chosen_by, slots[None, :, :] + 1, 0), axis=-1) - 1
    place = (z, y, x, c)
    zs = Z_SIZE // 2
    steps = range(1, Z_SIZE)
    rounds = Rounds()
    gate = rounds.gate

    small = jnp.concatenate(
        [router_weight, first_gain[:, None], second_gain[:, None]], axis=1
    )
    small = jnp.pad(small, ((0, 0), (0, 128 - small.shape[1])))
    shard = jnp.concatenate([qkv_weight, small], axis=1)
    out_shard = out_weight.T
    table = slot_table.astype(low)

    got = [move(shard, pairs_shift(s)) for s in steps]
    tables = [move(table, pairs_shift(s)) for s in steps]
    cuts = weight_chunks(gate_up_weight, down_weight)
    rounds.close(*got, *tables, *cuts)

    near, far, moved = [None] * 5, [None] * 5, [None] * 5

    def send_half(q):
        return shift_sends(rounds, cuts[q], z)

    def keep_half(q, got):
        moved[q] = along_z(lax.dynamic_index_in_dim(cuts[q], z, 0, keepdims=False), got, z)

    def send_near(q):
        moved[q] = gate(moved[q])
        near[q] = (move(moved[q], PAIRS_X), move(moved[q], PAIRS_Y))
        return near[q]

    def send_far(q):
        far[q] = (move(gate(near[q][1][:zs]), PAIRS_X), move(gate(near[q][0][zs:]), PAIRS_Y))
        return far[q]

    block = gate(along_z(shard, got, z))
    out_got = [move(s, pairs_shift(i + 1)) for i, s in enumerate([gate(out_shard)] * 3)]
    half_got = send_half(0)
    from_x, from_y = move(block, PAIRS_X), move(block, PAIRS_Y)
    block_c = move(block, PAIRS_C)
    tables = jnp.stack([table] + tables)
    tables_c = move(gate(tables), PAIRS_C)
    rounds.close(from_x, from_y, block_c, *out_got, *half_got, tables_c)
    keep_half(0, half_got)
    far_a, far_b = move(gate(from_y[:zs]), PAIRS_X), move(gate(from_x[zs:]), PAIRS_Y)
    from_x_c, from_y_c = move(gate(from_x), PAIRS_C), move(gate(from_y), PAIRS_C)
    out_block = gate(along_z(out_shard, out_got, z))
    out_x, out_y = move(out_block, PAIRS_X), move(out_block, PAIRS_Y)
    out_block_c = move(out_block, PAIRS_C)
    half_got = send_half(1)
    rounds.close(far_a, far_b, from_x_c, from_y_c, out_x, out_y, out_block_c, *half_got)
    keep_half(1, half_got)
    far_a_c, far_b_c = move(gate(far_a), PAIRS_C), move(gate(far_b), PAIRS_C)
    out_far_a, out_far_b = move(gate(out_y[:zs]), PAIRS_X), move(gate(out_x[zs:]), PAIRS_Y)
    out_x_c, out_y_c = move(gate(out_x), PAIRS_C), move(gate(out_y), PAIRS_C)
    half_got = send_half(2)
    rounds.close(far_a_c, far_b_c, out_far_a, out_far_b, out_x_c, out_y_c, *half_got, *send_near(0))
    keep_half(2, half_got)
    first_pack = dense_assemble(
        place,
        (block, from_x, from_y, far_a, far_b),
        (block_c, from_x_c, from_y_c, far_a_c, far_b_c),
    )
    small_full = first_pack[:, qkv_weight.shape[1] :]
    router_full = small_full[:, :EXPERTS]
    gain_one = small_full[:, EXPERTS].astype(full)
    gain_two = small_full[:, EXPERTS + 1].astype(full)

    inputs = tokens.astype(full)
    inverse_one = rms_inverse(inputs)
    normal_one = inputs * inverse_one
    cosine_table, sine_table = rope_tables(sequence_length)
    cosine_table = jnp.tile(cosine_table, (1, QUERY_LANES // HEAD_SIZE))
    sine_table = jnp.tile(sine_table, (1, QUERY_LANES // HEAD_SIZE))
    out_far_a_c, out_far_b_c = move(gate(out_far_a), PAIRS_C), move(gate(out_far_b), PAIRS_C)
    half_got = send_half(3)
    hidden_one, query_rows, keys, value_rows, mixed, log_totals = attention_forward(
        lengths, tokens, gain_one[None, :], first_pack, cosine_table, sine_table, rounds.after()
    )
    rounds.close(out_far_a_c, out_far_b_c, *half_got, *send_near(1), mixed)
    keep_half(3, half_got)
    out_t = dense_assemble(
        place,
        (out_block, out_x, out_y, out_far_a, out_far_b),
        (out_block_c, out_x_c, out_y_c, out_far_a_c, out_far_b_c),
    )
    half_got = send_half(4)
    branch = multiply_transposed(mixed, out_t)
    middle = inputs + residual_scale * branch
    inverse_two = rms_inverse(middle)
    normal_two = middle * inverse_two
    hidden_two = (normal_two * gain_two).astype(low)
    grad_out = cotangent.astype(full)

    rounds.close(*half_got, *send_near(2), hidden_two)
    keep_half(4, half_got)
    sent = gate(hidden_two)
    up, down = line_hop(1, sent, sent)
    own_c = move(sent, PAIRS_C)
    rounds.close(up, down, own_c, *send_near(3), *send_far(0))
    hops, hops_c = [(up, down)], []
    for step, sends in ((2, lambda: (*send_near(4), *send_far(1))), (3, lambda: (*send_far(2), *send_far(3)))):
        up, down = gate(hops[-1][0]), gate(hops[-1][1])
        hops[-1] = (up, down)
        hops_c.append((move(up, PAIRS_C), move(down, PAIRS_C)))
        hops.append(line_hop(step, up, down))
        rounds.close(*hops_c[-1], *hops[-1], *sends())
    up, down = hops[-1]
    hops_c.append((move(gate(up), PAIRS_C), move(gate(down), PAIRS_C)))
    rounds.close(*hops_c[-1], *send_far(4))

    def gathered(own, own_c, hops, hops_c):
        return line_blocks(
            z,
            (own, *[h[0] for h in hops], *[h[1] for h in hops]),
            (own_c, *[h[0] for h in hops_c], *[h[1] for h in hops_c]),
        )

    rows_in = gathered(hidden_two, own_c, hops, hops_c)
    rings = [
        (
            [p for q in range(*cut) for p in (moved[q], near[q][1])],
            [p for q in range(*cut) for p in (near[q][0], *far[q])],
        )
        for cut in UNIT_HALVES
    ]
    slots_in = jnp.concatenate([tables_c, tables], axis=0).astype(jnp.int32)
    logits_in = jnp.einsum("de,itd->iet", router_full, rows_in, preferred_element_type=full)
    chosen_in = slots_in >= 0
    peak_in = jnp.max(jnp.where(chosen_in, logits_in, -jnp.inf), axis=1, keepdims=True)
    exponent_in = jnp.where(chosen_in, jnp.exp(logits_in - peak_in), 0.0)
    gates_in = exponent_in / jnp.sum(exponent_in, axis=1, keepdims=True)

    units = range(len(UNIT_HALVES))
    even = z % 2 == 0
    ids = []
    for group in (1 - x, x):
        base = EXPERTS // (X_SIZE * C_SIZE) * (group * C_SIZE + c) + 5 * (z // 2)
        ids += [base + jnp.where(even, 0, 3), base + jnp.where(even, 1, 4), base + 2]
    unit_slots = [lax.dynamic_index_in_dim(slots_in, expert, 1, keepdims=True) for expert in ids]
    unit_gates = [lax.dynamic_index_in_dim(gates_in, expert, 1, keepdims=True) for expert in ids]
    pairs = len(UNIT_HALVES)
    sizes = [end - first for first, end in UNIT_HALVES]
    all_slots = jnp.concatenate(unit_slots, axis=1)
    infos = [jnp.stack([y, expert]).astype(jnp.int32) for expert in ids]
    buffer = None
    saved = {}

    def run_forward(pair, own):
        nonlocal buffer
        at = pair + (pairs if own else 0)
        buffer, *saved[at] = expert_forward(
            at,
            sizes[pair],
            infos[at],
            unit_slots[at],
            unit_gates[at],
            rows_in,
            rings[pair][0 if own else 1],
            buffer,
            rounds.after(),
        )

    sent = gate(cotangent)
    dy_c = move(sent, PAIRS_C)
    dy_hops, dy_hops_c = [], []
    up = down = sent
    for pair in range(pairs):
        if pair > 0:
            up, down = gate(up), gate(down)
            dy_hops[-1] = (up, down)
            dy_hops_c.append((move(up, PAIRS_C), move(down, PAIRS_C)))
        up, down = line_hop(pair + 1, up, down)
        dy_hops.append((up, down))
        run_forward(pair, False)
        run_forward(pair, True)
        rounds.close(up, down, saved[pair + pairs][0], *(dy_hops_c[-1] if dy_hops_c else (dy_c,)))
    up, down = gate(up), gate(down)
    dy_hops[-1] = (up, down)
    dy_hops_c.append((move(up, PAIRS_C), move(down, PAIRS_C)))
    mix_other, mix_own = combine(all_slots, buffer, rounds.after())
    rounds.close(mix_other, *dy_hops_c[-1])
    mix_moved = move(gate(mix_other), PAIRS_C)
    grads_in = gathered(cotangent, dy_c, dy_hops, dy_hops_c)
    rounds.close(mix_moved, grads_in)

    back = None
    grads = [[None, None] for _ in units]

    def run_back(pair, own):
        nonlocal back
        at = pair + (pairs if own else 0)
        back, grads[pair][1 if own else 0] = expert_backward(
            at,
            sizes[pair],
            infos[at],
            unit_slots[at],
            unit_gates[at],
            grads_in,
            *saved[at],
            rings[pair][0 if own else 1],
            back,
            rounds.after(),
        )

    vias, firsts, seconds = [None] * 3, [None] * 3, [None] * 3

    def send_via(u):
        vias[u] = (move(gate(grads[u][0][2]), PAIRS_X), move(gate(grads[u][0][3]), PAIRS_Y))
        return vias[u]

    def send_first(u):
        firsts[u] = (move(gate(grads[u][0][0]), PAIRS_X), move(gate(grads[u][1][3]), PAIRS_Y))
        return firsts[u]

    def send_second(u):
        via_x, via_y = vias[u]
        seconds[u] = (
            move(gate(plus(grads[u][0][1], via_y).astype(low)), PAIRS_X),
            move(gate(plus(grads[u][1][2], via_x).astype(low)), PAIRS_Y),
        )
        return seconds[u]

    def total_of(u):
        x_b, y_a = seconds[u]
        x_a, y_b = firsts[u]
        return ring_total(grads[u][1], x_a, (y_b, y_a, x_b))

    def hop_sum(step, terms, up, down):
        up = move(gate(up), pairs_up_below(step - 1))
        down = move(gate(down), pairs_down_above(Z_SIZE - step))
        return up, down

    terms = line_terms(mix_own, mix_moved)
    up, down = hop_sum(1, terms, terms[1], terms[3])
    run_back(0, False)
    rounds.close(up, down, grads[0][0][0])
    up, down = hop_sum(2, terms, plus(terms[2], up).astype(low), plus(terms[2], down).astype(low))
    run_back(0, True)
    rounds.close(up, down, grads[0][1][0], *send_via(0))
    up, down = hop_sum(3, terms, plus(terms[3], up).astype(low), plus(terms[1], down).astype(low))
    run_back(1, False)
    rounds.close(up, down, grads[1][0][0], *send_first(0))
    output = (middle + residual_scale * (terms[0] + plus(up, down))).astype(low)
    run_back(1, True)
    rounds.close(grads[1][1][0], *send_second(0))
    totals = [total_of(0), None, None]
    backs = [[], [], []]

    def send_back(u, step):
        backs[u] += shift_sends(rounds, totals[u], z, (step,), 1)
        return backs[u][-1:]

    run_back(2, False)
    rounds.close(grads[2][0][0], *send_via(1), *send_back(0, 1))
    run_back(2, True)
    rounds.close(grads[2][1][0], *send_first(1), *send_back(0, 2))
    copy_other, copy_own = combine(all_slots, back, rounds.after())
    rounds.close(copy_other, *send_second(1), *send_back(0, 3))
    copy_moved = move(gate(copy_other), PAIRS_C)
    rounds.close(copy_moved, *send_via(2))
    terms = line_terms(copy_own, copy_moved)
    up, down = hop_sum(1, terms, terms[1], terms[3])
    totals[1] = total_of(1)
    rounds.close(up, down, *send_first(2))
    up, down = hop_sum(2, terms, plus(terms[2], up).astype(low), plus(terms[2], down).astype(low))
    rounds.close(up, down, *send_second(2))
    up, down = hop_sum(3, terms, plus(terms[3], up).astype(low), plus(terms[1], down).astype(low))
    rounds.close(up, down)
    copy_sum = terms[0] + plus(up, down)
    totals[2] = total_of(2)
    grad_gates = copy_sum[:, width : width + EXPERTS] + copy_sum[:, width + 64 : width + 64 + EXPERTS]
    copy_sum = copy_sum[:, :width]

    chosen = (slot_table >= 0).T
    gates = dense_gates(jnp.dot(hidden_two, router_full, preferred_element_type=full), chosen)
    grad_logits = (
        gates * (grad_gates - jnp.sum(gates * grad_gates, axis=-1, keepdims=True))
    ).astype(low)
    grad_hidden_two = copy_sum + multiply_transposed(grad_logits, router_full)
    router_term = contract_rows(hidden_two, grad_logits)
    second_term, grad_norm_two = norm_backward(
        grad_hidden_two, normal_two, inverse_two, gain_two
    )
    grad_middle = grad_out + grad_norm_two
    branch_gradient = (residual_scale * grad_middle).astype(low)
    small_term = jnp.concatenate([router_term, second_term[:, None]], axis=1)
    out_pack = jnp.concatenate(
        [
            contract_rows(branch_gradient, mixed),
            jnp.pad(small_term, ((0, 0), (0, 128 - small_term.shape[1]))),
        ],
        axis=1,
    ).astype(low)
    out_scatter = DenseScatter(rounds, out_pack, place)

    def run_attention(first):
        return attention_backward(
            lengths,
            branch_gradient,
            out_t,
            query_rows,
            keys,
            value_rows,
            log_totals,
            hidden_one,
            first_pack,
            cosine_table,
            sine_table,
            first,
            2,
            rounds.after(),
        )

    rounds.close(out_scatter.theirs, branch_gradient, *send_back(1, 1))
    qkv_terms = [None, None]
    qkv_terms[0], part_one = run_attention(0)
    rounds.close(part_one, *out_scatter.cores(), *send_back(1, 2))
    qkv_terms[1], part_two = run_attention(2)
    qkv_scatter = [DenseScatter(rounds, qkv_terms[0], place)]
    rounds.close(part_two, *out_scatter.first(), *qkv_scatter[0].cores(), *send_back(1, 3))
    grad_hidden_one = part_one + part_two
    first_term, grad_norm_one = norm_backward(
        grad_hidden_one, normal_one, inverse_one, gain_one
    )
    grad_input = grad_middle + grad_norm_one

    first_pack_term = jnp.pad(first_term[:, None], ((0, 0), (0, 127))).astype(low)
    qkv_scatter.append(
        DenseScatter(rounds, jnp.concatenate([qkv_terms[1], first_pack_term], axis=1), place)
    )
    sent = [*out_scatter.second(), *qkv_scatter[0].first(), *qkv_scatter[1].cores()]
    for step in steps:
        sent += send_back(2, step)
    rounds.close(*sent)
    rounds.close(*out_scatter.along(), *qkv_scatter[0].second(), *qkv_scatter[1].first())
    rounds.close(*qkv_scatter[0].along(), *qkv_scatter[1].second())
    qkv_scatter[1].along()
    back = jnp.concatenate(
        [
            along_z(lax.dynamic_index_in_dim(totals[u], z, 1, keepdims=False), backs[u], z)
            for u in units
        ],
        axis=1,
    ).reshape(Z_SIZE * 5, rows, -1)
    weight_sums = jnp.stack([back[HALF_PLACE[q]] for q in range(Z_SIZE * 5)]).astype(full)
    weight_sums = weight_sums.reshape(EXPERTS // (X_SIZE * C_SIZE), 2, rows, 3 * FF // 2)
    parts = [
        weight_sums[..., i * FF // 2 : (i + 1) * FF // 2].transpose(0, 2, 1, 3).reshape(-1, rows, FF)
        for i in range(3)
    ]
    gate_up_grads = jnp.concatenate(parts[:2], axis=-1)
    down_grads = parts[2].transpose(0, 2, 1)

    qkv_sums = [scatter.result() for scatter in qkv_scatter]
    first_sum = qkv_sums[-1][:, -128]
    qkv_sums[-1] = qkv_sums[-1][:, :-128]
    qkv_sum = jnp.concatenate(qkv_sums, axis=1)
    qkv_sum = qkv_sum.reshape(qkv_sum.shape[0], -1, QUERY_LANES + 2 * KEY_LANES)
    qkv_sum = jnp.concatenate(
        [
            part.reshape(qkv_sum.shape[0], -1)
            for part in jnp.split(qkv_sum, (QUERY_LANES, QUERY_LANES + KEY_LANES), axis=2)
        ],
        axis=1,
    )
    out_sum = out_scatter.result()
    small_sum = out_sum[:, width:]
    return (
        output,
        grad_input,
        first_sum,
        qkv_sum,
        out_sum[:, :width].T,
        small_sum[:, EXPERTS],
        small_sum[:, :EXPERTS],
        gate_up_grads,
        down_grads,
    )


def solution(mesh):
    in_specs = (
        P(("dp", "expert"), None),
        P(("dp", "expert"), None),
        P(("dp", "expert")),
        P(("dp", "expert"), None),
        P(("dp", "expert"), None),
        P(("dp", "expert")),
        P(("dp", "expert"), None),
        P(None, ("dp", "expert")),
        P(("dp", "expert")),
        P(("dp", "expert"), None),
        P("expert", "dp", None),
        P("expert", None, "dp"),
    )
    out_specs = (
        P(("dp", "expert"), None),
        P(("dp", "expert"), None),
        P(("dp", "expert")),
        P(("dp", "expert"), None),
        P(None, ("dp", "expert")),
        P(("dp", "expert")),
        P(("dp", "expert"), None),
        P("expert", "dp", None),
        P("expert", None, "dp"),
    )
    fits = mesh.shape["dp"] == Z_SIZE * Y_SIZE and mesh.shape["expert"] == X_SIZE * C_SIZE
    chosen = body if fits else general_body
    return jax.shard_map(chosen, mesh=mesh, in_specs=in_specs, out_specs=out_specs, check_vma=False)
```

```python
import functools

import jax
import jax.numpy as jnp
from jax import lax
from jax.experimental import pallas as pl
from jax.experimental.pallas import tpu as pltpu
from jax.sharding import PartitionSpec as P

QUERY_HEADS = 24
KEY_VALUE_HEADS = 8
HEAD_SIZE = 64
FF = 512
EXPERTS = 40
TOP = 8
CAP = 152


epsilon = 1e-06
residual_scale = 0.22
score_scale = 0.015625
rope_base = 10000.0
masked_score = -1e30


def rope_tables(length):
    half = HEAD_SIZE // 2
    freqs = jnp.power(rope_base, -2.0 * jnp.arange(half, dtype=jnp.float32) / HEAD_SIZE)
    angles = jnp.arange(length, dtype=jnp.float32)[:, None] * freqs[None, :]
    cosine_table = jnp.concatenate([jnp.cos(angles), jnp.cos(angles)], axis=-1)
    sine_table = jnp.concatenate([jnp.sin(angles), jnp.sin(angles)], axis=-1)
    return (cosine_table, sine_table)


def rotate_half(value_rows):
    half = value_rows.shape[-1] // 2
    return jnp.concatenate([-value_rows[..., half:], value_rows[..., :half]], axis=-1)


def rotate_pairs(value_rows, cosine_table, sine_table):
    return value_rows * cosine_table[:, None, :] + rotate_half(value_rows) * sine_table[:, None, :]


def unrotate(grads, cosine_table, sine_table):
    return grads * cosine_table[:, None, :] - rotate_half(grads * sine_table[:, None, :])


def rms_inverse(value_rows):
    return lax.rsqrt(jnp.mean(value_rows * value_rows, axis=-1, keepdims=True) + epsilon)


def norm_backward(grad_normed, normal, inverse, gain):
    gain_term = jnp.sum(grad_normed * normal, axis=0)
    scaled = grad_normed * gain
    grad_input = inverse * (scaled - normal * jnp.mean(scaled * normal, axis=-1, keepdims=True))
    return (gain_term, grad_input)


def contract_rows(left, right):
    return lax.dot_general(
        left, right, (((0,), (0,)), ((), ())), preferred_element_type=jnp.float32
    )


def multiply_transposed(left, right):
    return lax.dot_general(
        left, right, (((1,), (1,)), ((), ())), preferred_element_type=jnp.float32
    )


def fetch_expert(gate_up_shard, down_shard):
    return (
        lax.all_gather(gate_up_shard, "dp", axis=0, tiled=True),
        lax.all_gather(down_shard, "dp", axis=1, tiled=True),
    )


def gate_values(hidden_rows, router_full, route_rows):
    logits = jnp.dot(hidden_rows, router_full, preferred_element_type=jnp.float32)
    chosen_mask = route_rows[:, :, None] == jnp.arange(EXPERTS)[None, None, :]
    chosen = jnp.sum(jnp.where(chosen_mask, logits[:, None, :], 0.0), axis=-1)
    return (chosen_mask, jax.nn.softmax(chosen, axis=-1))


def general_body(
    tokens,
    cotangent,
    lengths,
    routes,
    slots,
    first_gain,
    qkv_weight,
    out_weight,
    second_gain,
    router_weight,
    gate_up_weight,
    down_weight,
):
    sequence_length = tokens.shape[0]
    width = tokens.shape[1]
    query_group = QUERY_HEADS // KEY_VALUE_HEADS
    length = lengths[0]
    gathered = (
        lax.all_gather(first_gain, ("dp", "expert"), axis=0, tiled=True),
        lax.all_gather(qkv_weight, ("dp", "expert"), axis=0, tiled=True),
        lax.all_gather(out_weight, ("dp", "expert"), axis=1, tiled=True),
        lax.all_gather(second_gain, ("dp", "expert"), axis=0, tiled=True),
        lax.all_gather(router_weight, ("dp", "expert"), axis=0, tiled=True),
    )
    gain_one, qkv_full, out_full, gain_two, router_full = gathered
    inputs = tokens.astype(jnp.float32)
    inverse_one = rms_inverse(inputs)
    normal_one = inputs * inverse_one
    hidden_one = (normal_one * gain_one.astype(jnp.float32)).astype(jnp.bfloat16)
    projected_rows = jnp.dot(hidden_one, qkv_full, preferred_element_type=jnp.float32)
    cosine_table, sine_table = rope_tables(sequence_length)
    query_width_total = QUERY_HEADS * HEAD_SIZE
    key_width_total = KEY_VALUE_HEADS * HEAD_SIZE
    query_rows = rotate_pairs(
        projected_rows[:, :query_width_total].reshape(sequence_length, QUERY_HEADS, HEAD_SIZE),
        cosine_table,
        sine_table,
    ).astype(jnp.bfloat16)
    keys = rotate_pairs(
        projected_rows[:, query_width_total : query_width_total + key_width_total].reshape(
            sequence_length, KEY_VALUE_HEADS, HEAD_SIZE
        ),
        cosine_table,
        sine_table,
    ).astype(jnp.bfloat16)
    value_rows = (
        projected_rows[:, query_width_total + key_width_total :]
        .reshape(sequence_length, KEY_VALUE_HEADS, HEAD_SIZE)
        .astype(jnp.bfloat16)
    )
    row_index = jnp.arange(sequence_length)[:, None]
    column_index = jnp.arange(sequence_length)[None, :]
    allowed = (column_index <= row_index) & (column_index < length)

    def head_scores(head):
        head_query = lax.dynamic_slice_in_dim(query_rows, head * query_group, query_group, 1)
        head_key = lax.dynamic_index_in_dim(keys, head, 1, keepdims=False)
        head_value = lax.dynamic_index_in_dim(value_rows, head, 1, keepdims=False)
        scores = (
            jnp.einsum("qgd,kd->gqk", head_query, head_key, preferred_element_type=jnp.float32)
            * score_scale
        )
        return (head_query, head_key, head_value, jnp.where(allowed[None], scores, masked_score))

    def attention_head_forward(head):
        head_query, head_key, head_value, scores = head_scores(head)
        peak = jnp.max(scores, axis=-1, keepdims=True)
        exponent = jnp.exp(scores - peak)
        total = jnp.sum(exponent, axis=-1, keepdims=True)
        weights = (exponent / total).astype(jnp.bfloat16)
        head_mixed = jnp.einsum(
            "gqk,kd->qgd", weights, head_value, preferred_element_type=jnp.float32
        ).astype(jnp.bfloat16)
        return (head_mixed, (peak + jnp.log(total))[..., 0])

    mixed_head_output, log_sum_totals = lax.map(attention_head_forward, jnp.arange(KEY_VALUE_HEADS))
    mixed = mixed_head_output.transpose(1, 0, 2, 3).reshape(
        sequence_length, QUERY_HEADS * HEAD_SIZE
    )
    branch = jnp.dot(mixed, out_full, preferred_element_type=jnp.float32)
    middle = inputs + residual_scale * branch
    inverse_two = rms_inverse(middle)
    normal_two = middle * inverse_two
    hidden_two = (normal_two * gain_two.astype(jnp.float32)).astype(jnp.bfloat16)
    chosen_mask, gates = gate_values(hidden_two, router_full, routes)
    grad_out = cotangent.astype(jnp.float32)
    grad_mixture = residual_scale * grad_out

    def expert_forward(carry, pieces):
        rows, gate_up_shard, down_shard = pieces
        gate_up_full, down_full = fetch_expert(gate_up_shard, down_shard)
        gate_up = jnp.dot(rows, gate_up_full, preferred_element_type=jnp.float32)
        hidden = (jax.nn.silu(gate_up[:, :FF]) * gate_up[:, FF:]).astype(jnp.bfloat16)
        return (
            carry,
            jnp.dot(hidden, down_full, preferred_element_type=jnp.float32).astype(jnp.bfloat16),
        )

    copies = jnp.broadcast_to(hidden_two[:, None, :], (sequence_length, TOP, width))
    outgoing = jnp.zeros((EXPERTS, CAP, width), jnp.bfloat16).at[routes, slots].set(copies)
    received = lax.all_to_all(outgoing, "expert", split_axis=0, concat_axis=1, tiled=True)
    _, produced = lax.scan(expert_forward, None, (received, gate_up_weight, down_weight))
    returned = lax.all_to_all(produced, "expert", split_axis=1, concat_axis=0, tiled=True)
    expert_rows = returned[routes, slots].astype(jnp.float32)
    mixture = jnp.sum(gates[:, :, None] * expert_rows, axis=1)
    grad_gates = jnp.sum(expert_rows * grad_mixture[:, None, :], axis=-1)
    grad_rows = (gates[:, :, None] * grad_mixture[:, None, :]).astype(jnp.bfloat16)
    outgoing_grad = jnp.zeros((EXPERTS, CAP, width), jnp.bfloat16).at[routes, slots].set(grad_rows)
    grad_received = lax.all_to_all(outgoing_grad, "expert", split_axis=0, concat_axis=1, tiled=True)
    output = (middle + residual_scale * mixture).astype(jnp.bfloat16)
    again = (
        lax.all_gather(first_gain, ("dp", "expert"), axis=0, tiled=True),
        lax.all_gather(qkv_weight, ("dp", "expert"), axis=0, tiled=True),
        lax.all_gather(out_weight, ("dp", "expert"), axis=1, tiled=True),
        lax.all_gather(second_gain, ("dp", "expert"), axis=0, tiled=True),
        lax.all_gather(router_weight, ("dp", "expert"), axis=0, tiled=True),
    )
    gain_back, qkv_back, output_gradient, gain_two_back, router_back = again
    grad_chosen = gates * (grad_gates - jnp.sum(gates * grad_gates, axis=-1, keepdims=True))
    grad_logits = jnp.sum(jnp.where(chosen_mask, grad_chosen[:, :, None], 0.0), axis=1).astype(
        jnp.bfloat16
    )

    def expert_backward(carry, pieces):
        rows, grad_produced, gate_up_shard, down_shard = pieces
        gate_up_full, down_full = fetch_expert(gate_up_shard, down_shard)
        gate_up = jnp.dot(rows, gate_up_full, preferred_element_type=jnp.float32)
        gate = gate_up[:, :FF]
        upper = gate_up[:, FF:]
        sigmoid = jax.nn.sigmoid(gate)
        swish = gate * sigmoid
        hidden = (swish * upper).astype(jnp.bfloat16)
        grad_hidden = multiply_transposed(grad_produced, down_full)
        grad_gate_up = jnp.concatenate(
            [grad_hidden * upper * sigmoid * (1.0 + gate * (1.0 - sigmoid)), grad_hidden * swish],
            axis=-1,
        ).astype(jnp.bfloat16)
        grad_copy = multiply_transposed(grad_gate_up, gate_up_full).astype(jnp.bfloat16)
        gate_up_part = lax.psum_scatter(
            contract_rows(rows, grad_gate_up).astype(jnp.bfloat16),
            "dp",
            scatter_dimension=0,
            tiled=True,
        ).astype(jnp.float32)
        down_part = lax.psum_scatter(
            contract_rows(grad_produced, hidden).astype(jnp.bfloat16),
            "dp",
            scatter_dimension=0,
            tiled=True,
        ).astype(jnp.float32)
        return (carry, (grad_copy, gate_up_part, down_part.T))

    _, (grad_copies, gate_up_grads, down_grads) = lax.scan(
        expert_backward, None, (received, grad_received, gate_up_weight, down_weight)
    )
    grad_back = lax.all_to_all(grad_copies, "expert", split_axis=1, concat_axis=0, tiled=True)
    copy_sum = jnp.sum(grad_back[routes, slots].astype(jnp.float32), axis=1)
    grad_hidden_two = copy_sum + multiply_transposed(grad_logits, router_back)
    router_term = contract_rows(hidden_two, grad_logits)
    second_term, grad_norm_two = norm_backward(
        grad_hidden_two, normal_two, inverse_two, gain_two_back.astype(jnp.float32)
    )
    grad_middle = grad_out + grad_norm_two
    branch_gradient = (residual_scale * grad_middle).astype(jnp.bfloat16)
    out_term = contract_rows(mixed, branch_gradient)
    grad_mixed = (
        multiply_transposed(branch_gradient, output_gradient)
        .astype(jnp.bfloat16)
        .reshape(sequence_length, KEY_VALUE_HEADS, query_group, HEAD_SIZE)
    )

    def attention_head_backward(head):
        head_query, head_key, head_value, scores = head_scores(head)
        head_grad = lax.dynamic_index_in_dim(grad_mixed, head, 1, keepdims=False)
        head_total = lax.dynamic_index_in_dim(log_sum_totals, head, 0, keepdims=False)
        probs = jnp.exp(scores - head_total[..., None])
        grad_weights = jnp.einsum(
            "qgd,kd->gqk", head_grad, head_value, preferred_element_type=jnp.float32
        )
        grad_scores = (
            probs * (grad_weights - jnp.sum(probs * grad_weights, axis=-1, keepdims=True))
        ).astype(jnp.bfloat16)
        grad_query = (
            jnp.einsum("gqk,kd->qgd", grad_scores, head_key, preferred_element_type=jnp.float32)
            * score_scale
        )
        grad_key = (
            jnp.einsum("gqk,qgd->kd", grad_scores, head_query, preferred_element_type=jnp.float32)
            * score_scale
        )
        grad_value = jnp.einsum(
            "gqk,qgd->kd", probs.astype(jnp.bfloat16), head_grad, preferred_element_type=jnp.float32
        )
        return (grad_query, grad_key, grad_value)

    query_head_rows, key_head_rows, value_head_rows = lax.map(
        attention_head_backward, jnp.arange(KEY_VALUE_HEADS)
    )
    grad_query = unrotate(
        query_head_rows.transpose(1, 0, 2, 3).reshape(sequence_length, QUERY_HEADS, HEAD_SIZE),
        cosine_table,
        sine_table,
    )
    grad_key = unrotate(key_head_rows.transpose(1, 0, 2), cosine_table, sine_table)
    grad_value = value_head_rows.transpose(1, 0, 2)
    grad_projected = jnp.concatenate(
        [
            grad_query.reshape(sequence_length, query_width_total),
            grad_key.reshape(sequence_length, key_width_total),
            grad_value.reshape(sequence_length, key_width_total),
        ],
        axis=-1,
    ).astype(jnp.bfloat16)
    qkv_term = contract_rows(hidden_one, grad_projected)
    grad_hidden_one = multiply_transposed(grad_projected, qkv_back)
    first_term, grad_norm_one = norm_backward(
        grad_hidden_one, normal_one, inverse_one, gain_back.astype(jnp.float32)
    )
    grad_input = grad_middle + grad_norm_one
    summed = (
        lax.psum_scatter(first_term, ("dp", "expert"), scatter_dimension=0, tiled=True),
        lax.psum_scatter(qkv_term, ("dp", "expert"), scatter_dimension=0, tiled=True),
        lax.psum_scatter(out_term, ("dp", "expert"), scatter_dimension=1, tiled=True),
        lax.psum_scatter(second_term, ("dp", "expert"), scatter_dimension=0, tiled=True),
        lax.psum_scatter(router_term, ("dp", "expert"), scatter_dimension=0, tiled=True),
    )
    return (
        output,
        grad_input,
        summed[0],
        summed[1],
        summed[2],
        summed[3],
        summed[4],
        gate_up_grads,
        down_grads,
    )


WIDE = 160
Z_SIZE, Y_SIZE, X_SIZE, C_SIZE = 4, 2, 2, 2
MESH_AXES = ("dp", "expert")


def device_index(z, y, x, c):
    return ((z * Y_SIZE + y) * X_SIZE + x) * C_SIZE + c


def device_pairs(target):
    pairs = []
    for z in range(Z_SIZE):
        for y in range(Y_SIZE):
            for x in range(X_SIZE):
                for c in range(C_SIZE):
                    to = target(z, y, x, c)
                    if to is not None:
                        pairs.append((device_index(z, y, x, c), device_index(*to)))
    return pairs


PAIRS_X = device_pairs(lambda z, y, x, c: (z, y, 1 - x, c))
PAIRS_Y = device_pairs(lambda z, y, x, c: (z, 1 - y, x, c))
PAIRS_C = device_pairs(lambda z, y, x, c: (z, y, x, 1 - c))


Z_GROUPS = [[z * Y_SIZE + y for z in range(Z_SIZE)] for y in range(Y_SIZE)]


def tie_kernel(*refs):
    del refs


def tie(value, *after):
    any_spec = pl.BlockSpec(memory_space=pl.ANY)
    return pl.pallas_call(
        tie_kernel,
        in_specs=[any_spec] * (1 + len(after)),
        out_specs=any_spec,
        out_shape=jax.ShapeDtypeStruct(value.shape, value.dtype),
        input_output_aliases={0: 0},
        name="tie",
    )(value, *after)


def trade(value):
    return lax.all_to_all(
        value, "dp", split_axis=0, concat_axis=0, axis_index_groups=Z_GROUPS, tiled=True
    )


def spread(value):
    return trade(jnp.broadcast_to(value[None], (Z_SIZE, *value.shape)))


def join_kernel(*refs):
    refs[-1][...] = jnp.zeros_like(refs[-1])


class Rounds:
    def __init__(self):
        self.token = None

    def gate(self, value):
        return value if self.token is None else tie(value, self.token)

    def after(self):
        return () if self.token is None else (self.token,)

    def close(self, *arrays):
        arrays = list(arrays) + list(self.after())
        self.token = pl.pallas_call(
            join_kernel,
            in_specs=[pl.BlockSpec(memory_space=pl.ANY)] * len(arrays),
            out_specs=pl.BlockSpec(memory_space=pltpu.VMEM),
            out_shape=jax.ShapeDtypeStruct((8, 128), jnp.float32),
            name="join",
        )(*arrays)


def move(value, pairs):
    return lax.ppermute(value, MESH_AXES, pairs)


def assemble(plan, info, arrays, shape, name):
    any_spec = pl.BlockSpec(memory_space=pl.ANY)

    def kernel(info_ref, *refs):
        *parts, out, sem = refs
        copies = [
            pltpu.make_async_copy(source, target, sem.at[i])
            for i, (source, target) in enumerate(plan(info_ref, parts, out))
        ]
        for copy in copies:
            copy.start()
        for copy in copies:
            copy.wait()

    dtype = arrays[0].dtype
    size = 1
    for extent in shape:
        size *= extent
    return pl.pallas_call(
        kernel,
        grid_spec=pltpu.PrefetchScalarGridSpec(
            num_scalar_prefetch=1,
            grid=(),
            in_specs=[any_spec] * len(arrays),
            out_specs=pl.BlockSpec(memory_space=pltpu.VMEM),
            scratch_shapes=[pltpu.SemaphoreType.DMA((2 * len(arrays),))],
        ),
        out_shape=jax.ShapeDtypeStruct(shape, dtype),
        compiler_params=pltpu.CompilerParams(vmem_limit_bytes=32 * 1024 * 1024),
        cost_estimate=pl.CostEstimate(flops=0, bytes_accessed=4 * size, transcendentals=0),
        name=name,
    )(info, *arrays)


def dense_assemble(place, mine, other):
    z, y, x, c = place
    rows, n = mine[0].shape[1:]
    zs = Z_SIZE // 2

    def plan(info, parts, out):
        at_y, at_x = info[0], info[1]
        copies = []
        for k in range(2):
            at_c = info[2] if k == 0 else 1 - info[2]
            block, from_x, from_y, far_a, far_b = parts[5 * k : 5 * k + 5]
            copies += [
                (block, out.at[:, at_y, at_x, at_c]),
                (from_x, out.at[:, at_y, 1 - at_x, at_c]),
                (from_y, out.at[:, 1 - at_y, at_x, at_c]),
                (far_a, out.at[pl.ds(0, zs), 1 - at_y, 1 - at_x, at_c]),
                (far_b, out.at[pl.ds(zs, zs), 1 - at_y, 1 - at_x, at_c]),
            ]
        return copies

    shape = (Z_SIZE, Y_SIZE, X_SIZE, C_SIZE, rows, n)
    full = assemble(plan, jnp.stack([y, x, c]), (*mine, *other), shape, "dense_assemble")
    return full.reshape(-1, n)


def join_rows(other, own):
    counts = [part.shape[1] for part in own]

    def plan(info, parts, out):
        copies = []
        for k in range(2):
            at = 0
            for i, count in enumerate(counts):
                target = out.at[pl.ds(k * Z_SIZE, Z_SIZE), pl.ds(at, count)]
                copies.append((parts[k * len(counts) + i], target))
                at += count
        return copies

    shape = (2 * Z_SIZE, sum(counts), own[0].shape[2])
    return assemble(plan, jnp.zeros((1,), jnp.int32), (*other, *own), shape, "join_rows")


def half_order(z_to):
    first = 10 * (z_to // 2)
    if z_to % 2 == 0:
        return [first, first + 1, first + 2, first + 3, first + 4]
    return [first + 6, first + 7, first + 8, first + 9, first + 5]


HALF_ORDER = [half_order(z_to) for z_to in range(Z_SIZE)]
HALF_PLACE = [0] * (Z_SIZE * 5)
for order_z in range(Z_SIZE):
    for order_q in range(5):
        HALF_PLACE[HALF_ORDER[order_z][order_q]] = order_z * 5 + order_q
UNIT_HALVES = ((0, 2), (2, 4), (4, 5))


def dense_gates(logits, chosen):
    peak = jnp.max(jnp.where(chosen, logits, -jnp.inf), axis=-1, keepdims=True)
    exponent = jnp.where(chosen, jnp.exp(logits - peak), 0.0)
    return exponent / jnp.sum(exponent, axis=-1, keepdims=True)


def mm(left, right):
    return jnp.dot(left, right, preferred_element_type=jnp.float32)


def weight_loads(pieces, w_s, sem, y):
    copies = []
    for h in range(w_s.shape[0]):
        for piece, at_y in zip(pieces[2 * h : 2 * h + 2], (y, 1 - y)):
            copies.append(
                pltpu.make_async_copy(piece, w_s.at[h, :, at_y], sem.at[len(copies)])
            )
    return copies


def expert_forward_kernel(info, slots, gates, rows, *rest, count, waits):
    pieces = rest[:count]
    out, kept, gate_up_out, w_s, in_sem = rest[count + waits :]
    low = jnp.bfloat16
    step = pl.program_id(0)
    half = FF // 2
    halves = w_s.shape[0]
    loads = weight_loads(pieces, w_s, in_sem, info[0])

    @pl.when(step == 0)
    def _():
        for load in loads:
            load.start()

    group, length, width = rows.shape
    span = group * WIDE
    iota = lax.broadcasted_iota(jnp.int32, (WIDE, length), 0)
    gate_cols = []
    for j in range(group):
        pick = iota == slots[j]
        one_hot = jnp.where(pick, 1.0, 0.0).astype(low)
        gate_cols.append(jnp.sum(jnp.where(pick, gates[j], 0.0), axis=1, keepdims=True))
        kept[j * WIDE : (j + 1) * WIDE, :] = mm(one_hot, rows[j]).astype(low)
    gate_col = jnp.concatenate(gate_cols, axis=0)

    @pl.when(step == 0)
    def _():
        for load in loads:
            load.wait()

    produced = None
    for h in range(halves):
        gate_up_w = w_s[h, :, :, :, : 2 * half].reshape(width, 2 * half)
        down_t = w_s[h, :, :, :, 2 * half :].reshape(width, half)
        gate_up = mm(kept[...], gate_up_w)
        gate_up_out[:, 2 * h * half : 2 * (h + 1) * half] = gate_up
        gate = gate_up[:, :half]
        hidden = (gate * (1.0 / (1.0 + jnp.exp(-gate))) * gate_up[:, half:]).astype(low)
        term = multiply_transposed(hidden, down_t)
        produced = term if produced is None else produced + term
    out[...] = (produced * gate_col).astype(low).reshape(group, WIDE, width)


def expert_forward(place, halves, y, slots, gates, rows_in, pieces, buffer, after):
    sources, length, width = rows_in.shape
    _, rows, lanes = pieces[0].shape
    half = FF // 2
    low = jnp.bfloat16
    group = 2
    units = 2 * len(UNIT_HALVES)
    any_spec = pl.BlockSpec(memory_space=pl.ANY)
    row_spec = pl.BlockSpec((group, 1, length), lambda i, info: (i, 0, 0))
    waits = list(after)
    aliases = {}
    if buffer is not None:
        aliases = {4 + len(pieces): 0}
        waits = [buffer] + waits
    total = sources * WIDE
    span = group * WIDE
    return pl.pallas_call(
        functools.partial(expert_forward_kernel, count=len(pieces), waits=len(waits)),
        grid_spec=pltpu.PrefetchScalarGridSpec(
            num_scalar_prefetch=1,
            grid=(sources // group,),
            in_specs=[
                row_spec,
                row_spec,
                pl.BlockSpec((group, length, width), lambda i, info: (i, 0, 0)),
            ]
            + [any_spec] * (len(pieces) + len(waits)),
            out_specs=[
                pl.BlockSpec((group, WIDE, width), lambda i, info: (i, place, 0)),
                pl.BlockSpec((span, width), lambda i, info: (i, 0)),
                pl.BlockSpec((span, 2 * half * halves), lambda i, info: (i, 0)),
            ],
            scratch_shapes=[
                pltpu.VMEM((halves, Z_SIZE, Y_SIZE, rows, lanes), low),
                pltpu.SemaphoreType.DMA((4,)),
            ],
        ),
        out_shape=[
            jax.ShapeDtypeStruct((sources, units * WIDE, width), low),
            jax.ShapeDtypeStruct((total, width), low),
            jax.ShapeDtypeStruct((total, 2 * half * halves), jnp.float32),
        ],
        input_output_aliases=aliases,
        compiler_params=pltpu.CompilerParams(vmem_limit_bytes=60 * 1024 * 1024),
        cost_estimate=pl.CostEstimate(
            flops=2 * total * width * (3 * half * halves + length),
            bytes_accessed=2 * (sources * length * width + 2 * total * width)
            + 8 * total * half * halves
            + 2 * halves * width * lanes,
            transcendentals=total * half * halves,
        ),
        name="expert_forward",
    )(y, slots, gates, rows_in, *pieces, *waits)


def expert_back_kernel(info, slots, gates, dys, kept, gate_ups, *rest, count, waits):
    pieces = rest[:count]
    back, near_a_g, near_b_g, far_a_g, far_b_g = rest[count + waits : count + waits + 5]
    w_s, x_s, gd_s, dgu_s, hid_s, g_s, in_sem, out_sem = rest[count + waits + 5 :]
    low = jnp.bfloat16
    full = jnp.float32
    step = pl.program_id(0)
    y = info[0]
    expert = info[1]
    half = FF // 2
    zs = Z_SIZE // 2
    halves = w_s.shape[0]
    loads = weight_loads(pieces, w_s, in_sem, y)

    @pl.when(step == 0)
    def _():
        for load in loads:
            load.start()

    group, length, width = dys.shape
    span = group * WIDE
    here = pl.ds(pl.multiple_of(step * span, span), span)
    iota = lax.broadcasted_iota(jnp.int32, (WIDE, length), 0)
    gate_cols = []
    dy_parts = []
    for j in range(group):
        pick = iota == slots[j]
        one_hot = jnp.where(pick, 1.0, 0.0).astype(low)
        gate_col = jnp.sum(jnp.where(pick, gates[j], 0.0), axis=1, keepdims=True)
        at = pl.multiple_of(step * span + j * WIDE, WIDE)
        dy = mm(one_hot, dys[j])
        gd_s[pl.ds(at, WIDE), :] = (dy * (residual_scale * gate_col)).astype(low)
        dy_parts.append(dy.astype(low))
        gate_cols.append(gate_col)
    dy = jnp.concatenate(dy_parts, axis=0)
    gate_col = jnp.concatenate(gate_cols, axis=0)
    x_s[here, :] = kept[...]

    @pl.when(step == 0)
    def _():
        for load in loads:
            load.wait()

    grad_copy = None
    grad_gate = None
    for h in range(halves):
        gate_up_w = w_s[h, :, :, :, : 2 * half].reshape(width, 2 * half)
        down_t = w_s[h, :, :, :, 2 * half :].reshape(width, half)
        gate = gate_ups[:, 2 * h * half : (2 * h + 1) * half]
        upper = gate_ups[:, (2 * h + 1) * half : (2 * h + 2) * half]
        sigmoid = 1.0 / (1.0 + jnp.exp(-gate))
        swish = gate * sigmoid
        hidden = (swish * upper).astype(low)
        hid_s[here, h * half : (h + 1) * half] = hidden
        grad_plain = residual_scale * mm(dy, down_t)
        term = jnp.sum(hidden.astype(full) * grad_plain, axis=1, keepdims=True)
        grad_gate = term if grad_gate is None else grad_gate + term
        grad_hidden = grad_plain * gate_col
        dgu_s[here, 2 * h * half : (2 * h + 1) * half] = (
            grad_hidden * upper * sigmoid * (1.0 + gate * (1.0 - sigmoid))
        ).astype(low)
        dgu_s[here, (2 * h + 1) * half : (2 * h + 2) * half] = (grad_hidden * swish).astype(low)
        term = multiply_transposed(dgu_s[here, 2 * h * half : 2 * (h + 1) * half], gate_up_w)
        grad_copy = term if grad_copy is None else grad_copy + term
    back[:, :, :width] = grad_copy.astype(low).reshape(group, WIDE, width)
    lane = lax.broadcasted_iota(jnp.int32, (span, 128), 1)
    high = grad_gate.astype(low).astype(full)
    extra = jnp.where(lane == expert, high, 0.0) + jnp.where(
        lane == expert + 64, grad_gate - high, 0.0
    )
    back[:, :, width:] = extra.astype(low).reshape(group, WIDE, 128)

    @pl.when(step == pl.num_programs(0) - 1)
    def _():
        piece = width // Z_SIZE
        for h in range(halves):
            for zz in range(Z_SIZE):
                cols = slice(zz * piece, (zz + 1) * piece)
                got = contract_rows(x_s[:, cols], dgu_s[:, 2 * h * half : 2 * (h + 1) * half])
                g_s[h, zz, :, :, : 2 * half] = got.astype(low).reshape(2, piece // 2, 2 * half)
                got = contract_rows(gd_s[:, cols], hid_s[:, h * half : (h + 1) * half])
                g_s[h, zz, :, :, 2 * half :] = got.astype(low).reshape(2, piece // 2, half)
        stores = [
            (g_s.at[:, pl.ds(0, zs), y], near_a_g),
            (g_s.at[:, pl.ds(zs, zs), y], near_b_g),
            (g_s.at[:, pl.ds(0, zs), 1 - y], far_a_g),
            (g_s.at[:, pl.ds(zs, zs), 1 - y], far_b_g),
        ]
        stores = [pltpu.make_async_copy(a, b, out_sem.at[i]) for i, (a, b) in enumerate(stores)]
        for store in stores:
            store.start()
        for store in stores:
            store.wait()


def expert_backward(
    place, halves, info, slots, gates, grads_in, kept, gate_ups, pieces, buffer, after
):
    sources, length, width = grads_in.shape
    _, rows, lanes = pieces[0].shape
    half = FF // 2
    low = jnp.bfloat16
    group = 2
    units = 2 * len(UNIT_HALVES)
    any_spec = pl.BlockSpec(memory_space=pl.ANY)
    row_spec = pl.BlockSpec((group, 1, length), lambda i, info: (i, 0, 0))
    waits = list(after)
    aliases = {}
    if buffer is not None:
        aliases = {6 + len(pieces): 0}
        waits = [buffer] + waits
    total = sources * WIDE
    span = group * WIDE
    quarter = (halves, Z_SIZE // 2, rows, lanes)
    result = pl.pallas_call(
        functools.partial(expert_back_kernel, count=len(pieces), waits=len(waits)),
        grid_spec=pltpu.PrefetchScalarGridSpec(
            num_scalar_prefetch=1,
            grid=(sources // group,),
            in_specs=[
                row_spec,
                row_spec,
                pl.BlockSpec((group, length, width), lambda i, info: (i, 0, 0)),
                pl.BlockSpec((span, width), lambda i, info: (i, 0)),
                pl.BlockSpec((span, 2 * half * halves), lambda i, info: (i, 0)),
            ]
            + [any_spec] * (len(pieces) + len(waits)),
            out_specs=[
                pl.BlockSpec((group, WIDE, width + 128), lambda i, info: (i, place, 0)),
            ]
            + [any_spec] * 4,
            scratch_shapes=[
                pltpu.VMEM((halves, Z_SIZE, Y_SIZE, rows, lanes), low),
                pltpu.VMEM((total, width), low),
                pltpu.VMEM((total, width), low),
                pltpu.VMEM((total, 2 * half * halves), low),
                pltpu.VMEM((total, half * halves), low),
                pltpu.VMEM((halves, Z_SIZE, Y_SIZE, rows, lanes), low),
                pltpu.SemaphoreType.DMA((4,)),
                pltpu.SemaphoreType.DMA((4,)),
            ],
        ),
        out_shape=[jax.ShapeDtypeStruct((sources, units * WIDE, width + 128), low)]
        + [jax.ShapeDtypeStruct(quarter, low)] * 4,
        input_output_aliases=aliases,
        compiler_params=pltpu.CompilerParams(vmem_limit_bytes=60 * 1024 * 1024),
        cost_estimate=pl.CostEstimate(
            flops=2 * total * width * (6 * half * halves + length),
            bytes_accessed=2 * (sources * length * width + 2 * total * width)
            + 8 * total * half * halves
            + 4 * halves * width * lanes,
            transcendentals=total * half * halves,
        ),
        name="expert_backward",
    )(info, slots, gates, grads_in, kept, gate_ups, *pieces, *waits)
    return result[0], result[1:]


def middle_back_kernel(
    c_ref, got, gates, small, gain, middle, hidden, cotangent, mixed, dmiddle, dbranch, mine, theirs,
    g_s, sem,
):
    full = jnp.float32
    low = jnp.bfloat16
    c = c_ref[0]
    length, width = middle.shape
    total = got[0].astype(full)
    for z in range(1, Z_SIZE):
        total = total + got[z].astype(full)
    parts = total[:, width:]
    grad_gates = parts + pltpu.roll(parts, 64, 1)
    gate = gates[...]
    grad_logits = gate * (grad_gates - jnp.sum(gate * grad_gates, axis=1, keepdims=True))
    grad_logits = grad_logits.astype(low)
    dh2 = total[:, :width] + multiply_transposed(grad_logits, small[...])
    value = middle[...]
    inverse = rms_inverse(value)
    normal = value * inverse
    scaled = dh2 * gain[...]
    mean = jnp.mean(scaled * normal, axis=1, keepdims=True)
    grad = cotangent[...].astype(full) + inverse * (scaled - normal * mean)
    dmiddle[...] = grad
    branch = (residual_scale * grad).astype(low)
    dbranch[...] = branch
    blocks = g_s.shape[0]
    per = g_s.shape[2]
    step = width // Z_SIZE
    rows = blocks // Z_SIZE
    for z in range(Z_SIZE):
        part = slice(z * step, (z + 1) * step)
        here = slice(z * rows, (z + 1) * rows)
        term = contract_rows(branch[:, part], mixed[...]).astype(low)
        g_s[here, :, :, :width] = term.reshape(rows, C_SIZE, per, width)
        router = contract_rows(hidden[:, part], grad_logits)
        product = (dh2[:, part] * normal[:, part]).astype(low)
        second = contract_rows(product, jnp.ones((length, 128), low))
        lane = lax.broadcasted_iota(jnp.int32, router.shape, 1)
        router = jnp.where(lane == EXPERTS, second, router).astype(low)
        g_s[here, :, :, width:] = router.reshape(rows, C_SIZE, per, 128)
    copies = [
        pltpu.make_async_copy(g_s.at[:, c], mine, sem.at[0]),
        pltpu.make_async_copy(g_s.at[:, 1 - c], theirs, sem.at[1]),
    ]
    for copy in copies:
        copy.start()
    for copy in copies:
        copy.wait()


def middle_backward(c, got, gates, pack, small_at, gain, middle, hidden, cotangent, mixed):
    length, width = middle.shape
    low = jnp.bfloat16
    blocks = Z_SIZE * Y_SIZE * X_SIZE
    per = width // (blocks * C_SIZE)
    any_spec = pl.BlockSpec(memory_space=pl.ANY)
    whole = lambda a: pl.BlockSpec(a.shape, lambda i, n: (0,) * a.ndim)
    split = jax.ShapeDtypeStruct((blocks, per, width + 128), low)
    rows = pl.BlockSpec((length, width), lambda i, n: (0, 0))
    return pl.pallas_call(
        middle_back_kernel,
        grid_spec=pltpu.PrefetchScalarGridSpec(
            num_scalar_prefetch=1,
            grid=(1,),
            in_specs=[
                whole(got),
                whole(gates),
                pl.BlockSpec((width, 128), lambda i, n: (0, small_at // 128)),
                whole(gain),
                rows,
                rows,
                rows,
                rows,
            ],
            out_specs=[rows, rows, any_spec, any_spec],
            scratch_shapes=[
                pltpu.VMEM((blocks, C_SIZE, per, width + 128), low),
                pltpu.SemaphoreType.DMA((2,)),
            ],
        ),
        out_shape=[
            jax.ShapeDtypeStruct((length, width), jnp.float32),
            jax.ShapeDtypeStruct((length, width), low),
            split,
            split,
        ],
        compiler_params=pltpu.CompilerParams(vmem_limit_bytes=56 * 1024 * 1024),
        cost_estimate=pl.CostEstimate(
            flops=2 * length * width * (width + 384),
            bytes_accessed=length * width * 24 + 4 * width * width,
            transcendentals=0,
        ),
        name="middle_backward",
    )(c[None], got, gates, pack, gain, middle, hidden, cotangent, mixed)


def turn_halves(value):
    lanes = value.shape[-1]
    lane = lax.broadcasted_iota(jnp.int32, value.shape, 1)
    ahead = pltpu.roll(value, lanes - HEAD_SIZE // 2, 1)
    behind = pltpu.roll(value, HEAD_SIZE // 2, 1)
    return jnp.where(lane % HEAD_SIZE < HEAD_SIZE // 2, -ahead, behind)


def heads_of(value, first, count):
    return jnp.concatenate(
        [value[:, (first + i) * HEAD_SIZE : (first + i + 1) * HEAD_SIZE] for i in range(count)],
        axis=0,
    )


ROW_BLOCK = 128
PAIR = 2
GROUP = QUERY_HEADS // KEY_VALUE_HEADS
QUERY_LANES = PAIR * GROUP * HEAD_SIZE
KEY_LANES = PAIR * HEAD_SIZE


def block_mask(block, length):
    shape = (ROW_BLOCK, (block + 1) * ROW_BLOCK)
    row = lax.broadcasted_iota(jnp.int32, shape, 0) + block * ROW_BLOCK
    column = lax.broadcasted_iota(jnp.int32, shape, 1)
    allowed = jnp.where((column <= row) & (column < length), 1, 0)
    return jnp.concatenate([allowed] * GROUP, axis=0) > 0


def attention_kernel(
    length, tokens, gain, wq, wk, wv, cosine, sine, *rest
):
    h1, q, k, v, mixed, lse, h_s, lse_s = rest[-8:]
    step = pl.program_id(0)
    low = jnp.bfloat16
    rows = tokens.shape[0]

    @pl.when(step == 0)
    def _():
        value = tokens[...].astype(jnp.float32)
        hidden = (value * rms_inverse(value) * gain[...]).astype(low)
        h_s[...] = hidden
        h1[...] = hidden

    lane = lax.broadcasted_iota(jnp.int32, (rows, 128), 1)
    cos = cosine[...]
    sin = sine[...]
    query = mm(h_s[...], wq[...])
    query = (query * cos + turn_halves(query) * sin).astype(low)
    key = mm(h_s[...], wk[...])
    key = (key * cos[:, :KEY_LANES] + turn_halves(key) * sin[:, :KEY_LANES]).astype(low)
    value = mm(h_s[...], wv[...]).astype(low)
    q[...] = query
    k[...] = key
    v[...] = value
    blocks = rows // ROW_BLOCK
    totals = [[] for _ in range(PAIR * GROUP)]
    masks = [block_mask(block, length[0]) for block in range(blocks)]
    outs = [[] for _ in range(PAIR * GROUP)]
    for head in range(PAIR):
        key_h = key[:, head * HEAD_SIZE : (head + 1) * HEAD_SIZE]
        value_h = value[:, head * HEAD_SIZE : (head + 1) * HEAD_SIZE]
        for block in range(blocks):
            keys = (block + 1) * ROW_BLOCK
            query_h = heads_of(
                query[block * ROW_BLOCK : (block + 1) * ROW_BLOCK], head * GROUP, GROUP
            )
            scores = multiply_transposed(query_h, key_h[:keys]) * score_scale
            scores = jnp.where(masks[block], scores, masked_score)
            peak = jnp.max(scores, axis=1, keepdims=True)
            exponent = jnp.exp(scores - peak)
            total = jnp.sum(exponent, axis=1, keepdims=True)
            weights = (exponent / total).astype(low)
            out = mm(weights, value_h[:keys]).astype(low)
            log_total = peak + jnp.log(total)
            for i in range(GROUP):
                part = slice(i * ROW_BLOCK, (i + 1) * ROW_BLOCK)
                outs[head * GROUP + i].append(out[part])
                totals[head * GROUP + i].append(log_total[part])
    mixed[...] = jnp.concatenate([jnp.concatenate(o, axis=0) for o in outs], axis=1)

    @pl.when(step == 0)
    def _():
        lse_s[...] = jnp.zeros_like(lse_s)

    kept = lse_s[...]
    for i in range(PAIR * GROUP):
        column = jnp.concatenate(totals[i], axis=0)
        kept = jnp.where(lane == step * PAIR * GROUP + i, column, kept)
    lse_s[...] = kept
    lse[...] = kept


def attention_forward(length, tokens, gain, weight, cosine, sine, after=()):
    rows, width = tokens.shape
    steps = KEY_VALUE_HEADS // PAIR
    low = jnp.bfloat16
    query_total = QUERY_HEADS * HEAD_SIZE
    key_total = KEY_VALUE_HEADS * HEAD_SIZE
    key_at = query_total // KEY_LANES
    value_at = key_at + steps
    whole = lambda shape: pl.BlockSpec(shape, lambda i, n: (0, 0))
    cols = lambda lanes, at: pl.BlockSpec((width, lanes), lambda i, n: (0, at + i))
    part = lambda lanes: pl.BlockSpec((rows, lanes), lambda i, n: (0, i))
    return pl.pallas_call(
        attention_kernel,
        grid_spec=pltpu.PrefetchScalarGridSpec(
            num_scalar_prefetch=1,
            grid=(steps,),
            in_specs=[
                whole((rows, width)),
                whole((1, width)),
                cols(QUERY_LANES, 0),
                cols(KEY_LANES, key_at),
                cols(KEY_LANES, value_at),
                whole((rows, QUERY_LANES)),
                whole((rows, QUERY_LANES)),
            ]
            + [pl.BlockSpec(memory_space=pl.ANY)] * len(after),
            out_specs=[
                whole((rows, width)),
                part(QUERY_LANES),
                part(KEY_LANES),
                part(KEY_LANES),
                part(QUERY_LANES),
                whole((rows, 128)),
            ],
            scratch_shapes=[pltpu.VMEM((rows, width), low), pltpu.VMEM((rows, 128), jnp.float32)],
        ),
        out_shape=[
            jax.ShapeDtypeStruct((rows, width), low),
            jax.ShapeDtypeStruct((rows, query_total), low),
            jax.ShapeDtypeStruct((rows, key_total), low),
            jax.ShapeDtypeStruct((rows, key_total), low),
            jax.ShapeDtypeStruct((rows, query_total), low),
            jax.ShapeDtypeStruct((rows, 128), jnp.float32),
        ],
        compiler_params=pltpu.CompilerParams(vmem_limit_bytes=48 * 1024 * 1024),
        cost_estimate=pl.CostEstimate(
            flops=2 * rows * width * (query_total + 2 * key_total)
            + 4 * QUERY_HEADS * rows * rows * HEAD_SIZE,
            bytes_accessed=2 * width * (query_total + 2 * key_total) + 10 * rows * width,
            transcendentals=QUERY_HEADS * rows * rows,
        ),
        name="attention_forward",
    )(length, tokens, gain, weight, weight, weight, cosine, sine, *after)


def attention_back_kernel(
    length, dbranch, wo, q, k, v, lse, h1, wq, wk, wv, cosine, sine, tokens, *rest
):
    mine, theirs, dh1, dh_s, g_s = rest[-5:]
    c = length[1]
    step = pl.program_id(0)
    low = jnp.bfloat16
    full = jnp.float32
    rows = dbranch.shape[0]
    split = (Z_SIZE * Y_SIZE * X_SIZE, C_SIZE, h1.shape[1] // (Z_SIZE * Y_SIZE * X_SIZE * C_SIZE))

    @pl.when(step < pl.num_programs(0) - 1)
    def _():
        blocks = rows // ROW_BLOCK
        dmixed = mm(dbranch[...], wo[...]).astype(low)
        lane = lax.broadcasted_iota(jnp.int32, (rows, 128), 1)
        kept = lse[...]
        query, key, value = q[...], k[...], v[...]
        columns = [
            jnp.sum(jnp.where(lane == step * PAIR * GROUP + i, kept, 0.0), axis=1, keepdims=True)
            for i in range(PAIR * GROUP)
        ]
        masks = [block_mask(block, length[0]) for block in range(blocks)]
        dq = [[] for _ in range(PAIR * GROUP)]
        dks, dvs = [], []
        for head in range(PAIR):
            key_h = key[:, head * HEAD_SIZE : (head + 1) * HEAD_SIZE]
            value_h = value[:, head * HEAD_SIZE : (head + 1) * HEAD_SIZE]
            dk = [None] * blocks
            dv = [None] * blocks
            for block in range(blocks):
                keys = (block + 1) * ROW_BLOCK
                at = slice(block * ROW_BLOCK, (block + 1) * ROW_BLOCK)
                query_h = heads_of(query[at], head * GROUP, GROUP)
                dmixed_h = heads_of(dmixed[at], head * GROUP, GROUP)
                log_total = jnp.concatenate(
                    [columns[head * GROUP + i][at] for i in range(GROUP)], axis=0
                )
                scores = multiply_transposed(query_h, key_h[:keys]) * score_scale
                scores = jnp.where(masks[block], scores, masked_score)
                probs = jnp.exp(scores - log_total)
                dprobs = multiply_transposed(dmixed_h, value_h[:keys])
                delta = jnp.sum(probs * dprobs, axis=1, keepdims=True)
                dscores = (probs * (dprobs - delta)).astype(low)
                dquery = mm(dscores, key_h[:keys]) * score_scale
                dkey = contract_rows(dscores, query_h) * score_scale
                dvalue = contract_rows(probs.astype(low), dmixed_h)
                for i in range(GROUP):
                    dq[head * GROUP + i].append(dquery[i * ROW_BLOCK : (i + 1) * ROW_BLOCK])
                for b in range(block + 1):
                    part = slice(b * ROW_BLOCK, (b + 1) * ROW_BLOCK)
                    dk[b] = dkey[part] if dk[b] is None else dk[b] + dkey[part]
                    dv[b] = dvalue[part] if dv[b] is None else dv[b] + dvalue[part]
            dks.append(jnp.concatenate(dk, axis=0))
            dvs.append(jnp.concatenate(dv, axis=0))
        cos = cosine[...]
        sin = sine[...]
        dquery = jnp.concatenate([jnp.concatenate(o, axis=0) for o in dq], axis=1)
        dquery = (dquery * cos - turn_halves(dquery * sin)).astype(low)
        dkey = jnp.concatenate(dks, axis=1)
        dkey = (dkey * cos[:, :KEY_LANES] - turn_halves(dkey * sin[:, :KEY_LANES])).astype(low)
        dvalue = jnp.concatenate(dvs, axis=1).astype(low)
        hidden = h1[...]
        got = contract_rows(hidden, dquery).astype(low)
        g_s[:, :, :, :QUERY_LANES] = got.reshape(*split, QUERY_LANES)
        got = contract_rows(hidden, jnp.concatenate([dkey, dvalue], axis=1)).astype(low)
        g_s[:, :, :, QUERY_LANES:] = got.reshape(*split, 2 * KEY_LANES)
        mine[...] = g_s[:, c]
        theirs[...] = g_s[:, 1 - c]
        term = (
            multiply_transposed(dquery, wq[...])
            + multiply_transposed(dkey, wk[...])
            + multiply_transposed(dvalue, wv[...])
        )

        @pl.when(step == 0)
        def _():
            dh_s[...] = term

        @pl.when(step > 0)
        def _():
            dh_s[...] += term

    @pl.when(step == pl.num_programs(0) - 1)
    def _():
        total = dh_s[...]
        dh1[...] = total
        value = tokens[...].astype(full)
        product = (total * (value * rms_inverse(value))).astype(low)
        column = contract_rows(product, jnp.ones((rows, 128), low)).astype(low)
        g_s[:, :, :, :128] = column.reshape(*split, 128)
        mine[:, :, :128] = g_s[:, c, :, :128]
        theirs[:, :, :128] = g_s[:, 1 - c, :, :128]


def attention_backward(
    length, dbranch, q, k, v, lse, h1, weight, out_at, cosine, sine, tokens, after=()
):
    rows, width = dbranch.shape
    steps = KEY_VALUE_HEADS // PAIR
    low = jnp.bfloat16
    full = jnp.float32
    query_total = QUERY_HEADS * HEAD_SIZE
    key_total = KEY_VALUE_HEADS * HEAD_SIZE
    key_at = query_total // KEY_LANES
    value_at = key_at + steps
    whole = lambda shape: pl.BlockSpec(shape, lambda i, n: (0, 0))
    cols = lambda lanes, at: pl.BlockSpec((width, lanes), lambda i, n: (0, at + jnp.minimum(i, steps - 1)))
    part = lambda lanes: pl.BlockSpec((rows, lanes), lambda i, n: (0, jnp.minimum(i, steps - 1)))
    lanes = QUERY_LANES + 2 * KEY_LANES
    blocks = Z_SIZE * Y_SIZE * X_SIZE
    per = width // (blocks * C_SIZE)
    return pl.pallas_call(
        attention_back_kernel,
        grid_spec=pltpu.PrefetchScalarGridSpec(
            num_scalar_prefetch=1,
            grid=(steps + 1,),
            in_specs=[
                whole((rows, width)),
                cols(QUERY_LANES, out_at // QUERY_LANES),
                part(QUERY_LANES),
                part(KEY_LANES),
                part(KEY_LANES),
                whole((rows, 128)),
                whole((rows, width)),
                cols(QUERY_LANES, 0),
                cols(KEY_LANES, key_at),
                cols(KEY_LANES, value_at),
                whole((rows, QUERY_LANES)),
                whole((rows, QUERY_LANES)),
                whole((rows, width)),
            ]
            + [pl.BlockSpec(memory_space=pl.ANY)] * len(after),
            out_specs=[
                pl.BlockSpec((blocks, per, lanes), lambda i, n: (0, 0, i)),
                pl.BlockSpec((blocks, per, lanes), lambda i, n: (0, 0, i)),
                whole((rows, width)),
            ],
            scratch_shapes=[
                pltpu.VMEM((rows, width), full),
                pltpu.VMEM((blocks, C_SIZE, per, lanes), low),
            ],
        ),
        out_shape=[
            jax.ShapeDtypeStruct((blocks, per, steps * lanes + 128), low),
            jax.ShapeDtypeStruct((blocks, per, steps * lanes + 128), low),
            jax.ShapeDtypeStruct((rows, width), full),
        ],
        compiler_params=pltpu.CompilerParams(vmem_limit_bytes=48 * 1024 * 1024),
        cost_estimate=pl.CostEstimate(
            flops=4 * rows * width * (query_total + 2 * key_total)
            + 2 * rows * width * query_total
            + 10 * QUERY_HEADS * rows * rows * HEAD_SIZE,
            bytes_accessed=4 * width * (query_total + 2 * key_total) + 2 * width * width + 14 * rows * width,
            transcendentals=QUERY_HEADS * rows * rows,
        ),
        name="attention_backward",
    )(length, dbranch, weight, q, k, v, lse, h1, weight, weight, weight, cosine, sine, tokens, *after)


def combine_kernel(slots, values, *rest):
    other, own, p_s = rest[-3:]
    step = pl.program_id(0)
    length = slots.shape[2]
    iota = lax.broadcasted_iota(jnp.int32, (WIDE, length), 0)
    for u in range(slots.shape[1]):
        pick = iota == slots[0, u : u + 1, :]
        p_s[u * WIDE : (u + 1) * WIDE, :] = jnp.where(pick, 1.0, 0.0).astype(jnp.bfloat16)
    result = contract_rows(p_s[...], values[0]).astype(jnp.bfloat16)

    @pl.when(step < Z_SIZE)
    def _():
        other[0] = result

    @pl.when(step >= Z_SIZE)
    def _():
        own[0] = result


def combine(slots, values, after=()):
    sources, units, length = slots.shape
    n = values.shape[-1]
    low = jnp.bfloat16
    return pl.pallas_call(
        combine_kernel,
        grid=(sources,),
        in_specs=[
            pl.BlockSpec((1, units, length), lambda i: (i, 0, 0)),
            pl.BlockSpec((1, units * WIDE, n), lambda i: (i, 0, 0)),
        ]
        + [pl.BlockSpec(memory_space=pl.ANY)] * len(after),
        out_specs=[
            pl.BlockSpec((1, length, n), lambda i: (jnp.minimum(i, Z_SIZE - 1), 0, 0)),
            pl.BlockSpec((1, length, n), lambda i: (jnp.maximum(i - Z_SIZE, 0), 0, 0)),
        ],
        out_shape=[jax.ShapeDtypeStruct((Z_SIZE, length, n), low)] * 2,
        scratch_shapes=[pltpu.VMEM((units * WIDE, length), low)],
        compiler_params=pltpu.CompilerParams(vmem_limit_bytes=60 * 1024 * 1024),
        cost_estimate=pl.CostEstimate(
            flops=2 * sources * units * WIDE * length * n,
            bytes_accessed=sources * (units * WIDE + length) * n * 2,
            transcendentals=0,
        ),
        name="combine",
    )(slots, values, *after)


def weight_chunks(gate_up_weight, down_weight):
    experts, rows = gate_up_weight.shape[0], gate_up_weight.shape[1]
    gate, upper = gate_up_weight[..., :FF], gate_up_weight[..., FF:]
    down_t = down_weight.transpose(0, 2, 1)
    half = FF // 2

    def one(q):
        cols = slice((q % 2) * half, (q % 2 + 1) * half)
        return jnp.concatenate([part[q // 2, :, cols] for part in (gate, upper, down_t)], axis=-1)

    return [
        jnp.stack([one(HALF_ORDER[z_to][j]) for z_to in range(Z_SIZE)]) for j in range(5)
    ]


def finish_kernel(*refs):
    parts, gate_up, down = refs[:5], refs[-2], refs[-1]
    half = FF // 2
    full = jnp.float32
    for z_from in range(Z_SIZE):
        for j in range(5):
            expert, side = divmod(HALF_ORDER[z_from][j], 2)
            cols = slice(side * half, (side + 1) * half)
            gate_up[expert, :, cols] = parts[j][z_from, :, :half].astype(full)
            cols_up = slice(FF + side * half, FF + (side + 1) * half)
            gate_up[expert, :, cols_up] = parts[j][z_from, :, half : 2 * half].astype(full)
            down[expert, :, cols] = parts[j][z_from, :, 2 * half :].astype(full)


def finish_grads(backs, after):
    rows = backs[0].shape[1]
    experts = EXPERTS // (X_SIZE * C_SIZE)
    vmem = pl.BlockSpec(memory_space=pltpu.VMEM)
    return pl.pallas_call(
        finish_kernel,
        in_specs=[vmem] * 5 + [pl.BlockSpec(memory_space=pl.ANY)] * len(after),
        out_specs=[vmem, vmem],
        out_shape=[
            jax.ShapeDtypeStruct((experts, rows, 2 * FF), jnp.float32),
            jax.ShapeDtypeStruct((experts, rows, FF), jnp.float32),
        ],
        compiler_params=pltpu.CompilerParams(vmem_limit_bytes=40 * 1024 * 1024),
        cost_estimate=pl.CostEstimate(
            flops=0, bytes_accessed=experts * rows * FF * 18, transcendentals=0
        ),
        name="finish_grads",
    )(*backs, *after)


class DenseScatter:
    def __init__(self, mine, theirs, place):
        shape = (Z_SIZE, Y_SIZE, X_SIZE, *mine.shape[1:])
        self.mine, self.theirs, self.place = mine.reshape(shape), theirs.reshape(shape), place

    def block(self, other_y, other_x):
        y = 1 - self.place[1] if other_y else self.place[1]
        x = 1 - self.place[2] if other_x else self.place[2]
        size = (Z_SIZE, 1, 1, *self.mine.shape[3:])
        got = [
            lax.dynamic_slice(a, (0, y, x, 0, 0), size).reshape(Z_SIZE, *size[3:])
            for a in (self.mine, self.got)
        ]
        return plus(*got)

    def cores(self):
        self.got = move(self.theirs, PAIRS_C)
        return [self.got]

    def first(self):
        low = jnp.bfloat16
        zs = Z_SIZE // 2
        self.near, self.to_x, self.to_y, far = [
            self.block(*at) for at in ((False, False), (False, True), (True, False), (True, True))
        ]
        gate = lambda value: value
        self.via_x = move(gate(far[:zs].astype(low)), PAIRS_X)
        self.via_y = move(gate(far[zs:].astype(low)), PAIRS_Y)
        self.x_a = move(gate(self.to_x[:zs].astype(low)), PAIRS_X)
        self.y_b = move(gate(self.to_y[zs:].astype(low)), PAIRS_Y)
        return [self.via_x, self.via_y, self.x_a, self.y_b]

    def second(self):
        low = jnp.bfloat16
        zs = Z_SIZE // 2
        gate = lambda value: value
        self.x_b = move(gate(plus(self.to_x[zs:], self.via_y).astype(low)), PAIRS_X)
        self.y_a = move(gate(plus(self.to_y[:zs], self.via_x).astype(low)), PAIRS_Y)
        return [self.x_b, self.y_a]

    def along(self):
        zs = Z_SIZE // 2
        self.total = jnp.concatenate(
            [
                plus(self.near[:zs], self.x_a) + self.y_a.astype(jnp.float32),
                plus(self.near[zs:], self.x_b) + self.y_b.astype(jnp.float32),
            ]
        ).astype(jnp.bfloat16)
        self.parts = trade(self.total)
        return [self.parts]

    def result(self):
        return jnp.sum(self.parts.astype(jnp.float32), axis=0)


def of_core(term, c):
    rows = term.shape[0] // (Z_SIZE * Y_SIZE * X_SIZE * C_SIZE)
    blocks = term.reshape(Z_SIZE * Y_SIZE * X_SIZE, C_SIZE, rows, term.shape[1])
    return lax.dynamic_index_in_dim(blocks, c, 1, keepdims=False)


def plus(a, b):
    return a.astype(jnp.float32) + b.astype(jnp.float32)


def ring_total(own, first, second, h):
    x_a, y_b = first
    x_b, y_a = second
    return jnp.concatenate(
        [
            plus(own[0][h], x_a[h]) + y_a[h].astype(jnp.float32),
            plus(own[1][h], x_b[h]) + y_b[h].astype(jnp.float32),
        ]
    ).astype(jnp.bfloat16)


def body(
    tokens,
    cotangent,
    lengths,
    routes,
    slots,
    first_gain,
    qkv_weight,
    out_weight,
    second_gain,
    router_weight,
    gate_up_weight,
    down_weight,
):
    low = jnp.bfloat16
    full = jnp.float32
    dp_index = lax.axis_index("dp")
    expert_index = lax.axis_index("expert")
    z, y = dp_index // Y_SIZE, dp_index % Y_SIZE
    x, c = expert_index // C_SIZE, expert_index % C_SIZE
    sequence_length = tokens.shape[0]
    width = tokens.shape[1]
    rows = gate_up_weight.shape[1]

    chosen_by = routes[None, :, :] == jnp.arange(EXPERTS, dtype=jnp.int32)[:, None, None]
    slot_table = jnp.sum(jnp.where(chosen_by, slots[None, :, :] + 1, 0), axis=-1) - 1
    place = (z, y, x, c)
    zs = Z_SIZE // 2
    steps = range(1, Z_SIZE)
    rounds = Rounds()
    gate = rounds.gate

    small = jnp.concatenate(
        [router_weight, first_gain[:, None], second_gain[:, None]], axis=1
    )
    small = jnp.pad(small, ((0, 0), (0, 128 - small.shape[1])))
    shard = jnp.concatenate([qkv_weight, small, out_weight.T], axis=1)
    table = slot_table.astype(low)

    block = spread(shard)
    tables = spread(table)
    cuts = weight_chunks(gate_up_weight, down_weight)
    rounds.close(block, tables)

    near, far, moved = [None] * 5, [None] * 5, [None] * 5

    def send_half(q):
        moved[q] = trade(gate(cuts[q]))
        return [moved[q]]

    def send_near(q):
        near[q] = (move(moved[q], PAIRS_X), move(moved[q], PAIRS_Y))
        return near[q]

    def send_far(q):
        far[q] = move(near[q][1], PAIRS_X) if q % 2 == 0 else move(near[q][0], PAIRS_Y)
        return [far[q]]

    from_x, from_y = move(block, PAIRS_X), move(block, PAIRS_Y)
    block_c = move(block, PAIRS_C)
    tables_c = move(tables, PAIRS_C)
    rounds.close(from_x, from_y, block_c, tables_c, *send_half(0))
    far_a, far_b = move(from_y[:zs], PAIRS_X), move(from_x[zs:], PAIRS_Y)
    from_x_c, from_y_c = move(from_x, PAIRS_C), move(from_y, PAIRS_C)
    rounds.close(far_a, far_b, from_x_c, from_y_c, *send_half(1))
    far_a_c, far_b_c = move(far_a, PAIRS_C), move(far_b, PAIRS_C)
    moved[0] = gate(moved[0])
    send_half(2)
    pack = dense_assemble(
        place,
        (block, from_x, from_y, far_a, far_b),
        (block_c, from_x_c, from_y_c, far_a_c, far_b_c),
    )
    rounds.close(pack, moved[2], *send_near(0))
    out_at = qkv_weight.shape[1] + small.shape[1]
    out_t = pack[:, out_at:]
    small_full = pack[:, qkv_weight.shape[1] : out_at]
    router_full = small_full[:, :EXPERTS]
    gain_one = small_full[:, EXPERTS].astype(full)
    gain_two = small_full[:, EXPERTS + 1].astype(full)

    inputs = tokens.astype(full)
    inverse_one = rms_inverse(inputs)
    normal_one = inputs * inverse_one
    cosine_table, sine_table = rope_tables(sequence_length)
    cosine_table = jnp.tile(cosine_table, (1, QUERY_LANES // HEAD_SIZE))
    sine_table = jnp.tile(sine_table, (1, QUERY_LANES // HEAD_SIZE))
    hidden_one, query_rows, keys, value_rows, mixed, log_totals = attention_forward(
        lengths, tokens, gain_one[None, :], pack, cosine_table, sine_table, rounds.after()
    )
    moved[1] = gate(moved[1])
    rounds.close(*send_half(3), *send_near(1), mixed)
    moved[2] = gate(moved[2])
    send_half(4)
    branch = multiply_transposed(mixed, out_t)
    middle = inputs + residual_scale * branch
    inverse_two = rms_inverse(middle)
    normal_two = middle * inverse_two
    hidden_two = (normal_two * gain_two).astype(low)
    grad_out = cotangent.astype(full)

    rounds.close(moved[4], *send_near(2))
    rows_own = spread(gate(hidden_two))
    moved[3] = gate(moved[3])
    rounds.close(*send_near(3))
    moved[4] = gate(moved[4])
    rounds.close(*send_near(4))
    for first, second in ((0, 1), (2, 3)):
        near[first] = (near[first][0], gate(near[first][1]))
        near[second] = (gate(near[second][0]), near[second][1])
        rounds.close(*send_far(first), *send_far(second))
    rounds.close(rows_own)
    rows_own = gate(rows_own)
    rows_other = move(rows_own, PAIRS_C)
    rounds.close(rows_other)
    rows_in = join_rows([rows_other], [rows_own])
    slots_in = jnp.concatenate([tables_c, tables], axis=0).astype(jnp.int32)
    logits_in = jnp.einsum("de,itd->iet", router_full, rows_in, preferred_element_type=full)
    chosen_in = slots_in >= 0
    peak_in = jnp.max(jnp.where(chosen_in, logits_in, -jnp.inf), axis=1, keepdims=True)
    exponent_in = jnp.where(chosen_in, jnp.exp(logits_in - peak_in), 0.0)
    gates_in = exponent_in / jnp.sum(exponent_in, axis=1, keepdims=True)

    units = range(len(UNIT_HALVES))
    even = z % 2 == 0
    ids = []
    for group in (1 - x, x):
        base = EXPERTS // (X_SIZE * C_SIZE) * (group * C_SIZE + c) + 5 * (z // 2)
        ids += [base + jnp.where(even, 0, 3), base + jnp.where(even, 1, 4), base + 2]
    unit_slots = [lax.dynamic_index_in_dim(slots_in, expert, 1, keepdims=True) for expert in ids]
    unit_gates = [lax.dynamic_index_in_dim(gates_in, expert, 1, keepdims=True) for expert in ids]
    pairs = len(UNIT_HALVES)
    sizes = [end - first for first, end in UNIT_HALVES]
    all_slots = jnp.concatenate(unit_slots, axis=1)
    infos = [jnp.stack([y, expert]).astype(jnp.int32) for expert in ids]
    buffer = None
    saved = {}

    def ring(pair, own):
        halves = range(*UNIT_HALVES[pair])
        if own:
            return [p for q in halves for p in (moved[q], near[q][1])]
        return [p for q in halves for p in (near[q][0], far[q])]

    def run_forward(pair, own):
        nonlocal buffer
        at = pair + (pairs if own else 0)
        buffer, *saved[at] = expert_forward(
            at,
            sizes[pair],
            infos[at],
            unit_slots[at],
            unit_gates[at],
            rows_in,
            ring(pair, own),
            buffer,
            rounds.after(),
        )

    dy_own = spread(gate(cotangent))
    late = [(4,), (), ()]
    for pair in range(pairs):
        sent = []
        for q in late[pair]:
            near[q] = tuple(gate(part) for part in near[q])
            sent += send_far(q)
        run_forward(pair, False)
        run_forward(pair, True)
        rounds.close(saved[pair + pairs][0], *sent)
    mix_other, mix_own = combine(all_slots, buffer, rounds.after())
    rounds.close(mix_other, dy_own)
    mix_moved = move(mix_other, PAIRS_C)
    dy_other = move(dy_own, PAIRS_C)
    rounds.close(mix_moved, dy_other)
    grads_in = join_rows([dy_other], [dy_own])

    back = None
    grads = [[None, None] for _ in units]

    def run_back(pair, own):
        nonlocal back
        at = pair + (pairs if own else 0)
        back, grads[pair][1 if own else 0] = expert_backward(
            at,
            sizes[pair],
            infos[at],
            unit_slots[at],
            unit_gates[at],
            grads_in,
            *saved[at],
            ring(pair, own),
            back,
            rounds.after(),
        )

    vias, firsts, seconds = [None] * 3, [None] * 3, [None] * 3

    def send_via(u):
        vias[u] = (move(gate(grads[u][0][2]), PAIRS_X), move(gate(grads[u][0][3]), PAIRS_Y))
        return vias[u]

    def send_first(u):
        firsts[u] = (move(gate(grads[u][0][0]), PAIRS_X), move(gate(grads[u][1][3]), PAIRS_Y))
        return firsts[u]

    def send_second(u):
        via_x, via_y = vias[u]
        seconds[u] = (
            move(gate(plus(grads[u][0][1], via_y).astype(low)), PAIRS_X),
            move(gate(plus(grads[u][1][2], via_x).astype(low)), PAIRS_Y),
        )
        return seconds[u]

    def total_of(u):
        return [ring_total(grads[u][1], firsts[u], seconds[u], h) for h in range(sizes[u])]

    terms = plus(mix_own, mix_moved).astype(low)
    mix_got = trade(gate(terms))
    run_back(0, False)
    rounds.close(grads[0][0][0])
    run_back(0, True)
    rounds.close(grads[0][1][0], *send_via(0))
    run_back(1, False)
    rounds.close(grads[1][0][0], *send_first(0))
    run_back(1, True)
    rounds.close(mix_got, grads[1][1][0], *send_second(0))
    mixture = jnp.sum(mix_got.astype(full), axis=0)
    output = (middle + residual_scale * mixture).astype(low)
    totals = total_of(0)
    backs = []

    def send_back():
        q = len(backs)
        backs.append(trade(gate(totals[q])))
        return backs[-1:]

    run_back(2, False)
    rounds.close(grads[2][0][0], *send_via(1), *send_back())
    run_back(2, True)
    rounds.close(grads[2][1][0], *send_first(1), *send_back())
    copy_other, copy_own = combine(all_slots, back, rounds.after())
    rounds.close(copy_other, *send_second(1), *send_via(2))
    copy_moved = move(copy_other, PAIRS_C)
    rounds.close(copy_moved)
    copy_got = trade(plus(copy_own, copy_moved).astype(low))
    rounds.close(copy_got)
    totals += total_of(1)
    chosen = (slot_table >= 0).T
    gates = dense_gates(jnp.dot(hidden_two, router_full, preferred_element_type=full), chosen)
    grad_middle, branch_gradient, out_mine, out_theirs = middle_backward(
        c,
        copy_got,
        jnp.pad(gates, ((0, 0), (0, 128 - EXPERTS))),
        pack,
        qkv_weight.shape[1],
        gain_two[None, :],
        middle,
        hidden_two,
        cotangent,
        mixed,
    )
    out_scatter = DenseScatter(out_mine, out_theirs, place)
    rounds.close(out_scatter.theirs, branch_gradient)
    qkv_mine, qkv_theirs, grad_hidden_one = attention_backward(
        jnp.concatenate([lengths, c[None]]),
        branch_gradient,
        query_rows,
        keys,
        value_rows,
        log_totals,
        hidden_one,
        pack,
        out_at,
        cosine_table,
        sine_table,
        tokens,
        rounds.after(),
    )
    rounds.close(grad_hidden_one, *out_scatter.cores(), *send_back(), *send_first(2))
    qkv_scatter = DenseScatter(qkv_mine, qkv_theirs, place)
    rounds.close(*qkv_scatter.cores(), *out_scatter.first(), *send_back(), *send_second(2))
    totals += total_of(2)
    rounds.close(*qkv_scatter.first(), *out_scatter.second(), *send_back())
    rounds.close(*qkv_scatter.second(), *out_scatter.along())
    qkv_scatter.along()
    gate_up_grads, down_grads = finish_grads(backs, [qkv_scatter.total])
    down_grads = down_grads.transpose(0, 2, 1)
    _, grad_norm_one = norm_backward(
        grad_hidden_one, normal_one, inverse_one, gain_one
    )
    grad_input = grad_middle + grad_norm_one

    qkv_sum = qkv_scatter.result()
    first_sum = qkv_sum[:, -128]
    qkv_sum = qkv_sum[:, :-128]
    qkv_sum = qkv_sum.reshape(qkv_sum.shape[0], -1, QUERY_LANES + 2 * KEY_LANES)
    qkv_sum = jnp.concatenate(
        [
            part.reshape(qkv_sum.shape[0], -1)
            for part in jnp.split(qkv_sum, (QUERY_LANES, QUERY_LANES + KEY_LANES), axis=2)
        ],
        axis=1,
    )
    out_sum = out_scatter.result()
    small_sum = out_sum[:, width:]
    return (
        output,
        grad_input,
        first_sum,
        qkv_sum,
        out_sum[:, :width].T,
        small_sum[:, EXPERTS],
        small_sum[:, :EXPERTS],
        gate_up_grads,
        down_grads,
    )


def solution(mesh):
    in_specs = (
        P(("dp", "expert"), None),
        P(("dp", "expert"), None),
        P(("dp", "expert")),
        P(("dp", "expert"), None),
        P(("dp", "expert"), None),
        P(("dp", "expert")),
        P(("dp", "expert"), None),
        P(None, ("dp", "expert")),
        P(("dp", "expert")),
        P(("dp", "expert"), None),
        P("expert", "dp", None),
        P("expert", None, "dp"),
    )
    out_specs = (
        P(("dp", "expert"), None),
        P(("dp", "expert"), None),
        P(("dp", "expert")),
        P(("dp", "expert"), None),
        P(None, ("dp", "expert")),
        P(("dp", "expert")),
        P(("dp", "expert"), None),
        P("expert", "dp", None),
        P("expert", None, "dp"),
    )
    fits = mesh.shape["dp"] == Z_SIZE * Y_SIZE and mesh.shape["expert"] == X_SIZE * C_SIZE
    chosen = body if fits else general_body
    return jax.shard_map(chosen, mesh=mesh, in_specs=in_specs, out_specs=out_specs, check_vma=False)
```

```python
import functools

import jax
import jax.numpy as jnp
from jax import lax
from jax.experimental import pallas as pl
from jax.experimental.pallas import tpu as pltpu
from jax.sharding import PartitionSpec as P

QUERY_HEADS = 24
KEY_VALUE_HEADS = 8
HEAD_SIZE = 64
FF = 512
EXPERTS = 40
TOP = 8
CAP = 152


epsilon = 1e-06
residual_scale = 0.22
score_scale = 0.015625
rope_base = 10000.0
masked_score = -1e30


def rope_tables(length):
    half = HEAD_SIZE // 2
    freqs = jnp.power(rope_base, -2.0 * jnp.arange(half, dtype=jnp.float32) / HEAD_SIZE)
    angles = jnp.arange(length, dtype=jnp.float32)[:, None] * freqs[None, :]
    cosine_table = jnp.concatenate([jnp.cos(angles), jnp.cos(angles)], axis=-1)
    sine_table = jnp.concatenate([jnp.sin(angles), jnp.sin(angles)], axis=-1)
    return (cosine_table, sine_table)


def rotate_half(value_rows):
    half = value_rows.shape[-1] // 2
    return jnp.concatenate([-value_rows[..., half:], value_rows[..., :half]], axis=-1)


def rotate_pairs(value_rows, cosine_table, sine_table):
    return value_rows * cosine_table[:, None, :] + rotate_half(value_rows) * sine_table[:, None, :]


def unrotate(grads, cosine_table, sine_table):
    return grads * cosine_table[:, None, :] - rotate_half(grads * sine_table[:, None, :])


def rms_inverse(value_rows):
    return lax.rsqrt(jnp.mean(value_rows * value_rows, axis=-1, keepdims=True) + epsilon)


def norm_backward(grad_normed, normal, inverse, gain):
    gain_term = jnp.sum(grad_normed * normal, axis=0)
    scaled = grad_normed * gain
    grad_input = inverse * (scaled - normal * jnp.mean(scaled * normal, axis=-1, keepdims=True))
    return (gain_term, grad_input)


def contract_rows(left, right):
    return lax.dot_general(
        left, right, (((0,), (0,)), ((), ())), preferred_element_type=jnp.float32
    )


def multiply_transposed(left, right):
    return lax.dot_general(
        left, right, (((1,), (1,)), ((), ())), preferred_element_type=jnp.float32
    )


def fetch_expert(gate_up_shard, down_shard):
    return (
        lax.all_gather(gate_up_shard, "dp", axis=0, tiled=True),
        lax.all_gather(down_shard, "dp", axis=1, tiled=True),
    )


def gate_values(hidden_rows, router_full, route_rows):
    logits = jnp.dot(hidden_rows, router_full, preferred_element_type=jnp.float32)
    chosen_mask = route_rows[:, :, None] == jnp.arange(EXPERTS)[None, None, :]
    chosen = jnp.sum(jnp.where(chosen_mask, logits[:, None, :], 0.0), axis=-1)
    return (chosen_mask, jax.nn.softmax(chosen, axis=-1))


def general_body(
    tokens,
    cotangent,
    lengths,
    routes,
    slots,
    first_gain,
    qkv_weight,
    out_weight,
    second_gain,
    router_weight,
    gate_up_weight,
    down_weight,
):
    sequence_length = tokens.shape[0]
    width = tokens.shape[1]
    query_group = QUERY_HEADS // KEY_VALUE_HEADS
    length = lengths[0]
    gathered = (
        lax.all_gather(first_gain, ("dp", "expert"), axis=0, tiled=True),
        lax.all_gather(qkv_weight, ("dp", "expert"), axis=0, tiled=True),
        lax.all_gather(out_weight, ("dp", "expert"), axis=1, tiled=True),
        lax.all_gather(second_gain, ("dp", "expert"), axis=0, tiled=True),
        lax.all_gather(router_weight, ("dp", "expert"), axis=0, tiled=True),
    )
    gain_one, qkv_full, out_full, gain_two, router_full = gathered
    inputs = tokens.astype(jnp.float32)
    inverse_one = rms_inverse(inputs)
    normal_one = inputs * inverse_one
    hidden_one = (normal_one * gain_one.astype(jnp.float32)).astype(jnp.bfloat16)
    projected_rows = jnp.dot(hidden_one, qkv_full, preferred_element_type=jnp.float32)
    cosine_table, sine_table = rope_tables(sequence_length)
    query_width_total = QUERY_HEADS * HEAD_SIZE
    key_width_total = KEY_VALUE_HEADS * HEAD_SIZE
    query_rows = rotate_pairs(
        projected_rows[:, :query_width_total].reshape(sequence_length, QUERY_HEADS, HEAD_SIZE),
        cosine_table,
        sine_table,
    ).astype(jnp.bfloat16)
    keys = rotate_pairs(
        projected_rows[:, query_width_total : query_width_total + key_width_total].reshape(
            sequence_length, KEY_VALUE_HEADS, HEAD_SIZE
        ),
        cosine_table,
        sine_table,
    ).astype(jnp.bfloat16)
    value_rows = (
        projected_rows[:, query_width_total + key_width_total :]
        .reshape(sequence_length, KEY_VALUE_HEADS, HEAD_SIZE)
        .astype(jnp.bfloat16)
    )
    row_index = jnp.arange(sequence_length)[:, None]
    column_index = jnp.arange(sequence_length)[None, :]
    allowed = (column_index <= row_index) & (column_index < length)

    def head_scores(head):
        head_query = lax.dynamic_slice_in_dim(query_rows, head * query_group, query_group, 1)
        head_key = lax.dynamic_index_in_dim(keys, head, 1, keepdims=False)
        head_value = lax.dynamic_index_in_dim(value_rows, head, 1, keepdims=False)
        scores = (
            jnp.einsum("qgd,kd->gqk", head_query, head_key, preferred_element_type=jnp.float32)
            * score_scale
        )
        return (head_query, head_key, head_value, jnp.where(allowed[None], scores, masked_score))

    def attention_head_forward(head):
        head_query, head_key, head_value, scores = head_scores(head)
        peak = jnp.max(scores, axis=-1, keepdims=True)
        exponent = jnp.exp(scores - peak)
        total = jnp.sum(exponent, axis=-1, keepdims=True)
        weights = (exponent / total).astype(jnp.bfloat16)
        head_mixed = jnp.einsum(
            "gqk,kd->qgd", weights, head_value, preferred_element_type=jnp.float32
        ).astype(jnp.bfloat16)
        return (head_mixed, (peak + jnp.log(total))[..., 0])

    mixed_head_output, log_sum_totals = lax.map(attention_head_forward, jnp.arange(KEY_VALUE_HEADS))
    mixed = mixed_head_output.transpose(1, 0, 2, 3).reshape(
        sequence_length, QUERY_HEADS * HEAD_SIZE
    )
    branch = jnp.dot(mixed, out_full, preferred_element_type=jnp.float32)
    middle = inputs + residual_scale * branch
    inverse_two = rms_inverse(middle)
    normal_two = middle * inverse_two
    hidden_two = (normal_two * gain_two.astype(jnp.float32)).astype(jnp.bfloat16)
    chosen_mask, gates = gate_values(hidden_two, router_full, routes)
    grad_out = cotangent.astype(jnp.float32)
    grad_mixture = residual_scale * grad_out

    def expert_forward(carry, pieces):
        rows, gate_up_shard, down_shard = pieces
        gate_up_full, down_full = fetch_expert(gate_up_shard, down_shard)
        gate_up = jnp.dot(rows, gate_up_full, preferred_element_type=jnp.float32)
        hidden = (jax.nn.silu(gate_up[:, :FF]) * gate_up[:, FF:]).astype(jnp.bfloat16)
        return (
            carry,
            jnp.dot(hidden, down_full, preferred_element_type=jnp.float32).astype(jnp.bfloat16),
        )

    copies = jnp.broadcast_to(hidden_two[:, None, :], (sequence_length, TOP, width))
    outgoing = jnp.zeros((EXPERTS, CAP, width), jnp.bfloat16).at[routes, slots].set(copies)
    received = lax.all_to_all(outgoing, "expert", split_axis=0, concat_axis=1, tiled=True)
    _, produced = lax.scan(expert_forward, None, (received, gate_up_weight, down_weight))
    returned = lax.all_to_all(produced, "expert", split_axis=1, concat_axis=0, tiled=True)
    expert_rows = returned[routes, slots].astype(jnp.float32)
    mixture = jnp.sum(gates[:, :, None] * expert_rows, axis=1)
    grad_gates = jnp.sum(expert_rows * grad_mixture[:, None, :], axis=-1)
    grad_rows = (gates[:, :, None] * grad_mixture[:, None, :]).astype(jnp.bfloat16)
    outgoing_grad = jnp.zeros((EXPERTS, CAP, width), jnp.bfloat16).at[routes, slots].set(grad_rows)
    grad_received = lax.all_to_all(outgoing_grad, "expert", split_axis=0, concat_axis=1, tiled=True)
    output = (middle + residual_scale * mixture).astype(jnp.bfloat16)
    again = (
        lax.all_gather(first_gain, ("dp", "expert"), axis=0, tiled=True),
        lax.all_gather(qkv_weight, ("dp", "expert"), axis=0, tiled=True),
        lax.all_gather(out_weight, ("dp", "expert"), axis=1, tiled=True),
        lax.all_gather(second_gain, ("dp", "expert"), axis=0, tiled=True),
        lax.all_gather(router_weight, ("dp", "expert"), axis=0, tiled=True),
    )
    gain_back, qkv_back, output_gradient, gain_two_back, router_back = again
    grad_chosen = gates * (grad_gates - jnp.sum(gates * grad_gates, axis=-1, keepdims=True))
    grad_logits = jnp.sum(jnp.where(chosen_mask, grad_chosen[:, :, None], 0.0), axis=1).astype(
        jnp.bfloat16
    )

    def expert_backward(carry, pieces):
        rows, grad_produced, gate_up_shard, down_shard = pieces
        gate_up_full, down_full = fetch_expert(gate_up_shard, down_shard)
        gate_up = jnp.dot(rows, gate_up_full, preferred_element_type=jnp.float32)
        gate = gate_up[:, :FF]
        upper = gate_up[:, FF:]
        sigmoid = jax.nn.sigmoid(gate)
        swish = gate * sigmoid
        hidden = (swish * upper).astype(jnp.bfloat16)
        grad_hidden = multiply_transposed(grad_produced, down_full)
        grad_gate_up = jnp.concatenate(
            [grad_hidden * upper * sigmoid * (1.0 + gate * (1.0 - sigmoid)), grad_hidden * swish],
            axis=-1,
        ).astype(jnp.bfloat16)
        grad_copy = multiply_transposed(grad_gate_up, gate_up_full).astype(jnp.bfloat16)
        gate_up_part = lax.psum_scatter(
            contract_rows(rows, grad_gate_up).astype(jnp.bfloat16),
            "dp",
            scatter_dimension=0,
            tiled=True,
        ).astype(jnp.float32)
        down_part = lax.psum_scatter(
            contract_rows(grad_produced, hidden).astype(jnp.bfloat16),
            "dp",
            scatter_dimension=0,
            tiled=True,
        ).astype(jnp.float32)
        return (carry, (grad_copy, gate_up_part, down_part.T))

    _, (grad_copies, gate_up_grads, down_grads) = lax.scan(
        expert_backward, None, (received, grad_received, gate_up_weight, down_weight)
    )
    grad_back = lax.all_to_all(grad_copies, "expert", split_axis=1, concat_axis=0, tiled=True)
    copy_sum = jnp.sum(grad_back[routes, slots].astype(jnp.float32), axis=1)
    grad_hidden_two = copy_sum + multiply_transposed(grad_logits, router_back)
    router_term = contract_rows(hidden_two, grad_logits)
    second_term, grad_norm_two = norm_backward(
        grad_hidden_two, normal_two, inverse_two, gain_two_back.astype(jnp.float32)
    )
    grad_middle = grad_out + grad_norm_two
    branch_gradient = (residual_scale * grad_middle).astype(jnp.bfloat16)
    out_term = contract_rows(mixed, branch_gradient)
    grad_mixed = (
        multiply_transposed(branch_gradient, output_gradient)
        .astype(jnp.bfloat16)
        .reshape(sequence_length, KEY_VALUE_HEADS, query_group, HEAD_SIZE)
    )

    def attention_head_backward(head):
        head_query, head_key, head_value, scores = head_scores(head)
        head_grad = lax.dynamic_index_in_dim(grad_mixed, head, 1, keepdims=False)
        head_total = lax.dynamic_index_in_dim(log_sum_totals, head, 0, keepdims=False)
        probs = jnp.exp(scores - head_total[..., None])
        grad_weights = jnp.einsum(
            "qgd,kd->gqk", head_grad, head_value, preferred_element_type=jnp.float32
        )
        grad_scores = (
            probs * (grad_weights - jnp.sum(probs * grad_weights, axis=-1, keepdims=True))
        ).astype(jnp.bfloat16)
        grad_query = (
            jnp.einsum("gqk,kd->qgd", grad_scores, head_key, preferred_element_type=jnp.float32)
            * score_scale
        )
        grad_key = (
            jnp.einsum("gqk,qgd->kd", grad_scores, head_query, preferred_element_type=jnp.float32)
            * score_scale
        )
        grad_value = jnp.einsum(
            "gqk,qgd->kd", probs.astype(jnp.bfloat16), head_grad, preferred_element_type=jnp.float32
        )
        return (grad_query, grad_key, grad_value)

    query_head_rows, key_head_rows, value_head_rows = lax.map(
        attention_head_backward, jnp.arange(KEY_VALUE_HEADS)
    )
    grad_query = unrotate(
        query_head_rows.transpose(1, 0, 2, 3).reshape(sequence_length, QUERY_HEADS, HEAD_SIZE),
        cosine_table,
        sine_table,
    )
    grad_key = unrotate(key_head_rows.transpose(1, 0, 2), cosine_table, sine_table)
    grad_value = value_head_rows.transpose(1, 0, 2)
    grad_projected = jnp.concatenate(
        [
            grad_query.reshape(sequence_length, query_width_total),
            grad_key.reshape(sequence_length, key_width_total),
            grad_value.reshape(sequence_length, key_width_total),
        ],
        axis=-1,
    ).astype(jnp.bfloat16)
    qkv_term = contract_rows(hidden_one, grad_projected)
    grad_hidden_one = multiply_transposed(grad_projected, qkv_back)
    first_term, grad_norm_one = norm_backward(
        grad_hidden_one, normal_one, inverse_one, gain_back.astype(jnp.float32)
    )
    grad_input = grad_middle + grad_norm_one
    summed = (
        lax.psum_scatter(first_term, ("dp", "expert"), scatter_dimension=0, tiled=True),
        lax.psum_scatter(qkv_term, ("dp", "expert"), scatter_dimension=0, tiled=True),
        lax.psum_scatter(out_term, ("dp", "expert"), scatter_dimension=1, tiled=True),
        lax.psum_scatter(second_term, ("dp", "expert"), scatter_dimension=0, tiled=True),
        lax.psum_scatter(router_term, ("dp", "expert"), scatter_dimension=0, tiled=True),
    )
    return (
        output,
        grad_input,
        summed[0],
        summed[1],
        summed[2],
        summed[3],
        summed[4],
        gate_up_grads,
        down_grads,
    )


WIDE = 160
Z_SIZE, Y_SIZE, X_SIZE, C_SIZE = 4, 2, 2, 2
MESH_AXES = ("dp", "expert")


def device_index(z, y, x, c):
    return ((z * Y_SIZE + y) * X_SIZE + x) * C_SIZE + c


def device_pairs(target):
    pairs = []
    for z in range(Z_SIZE):
        for y in range(Y_SIZE):
            for x in range(X_SIZE):
                for c in range(C_SIZE):
                    to = target(z, y, x, c)
                    if to is not None:
                        pairs.append((device_index(z, y, x, c), device_index(*to)))
    return pairs


PAIRS_X = device_pairs(lambda z, y, x, c: (z, y, 1 - x, c))
PAIRS_Y = device_pairs(lambda z, y, x, c: (z, 1 - y, x, c))
PAIRS_C = device_pairs(lambda z, y, x, c: (z, y, x, 1 - c))


Z_GROUPS = [[z * Y_SIZE + y for z in range(Z_SIZE)] for y in range(Y_SIZE)]


def tie_kernel(*refs):
    del refs


def tie(value, *after):
    any_spec = pl.BlockSpec(memory_space=pl.ANY)
    return pl.pallas_call(
        tie_kernel,
        in_specs=[any_spec] * (1 + len(after)),
        out_specs=any_spec,
        out_shape=jax.ShapeDtypeStruct(value.shape, value.dtype),
        input_output_aliases={0: 0},
        name="tie",
    )(value, *after)


def trade(value):
    return lax.all_to_all(
        value, "dp", split_axis=0, concat_axis=0, axis_index_groups=Z_GROUPS, tiled=True
    )


def spread(value):
    return trade(jnp.broadcast_to(value[None], (Z_SIZE, *value.shape)))


def join_kernel(*refs):
    refs[-1][...] = jnp.zeros_like(refs[-1])


class Rounds:
    def __init__(self):
        self.token = None

    def gate(self, value):
        return value if self.token is None else tie(value, self.token)

    def after(self):
        return () if self.token is None else (self.token,)

    def close(self, *arrays):
        arrays = list(arrays) + list(self.after())
        self.token = pl.pallas_call(
            join_kernel,
            in_specs=[pl.BlockSpec(memory_space=pl.ANY)] * len(arrays),
            out_specs=pl.BlockSpec(memory_space=pltpu.VMEM),
            out_shape=jax.ShapeDtypeStruct((8, 128), jnp.float32),
            name="join",
        )(*arrays)


def move(value, pairs):
    return lax.ppermute(value, MESH_AXES, pairs)


def assemble(plan, info, arrays, shape, name):
    any_spec = pl.BlockSpec(memory_space=pl.ANY)

    def kernel(info_ref, *refs):
        *parts, out, sem = refs
        copies = [
            pltpu.make_async_copy(source, target, sem.at[i])
            for i, (source, target) in enumerate(plan(info_ref, parts, out))
        ]
        for copy in copies:
            copy.start()
        for copy in copies:
            copy.wait()

    dtype = arrays[0].dtype
    size = 1
    for extent in shape:
        size *= extent
    return pl.pallas_call(
        kernel,
        grid_spec=pltpu.PrefetchScalarGridSpec(
            num_scalar_prefetch=1,
            grid=(),
            in_specs=[any_spec] * len(arrays),
            out_specs=pl.BlockSpec(memory_space=pltpu.VMEM),
            scratch_shapes=[pltpu.SemaphoreType.DMA((2 * len(arrays),))],
        ),
        out_shape=jax.ShapeDtypeStruct(shape, dtype),
        compiler_params=pltpu.CompilerParams(vmem_limit_bytes=32 * 1024 * 1024),
        cost_estimate=pl.CostEstimate(flops=0, bytes_accessed=4 * size, transcendentals=0),
        name=name,
    )(info, *arrays)


def dense_assemble(place, mine, other):
    z, y, x, c = place
    rows, n = mine[0].shape[1:]
    zs = Z_SIZE // 2

    def plan(info, parts, out):
        at_y, at_x = info[0], info[1]
        copies = []
        for k in range(2):
            at_c = info[2] if k == 0 else 1 - info[2]
            block, from_x, from_y, far_a, far_b = parts[5 * k : 5 * k + 5]
            copies += [
                (block, out.at[:, at_y, at_x, at_c]),
                (from_x, out.at[:, at_y, 1 - at_x, at_c]),
                (from_y, out.at[:, 1 - at_y, at_x, at_c]),
                (far_a, out.at[pl.ds(0, zs), 1 - at_y, 1 - at_x, at_c]),
                (far_b, out.at[pl.ds(zs, zs), 1 - at_y, 1 - at_x, at_c]),
            ]
        return copies

    shape = (Z_SIZE, Y_SIZE, X_SIZE, C_SIZE, rows, n)
    full = assemble(plan, jnp.stack([y, x, c]), (*mine, *other), shape, "dense_assemble")
    return full.reshape(-1, n)


def join_rows(other, own):
    counts = [part.shape[1] for part in own]

    def plan(info, parts, out):
        copies = []
        for k in range(2):
            at = 0
            for i, count in enumerate(counts):
                target = out.at[pl.ds(k * Z_SIZE, Z_SIZE), pl.ds(at, count)]
                copies.append((parts[k * len(counts) + i], target))
                at += count
        return copies

    shape = (2 * Z_SIZE, sum(counts), own[0].shape[2])
    return assemble(plan, jnp.zeros((1,), jnp.int32), (*other, *own), shape, "join_rows")


def half_order(z_to):
    first = 10 * (z_to // 2)
    if z_to % 2 == 0:
        return [first, first + 1, first + 2, first + 3, first + 4]
    return [first + 6, first + 7, first + 8, first + 9, first + 5]


HALF_ORDER = [half_order(z_to) for z_to in range(Z_SIZE)]
HALF_PLACE = [0] * (Z_SIZE * 5)
for order_z in range(Z_SIZE):
    for order_q in range(5):
        HALF_PLACE[HALF_ORDER[order_z][order_q]] = order_z * 5 + order_q
UNIT_HALVES = ((0, 2), (2, 4), (4, 5))


def dense_gates(logits, chosen):
    peak = jnp.max(jnp.where(chosen, logits, -jnp.inf), axis=-1, keepdims=True)
    exponent = jnp.where(chosen, jnp.exp(logits - peak), 0.0)
    return exponent / jnp.sum(exponent, axis=-1, keepdims=True)


def mm(left, right):
    return jnp.dot(left, right, preferred_element_type=jnp.float32)


def weight_loads(pieces, w_s, sem, y):
    copies = []
    for h in range(w_s.shape[0]):
        for piece, at_y in zip(pieces[2 * h : 2 * h + 2], (y, 1 - y)):
            copies.append(
                pltpu.make_async_copy(piece, w_s.at[h, :, at_y], sem.at[len(copies)])
            )
    return copies


def expert_forward_kernel(info, slots, gates, rows, *rest, count, waits):
    pieces = rest[:count]
    out, kept, gate_up_out, w_s, in_sem = rest[count + waits :]
    low = jnp.bfloat16
    step = pl.program_id(0)
    half = FF // 2
    halves = w_s.shape[0]
    loads = weight_loads(pieces, w_s, in_sem, info[0])

    @pl.when(step == 0)
    def _():
        for load in loads:
            load.start()

    group, length, width = rows.shape
    span = group * WIDE
    iota = lax.broadcasted_iota(jnp.int32, (WIDE, length), 0)
    gate_cols = []
    for j in range(group):
        pick = iota == slots[j]
        one_hot = jnp.where(pick, 1.0, 0.0).astype(low)
        gate_cols.append(jnp.sum(jnp.where(pick, gates[j], 0.0), axis=1, keepdims=True))
        kept[j * WIDE : (j + 1) * WIDE, :] = mm(one_hot, rows[j]).astype(low)
    gate_col = jnp.concatenate(gate_cols, axis=0)

    @pl.when(step == 0)
    def _():
        for load in loads:
            load.wait()

    produced = None
    for h in range(halves):
        gate_up_w = w_s[h, :, :, :, : 2 * half].reshape(width, 2 * half)
        down_t = w_s[h, :, :, :, 2 * half :].reshape(width, half)
        gate_up = mm(kept[...], gate_up_w)
        gate_up_out[:, 2 * h * half : 2 * (h + 1) * half] = gate_up
        gate = gate_up[:, :half]
        hidden = (gate * (1.0 / (1.0 + jnp.exp(-gate))) * gate_up[:, half:]).astype(low)
        term = multiply_transposed(hidden, down_t)
        produced = term if produced is None else produced + term
    out[...] = (produced * gate_col).astype(low).reshape(group, WIDE, width)


def expert_forward(place, halves, y, slots, gates, rows_in, pieces, buffer, after):
    sources, length, width = rows_in.shape
    _, rows, lanes = pieces[0].shape
    half = FF // 2
    low = jnp.bfloat16
    group = 2
    units = 2 * len(UNIT_HALVES)
    any_spec = pl.BlockSpec(memory_space=pl.ANY)
    row_spec = pl.BlockSpec((group, 1, length), lambda i, info: (i, 0, 0))
    waits = list(after)
    aliases = {}
    if buffer is not None:
        aliases = {4 + len(pieces): 0}
        waits = [buffer] + waits
    total = sources * WIDE
    span = group * WIDE
    return pl.pallas_call(
        functools.partial(expert_forward_kernel, count=len(pieces), waits=len(waits)),
        grid_spec=pltpu.PrefetchScalarGridSpec(
            num_scalar_prefetch=1,
            grid=(sources // group,),
            in_specs=[
                row_spec,
                row_spec,
                pl.BlockSpec((group, length, width), lambda i, info: (i, 0, 0)),
            ]
            + [any_spec] * (len(pieces) + len(waits)),
            out_specs=[
                pl.BlockSpec((group, WIDE, width), lambda i, info: (i, place, 0)),
                pl.BlockSpec((span, width), lambda i, info: (i, 0)),
                pl.BlockSpec((span, 2 * half * halves), lambda i, info: (i, 0)),
            ],
            scratch_shapes=[
                pltpu.VMEM((halves, Z_SIZE, Y_SIZE, rows, lanes), low),
                pltpu.SemaphoreType.DMA((4,)),
            ],
        ),
        out_shape=[
            jax.ShapeDtypeStruct((sources, units * WIDE, width), low),
            jax.ShapeDtypeStruct((total, width), low),
            jax.ShapeDtypeStruct((total, 2 * half * halves), jnp.float32),
        ],
        input_output_aliases=aliases,
        compiler_params=pltpu.CompilerParams(vmem_limit_bytes=60 * 1024 * 1024),
        cost_estimate=pl.CostEstimate(
            flops=2 * total * width * (3 * half * halves + length),
            bytes_accessed=2 * (sources * length * width + 2 * total * width)
            + 8 * total * half * halves
            + 2 * halves * width * lanes,
            transcendentals=total * half * halves,
        ),
        name="expert_forward",
    )(y, slots, gates, rows_in, *pieces, *waits)


def expert_back_kernel(info, slots, gates, dys, kept, gate_ups, *rest, count, waits):
    pieces = rest[:count]
    back, near_a_g, near_b_g, far_a_g, far_b_g = rest[count + waits : count + waits + 5]
    w_s, x_s, gd_s, dgu_s, hid_s, g_s, in_sem, out_sem = rest[count + waits + 5 :]
    low = jnp.bfloat16
    full = jnp.float32
    step = pl.program_id(0)
    y = info[0]
    expert = info[1]
    half = FF // 2
    zs = Z_SIZE // 2
    halves = w_s.shape[0]
    loads = weight_loads(pieces, w_s, in_sem, y)

    @pl.when(step == 0)
    def _():
        for load in loads:
            load.start()

    group, length, width = dys.shape
    span = group * WIDE
    here = pl.ds(pl.multiple_of(step * span, span), span)
    iota = lax.broadcasted_iota(jnp.int32, (WIDE, length), 0)
    gate_cols = []
    dy_parts = []
    for j in range(group):
        pick = iota == slots[j]
        one_hot = jnp.where(pick, 1.0, 0.0).astype(low)
        gate_col = jnp.sum(jnp.where(pick, gates[j], 0.0), axis=1, keepdims=True)
        at = pl.multiple_of(step * span + j * WIDE, WIDE)
        dy = mm(one_hot, dys[j])
        gd_s[pl.ds(at, WIDE), :] = (dy * (residual_scale * gate_col)).astype(low)
        dy_parts.append(dy.astype(low))
        gate_cols.append(gate_col)
    dy = jnp.concatenate(dy_parts, axis=0)
    gate_col = jnp.concatenate(gate_cols, axis=0)
    x_s[here, :] = kept[...]

    @pl.when(step == 0)
    def _():
        for load in loads:
            load.wait()

    grad_copy = None
    grad_gate = None
    for h in range(halves):
        gate_up_w = w_s[h, :, :, :, : 2 * half].reshape(width, 2 * half)
        down_t = w_s[h, :, :, :, 2 * half :].reshape(width, half)
        gate = gate_ups[:, 2 * h * half : (2 * h + 1) * half]
        upper = gate_ups[:, (2 * h + 1) * half : (2 * h + 2) * half]
        sigmoid = 1.0 / (1.0 + jnp.exp(-gate))
        swish = gate * sigmoid
        hidden = (swish * upper).astype(low)
        hid_s[here, h * half : (h + 1) * half] = hidden
        grad_plain = residual_scale * mm(dy, down_t)
        term = jnp.sum(hidden.astype(full) * grad_plain, axis=1, keepdims=True)
        grad_gate = term if grad_gate is None else grad_gate + term
        grad_hidden = grad_plain * gate_col
        dgu_s[here, 2 * h * half : (2 * h + 1) * half] = (
            grad_hidden * upper * sigmoid * (1.0 + gate * (1.0 - sigmoid))
        ).astype(low)
        dgu_s[here, (2 * h + 1) * half : (2 * h + 2) * half] = (grad_hidden * swish).astype(low)
        term = multiply_transposed(dgu_s[here, 2 * h * half : 2 * (h + 1) * half], gate_up_w)
        grad_copy = term if grad_copy is None else grad_copy + term
    back[:, :, :width] = grad_copy.astype(low).reshape(group, WIDE, width)
    lane = lax.broadcasted_iota(jnp.int32, (span, 128), 1)
    high = grad_gate.astype(low).astype(full)
    extra = jnp.where(lane == expert, high, 0.0) + jnp.where(
        lane == expert + 64, grad_gate - high, 0.0
    )
    back[:, :, width:] = extra.astype(low).reshape(group, WIDE, 128)

    @pl.when(step == pl.num_programs(0) - 1)
    def _():
        piece = width // Z_SIZE
        for h in range(halves):
            for zz in range(Z_SIZE):
                cols = slice(zz * piece, (zz + 1) * piece)
                got = contract_rows(x_s[:, cols], dgu_s[:, 2 * h * half : 2 * (h + 1) * half])
                g_s[h, zz, :, :, : 2 * half] = got.astype(low).reshape(2, piece // 2, 2 * half)
                got = contract_rows(gd_s[:, cols], hid_s[:, h * half : (h + 1) * half])
                g_s[h, zz, :, :, 2 * half :] = got.astype(low).reshape(2, piece // 2, half)
        stores = [
            (g_s.at[:, pl.ds(0, zs), y], near_a_g),
            (g_s.at[:, pl.ds(zs, zs), y], near_b_g),
            (g_s.at[:, pl.ds(0, zs), 1 - y], far_a_g),
            (g_s.at[:, pl.ds(zs, zs), 1 - y], far_b_g),
        ]
        stores = [pltpu.make_async_copy(a, b, out_sem.at[i]) for i, (a, b) in enumerate(stores)]
        for store in stores:
            store.start()
        for store in stores:
            store.wait()


def expert_backward(
    place, halves, info, slots, gates, grads_in, kept, gate_ups, pieces, buffer, after
):
    sources, length, width = grads_in.shape
    _, rows, lanes = pieces[0].shape
    half = FF // 2
    low = jnp.bfloat16
    group = 2
    units = 2 * len(UNIT_HALVES)
    any_spec = pl.BlockSpec(memory_space=pl.ANY)
    row_spec = pl.BlockSpec((group, 1, length), lambda i, info: (i, 0, 0))
    waits = list(after)
    aliases = {}
    if buffer is not None:
        aliases = {6 + len(pieces): 0}
        waits = [buffer] + waits
    total = sources * WIDE
    span = group * WIDE
    quarter = (halves, Z_SIZE // 2, rows, lanes)
    result = pl.pallas_call(
        functools.partial(expert_back_kernel, count=len(pieces), waits=len(waits)),
        grid_spec=pltpu.PrefetchScalarGridSpec(
            num_scalar_prefetch=1,
            grid=(sources // group,),
            in_specs=[
                row_spec,
                row_spec,
                pl.BlockSpec((group, length, width), lambda i, info: (i, 0, 0)),
                pl.BlockSpec((span, width), lambda i, info: (i, 0)),
                pl.BlockSpec((span, 2 * half * halves), lambda i, info: (i, 0)),
            ]
            + [any_spec] * (len(pieces) + len(waits)),
            out_specs=[
                pl.BlockSpec((group, WIDE, width + 128), lambda i, info: (i, place, 0)),
            ]
            + [any_spec] * 4,
            scratch_shapes=[
                pltpu.VMEM((halves, Z_SIZE, Y_SIZE, rows, lanes), low),
                pltpu.VMEM((total, width), low),
                pltpu.VMEM((total, width), low),
                pltpu.VMEM((total, 2 * half * halves), low),
                pltpu.VMEM((total, half * halves), low),
                pltpu.VMEM((halves, Z_SIZE, Y_SIZE, rows, lanes), low),
                pltpu.SemaphoreType.DMA((4,)),
                pltpu.SemaphoreType.DMA((4,)),
            ],
        ),
        out_shape=[jax.ShapeDtypeStruct((sources, units * WIDE, width + 128), low)]
        + [jax.ShapeDtypeStruct(quarter, low)] * 4,
        input_output_aliases=aliases,
        compiler_params=pltpu.CompilerParams(vmem_limit_bytes=60 * 1024 * 1024),
        cost_estimate=pl.CostEstimate(
            flops=2 * total * width * (6 * half * halves + length),
            bytes_accessed=2 * (sources * length * width + 2 * total * width)
            + 8 * total * half * halves
            + 4 * halves * width * lanes,
            transcendentals=total * half * halves,
        ),
        name="expert_backward",
    )(info, slots, gates, grads_in, kept, gate_ups, *pieces, *waits)
    return result[0], result[1:]


def middle_back_kernel(
    c_ref, got, gates, small, gain, middle, hidden, cotangent, mixed, dmiddle, dbranch, mine, theirs,
    g_s, sem,
):
    full = jnp.float32
    low = jnp.bfloat16
    c = c_ref[0]
    length, width = middle.shape
    total = got[0].astype(full)
    for z in range(1, Z_SIZE):
        total = total + got[z].astype(full)
    parts = total[:, width:]
    grad_gates = parts + pltpu.roll(parts, 64, 1)
    gate = gates[...]
    grad_logits = gate * (grad_gates - jnp.sum(gate * grad_gates, axis=1, keepdims=True))
    grad_logits = grad_logits.astype(low)
    dh2 = total[:, :width] + multiply_transposed(grad_logits, small[...])
    value = middle[...]
    inverse = rms_inverse(value)
    normal = value * inverse
    scaled = dh2 * gain[...]
    mean = jnp.mean(scaled * normal, axis=1, keepdims=True)
    grad = cotangent[...].astype(full) + inverse * (scaled - normal * mean)
    dmiddle[...] = grad
    branch = (residual_scale * grad).astype(low)
    dbranch[...] = branch
    per = g_s.shape[3]
    step = width // Z_SIZE
    rows = Y_SIZE * X_SIZE
    for z in range(Z_SIZE):
        part = slice(z * step, (z + 1) * step)
        term = contract_rows(branch[:, part], mixed[...]).astype(low)
        g_s[:, z, :, :, :width] = term.reshape(rows, C_SIZE, per, width)
        router = contract_rows(hidden[:, part], grad_logits)
        product = (dh2[:, part] * normal[:, part]).astype(low)
        second = contract_rows(product, jnp.ones((length, 128), low))
        lane = lax.broadcasted_iota(jnp.int32, router.shape, 1)
        router = jnp.where(lane == EXPERTS, second, router).astype(low)
        g_s[:, z, :, :, width:] = router.reshape(rows, C_SIZE, per, 128)
    copies = [
        pltpu.make_async_copy(g_s.at[:, :, c], mine, sem.at[0]),
        pltpu.make_async_copy(g_s.at[:, :, 1 - c], theirs, sem.at[1]),
    ]
    for copy in copies:
        copy.start()
    for copy in copies:
        copy.wait()


def middle_backward(c, got, gates, pack, small_at, gain, middle, hidden, cotangent, mixed):
    length, width = middle.shape
    low = jnp.bfloat16
    blocks = (Y_SIZE * X_SIZE, Z_SIZE)
    per = width // (Y_SIZE * X_SIZE * Z_SIZE * C_SIZE)
    any_spec = pl.BlockSpec(memory_space=pl.ANY)
    whole = lambda a: pl.BlockSpec(a.shape, lambda i, n: (0,) * a.ndim)
    split = jax.ShapeDtypeStruct((*blocks, per, width + 128), low)
    rows = pl.BlockSpec((length, width), lambda i, n: (0, 0))
    return pl.pallas_call(
        middle_back_kernel,
        grid_spec=pltpu.PrefetchScalarGridSpec(
            num_scalar_prefetch=1,
            grid=(1,),
            in_specs=[
                whole(got),
                whole(gates),
                pl.BlockSpec((width, 128), lambda i, n: (0, small_at // 128)),
                whole(gain),
                rows,
                rows,
                rows,
                rows,
            ],
            out_specs=[rows, rows, any_spec, any_spec],
            scratch_shapes=[
                pltpu.VMEM((*blocks, C_SIZE, per, width + 128), low),
                pltpu.SemaphoreType.DMA((2,)),
            ],
        ),
        out_shape=[
            jax.ShapeDtypeStruct((length, width), jnp.float32),
            jax.ShapeDtypeStruct((length, width), low),
            split,
            split,
        ],
        compiler_params=pltpu.CompilerParams(vmem_limit_bytes=56 * 1024 * 1024),
        cost_estimate=pl.CostEstimate(
            flops=2 * length * width * (width + 384),
            bytes_accessed=length * width * 24 + 4 * width * width,
            transcendentals=0,
        ),
        name="middle_backward",
    )(c[None], got, gates, pack, gain, middle, hidden, cotangent, mixed)


def turn_halves(value):
    lanes = value.shape[-1]
    lane = lax.broadcasted_iota(jnp.int32, value.shape, 1)
    ahead = pltpu.roll(value, lanes - HEAD_SIZE // 2, 1)
    behind = pltpu.roll(value, HEAD_SIZE // 2, 1)
    return jnp.where(lane % HEAD_SIZE < HEAD_SIZE // 2, -ahead, behind)


def heads_of(value, first, count):
    return jnp.concatenate(
        [value[:, (first + i) * HEAD_SIZE : (first + i + 1) * HEAD_SIZE] for i in range(count)],
        axis=0,
    )


ROW_BLOCK = 128
PAIR = 2
GROUP = QUERY_HEADS // KEY_VALUE_HEADS
QUERY_LANES = PAIR * GROUP * HEAD_SIZE
KEY_LANES = PAIR * HEAD_SIZE


def block_mask(block, length):
    shape = (ROW_BLOCK, (block + 1) * ROW_BLOCK)
    row = lax.broadcasted_iota(jnp.int32, shape, 0) + block * ROW_BLOCK
    column = lax.broadcasted_iota(jnp.int32, shape, 1)
    allowed = jnp.where((column <= row) & (column < length), 1, 0)
    return jnp.concatenate([allowed] * GROUP, axis=0) > 0


def attention_kernel(
    length, tokens, gain, wq, wk, wv, cosine, sine, *rest
):
    h1, q, k, v, mixed, lse, h_s, lse_s = rest[-8:]
    step = pl.program_id(0)
    low = jnp.bfloat16
    rows = tokens.shape[0]

    @pl.when(step == 0)
    def _():
        value = tokens[...].astype(jnp.float32)
        hidden = (value * rms_inverse(value) * gain[...]).astype(low)
        h_s[...] = hidden
        h1[...] = hidden

    lane = lax.broadcasted_iota(jnp.int32, (rows, 128), 1)
    cos = cosine[...]
    sin = sine[...]
    query = mm(h_s[...], wq[...])
    query = (query * cos + turn_halves(query) * sin).astype(low)
    key = mm(h_s[...], wk[...])
    key = (key * cos[:, :KEY_LANES] + turn_halves(key) * sin[:, :KEY_LANES]).astype(low)
    value = mm(h_s[...], wv[...]).astype(low)
    q[...] = query
    k[...] = key
    v[...] = value
    blocks = rows // ROW_BLOCK
    totals = [[] for _ in range(PAIR * GROUP)]
    masks = [block_mask(block, length[0]) for block in range(blocks)]
    outs = [[] for _ in range(PAIR * GROUP)]
    for head in range(PAIR):
        key_h = key[:, head * HEAD_SIZE : (head + 1) * HEAD_SIZE]
        value_h = value[:, head * HEAD_SIZE : (head + 1) * HEAD_SIZE]
        for block in range(blocks):
            keys = (block + 1) * ROW_BLOCK
            query_h = heads_of(
                query[block * ROW_BLOCK : (block + 1) * ROW_BLOCK], head * GROUP, GROUP
            )
            scores = multiply_transposed(query_h, key_h[:keys]) * score_scale
            scores = jnp.where(masks[block], scores, masked_score)
            peak = jnp.max(scores, axis=1, keepdims=True)
            exponent = jnp.exp(scores - peak)
            total = jnp.sum(exponent, axis=1, keepdims=True)
            weights = (exponent / total).astype(low)
            out = mm(weights, value_h[:keys]).astype(low)
            log_total = peak + jnp.log(total)
            for i in range(GROUP):
                part = slice(i * ROW_BLOCK, (i + 1) * ROW_BLOCK)
                outs[head * GROUP + i].append(out[part])
                totals[head * GROUP + i].append(log_total[part])
    mixed[...] = jnp.concatenate([jnp.concatenate(o, axis=0) for o in outs], axis=1)

    @pl.when(step == 0)
    def _():
        lse_s[...] = jnp.zeros_like(lse_s)

    kept = lse_s[...]
    for i in range(PAIR * GROUP):
        column = jnp.concatenate(totals[i], axis=0)
        kept = jnp.where(lane == step * PAIR * GROUP + i, column, kept)
    lse_s[...] = kept
    lse[...] = kept


def attention_forward(length, tokens, gain, weight, cosine, sine, after=()):
    rows, width = tokens.shape
    steps = KEY_VALUE_HEADS // PAIR
    low = jnp.bfloat16
    query_total = QUERY_HEADS * HEAD_SIZE
    key_total = KEY_VALUE_HEADS * HEAD_SIZE
    key_at = query_total // KEY_LANES
    value_at = key_at + steps
    whole = lambda shape: pl.BlockSpec(shape, lambda i, n: (0, 0))
    cols = lambda lanes, at: pl.BlockSpec((width, lanes), lambda i, n: (0, at + i))
    part = lambda lanes: pl.BlockSpec((rows, lanes), lambda i, n: (0, i))
    return pl.pallas_call(
        attention_kernel,
        grid_spec=pltpu.PrefetchScalarGridSpec(
            num_scalar_prefetch=1,
            grid=(steps,),
            in_specs=[
                whole((rows, width)),
                whole((1, width)),
                cols(QUERY_LANES, 0),
                cols(KEY_LANES, key_at),
                cols(KEY_LANES, value_at),
                whole((rows, QUERY_LANES)),
                whole((rows, QUERY_LANES)),
            ]
            + [pl.BlockSpec(memory_space=pl.ANY)] * len(after),
            out_specs=[
                whole((rows, width)),
                part(QUERY_LANES),
                part(KEY_LANES),
                part(KEY_LANES),
                part(QUERY_LANES),
                whole((rows, 128)),
            ],
            scratch_shapes=[pltpu.VMEM((rows, width), low), pltpu.VMEM((rows, 128), jnp.float32)],
        ),
        out_shape=[
            jax.ShapeDtypeStruct((rows, width), low),
            jax.ShapeDtypeStruct((rows, query_total), low),
            jax.ShapeDtypeStruct((rows, key_total), low),
            jax.ShapeDtypeStruct((rows, key_total), low),
            jax.ShapeDtypeStruct((rows, query_total), low),
            jax.ShapeDtypeStruct((rows, 128), jnp.float32),
        ],
        compiler_params=pltpu.CompilerParams(vmem_limit_bytes=48 * 1024 * 1024),
        cost_estimate=pl.CostEstimate(
            flops=2 * rows * width * (query_total + 2 * key_total)
            + 4 * QUERY_HEADS * rows * rows * HEAD_SIZE,
            bytes_accessed=2 * width * (query_total + 2 * key_total) + 10 * rows * width,
            transcendentals=QUERY_HEADS * rows * rows,
        ),
        name="attention_forward",
    )(length, tokens, gain, weight, weight, weight, cosine, sine, *after)


def attention_back_kernel(
    length, dbranch, wo, q, k, v, lse, h1, wq, wk, wv, cosine, sine, tokens, *rest
):
    mine, theirs, dh1, dh_s, g_s = rest[-5:]
    c = length[1]
    step = pl.program_id(0)
    low = jnp.bfloat16
    full = jnp.float32
    rows = dbranch.shape[0]
    span = h1.shape[1] // Z_SIZE
    split = (Y_SIZE * X_SIZE, C_SIZE, span // (Y_SIZE * X_SIZE * C_SIZE))

    @pl.when(step < pl.num_programs(0) - 1)
    def _():
        blocks = rows // ROW_BLOCK
        dmixed = mm(dbranch[...], wo[...]).astype(low)
        lane = lax.broadcasted_iota(jnp.int32, (rows, 128), 1)
        kept = lse[...]
        query, key, value = q[...], k[...], v[...]
        columns = [
            jnp.sum(jnp.where(lane == step * PAIR * GROUP + i, kept, 0.0), axis=1, keepdims=True)
            for i in range(PAIR * GROUP)
        ]
        masks = [block_mask(block, length[0]) for block in range(blocks)]
        dq = [[] for _ in range(PAIR * GROUP)]
        dks, dvs = [], []
        for head in range(PAIR):
            key_h = key[:, head * HEAD_SIZE : (head + 1) * HEAD_SIZE]
            value_h = value[:, head * HEAD_SIZE : (head + 1) * HEAD_SIZE]
            dk = [None] * blocks
            dv = [None] * blocks
            for block in range(blocks):
                keys = (block + 1) * ROW_BLOCK
                at = slice(block * ROW_BLOCK, (block + 1) * ROW_BLOCK)
                query_h = heads_of(query[at], head * GROUP, GROUP)
                dmixed_h = heads_of(dmixed[at], head * GROUP, GROUP)
                log_total = jnp.concatenate(
                    [columns[head * GROUP + i][at] for i in range(GROUP)], axis=0
                )
                scores = multiply_transposed(query_h, key_h[:keys]) * score_scale
                scores = jnp.where(masks[block], scores, masked_score)
                probs = jnp.exp(scores - log_total)
                dprobs = multiply_transposed(dmixed_h, value_h[:keys])
                delta = jnp.sum(probs * dprobs, axis=1, keepdims=True)
                dscores = (probs * (dprobs - delta)).astype(low)
                dquery = mm(dscores, key_h[:keys]) * score_scale
                dkey = contract_rows(dscores, query_h) * score_scale
                dvalue = contract_rows(probs.astype(low), dmixed_h)
                for i in range(GROUP):
                    dq[head * GROUP + i].append(dquery[i * ROW_BLOCK : (i + 1) * ROW_BLOCK])
                for b in range(block + 1):
                    part = slice(b * ROW_BLOCK, (b + 1) * ROW_BLOCK)
                    dk[b] = dkey[part] if dk[b] is None else dk[b] + dkey[part]
                    dv[b] = dvalue[part] if dv[b] is None else dv[b] + dvalue[part]
            dks.append(jnp.concatenate(dk, axis=0))
            dvs.append(jnp.concatenate(dv, axis=0))
        cos = cosine[...]
        sin = sine[...]
        dquery = jnp.concatenate([jnp.concatenate(o, axis=0) for o in dq], axis=1)
        dquery = (dquery * cos - turn_halves(dquery * sin)).astype(low)
        dkey = jnp.concatenate(dks, axis=1)
        dkey = (dkey * cos[:, :KEY_LANES] - turn_halves(dkey * sin[:, :KEY_LANES])).astype(low)
        dvalue = jnp.concatenate(dvs, axis=1).astype(low)
        hidden = h1[...]
        got = contract_rows(hidden, dquery).astype(low)
        for z in range(Z_SIZE):
            part = got[z * span : (z + 1) * span]
            g_s[:, z, :, :, :QUERY_LANES] = part.reshape(*split, QUERY_LANES)
        got = contract_rows(hidden, jnp.concatenate([dkey, dvalue], axis=1)).astype(low)
        for z in range(Z_SIZE):
            part = got[z * span : (z + 1) * span]
            g_s[:, z, :, :, QUERY_LANES:] = part.reshape(*split, 2 * KEY_LANES)
        mine[...] = g_s[:, :, c]
        theirs[...] = g_s[:, :, 1 - c]
        term = (
            multiply_transposed(dquery, wq[...])
            + multiply_transposed(dkey, wk[...])
            + multiply_transposed(dvalue, wv[...])
        )

        @pl.when(step == 0)
        def _():
            dh_s[...] = term

        @pl.when(step > 0)
        def _():
            dh_s[...] += term

    @pl.when(step == pl.num_programs(0) - 1)
    def _():
        total = dh_s[...]
        dh1[...] = total
        value = tokens[...].astype(full)
        product = (total * (value * rms_inverse(value))).astype(low)
        column = contract_rows(product, jnp.ones((rows, 128), low)).astype(low)
        for z in range(Z_SIZE):
            part = column[z * span : (z + 1) * span]
            g_s[:, z, :, :, :128] = part.reshape(*split, 128)
        mine[:, :, :, :128] = g_s[:, :, c, :, :128]
        theirs[:, :, :, :128] = g_s[:, :, 1 - c, :, :128]


def attention_backward(
    length, dbranch, q, k, v, lse, h1, weight, out_at, cosine, sine, tokens, after=()
):
    rows, width = dbranch.shape
    steps = KEY_VALUE_HEADS // PAIR
    low = jnp.bfloat16
    full = jnp.float32
    query_total = QUERY_HEADS * HEAD_SIZE
    key_total = KEY_VALUE_HEADS * HEAD_SIZE
    key_at = query_total // KEY_LANES
    value_at = key_at + steps
    whole = lambda shape: pl.BlockSpec(shape, lambda i, n: (0, 0))
    cols = lambda lanes, at: pl.BlockSpec((width, lanes), lambda i, n: (0, at + jnp.minimum(i, steps - 1)))
    part = lambda lanes: pl.BlockSpec((rows, lanes), lambda i, n: (0, jnp.minimum(i, steps - 1)))
    lanes = QUERY_LANES + 2 * KEY_LANES
    blocks = (Y_SIZE * X_SIZE, Z_SIZE)
    per = width // (Y_SIZE * X_SIZE * Z_SIZE * C_SIZE)
    return pl.pallas_call(
        attention_back_kernel,
        grid_spec=pltpu.PrefetchScalarGridSpec(
            num_scalar_prefetch=1,
            grid=(steps + 1,),
            in_specs=[
                whole((rows, width)),
                cols(QUERY_LANES, out_at // QUERY_LANES),
                part(QUERY_LANES),
                part(KEY_LANES),
                part(KEY_LANES),
                whole((rows, 128)),
                whole((rows, width)),
                cols(QUERY_LANES, 0),
                cols(KEY_LANES, key_at),
                cols(KEY_LANES, value_at),
                whole((rows, QUERY_LANES)),
                whole((rows, QUERY_LANES)),
                whole((rows, width)),
            ]
            + [pl.BlockSpec(memory_space=pl.ANY)] * len(after),
            out_specs=[
                pl.BlockSpec((*blocks, per, lanes), lambda i, n: (0, 0, 0, i)),
                pl.BlockSpec((*blocks, per, lanes), lambda i, n: (0, 0, 0, i)),
                whole((rows, width)),
            ],
            scratch_shapes=[
                pltpu.VMEM((rows, width), full),
                pltpu.VMEM((*blocks, C_SIZE, per, lanes), low),
            ],
        ),
        out_shape=[
            jax.ShapeDtypeStruct((*blocks, per, steps * lanes + 128), low),
            jax.ShapeDtypeStruct((*blocks, per, steps * lanes + 128), low),
            jax.ShapeDtypeStruct((rows, width), full),
        ],
        compiler_params=pltpu.CompilerParams(vmem_limit_bytes=48 * 1024 * 1024),
        cost_estimate=pl.CostEstimate(
            flops=4 * rows * width * (query_total + 2 * key_total)
            + 2 * rows * width * query_total
            + 10 * QUERY_HEADS * rows * rows * HEAD_SIZE,
            bytes_accessed=4 * width * (query_total + 2 * key_total) + 2 * width * width + 14 * rows * width,
            transcendentals=QUERY_HEADS * rows * rows,
        ),
        name="attention_backward",
    )(length, dbranch, weight, q, k, v, lse, h1, weight, weight, weight, cosine, sine, tokens, *after)


def combine_kernel(slots, values, *rest):
    other, own, p_s = rest[-3:]
    step = pl.program_id(0)
    length = slots.shape[2]
    iota = lax.broadcasted_iota(jnp.int32, (WIDE, length), 0)
    for u in range(slots.shape[1]):
        pick = iota == slots[0, u : u + 1, :]
        p_s[u * WIDE : (u + 1) * WIDE, :] = jnp.where(pick, 1.0, 0.0).astype(jnp.bfloat16)
    result = contract_rows(p_s[...], values[0]).astype(jnp.bfloat16)

    @pl.when(step < Z_SIZE)
    def _():
        other[0] = result

    @pl.when(step >= Z_SIZE)
    def _():
        own[0] = result


def combine(slots, values, after=()):
    sources, units, length = slots.shape
    n = values.shape[-1]
    low = jnp.bfloat16
    return pl.pallas_call(
        combine_kernel,
        grid=(sources,),
        in_specs=[
            pl.BlockSpec((1, units, length), lambda i: (i, 0, 0)),
            pl.BlockSpec((1, units * WIDE, n), lambda i: (i, 0, 0)),
        ]
        + [pl.BlockSpec(memory_space=pl.ANY)] * len(after),
        out_specs=[
            pl.BlockSpec((1, length, n), lambda i: (jnp.minimum(i, Z_SIZE - 1), 0, 0)),
            pl.BlockSpec((1, length, n), lambda i: (jnp.maximum(i - Z_SIZE, 0), 0, 0)),
        ],
        out_shape=[jax.ShapeDtypeStruct((Z_SIZE, length, n), low)] * 2,
        scratch_shapes=[pltpu.VMEM((units * WIDE, length), low)],
        compiler_params=pltpu.CompilerParams(vmem_limit_bytes=60 * 1024 * 1024),
        cost_estimate=pl.CostEstimate(
            flops=2 * sources * units * WIDE * length * n,
            bytes_accessed=sources * (units * WIDE + length) * n * 2,
            transcendentals=0,
        ),
        name="combine",
    )(slots, values, *after)


def weight_chunks(gate_up_weight, down_weight):
    experts, rows = gate_up_weight.shape[0], gate_up_weight.shape[1]
    gate, upper = gate_up_weight[..., :FF], gate_up_weight[..., FF:]
    down_t = down_weight.transpose(0, 2, 1)
    half = FF // 2

    def one(q):
        cols = slice((q % 2) * half, (q % 2 + 1) * half)
        return jnp.concatenate([part[q // 2, :, cols] for part in (gate, upper, down_t)], axis=-1)

    return [
        jnp.stack([one(HALF_ORDER[z_to][j]) for z_to in range(Z_SIZE)]) for j in range(5)
    ]


def finish_kernel(*refs):
    gate_up, down = refs[-2:]
    rows = gate_up.shape[1]
    places = [(ref, i) for ref in refs[:4] for i in range(ref.shape[1] // rows)]
    half = FF // 2
    full = jnp.float32
    for z_from in range(Z_SIZE):
        for j in range(5):
            expert, side = divmod(HALF_ORDER[z_from][j], 2)
            part, i = places[j]
            at = slice(i * rows, (i + 1) * rows)
            cols = slice(side * half, (side + 1) * half)
            gate_up[expert, :, cols] = part[z_from, at, :half].astype(full)
            cols_up = slice(FF + side * half, FF + (side + 1) * half)
            gate_up[expert, :, cols_up] = part[z_from, at, half : 2 * half].astype(full)
            down[expert, :, cols] = part[z_from, at, 2 * half :].astype(full)


def finish_grads(backs, after):
    rows = backs[0].shape[1]
    experts = EXPERTS // (X_SIZE * C_SIZE)
    vmem = pl.BlockSpec(memory_space=pltpu.VMEM)
    return pl.pallas_call(
        finish_kernel,
        in_specs=[vmem] * len(backs) + [pl.BlockSpec(memory_space=pl.ANY)] * len(after),
        out_specs=[vmem, vmem],
        out_shape=[
            jax.ShapeDtypeStruct((experts, rows, 2 * FF), jnp.float32),
            jax.ShapeDtypeStruct((experts, rows, FF), jnp.float32),
        ],
        compiler_params=pltpu.CompilerParams(vmem_limit_bytes=40 * 1024 * 1024),
        cost_estimate=pl.CostEstimate(
            flops=0, bytes_accessed=experts * rows * FF * 18, transcendentals=0
        ),
        name="finish_grads",
    )(*backs, *after)


class DenseScatter:
    def __init__(self, mine, theirs, place):
        shape = (Y_SIZE, X_SIZE, *mine.shape[1:])
        self.mine, self.theirs, self.place = mine.reshape(shape), theirs.reshape(shape), place

    def block(self, other_y, other_x):
        y = 1 - self.place[1] if other_y else self.place[1]
        x = 1 - self.place[2] if other_x else self.place[2]
        size = (1, 1, *self.mine.shape[2:])
        got = [
            lax.dynamic_slice(a, (y, x, 0, 0, 0), size).reshape(size[2:])
            for a in (self.mine, self.got)
        ]
        return plus(*got)

    def cores(self):
        self.got = move(self.theirs, PAIRS_C)
        return [self.got]

    def first(self):
        low = jnp.bfloat16
        zs = Z_SIZE // 2
        self.near, self.to_x, self.to_y, far = [
            self.block(*at) for at in ((False, False), (False, True), (True, False), (True, True))
        ]
        gate = lambda value: value
        self.via_x = move(gate(far[:zs].astype(low)), PAIRS_X)
        self.via_y = move(gate(far[zs:].astype(low)), PAIRS_Y)
        self.x_a = move(gate(self.to_x[:zs].astype(low)), PAIRS_X)
        self.y_b = move(gate(self.to_y[zs:].astype(low)), PAIRS_Y)
        return [self.via_x, self.via_y, self.x_a, self.y_b]

    def second(self):
        low = jnp.bfloat16
        zs = Z_SIZE // 2
        gate = lambda value: value
        self.x_b = move(gate(plus(self.to_x[zs:], self.via_y).astype(low)), PAIRS_X)
        self.y_a = move(gate(plus(self.to_y[:zs], self.via_x).astype(low)), PAIRS_Y)
        return [self.x_b, self.y_a]

    def sum_up(self):
        zs = Z_SIZE // 2
        return jnp.concatenate(
            [
                plus(self.near[:zs], self.x_a) + self.y_a.astype(jnp.float32),
                plus(self.near[zs:], self.x_b) + self.y_b.astype(jnp.float32),
            ]
        ).astype(jnp.bfloat16)

    def result(self):
        return jnp.sum(self.parts.astype(jnp.float32), axis=0)


def plus(a, b):
    return a.astype(jnp.float32) + b.astype(jnp.float32)


def ring_total(own, first, second, h):
    x_a, y_b = first
    x_b, y_a = second
    return jnp.concatenate(
        [
            plus(own[0][h], x_a[h]) + y_a[h].astype(jnp.float32),
            plus(own[1][h], x_b[h]) + y_b[h].astype(jnp.float32),
        ]
    ).astype(jnp.bfloat16)


def body(
    tokens,
    cotangent,
    lengths,
    routes,
    slots,
    first_gain,
    qkv_weight,
    out_weight,
    second_gain,
    router_weight,
    gate_up_weight,
    down_weight,
):
    low = jnp.bfloat16
    full = jnp.float32
    dp_index = lax.axis_index("dp")
    expert_index = lax.axis_index("expert")
    z, y = dp_index // Y_SIZE, dp_index % Y_SIZE
    x, c = expert_index // C_SIZE, expert_index % C_SIZE
    sequence_length = tokens.shape[0]
    width = tokens.shape[1]
    rows = gate_up_weight.shape[1]

    chosen_by = routes[None, :, :] == jnp.arange(EXPERTS, dtype=jnp.int32)[:, None, None]
    slot_table = jnp.sum(jnp.where(chosen_by, slots[None, :, :] + 1, 0), axis=-1) - 1
    place = (z, y, x, c)
    zs = Z_SIZE // 2
    steps = range(1, Z_SIZE)
    rounds = Rounds()
    gate = rounds.gate

    small = jnp.concatenate(
        [router_weight, first_gain[:, None], second_gain[:, None]], axis=1
    )
    small = jnp.pad(small, ((0, 0), (0, 128 - small.shape[1])))
    shard = jnp.concatenate([qkv_weight, small, out_weight.T], axis=1)
    table = slot_table.astype(low)

    block = spread(shard)
    tables = spread(table)
    cuts = weight_chunks(gate_up_weight, down_weight)
    rounds.close(block, tables)

    near, far, moved = [None] * 5, [None] * 5, [None] * 5

    def send_half(q):
        moved[q] = trade(gate(cuts[q]))
        return [moved[q]]

    def send_near(q):
        near[q] = (move(moved[q], PAIRS_X), move(moved[q], PAIRS_Y))
        return near[q]

    def send_far(q):
        far[q] = move(near[q][1], PAIRS_X) if q % 2 == 0 else move(near[q][0], PAIRS_Y)
        return [far[q]]

    from_x, from_y = move(block, PAIRS_X), move(block, PAIRS_Y)
    block_c = move(block, PAIRS_C)
    tables_c = move(tables, PAIRS_C)
    rounds.close(from_x, from_y, block_c, tables_c, *send_half(0))
    far_a, far_b = move(from_y[:zs], PAIRS_X), move(from_x[zs:], PAIRS_Y)
    from_x_c, from_y_c = move(from_x, PAIRS_C), move(from_y, PAIRS_C)
    rounds.close(far_a, far_b, from_x_c, from_y_c, *send_half(1))
    far_a_c, far_b_c = move(far_a, PAIRS_C), move(far_b, PAIRS_C)
    moved[0] = gate(moved[0])
    send_half(2)
    pack = dense_assemble(
        place,
        (block, from_x, from_y, far_a, far_b),
        (block_c, from_x_c, from_y_c, far_a_c, far_b_c),
    )
    rounds.close(pack, moved[2], *send_near(0))
    out_at = qkv_weight.shape[1] + small.shape[1]
    out_t = pack[:, out_at:]
    small_full = pack[:, qkv_weight.shape[1] : out_at]
    router_full = small_full[:, :EXPERTS]
    gain_one = small_full[:, EXPERTS].astype(full)
    gain_two = small_full[:, EXPERTS + 1].astype(full)

    inputs = tokens.astype(full)
    inverse_one = rms_inverse(inputs)
    normal_one = inputs * inverse_one
    cosine_table, sine_table = rope_tables(sequence_length)
    cosine_table = jnp.tile(cosine_table, (1, QUERY_LANES // HEAD_SIZE))
    sine_table = jnp.tile(sine_table, (1, QUERY_LANES // HEAD_SIZE))
    hidden_one, query_rows, keys, value_rows, mixed, log_totals = attention_forward(
        lengths, tokens, gain_one[None, :], pack, cosine_table, sine_table, rounds.after()
    )
    moved[1] = gate(moved[1])
    rounds.close(*send_half(3), *send_near(1), mixed)
    moved[2] = gate(moved[2])
    send_half(4)
    branch = multiply_transposed(mixed, out_t)
    middle = inputs + residual_scale * branch
    inverse_two = rms_inverse(middle)
    normal_two = middle * inverse_two
    hidden_two = (normal_two * gain_two).astype(low)
    grad_out = cotangent.astype(full)

    rounds.close(moved[4], *send_near(2))
    rows_own = spread(gate(hidden_two))
    moved[3] = gate(moved[3])
    rounds.close(*send_near(3))
    moved[4] = gate(moved[4])
    rounds.close(*send_near(4))
    for first, second in ((0, 1), (2, 3)):
        near[first] = (near[first][0], gate(near[first][1]))
        near[second] = (gate(near[second][0]), near[second][1])
        rounds.close(*send_far(first), *send_far(second))
    rounds.close(rows_own)
    rows_own = gate(rows_own)
    rows_other = move(rows_own, PAIRS_C)
    rounds.close(rows_other)
    rows_in = join_rows([rows_other], [rows_own])
    slots_in = jnp.concatenate([tables_c, tables], axis=0).astype(jnp.int32)
    logits_in = jnp.einsum("de,itd->iet", router_full, rows_in, preferred_element_type=full)
    chosen_in = slots_in >= 0
    peak_in = jnp.max(jnp.where(chosen_in, logits_in, -jnp.inf), axis=1, keepdims=True)
    exponent_in = jnp.where(chosen_in, jnp.exp(logits_in - peak_in), 0.0)
    gates_in = exponent_in / jnp.sum(exponent_in, axis=1, keepdims=True)

    units = range(len(UNIT_HALVES))
    even = z % 2 == 0
    ids = []
    for group in (1 - x, x):
        base = EXPERTS // (X_SIZE * C_SIZE) * (group * C_SIZE + c) + 5 * (z // 2)
        ids += [base + jnp.where(even, 0, 3), base + jnp.where(even, 1, 4), base + 2]
    unit_slots = [lax.dynamic_index_in_dim(slots_in, expert, 1, keepdims=True) for expert in ids]
    unit_gates = [lax.dynamic_index_in_dim(gates_in, expert, 1, keepdims=True) for expert in ids]
    pairs = len(UNIT_HALVES)
    sizes = [end - first for first, end in UNIT_HALVES]
    all_slots = jnp.concatenate(unit_slots, axis=1)
    infos = [jnp.stack([y, expert]).astype(jnp.int32) for expert in ids]
    buffer = None
    saved = {}

    def ring(pair, own):
        halves = range(*UNIT_HALVES[pair])
        if own:
            return [p for q in halves for p in (moved[q], near[q][1])]
        return [p for q in halves for p in (near[q][0], far[q])]

    def run_forward(pair, own):
        nonlocal buffer
        at = pair + (pairs if own else 0)
        buffer, *saved[at] = expert_forward(
            at,
            sizes[pair],
            infos[at],
            unit_slots[at],
            unit_gates[at],
            rows_in,
            ring(pair, own),
            buffer,
            rounds.after(),
        )

    dy_own = spread(gate(cotangent))
    late = [(4,), (), ()]
    for pair in range(pairs):
        sent = []
        for q in late[pair]:
            near[q] = tuple(gate(part) for part in near[q])
            sent += send_far(q)
        run_forward(pair, False)
        run_forward(pair, True)
        rounds.close(saved[pair + pairs][0], *sent, *([dy_own] if pair == 2 else []))
    dy_own = gate(dy_own)
    dy_other = move(dy_own, PAIRS_C)
    mix_other, mix_own = combine(all_slots, buffer, rounds.after())
    rounds.close(mix_other, dy_other)
    mix_moved = move(mix_other, PAIRS_C)
    grads_in = join_rows([dy_other], [dy_own])
    rounds.close(mix_moved, grads_in)

    back = None
    grads = [[None, None] for _ in units]

    def run_back(pair, own):
        nonlocal back
        at = pair + (pairs if own else 0)
        back, grads[pair][1 if own else 0] = expert_backward(
            at,
            sizes[pair],
            infos[at],
            unit_slots[at],
            unit_gates[at],
            grads_in,
            *saved[at],
            ring(pair, own),
            back,
            rounds.after(),
        )

    vias, firsts, seconds = [None] * 3, [None] * 3, [None] * 3

    def send_via(u):
        vias[u] = (move(gate(grads[u][0][2]), PAIRS_X), move(gate(grads[u][0][3]), PAIRS_Y))
        return vias[u]

    def send_first(u):
        firsts[u] = (move(gate(grads[u][0][0]), PAIRS_X), move(gate(grads[u][1][3]), PAIRS_Y))
        return firsts[u]

    def send_second(u):
        via_x, via_y = vias[u]
        seconds[u] = (
            move(gate(plus(grads[u][0][1], via_y).astype(low)), PAIRS_X),
            move(gate(plus(grads[u][1][2], via_x).astype(low)), PAIRS_Y),
        )
        return seconds[u]

    def total_of(u):
        return [ring_total(grads[u][1], firsts[u], seconds[u], h) for h in range(sizes[u])]

    terms = plus(mix_own, mix_moved).astype(low)
    mix_got = trade(gate(terms))
    run_back(0, False)
    rounds.close(grads[0][0][0])
    run_back(0, True)
    rounds.close(grads[0][1][0], *send_via(0))
    run_back(1, False)
    rounds.close(grads[1][0][0], *send_first(0))
    run_back(1, True)
    rounds.close(mix_got, grads[1][1][0], *send_second(0))
    mixture = jnp.sum(mix_got.astype(full), axis=0)
    output = (middle + residual_scale * mixture).astype(low)
    totals = total_of(0)
    backs = []

    def send_back(*parts):
        backs.append(trade(gate(parts[0] if len(parts) == 1 else jnp.concatenate(parts, axis=1))))
        return backs[-1:]

    run_back(2, False)
    rounds.close(grads[2][0][0], *send_via(1), *send_back(totals[0]))
    run_back(2, True)
    rounds.close(grads[2][1][0], *send_first(1), *send_back(totals[1]))
    copy_other, copy_own = combine(all_slots, back, rounds.after())
    rounds.close(copy_other, *send_second(1), *send_via(2))
    copy_moved = move(copy_other, PAIRS_C)
    rounds.close(copy_moved)
    copy_got = trade(plus(copy_own, copy_moved).astype(low))
    rounds.close(*send_first(2))
    rounds.close(*send_second(2))
    totals += total_of(1) + total_of(2)
    rounds.close(copy_got, output, totals[2])
    copy_got = gate(copy_got)
    chosen = (slot_table >= 0).T
    gates = dense_gates(jnp.dot(hidden_two, router_full, preferred_element_type=full), chosen)
    grad_middle, branch_gradient, out_mine, out_theirs = middle_backward(
        c,
        copy_got,
        jnp.pad(gates, ((0, 0), (0, 128 - EXPERTS))),
        pack,
        qkv_weight.shape[1],
        gain_two[None, :],
        middle,
        hidden_two,
        cotangent,
        mixed,
    )
    out_scatter = DenseScatter(out_mine, out_theirs, place)
    out_scatter.cores()
    qkv_mine, qkv_theirs, grad_hidden_one = attention_backward(
        jnp.concatenate([lengths, c[None]]),
        branch_gradient,
        query_rows,
        keys,
        value_rows,
        log_totals,
        hidden_one,
        pack,
        out_at,
        cosine_table,
        sine_table,
        tokens,
        rounds.after(),
    )
    rounds.close(grad_hidden_one, *send_back(totals[2]), *out_scatter.first())
    qkv_scatter = DenseScatter(qkv_mine, gate(qkv_theirs), place)
    sent = send_back(*totals[3:])
    rounds.close(*qkv_scatter.cores(), *out_scatter.second())
    rounds.close(*qkv_scatter.first())
    rounds.close(*qkv_scatter.second(), *sent)
    both = jnp.concatenate([out_scatter.sum_up(), qkv_scatter.sum_up()], axis=-1)
    parts = trade(both)
    out_scatter.parts = parts[..., : width + 128]
    qkv_scatter.parts = parts[..., width + 128 :]
    gate_up_grads, down_grads = finish_grads(backs, [both])
    down_grads = down_grads.transpose(0, 2, 1)
    _, grad_norm_one = norm_backward(
        grad_hidden_one, normal_one, inverse_one, gain_one
    )
    grad_input = grad_middle + grad_norm_one

    qkv_sum = qkv_scatter.result()
    first_sum = qkv_sum[:, -128]
    qkv_sum = qkv_sum[:, :-128]
    qkv_sum = qkv_sum.reshape(qkv_sum.shape[0], -1, QUERY_LANES + 2 * KEY_LANES)
    qkv_sum = jnp.concatenate(
        [
            part.reshape(qkv_sum.shape[0], -1)
            for part in jnp.split(qkv_sum, (QUERY_LANES, QUERY_LANES + KEY_LANES), axis=2)
        ],
        axis=1,
    )
    out_sum = out_scatter.result()
    small_sum = out_sum[:, width:]
    return (
        output,
        grad_input,
        first_sum,
        qkv_sum,
        out_sum[:, :width].T,
        small_sum[:, EXPERTS],
        small_sum[:, :EXPERTS],
        gate_up_grads,
        down_grads,
    )


def solution(mesh):
    in_specs = (
        P(("dp", "expert"), None),
        P(("dp", "expert"), None),
        P(("dp", "expert")),
        P(("dp", "expert"), None),
        P(("dp", "expert"), None),
        P(("dp", "expert")),
        P(("dp", "expert"), None),
        P(None, ("dp", "expert")),
        P(("dp", "expert")),
        P(("dp", "expert"), None),
        P("expert", "dp", None),
        P("expert", None, "dp"),
    )
    out_specs = (
        P(("dp", "expert"), None),
        P(("dp", "expert"), None),
        P(("dp", "expert")),
        P(("dp", "expert"), None),
        P(None, ("dp", "expert")),
        P(("dp", "expert")),
        P(("dp", "expert"), None),
        P("expert", "dp", None),
        P("expert", None, "dp"),
    )
    fits = mesh.shape["dp"] == Z_SIZE * Y_SIZE and mesh.shape["expert"] == X_SIZE * C_SIZE
    chosen = body if fits else general_body
    return jax.shard_map(chosen, mesh=mesh, in_specs=in_specs, out_specs=out_specs, check_vma=False)
```

```python
import functools

import jax
import jax.numpy as jnp
from jax import lax
from jax.experimental import pallas as pl
from jax.experimental.pallas import tpu as pltpu
from jax.sharding import PartitionSpec as P

QUERY_HEADS = 24
KEY_VALUE_HEADS = 8
HEAD_SIZE = 64
FF = 512
EXPERTS = 40
TOP = 8
CAP = 152


epsilon = 1e-06
residual_scale = 0.22
score_scale = 0.015625
rope_base = 10000.0
masked_score = -1e30


def rope_tables(length):
    half = HEAD_SIZE // 2
    freqs = jnp.power(rope_base, -2.0 * jnp.arange(half, dtype=jnp.float32) / HEAD_SIZE)
    angles = jnp.arange(length, dtype=jnp.float32)[:, None] * freqs[None, :]
    cosine_table = jnp.concatenate([jnp.cos(angles), jnp.cos(angles)], axis=-1)
    sine_table = jnp.concatenate([jnp.sin(angles), jnp.sin(angles)], axis=-1)
    return (cosine_table, sine_table)


def rotate_half(value_rows):
    half = value_rows.shape[-1] // 2
    return jnp.concatenate([-value_rows[..., half:], value_rows[..., :half]], axis=-1)


def rotate_pairs(value_rows, cosine_table, sine_table):
    return value_rows * cosine_table[:, None, :] + rotate_half(value_rows) * sine_table[:, None, :]


def unrotate(grads, cosine_table, sine_table):
    return grads * cosine_table[:, None, :] - rotate_half(grads * sine_table[:, None, :])


def rms_inverse(value_rows):
    return lax.rsqrt(jnp.mean(value_rows * value_rows, axis=-1, keepdims=True) + epsilon)


def norm_backward(grad_normed, normal, inverse, gain):
    gain_term = jnp.sum(grad_normed * normal, axis=0)
    scaled = grad_normed * gain
    grad_input = inverse * (scaled - normal * jnp.mean(scaled * normal, axis=-1, keepdims=True))
    return (gain_term, grad_input)


def contract_rows(left, right):
    return lax.dot_general(
        left, right, (((0,), (0,)), ((), ())), preferred_element_type=jnp.float32
    )


def multiply_transposed(left, right):
    return lax.dot_general(
        left, right, (((1,), (1,)), ((), ())), preferred_element_type=jnp.float32
    )


def fetch_expert(gate_up_shard, down_shard):
    return (
        lax.all_gather(gate_up_shard, "dp", axis=0, tiled=True),
        lax.all_gather(down_shard, "dp", axis=1, tiled=True),
    )


def gate_values(hidden_rows, router_full, route_rows):
    logits = jnp.dot(hidden_rows, router_full, preferred_element_type=jnp.float32)
    chosen_mask = route_rows[:, :, None] == jnp.arange(EXPERTS)[None, None, :]
    chosen = jnp.sum(jnp.where(chosen_mask, logits[:, None, :], 0.0), axis=-1)
    return (chosen_mask, jax.nn.softmax(chosen, axis=-1))


def general_body(
    tokens,
    cotangent,
    lengths,
    routes,
    slots,
    first_gain,
    qkv_weight,
    out_weight,
    second_gain,
    router_weight,
    gate_up_weight,
    down_weight,
):
    sequence_length = tokens.shape[0]
    width = tokens.shape[1]
    query_group = QUERY_HEADS // KEY_VALUE_HEADS
    length = lengths[0]
    gathered = (
        lax.all_gather(first_gain, ("dp", "expert"), axis=0, tiled=True),
        lax.all_gather(qkv_weight, ("dp", "expert"), axis=0, tiled=True),
        lax.all_gather(out_weight, ("dp", "expert"), axis=1, tiled=True),
        lax.all_gather(second_gain, ("dp", "expert"), axis=0, tiled=True),
        lax.all_gather(router_weight, ("dp", "expert"), axis=0, tiled=True),
    )
    gain_one, qkv_full, out_full, gain_two, router_full = gathered
    inputs = tokens.astype(jnp.float32)
    inverse_one = rms_inverse(inputs)
    normal_one = inputs * inverse_one
    hidden_one = (normal_one * gain_one.astype(jnp.float32)).astype(jnp.bfloat16)
    projected_rows = jnp.dot(hidden_one, qkv_full, preferred_element_type=jnp.float32)
    cosine_table, sine_table = rope_tables(sequence_length)
    query_width_total = QUERY_HEADS * HEAD_SIZE
    key_width_total = KEY_VALUE_HEADS * HEAD_SIZE
    query_rows = rotate_pairs(
        projected_rows[:, :query_width_total].reshape(sequence_length, QUERY_HEADS, HEAD_SIZE),
        cosine_table,
        sine_table,
    ).astype(jnp.bfloat16)
    keys = rotate_pairs(
        projected_rows[:, query_width_total : query_width_total + key_width_total].reshape(
            sequence_length, KEY_VALUE_HEADS, HEAD_SIZE
        ),
        cosine_table,
        sine_table,
    ).astype(jnp.bfloat16)
    value_rows = (
        projected_rows[:, query_width_total + key_width_total :]
        .reshape(sequence_length, KEY_VALUE_HEADS, HEAD_SIZE)
        .astype(jnp.bfloat16)
    )
    row_index = jnp.arange(sequence_length)[:, None]
    column_index = jnp.arange(sequence_length)[None, :]
    allowed = (column_index <= row_index) & (column_index < length)

    def head_scores(head):
        head_query = lax.dynamic_slice_in_dim(query_rows, head * query_group, query_group, 1)
        head_key = lax.dynamic_index_in_dim(keys, head, 1, keepdims=False)
        head_value = lax.dynamic_index_in_dim(value_rows, head, 1, keepdims=False)
        scores = (
            jnp.einsum("qgd,kd->gqk", head_query, head_key, preferred_element_type=jnp.float32)
            * score_scale
        )
        return (head_query, head_key, head_value, jnp.where(allowed[None], scores, masked_score))

    def attention_head_forward(head):
        head_query, head_key, head_value, scores = head_scores(head)
        peak = jnp.max(scores, axis=-1, keepdims=True)
        exponent = jnp.exp(scores - peak)
        total = jnp.sum(exponent, axis=-1, keepdims=True)
        weights = (exponent / total).astype(jnp.bfloat16)
        head_mixed = jnp.einsum(
            "gqk,kd->qgd", weights, head_value, preferred_element_type=jnp.float32
        ).astype(jnp.bfloat16)
        return (head_mixed, (peak + jnp.log(total))[..., 0])

    mixed_head_output, log_sum_totals = lax.map(attention_head_forward, jnp.arange(KEY_VALUE_HEADS))
    mixed = mixed_head_output.transpose(1, 0, 2, 3).reshape(
        sequence_length, QUERY_HEADS * HEAD_SIZE
    )
    branch = jnp.dot(mixed, out_full, preferred_element_type=jnp.float32)
    middle = inputs + residual_scale * branch
    inverse_two = rms_inverse(middle)
    normal_two = middle * inverse_two
    hidden_two = (normal_two * gain_two.astype(jnp.float32)).astype(jnp.bfloat16)
    chosen_mask, gates = gate_values(hidden_two, router_full, routes)
    grad_out = cotangent.astype(jnp.float32)
    grad_mixture = residual_scale * grad_out

    def expert_forward(carry, pieces):
        rows, gate_up_shard, down_shard = pieces
        gate_up_full, down_full = fetch_expert(gate_up_shard, down_shard)
        gate_up = jnp.dot(rows, gate_up_full, preferred_element_type=jnp.float32)
        hidden = (jax.nn.silu(gate_up[:, :FF]) * gate_up[:, FF:]).astype(jnp.bfloat16)
        return (
            carry,
            jnp.dot(hidden, down_full, preferred_element_type=jnp.float32).astype(jnp.bfloat16),
        )

    copies = jnp.broadcast_to(hidden_two[:, None, :], (sequence_length, TOP, width))
    outgoing = jnp.zeros((EXPERTS, CAP, width), jnp.bfloat16).at[routes, slots].set(copies)
    received = lax.all_to_all(outgoing, "expert", split_axis=0, concat_axis=1, tiled=True)
    _, produced = lax.scan(expert_forward, None, (received, gate_up_weight, down_weight))
    returned = lax.all_to_all(produced, "expert", split_axis=1, concat_axis=0, tiled=True)
    expert_rows = returned[routes, slots].astype(jnp.float32)
    mixture = jnp.sum(gates[:, :, None] * expert_rows, axis=1)
    grad_gates = jnp.sum(expert_rows * grad_mixture[:, None, :], axis=-1)
    grad_rows = (gates[:, :, None] * grad_mixture[:, None, :]).astype(jnp.bfloat16)
    outgoing_grad = jnp.zeros((EXPERTS, CAP, width), jnp.bfloat16).at[routes, slots].set(grad_rows)
    grad_received = lax.all_to_all(outgoing_grad, "expert", split_axis=0, concat_axis=1, tiled=True)
    output = (middle + residual_scale * mixture).astype(jnp.bfloat16)
    again = (
        lax.all_gather(first_gain, ("dp", "expert"), axis=0, tiled=True),
        lax.all_gather(qkv_weight, ("dp", "expert"), axis=0, tiled=True),
        lax.all_gather(out_weight, ("dp", "expert"), axis=1, tiled=True),
        lax.all_gather(second_gain, ("dp", "expert"), axis=0, tiled=True),
        lax.all_gather(router_weight, ("dp", "expert"), axis=0, tiled=True),
    )
    gain_back, qkv_back, output_gradient, gain_two_back, router_back = again
    grad_chosen = gates * (grad_gates - jnp.sum(gates * grad_gates, axis=-1, keepdims=True))
    grad_logits = jnp.sum(jnp.where(chosen_mask, grad_chosen[:, :, None], 0.0), axis=1).astype(
        jnp.bfloat16
    )

    def expert_backward(carry, pieces):
        rows, grad_produced, gate_up_shard, down_shard = pieces
        gate_up_full, down_full = fetch_expert(gate_up_shard, down_shard)
        gate_up = jnp.dot(rows, gate_up_full, preferred_element_type=jnp.float32)
        gate = gate_up[:, :FF]
        upper = gate_up[:, FF:]
        sigmoid = jax.nn.sigmoid(gate)
        swish = gate * sigmoid
        hidden = (swish * upper).astype(jnp.bfloat16)
        grad_hidden = multiply_transposed(grad_produced, down_full)
        grad_gate_up = jnp.concatenate(
            [grad_hidden * upper * sigmoid * (1.0 + gate * (1.0 - sigmoid)), grad_hidden * swish],
            axis=-1,
        ).astype(jnp.bfloat16)
        grad_copy = multiply_transposed(grad_gate_up, gate_up_full).astype(jnp.bfloat16)
        gate_up_part = lax.psum_scatter(
            contract_rows(rows, grad_gate_up).astype(jnp.bfloat16),
            "dp",
            scatter_dimension=0,
            tiled=True,
        ).astype(jnp.float32)
        down_part = lax.psum_scatter(
            contract_rows(grad_produced, hidden).astype(jnp.bfloat16),
            "dp",
            scatter_dimension=0,
            tiled=True,
        ).astype(jnp.float32)
        return (carry, (grad_copy, gate_up_part, down_part.T))

    _, (grad_copies, gate_up_grads, down_grads) = lax.scan(
        expert_backward, None, (received, grad_received, gate_up_weight, down_weight)
    )
    grad_back = lax.all_to_all(grad_copies, "expert", split_axis=1, concat_axis=0, tiled=True)
    copy_sum = jnp.sum(grad_back[routes, slots].astype(jnp.float32), axis=1)
    grad_hidden_two = copy_sum + multiply_transposed(grad_logits, router_back)
    router_term = contract_rows(hidden_two, grad_logits)
    second_term, grad_norm_two = norm_backward(
        grad_hidden_two, normal_two, inverse_two, gain_two_back.astype(jnp.float32)
    )
    grad_middle = grad_out + grad_norm_two
    branch_gradient = (residual_scale * grad_middle).astype(jnp.bfloat16)
    out_term = contract_rows(mixed, branch_gradient)
    grad_mixed = (
        multiply_transposed(branch_gradient, output_gradient)
        .astype(jnp.bfloat16)
        .reshape(sequence_length, KEY_VALUE_HEADS, query_group, HEAD_SIZE)
    )

    def attention_head_backward(head):
        head_query, head_key, head_value, scores = head_scores(head)
        head_grad = lax.dynamic_index_in_dim(grad_mixed, head, 1, keepdims=False)
        head_total = lax.dynamic_index_in_dim(log_sum_totals, head, 0, keepdims=False)
        probs = jnp.exp(scores - head_total[..., None])
        grad_weights = jnp.einsum(
            "qgd,kd->gqk", head_grad, head_value, preferred_element_type=jnp.float32
        )
        grad_scores = (
            probs * (grad_weights - jnp.sum(probs * grad_weights, axis=-1, keepdims=True))
        ).astype(jnp.bfloat16)
        grad_query = (
            jnp.einsum("gqk,kd->qgd", grad_scores, head_key, preferred_element_type=jnp.float32)
            * score_scale
        )
        grad_key = (
            jnp.einsum("gqk,qgd->kd", grad_scores, head_query, preferred_element_type=jnp.float32)
            * score_scale
        )
        grad_value = jnp.einsum(
            "gqk,qgd->kd", probs.astype(jnp.bfloat16), head_grad, preferred_element_type=jnp.float32
        )
        return (grad_query, grad_key, grad_value)

    query_head_rows, key_head_rows, value_head_rows = lax.map(
        attention_head_backward, jnp.arange(KEY_VALUE_HEADS)
    )
    grad_query = unrotate(
        query_head_rows.transpose(1, 0, 2, 3).reshape(sequence_length, QUERY_HEADS, HEAD_SIZE),
        cosine_table,
        sine_table,
    )
    grad_key = unrotate(key_head_rows.transpose(1, 0, 2), cosine_table, sine_table)
    grad_value = value_head_rows.transpose(1, 0, 2)
    grad_projected = jnp.concatenate(
        [
            grad_query.reshape(sequence_length, query_width_total),
            grad_key.reshape(sequence_length, key_width_total),
            grad_value.reshape(sequence_length, key_width_total),
        ],
        axis=-1,
    ).astype(jnp.bfloat16)
    qkv_term = contract_rows(hidden_one, grad_projected)
    grad_hidden_one = multiply_transposed(grad_projected, qkv_back)
    first_term, grad_norm_one = norm_backward(
        grad_hidden_one, normal_one, inverse_one, gain_back.astype(jnp.float32)
    )
    grad_input = grad_middle + grad_norm_one
    summed = (
        lax.psum_scatter(first_term, ("dp", "expert"), scatter_dimension=0, tiled=True),
        lax.psum_scatter(qkv_term, ("dp", "expert"), scatter_dimension=0, tiled=True),
        lax.psum_scatter(out_term, ("dp", "expert"), scatter_dimension=1, tiled=True),
        lax.psum_scatter(second_term, ("dp", "expert"), scatter_dimension=0, tiled=True),
        lax.psum_scatter(router_term, ("dp", "expert"), scatter_dimension=0, tiled=True),
    )
    return (
        output,
        grad_input,
        summed[0],
        summed[1],
        summed[2],
        summed[3],
        summed[4],
        gate_up_grads,
        down_grads,
    )


WIDE = 160
Z_SIZE, Y_SIZE, X_SIZE, C_SIZE = 4, 2, 2, 2
MESH_AXES = ("dp", "expert")


def device_index(z, y, x, c):
    return ((z * Y_SIZE + y) * X_SIZE + x) * C_SIZE + c


def device_pairs(target):
    pairs = []
    for z in range(Z_SIZE):
        for y in range(Y_SIZE):
            for x in range(X_SIZE):
                for c in range(C_SIZE):
                    to = target(z, y, x, c)
                    if to is not None:
                        pairs.append((device_index(z, y, x, c), device_index(*to)))
    return pairs


PAIRS_X = device_pairs(lambda z, y, x, c: (z, y, 1 - x, c))
PAIRS_Y = device_pairs(lambda z, y, x, c: (z, 1 - y, x, c))
PAIRS_C = device_pairs(lambda z, y, x, c: (z, y, x, 1 - c))


Z_GROUPS = [[z * Y_SIZE + y for z in range(Z_SIZE)] for y in range(Y_SIZE)]


def tie_kernel(*refs):
    del refs


def tie(value, *after):
    any_spec = pl.BlockSpec(memory_space=pl.ANY)
    return pl.pallas_call(
        tie_kernel,
        in_specs=[any_spec] * (1 + len(after)),
        out_specs=any_spec,
        out_shape=jax.ShapeDtypeStruct(value.shape, value.dtype),
        input_output_aliases={0: 0},
        name="tie",
    )(value, *after)


def trade(value):
    return lax.all_to_all(
        value, "dp", split_axis=0, concat_axis=0, axis_index_groups=Z_GROUPS, tiled=True
    )


def spread(value):
    return trade(jnp.broadcast_to(value[None], (Z_SIZE, *value.shape)))


def join_kernel(*refs):
    refs[-1][...] = jnp.zeros_like(refs[-1])


class Rounds:
    def __init__(self):
        self.token = None

    def gate(self, value):
        return value if self.token is None else tie(value, self.token)

    def after(self):
        return () if self.token is None else (self.token,)

    def close(self, *arrays):
        arrays = list(arrays) + list(self.after())
        self.token = pl.pallas_call(
            join_kernel,
            in_specs=[pl.BlockSpec(memory_space=pl.ANY)] * len(arrays),
            out_specs=pl.BlockSpec(memory_space=pltpu.VMEM),
            out_shape=jax.ShapeDtypeStruct((8, 128), jnp.float32),
            name="join",
        )(*arrays)


def move(value, pairs):
    return lax.ppermute(value, MESH_AXES, pairs)


def assemble(plan, info, arrays, shape, name):
    any_spec = pl.BlockSpec(memory_space=pl.ANY)

    def kernel(info_ref, *refs):
        *parts, out, sem = refs
        copies = [
            pltpu.make_async_copy(source, target, sem.at[i])
            for i, (source, target) in enumerate(plan(info_ref, parts, out))
        ]
        for copy in copies:
            copy.start()
        for copy in copies:
            copy.wait()

    dtype = arrays[0].dtype
    size = 1
    for extent in shape:
        size *= extent
    return pl.pallas_call(
        kernel,
        grid_spec=pltpu.PrefetchScalarGridSpec(
            num_scalar_prefetch=1,
            grid=(),
            in_specs=[any_spec] * len(arrays),
            out_specs=pl.BlockSpec(memory_space=pltpu.VMEM),
            scratch_shapes=[pltpu.SemaphoreType.DMA((2 * len(arrays),))],
        ),
        out_shape=jax.ShapeDtypeStruct(shape, dtype),
        compiler_params=pltpu.CompilerParams(vmem_limit_bytes=32 * 1024 * 1024),
        cost_estimate=pl.CostEstimate(flops=0, bytes_accessed=4 * size, transcendentals=0),
        name=name,
    )(info, *arrays)


def dense_assemble(place, mine, other):
    z, y, x, c = place
    rows, n = mine[0].shape[1:]
    zs = Z_SIZE // 2

    def plan(info, parts, out):
        at_y, at_x = info[0], info[1]
        copies = []
        for k in range(2):
            at_c = info[2] if k == 0 else 1 - info[2]
            block, from_x, from_y, far_a, far_b = parts[5 * k : 5 * k + 5]
            copies += [
                (block, out.at[:, at_y, at_x, at_c]),
                (from_x, out.at[:, at_y, 1 - at_x, at_c]),
                (from_y, out.at[:, 1 - at_y, at_x, at_c]),
                (far_a, out.at[pl.ds(0, zs), 1 - at_y, 1 - at_x, at_c]),
                (far_b, out.at[pl.ds(zs, zs), 1 - at_y, 1 - at_x, at_c]),
            ]
        return copies

    shape = (Z_SIZE, Y_SIZE, X_SIZE, C_SIZE, rows, n)
    full = assemble(plan, jnp.stack([y, x, c]), (*mine, *other), shape, "dense_assemble")
    return full.reshape(-1, n)


def join_rows(other, own):
    counts = [part.shape[1] for part in own]

    def plan(info, parts, out):
        copies = []
        for k in range(2):
            at = 0
            for i, count in enumerate(counts):
                target = out.at[pl.ds(k * Z_SIZE, Z_SIZE), pl.ds(at, count)]
                copies.append((parts[k * len(counts) + i], target))
                at += count
        return copies

    shape = (2 * Z_SIZE, sum(counts), own[0].shape[2])
    return assemble(plan, jnp.zeros((1,), jnp.int32), (*other, *own), shape, "join_rows")


def half_order(z_to):
    first = 10 * (z_to // 2)
    if z_to % 2 == 0:
        return [first, first + 1, first + 2, first + 3, first + 4]
    return [first + 6, first + 7, first + 8, first + 9, first + 5]


HALF_ORDER = [half_order(z_to) for z_to in range(Z_SIZE)]
HALF_PLACE = [0] * (Z_SIZE * 5)
for order_z in range(Z_SIZE):
    for order_q in range(5):
        HALF_PLACE[HALF_ORDER[order_z][order_q]] = order_z * 5 + order_q
UNIT_HALVES = ((0, 2), (2, 4), (4, 5))


def dense_gates(logits, chosen):
    peak = jnp.max(jnp.where(chosen, logits, -jnp.inf), axis=-1, keepdims=True)
    exponent = jnp.where(chosen, jnp.exp(logits - peak), 0.0)
    return exponent / jnp.sum(exponent, axis=-1, keepdims=True)


def mm(left, right):
    return jnp.dot(left, right, preferred_element_type=jnp.float32)


def weight_loads(pieces, w_s, sem, y):
    copies = []
    for h in range(w_s.shape[0]):
        for piece, at_y in zip(pieces[2 * h : 2 * h + 2], (y, 1 - y)):
            copies.append(
                pltpu.make_async_copy(piece, w_s.at[h, :, at_y], sem.at[len(copies)])
            )
    return copies


def expert_forward_kernel(info, slots, gates, rows, *rest, count, waits):
    pieces = rest[:count]
    out, kept, gate_up_out, w_s, in_sem = rest[count + waits :]
    low = jnp.bfloat16
    step = pl.program_id(0)
    half = FF // 2
    halves = w_s.shape[0]
    loads = weight_loads(pieces, w_s, in_sem, info[0])

    @pl.when(step == 0)
    def _():
        for load in loads:
            load.start()

    group, length, width = rows.shape
    span = group * WIDE
    iota = lax.broadcasted_iota(jnp.int32, (WIDE, length), 0)
    gate_cols = []
    for j in range(group):
        pick = iota == slots[j]
        one_hot = jnp.where(pick, 1.0, 0.0).astype(low)
        gate_cols.append(jnp.sum(jnp.where(pick, gates[j], 0.0), axis=1, keepdims=True))
        kept[j * WIDE : (j + 1) * WIDE, :] = mm(one_hot, rows[j]).astype(low)
    gate_col = jnp.concatenate(gate_cols, axis=0)

    @pl.when(step == 0)
    def _():
        for load in loads:
            load.wait()

    produced = None
    for h in range(halves):
        gate_up_w = w_s[h, :, :, :, : 2 * half].reshape(width, 2 * half)
        down_t = w_s[h, :, :, :, 2 * half :].reshape(width, half)
        gate_up = mm(kept[...], gate_up_w)
        gate_up_out[:, 2 * h * half : 2 * (h + 1) * half] = gate_up
        gate = gate_up[:, :half]
        hidden = (gate * (1.0 / (1.0 + jnp.exp(-gate))) * gate_up[:, half:]).astype(low)
        term = multiply_transposed(hidden, down_t)
        produced = term if produced is None else produced + term
    out[...] = (produced * gate_col).astype(low).reshape(group, WIDE, width)


def expert_forward(place, halves, y, slots, gates, rows_in, pieces, buffer, after):
    sources, length, width = rows_in.shape
    _, rows, lanes = pieces[0].shape
    half = FF // 2
    low = jnp.bfloat16
    group = 2
    units = 2 * len(UNIT_HALVES)
    any_spec = pl.BlockSpec(memory_space=pl.ANY)
    row_spec = pl.BlockSpec((group, 1, length), lambda i, info: (i, 0, 0))
    waits = list(after)
    aliases = {}
    if buffer is not None:
        aliases = {4 + len(pieces): 0}
        waits = [buffer] + waits
    total = sources * WIDE
    span = group * WIDE
    return pl.pallas_call(
        functools.partial(expert_forward_kernel, count=len(pieces), waits=len(waits)),
        grid_spec=pltpu.PrefetchScalarGridSpec(
            num_scalar_prefetch=1,
            grid=(sources // group,),
            in_specs=[
                row_spec,
                row_spec,
                pl.BlockSpec((group, length, width), lambda i, info: (i, 0, 0)),
            ]
            + [any_spec] * (len(pieces) + len(waits)),
            out_specs=[
                pl.BlockSpec((group, WIDE, width), lambda i, info: (i, place, 0)),
                pl.BlockSpec((span, width), lambda i, info: (i, 0)),
                pl.BlockSpec((span, 2 * half * halves), lambda i, info: (i, 0)),
            ],
            scratch_shapes=[
                pltpu.VMEM((halves, Z_SIZE, Y_SIZE, rows, lanes), low),
                pltpu.SemaphoreType.DMA((4,)),
            ],
        ),
        out_shape=[
            jax.ShapeDtypeStruct((sources, units * WIDE, width), low),
            jax.ShapeDtypeStruct((total, width), low),
            jax.ShapeDtypeStruct((total, 2 * half * halves), jnp.float32),
        ],
        input_output_aliases=aliases,
        compiler_params=pltpu.CompilerParams(vmem_limit_bytes=60 * 1024 * 1024),
        cost_estimate=pl.CostEstimate(
            flops=2 * total * width * (3 * half * halves + length),
            bytes_accessed=2 * (sources * length * width + 2 * total * width)
            + 8 * total * half * halves
            + 2 * halves * width * lanes,
            transcendentals=total * half * halves,
        ),
        name="expert_forward",
    )(y, slots, gates, rows_in, *pieces, *waits)


def expert_back_kernel(info, slots, gates, dys, kept, gate_ups, *rest, count, waits):
    pieces = rest[:count]
    back, near_a_g, near_b_g, far_a_g, far_b_g = rest[count + waits : count + waits + 5]
    w_s, x_s, gd_s, dgu_s, hid_s, g_s, in_sem, out_sem = rest[count + waits + 5 :]
    low = jnp.bfloat16
    full = jnp.float32
    step = pl.program_id(0)
    y = info[0]
    expert = info[1]
    half = FF // 2
    zs = Z_SIZE // 2
    halves = w_s.shape[0]
    loads = weight_loads(pieces, w_s, in_sem, y)

    @pl.when(step == 0)
    def _():
        for load in loads:
            load.start()

    group, length, width = dys.shape
    span = group * WIDE
    here = pl.ds(pl.multiple_of(step * span, span), span)
    iota = lax.broadcasted_iota(jnp.int32, (WIDE, length), 0)
    gate_cols = []
    dy_parts = []
    for j in range(group):
        pick = iota == slots[j]
        one_hot = jnp.where(pick, 1.0, 0.0).astype(low)
        gate_col = jnp.sum(jnp.where(pick, gates[j], 0.0), axis=1, keepdims=True)
        at = pl.multiple_of(step * span + j * WIDE, WIDE)
        dy = mm(one_hot, dys[j])
        gd_s[pl.ds(at, WIDE), :] = (dy * (residual_scale * gate_col)).astype(low)
        dy_parts.append(dy.astype(low))
        gate_cols.append(gate_col)
    dy = jnp.concatenate(dy_parts, axis=0)
    gate_col = jnp.concatenate(gate_cols, axis=0)
    x_s[here, :] = kept[...]

    @pl.when(step == 0)
    def _():
        for load in loads:
            load.wait()

    grad_copy = None
    grad_gate = None
    for h in range(halves):
        gate_up_w = w_s[h, :, :, :, : 2 * half].reshape(width, 2 * half)
        down_t = w_s[h, :, :, :, 2 * half :].reshape(width, half)
        gate = gate_ups[:, 2 * h * half : (2 * h + 1) * half]
        upper = gate_ups[:, (2 * h + 1) * half : (2 * h + 2) * half]
        sigmoid = 1.0 / (1.0 + jnp.exp(-gate))
        swish = gate * sigmoid
        hidden = (swish * upper).astype(low)
        hid_s[here, h * half : (h + 1) * half] = hidden
        grad_plain = residual_scale * mm(dy, down_t)
        term = jnp.sum(hidden.astype(full) * grad_plain, axis=1, keepdims=True)
        grad_gate = term if grad_gate is None else grad_gate + term
        grad_hidden = grad_plain * gate_col
        dgu_s[here, 2 * h * half : (2 * h + 1) * half] = (
            grad_hidden * upper * sigmoid * (1.0 + gate * (1.0 - sigmoid))
        ).astype(low)
        dgu_s[here, (2 * h + 1) * half : (2 * h + 2) * half] = (grad_hidden * swish).astype(low)
        term = multiply_transposed(dgu_s[here, 2 * h * half : 2 * (h + 1) * half], gate_up_w)
        grad_copy = term if grad_copy is None else grad_copy + term
    back[:, :, :width] = grad_copy.astype(low).reshape(group, WIDE, width)
    lane = lax.broadcasted_iota(jnp.int32, (span, 128), 1)
    high = grad_gate.astype(low).astype(full)
    extra = jnp.where(lane == expert, high, 0.0) + jnp.where(
        lane == expert + 64, grad_gate - high, 0.0
    )
    back[:, :, width:] = extra.astype(low).reshape(group, WIDE, 128)

    @pl.when(step == pl.num_programs(0) - 1)
    def _():
        piece = width // Z_SIZE
        for h in range(halves):
            for zz in range(Z_SIZE):
                cols = slice(zz * piece, (zz + 1) * piece)
                got = contract_rows(x_s[:, cols], dgu_s[:, 2 * h * half : 2 * (h + 1) * half])
                g_s[h, zz, :, :, : 2 * half] = got.astype(low).reshape(2, piece // 2, 2 * half)
                got = contract_rows(gd_s[:, cols], hid_s[:, h * half : (h + 1) * half])
                g_s[h, zz, :, :, 2 * half :] = got.astype(low).reshape(2, piece // 2, half)
        stores = [
            (g_s.at[:, pl.ds(0, zs), y], near_a_g),
            (g_s.at[:, pl.ds(zs, zs), y], near_b_g),
            (g_s.at[:, pl.ds(0, zs), 1 - y], far_a_g),
            (g_s.at[:, pl.ds(zs, zs), 1 - y], far_b_g),
        ]
        stores = [pltpu.make_async_copy(a, b, out_sem.at[i]) for i, (a, b) in enumerate(stores)]
        for store in stores:
            store.start()
        for store in stores:
            store.wait()


def expert_backward(
    place, halves, info, slots, gates, grads_in, kept, gate_ups, pieces, buffer, after
):
    sources, length, width = grads_in.shape
    _, rows, lanes = pieces[0].shape
    half = FF // 2
    low = jnp.bfloat16
    group = 2
    units = 2 * len(UNIT_HALVES)
    any_spec = pl.BlockSpec(memory_space=pl.ANY)
    row_spec = pl.BlockSpec((group, 1, length), lambda i, info: (i, 0, 0))
    waits = list(after)
    aliases = {}
    if buffer is not None:
        aliases = {6 + len(pieces): 0}
        waits = [buffer] + waits
    total = sources * WIDE
    span = group * WIDE
    quarter = (halves, Z_SIZE // 2, rows, lanes)
    result = pl.pallas_call(
        functools.partial(expert_back_kernel, count=len(pieces), waits=len(waits)),
        grid_spec=pltpu.PrefetchScalarGridSpec(
            num_scalar_prefetch=1,
            grid=(sources // group,),
            in_specs=[
                row_spec,
                row_spec,
                pl.BlockSpec((group, length, width), lambda i, info: (i, 0, 0)),
                pl.BlockSpec((span, width), lambda i, info: (i, 0)),
                pl.BlockSpec((span, 2 * half * halves), lambda i, info: (i, 0)),
            ]
            + [any_spec] * (len(pieces) + len(waits)),
            out_specs=[
                pl.BlockSpec((group, WIDE, width + 128), lambda i, info: (i, place, 0)),
            ]
            + [any_spec] * 4,
            scratch_shapes=[
                pltpu.VMEM((halves, Z_SIZE, Y_SIZE, rows, lanes), low),
                pltpu.VMEM((total, width), low),
                pltpu.VMEM((total, width), low),
                pltpu.VMEM((total, 2 * half * halves), low),
                pltpu.VMEM((total, half * halves), low),
                pltpu.VMEM((halves, Z_SIZE, Y_SIZE, rows, lanes), low),
                pltpu.SemaphoreType.DMA((4,)),
                pltpu.SemaphoreType.DMA((4,)),
            ],
        ),
        out_shape=[jax.ShapeDtypeStruct((sources, units * WIDE, width + 128), low)]
        + [jax.ShapeDtypeStruct(quarter, low)] * 4,
        input_output_aliases=aliases,
        compiler_params=pltpu.CompilerParams(vmem_limit_bytes=60 * 1024 * 1024),
        cost_estimate=pl.CostEstimate(
            flops=2 * total * width * (6 * half * halves + length),
            bytes_accessed=2 * (sources * length * width + 2 * total * width)
            + 8 * total * half * halves
            + 4 * halves * width * lanes,
            transcendentals=total * half * halves,
        ),
        name="expert_backward",
    )(info, slots, gates, grads_in, kept, gate_ups, *pieces, *waits)
    return result[0], result[1:]


def middle_back_kernel(
    c_ref, got, gates, small, gain, middle, hidden, cotangent, mixed, dmiddle, dbranch, mine, theirs,
    g_s, sem,
):
    full = jnp.float32
    low = jnp.bfloat16
    c = c_ref[0]
    length, width = middle.shape
    total = got[0].astype(full)
    for z in range(1, Z_SIZE):
        total = total + got[z].astype(full)
    parts = total[:, width:]
    grad_gates = parts + pltpu.roll(parts, 64, 1)
    gate = gates[...]
    grad_logits = gate * (grad_gates - jnp.sum(gate * grad_gates, axis=1, keepdims=True))
    grad_logits = grad_logits.astype(low)
    dh2 = total[:, :width] + multiply_transposed(grad_logits, small[...])
    value = middle[...]
    inverse = rms_inverse(value)
    normal = value * inverse
    scaled = dh2 * gain[...]
    mean = jnp.mean(scaled * normal, axis=1, keepdims=True)
    grad = cotangent[...].astype(full) + inverse * (scaled - normal * mean)
    dmiddle[...] = grad
    branch = (residual_scale * grad).astype(low)
    dbranch[...] = branch
    per = g_s.shape[3]
    step = width // Z_SIZE
    rows = Y_SIZE * X_SIZE
    for z in range(Z_SIZE):
        part = slice(z * step, (z + 1) * step)
        term = contract_rows(branch[:, part], mixed[...]).astype(low)
        g_s[:, z, :, :, :width] = term.reshape(rows, C_SIZE, per, width)
        router = contract_rows(hidden[:, part], grad_logits)
        product = (dh2[:, part] * normal[:, part]).astype(low)
        second = contract_rows(product, jnp.ones((length, 128), low))
        lane = lax.broadcasted_iota(jnp.int32, router.shape, 1)
        router = jnp.where(lane == EXPERTS, second, router).astype(low)
        g_s[:, z, :, :, width:] = router.reshape(rows, C_SIZE, per, 128)
    copies = [
        pltpu.make_async_copy(g_s.at[:, :, c], mine, sem.at[0]),
        pltpu.make_async_copy(g_s.at[:, :, 1 - c], theirs, sem.at[1]),
    ]
    for copy in copies:
        copy.start()
    for copy in copies:
        copy.wait()


def middle_backward(c, got, gates, pack, small_at, gain, middle, hidden, cotangent, mixed):
    length, width = middle.shape
    low = jnp.bfloat16
    blocks = (Y_SIZE * X_SIZE, Z_SIZE)
    per = width // (Y_SIZE * X_SIZE * Z_SIZE * C_SIZE)
    any_spec = pl.BlockSpec(memory_space=pl.ANY)
    whole = lambda a: pl.BlockSpec(a.shape, lambda i, n: (0,) * a.ndim)
    split = jax.ShapeDtypeStruct((*blocks, per, width + 128), low)
    rows = pl.BlockSpec((length, width), lambda i, n: (0, 0))
    return pl.pallas_call(
        middle_back_kernel,
        grid_spec=pltpu.PrefetchScalarGridSpec(
            num_scalar_prefetch=1,
            grid=(1,),
            in_specs=[
                whole(got),
                whole(gates),
                pl.BlockSpec((width, 128), lambda i, n: (0, small_at // 128)),
                whole(gain),
                rows,
                rows,
                rows,
                rows,
            ],
            out_specs=[rows, rows, any_spec, any_spec],
            scratch_shapes=[
                pltpu.VMEM((*blocks, C_SIZE, per, width + 128), low),
                pltpu.SemaphoreType.DMA((2,)),
            ],
        ),
        out_shape=[
            jax.ShapeDtypeStruct((length, width), jnp.float32),
            jax.ShapeDtypeStruct((length, width), low),
            split,
            split,
        ],
        compiler_params=pltpu.CompilerParams(vmem_limit_bytes=56 * 1024 * 1024),
        cost_estimate=pl.CostEstimate(
            flops=2 * length * width * (width + 384),
            bytes_accessed=length * width * 24 + 4 * width * width,
            transcendentals=0,
        ),
        name="middle_backward",
    )(c[None], got, gates, pack, gain, middle, hidden, cotangent, mixed)


def turn_halves(value):
    lanes = value.shape[-1]
    lane = lax.broadcasted_iota(jnp.int32, value.shape, 1)
    ahead = pltpu.roll(value, lanes - HEAD_SIZE // 2, 1)
    behind = pltpu.roll(value, HEAD_SIZE // 2, 1)
    return jnp.where(lane % HEAD_SIZE < HEAD_SIZE // 2, -ahead, behind)


def heads_of(value, first, count):
    return jnp.concatenate(
        [value[:, (first + i) * HEAD_SIZE : (first + i + 1) * HEAD_SIZE] for i in range(count)],
        axis=0,
    )


ROW_BLOCK = 128
PAIR = 2
GROUP = QUERY_HEADS // KEY_VALUE_HEADS
QUERY_LANES = PAIR * GROUP * HEAD_SIZE
KEY_LANES = PAIR * HEAD_SIZE


def block_mask(block, length):
    shape = (ROW_BLOCK, (block + 1) * ROW_BLOCK)
    row = lax.broadcasted_iota(jnp.int32, shape, 0) + block * ROW_BLOCK
    column = lax.broadcasted_iota(jnp.int32, shape, 1)
    allowed = jnp.where((column <= row) & (column < length), 1, 0)
    return jnp.concatenate([allowed] * GROUP, axis=0) > 0


def attention_kernel(
    length, tokens, gain, wq, wk, wv, cosine, sine, *rest
):
    h1, q, k, v, mixed, lse, h_s, lse_s = rest[-8:]
    step = pl.program_id(0)
    low = jnp.bfloat16
    rows = tokens.shape[0]

    @pl.when(step == 0)
    def _():
        value = tokens[...].astype(jnp.float32)
        hidden = (value * rms_inverse(value) * gain[...]).astype(low)
        h_s[...] = hidden
        h1[...] = hidden

    lane = lax.broadcasted_iota(jnp.int32, (rows, 128), 1)
    cos = cosine[...]
    sin = sine[...]
    query = mm(h_s[...], wq[...])
    query = (query * cos + turn_halves(query) * sin).astype(low)
    key = mm(h_s[...], wk[...])
    key = (key * cos[:, :KEY_LANES] + turn_halves(key) * sin[:, :KEY_LANES]).astype(low)
    value = mm(h_s[...], wv[...]).astype(low)
    q[...] = query
    k[...] = key
    v[...] = value
    blocks = rows // ROW_BLOCK
    totals = [[] for _ in range(PAIR * GROUP)]
    masks = [block_mask(block, length[0]) for block in range(blocks)]
    outs = [[] for _ in range(PAIR * GROUP)]
    for head in range(PAIR):
        key_h = key[:, head * HEAD_SIZE : (head + 1) * HEAD_SIZE]
        value_h = value[:, head * HEAD_SIZE : (head + 1) * HEAD_SIZE]
        for block in range(blocks):
            keys = (block + 1) * ROW_BLOCK
            query_h = heads_of(
                query[block * ROW_BLOCK : (block + 1) * ROW_BLOCK], head * GROUP, GROUP
            )
            scores = multiply_transposed(query_h, key_h[:keys]) * score_scale
            scores = jnp.where(masks[block], scores, masked_score)
            peak = jnp.max(scores, axis=1, keepdims=True)
            exponent = jnp.exp(scores - peak)
            total = jnp.sum(exponent, axis=1, keepdims=True)
            weights = (exponent / total).astype(low)
            out = mm(weights, value_h[:keys]).astype(low)
            log_total = peak + jnp.log(total)
            for i in range(GROUP):
                part = slice(i * ROW_BLOCK, (i + 1) * ROW_BLOCK)
                outs[head * GROUP + i].append(out[part])
                totals[head * GROUP + i].append(log_total[part])
    mixed[...] = jnp.concatenate([jnp.concatenate(o, axis=0) for o in outs], axis=1)

    @pl.when(step == 0)
    def _():
        lse_s[...] = jnp.zeros_like(lse_s)

    kept = lse_s[...]
    for i in range(PAIR * GROUP):
        column = jnp.concatenate(totals[i], axis=0)
        kept = jnp.where(lane == step * PAIR * GROUP + i, column, kept)
    lse_s[...] = kept
    lse[...] = kept


def attention_forward(length, tokens, gain, weight, cosine, sine, after=()):
    rows, width = tokens.shape
    steps = KEY_VALUE_HEADS // PAIR
    low = jnp.bfloat16
    query_total = QUERY_HEADS * HEAD_SIZE
    key_total = KEY_VALUE_HEADS * HEAD_SIZE
    key_at = query_total // KEY_LANES
    value_at = key_at + steps
    whole = lambda shape: pl.BlockSpec(shape, lambda i, n: (0, 0))
    cols = lambda lanes, at: pl.BlockSpec((width, lanes), lambda i, n: (0, at + i))
    part = lambda lanes: pl.BlockSpec((rows, lanes), lambda i, n: (0, i))
    return pl.pallas_call(
        attention_kernel,
        grid_spec=pltpu.PrefetchScalarGridSpec(
            num_scalar_prefetch=1,
            grid=(steps,),
            in_specs=[
                whole((rows, width)),
                whole((1, width)),
                cols(QUERY_LANES, 0),
                cols(KEY_LANES, key_at),
                cols(KEY_LANES, value_at),
                whole((rows, QUERY_LANES)),
                whole((rows, QUERY_LANES)),
            ]
            + [pl.BlockSpec(memory_space=pl.ANY)] * len(after),
            out_specs=[
                whole((rows, width)),
                part(QUERY_LANES),
                part(KEY_LANES),
                part(KEY_LANES),
                part(QUERY_LANES),
                whole((rows, 128)),
            ],
            scratch_shapes=[pltpu.VMEM((rows, width), low), pltpu.VMEM((rows, 128), jnp.float32)],
        ),
        out_shape=[
            jax.ShapeDtypeStruct((rows, width), low),
            jax.ShapeDtypeStruct((rows, query_total), low),
            jax.ShapeDtypeStruct((rows, key_total), low),
            jax.ShapeDtypeStruct((rows, key_total), low),
            jax.ShapeDtypeStruct((rows, query_total), low),
            jax.ShapeDtypeStruct((rows, 128), jnp.float32),
        ],
        compiler_params=pltpu.CompilerParams(vmem_limit_bytes=48 * 1024 * 1024),
        cost_estimate=pl.CostEstimate(
            flops=2 * rows * width * (query_total + 2 * key_total)
            + 4 * QUERY_HEADS * rows * rows * HEAD_SIZE,
            bytes_accessed=2 * width * (query_total + 2 * key_total) + 10 * rows * width,
            transcendentals=QUERY_HEADS * rows * rows,
        ),
        name="attention_forward",
    )(length, tokens, gain, weight, weight, weight, cosine, sine, *after)


def attention_back_kernel(
    length, dbranch, wo, q, k, v, lse, h1, wq, wk, wv, cosine, sine, tokens, *rest
):
    mine, theirs, dh1, dh_s, g_s = rest[-5:]
    c = length[1]
    step = pl.program_id(0)
    low = jnp.bfloat16
    full = jnp.float32
    rows = dbranch.shape[0]
    span = h1.shape[1] // Z_SIZE
    split = (Y_SIZE * X_SIZE, C_SIZE, span // (Y_SIZE * X_SIZE * C_SIZE))

    @pl.when(step < pl.num_programs(0) - 1)
    def _():
        blocks = rows // ROW_BLOCK
        dmixed = mm(dbranch[...], wo[...]).astype(low)
        lane = lax.broadcasted_iota(jnp.int32, (rows, 128), 1)
        kept = lse[...]
        query, key, value = q[...], k[...], v[...]
        columns = [
            jnp.sum(jnp.where(lane == step * PAIR * GROUP + i, kept, 0.0), axis=1, keepdims=True)
            for i in range(PAIR * GROUP)
        ]
        masks = [block_mask(block, length[0]) for block in range(blocks)]
        dq = [[] for _ in range(PAIR * GROUP)]
        dks, dvs = [], []
        for head in range(PAIR):
            key_h = key[:, head * HEAD_SIZE : (head + 1) * HEAD_SIZE]
            value_h = value[:, head * HEAD_SIZE : (head + 1) * HEAD_SIZE]
            dk = [None] * blocks
            dv = [None] * blocks
            for block in range(blocks):
                keys = (block + 1) * ROW_BLOCK
                at = slice(block * ROW_BLOCK, (block + 1) * ROW_BLOCK)
                query_h = heads_of(query[at], head * GROUP, GROUP)
                dmixed_h = heads_of(dmixed[at], head * GROUP, GROUP)
                log_total = jnp.concatenate(
                    [columns[head * GROUP + i][at] for i in range(GROUP)], axis=0
                )
                scores = multiply_transposed(query_h, key_h[:keys]) * score_scale
                scores = jnp.where(masks[block], scores, masked_score)
                probs = jnp.exp(scores - log_total)
                dprobs = multiply_transposed(dmixed_h, value_h[:keys])
                delta = jnp.sum(probs * dprobs, axis=1, keepdims=True)
                dscores = (probs * (dprobs - delta)).astype(low)
                dquery = mm(dscores, key_h[:keys]) * score_scale
                dkey = contract_rows(dscores, query_h) * score_scale
                dvalue = contract_rows(probs.astype(low), dmixed_h)
                for i in range(GROUP):
                    dq[head * GROUP + i].append(dquery[i * ROW_BLOCK : (i + 1) * ROW_BLOCK])
                for b in range(block + 1):
                    part = slice(b * ROW_BLOCK, (b + 1) * ROW_BLOCK)
                    dk[b] = dkey[part] if dk[b] is None else dk[b] + dkey[part]
                    dv[b] = dvalue[part] if dv[b] is None else dv[b] + dvalue[part]
            dks.append(jnp.concatenate(dk, axis=0))
            dvs.append(jnp.concatenate(dv, axis=0))
        cos = cosine[...]
        sin = sine[...]
        dquery = jnp.concatenate([jnp.concatenate(o, axis=0) for o in dq], axis=1)
        dquery = (dquery * cos - turn_halves(dquery * sin)).astype(low)
        dkey = jnp.concatenate(dks, axis=1)
        dkey = (dkey * cos[:, :KEY_LANES] - turn_halves(dkey * sin[:, :KEY_LANES])).astype(low)
        dvalue = jnp.concatenate(dvs, axis=1).astype(low)
        hidden = h1[...]
        got = contract_rows(hidden, dquery).astype(low)
        for z in range(Z_SIZE):
            part = got[z * span : (z + 1) * span]
            g_s[:, z, :, :, :QUERY_LANES] = part.reshape(*split, QUERY_LANES)
        got = contract_rows(hidden, jnp.concatenate([dkey, dvalue], axis=1)).astype(low)
        for z in range(Z_SIZE):
            part = got[z * span : (z + 1) * span]
            g_s[:, z, :, :, QUERY_LANES:] = part.reshape(*split, 2 * KEY_LANES)
        mine[...] = g_s[:, :, c]
        theirs[...] = g_s[:, :, 1 - c]
        term = (
            multiply_transposed(dquery, wq[...])
            + multiply_transposed(dkey, wk[...])
            + multiply_transposed(dvalue, wv[...])
        )

        @pl.when(step == 0)
        def _():
            dh_s[...] = term

        @pl.when(step > 0)
        def _():
            dh_s[...] += term

    @pl.when(step == pl.num_programs(0) - 1)
    def _():
        total = dh_s[...]
        dh1[...] = total
        value = tokens[...].astype(full)
        product = (total * (value * rms_inverse(value))).astype(low)
        column = contract_rows(product, jnp.ones((rows, 128), low)).astype(low)
        for z in range(Z_SIZE):
            part = column[z * span : (z + 1) * span]
            g_s[:, z, :, :, :128] = part.reshape(*split, 128)
        mine[:, :, :, :128] = g_s[:, :, c, :, :128]
        theirs[:, :, :, :128] = g_s[:, :, 1 - c, :, :128]


def attention_backward(
    length, dbranch, q, k, v, lse, h1, weight, out_at, cosine, sine, tokens, after=()
):
    rows, width = dbranch.shape
    steps = KEY_VALUE_HEADS // PAIR
    low = jnp.bfloat16
    full = jnp.float32
    query_total = QUERY_HEADS * HEAD_SIZE
    key_total = KEY_VALUE_HEADS * HEAD_SIZE
    key_at = query_total // KEY_LANES
    value_at = key_at + steps
    whole = lambda shape: pl.BlockSpec(shape, lambda i, n: (0, 0))
    cols = lambda lanes, at: pl.BlockSpec((width, lanes), lambda i, n: (0, at + jnp.minimum(i, steps - 1)))
    part = lambda lanes: pl.BlockSpec((rows, lanes), lambda i, n: (0, jnp.minimum(i, steps - 1)))
    lanes = QUERY_LANES + 2 * KEY_LANES
    blocks = (Y_SIZE * X_SIZE, Z_SIZE)
    per = width // (Y_SIZE * X_SIZE * Z_SIZE * C_SIZE)
    return pl.pallas_call(
        attention_back_kernel,
        grid_spec=pltpu.PrefetchScalarGridSpec(
            num_scalar_prefetch=1,
            grid=(steps + 1,),
            in_specs=[
                whole((rows, width)),
                cols(QUERY_LANES, out_at // QUERY_LANES),
                part(QUERY_LANES),
                part(KEY_LANES),
                part(KEY_LANES),
                whole((rows, 128)),
                whole((rows, width)),
                cols(QUERY_LANES, 0),
                cols(KEY_LANES, key_at),
                cols(KEY_LANES, value_at),
                whole((rows, QUERY_LANES)),
                whole((rows, QUERY_LANES)),
                whole((rows, width)),
            ]
            + [pl.BlockSpec(memory_space=pl.ANY)] * len(after),
            out_specs=[
                pl.BlockSpec((*blocks, per, lanes), lambda i, n: (0, 0, 0, i)),
                pl.BlockSpec((*blocks, per, lanes), lambda i, n: (0, 0, 0, i)),
                whole((rows, width)),
            ],
            scratch_shapes=[
                pltpu.VMEM((rows, width), full),
                pltpu.VMEM((*blocks, C_SIZE, per, lanes), low),
            ],
        ),
        out_shape=[
            jax.ShapeDtypeStruct((*blocks, per, steps * lanes + 128), low),
            jax.ShapeDtypeStruct((*blocks, per, steps * lanes + 128), low),
            jax.ShapeDtypeStruct((rows, width), full),
        ],
        compiler_params=pltpu.CompilerParams(vmem_limit_bytes=48 * 1024 * 1024),
        cost_estimate=pl.CostEstimate(
            flops=4 * rows * width * (query_total + 2 * key_total)
            + 2 * rows * width * query_total
            + 10 * QUERY_HEADS * rows * rows * HEAD_SIZE,
            bytes_accessed=4 * width * (query_total + 2 * key_total) + 2 * width * width + 14 * rows * width,
            transcendentals=QUERY_HEADS * rows * rows,
        ),
        name="attention_backward",
    )(length, dbranch, weight, q, k, v, lse, h1, weight, weight, weight, cosine, sine, tokens, *after)


def combine_kernel(slots, values, *rest):
    out, p_s = rest[-2:]
    length = slots.shape[2]
    iota = lax.broadcasted_iota(jnp.int32, (WIDE, length), 0)
    for u in range(slots.shape[1]):
        pick = iota == slots[0, u : u + 1, :]
        p_s[u * WIDE : (u + 1) * WIDE, :] = jnp.where(pick, 1.0, 0.0).astype(jnp.bfloat16)
    out[0] = contract_rows(p_s[...], values[0]).astype(jnp.bfloat16)


def combine(slots, values, first, after=()):
    _, units, length = slots.shape
    n = values.shape[-1]
    low = jnp.bfloat16
    return pl.pallas_call(
        combine_kernel,
        grid=(Z_SIZE,),
        in_specs=[
            pl.BlockSpec((1, units, length), lambda i: (first + i, 0, 0)),
            pl.BlockSpec((1, units * WIDE, n), lambda i: (first + i, 0, 0)),
        ]
        + [pl.BlockSpec(memory_space=pl.ANY)] * len(after),
        out_specs=pl.BlockSpec((1, length, n), lambda i: (i, 0, 0)),
        out_shape=jax.ShapeDtypeStruct((Z_SIZE, length, n), low),
        scratch_shapes=[pltpu.VMEM((units * WIDE, length), low)],
        compiler_params=pltpu.CompilerParams(vmem_limit_bytes=60 * 1024 * 1024),
        cost_estimate=pl.CostEstimate(
            flops=2 * Z_SIZE * units * WIDE * length * n,
            bytes_accessed=Z_SIZE * (units * WIDE + length) * n * 2,
            transcendentals=0,
        ),
        name="combine",
    )(slots, values, *after)


def weight_chunks(gate_up_weight, down_weight):
    experts, rows = gate_up_weight.shape[0], gate_up_weight.shape[1]
    gate, upper = gate_up_weight[..., :FF], gate_up_weight[..., FF:]
    down_t = down_weight.transpose(0, 2, 1)
    half = FF // 2

    def one(q):
        cols = slice((q % 2) * half, (q % 2 + 1) * half)
        return jnp.concatenate([part[q // 2, :, cols] for part in (gate, upper, down_t)], axis=-1)

    return [
        jnp.stack([one(HALF_ORDER[z_to][j]) for z_to in range(Z_SIZE)]) for j in range(5)
    ]


def finish_kernel(*refs):
    gate_up, down = refs[-2:]
    rows = gate_up.shape[1]
    places = [(ref, i) for ref in refs[:4] for i in range(ref.shape[1] // rows)]
    half = FF // 2
    full = jnp.float32
    for z_from in range(Z_SIZE):
        for j in range(5):
            expert, side = divmod(HALF_ORDER[z_from][j], 2)
            part, i = places[j]
            at = slice(i * rows, (i + 1) * rows)
            cols = slice(side * half, (side + 1) * half)
            gate_up[expert, :, cols] = part[z_from, at, :half].astype(full)
            cols_up = slice(FF + side * half, FF + (side + 1) * half)
            gate_up[expert, :, cols_up] = part[z_from, at, half : 2 * half].astype(full)
            down[expert, :, cols] = part[z_from, at, 2 * half :].astype(full)


def finish_grads(backs, after):
    rows = backs[0].shape[1]
    experts = EXPERTS // (X_SIZE * C_SIZE)
    vmem = pl.BlockSpec(memory_space=pltpu.VMEM)
    return pl.pallas_call(
        finish_kernel,
        in_specs=[vmem] * len(backs) + [pl.BlockSpec(memory_space=pl.ANY)] * len(after),
        out_specs=[vmem, vmem],
        out_shape=[
            jax.ShapeDtypeStruct((experts, rows, 2 * FF), jnp.float32),
            jax.ShapeDtypeStruct((experts, rows, FF), jnp.float32),
        ],
        compiler_params=pltpu.CompilerParams(vmem_limit_bytes=40 * 1024 * 1024),
        cost_estimate=pl.CostEstimate(
            flops=0, bytes_accessed=experts * rows * FF * 18, transcendentals=0
        ),
        name="finish_grads",
    )(*backs, *after)


class DenseScatter:
    def __init__(self, mine, theirs, place):
        shape = (Y_SIZE, X_SIZE, *mine.shape[1:])
        self.mine, self.theirs, self.place = mine.reshape(shape), theirs.reshape(shape), place

    def block(self, other_y, other_x):
        y = 1 - self.place[1] if other_y else self.place[1]
        x = 1 - self.place[2] if other_x else self.place[2]
        size = (1, 1, *self.mine.shape[2:])
        got = [
            lax.dynamic_slice(a, (y, x, 0, 0, 0), size).reshape(size[2:])
            for a in (self.mine, self.got)
        ]
        return plus(*got)

    def cores(self):
        self.got = move(self.theirs, PAIRS_C)
        return [self.got]

    def first(self):
        low = jnp.bfloat16
        zs = Z_SIZE // 2
        self.near, self.to_x, self.to_y, far = [
            self.block(*at) for at in ((False, False), (False, True), (True, False), (True, True))
        ]
        gate = lambda value: value
        self.via_x = move(gate(far[:zs].astype(low)), PAIRS_X)
        self.via_y = move(gate(far[zs:].astype(low)), PAIRS_Y)
        self.x_a = move(gate(self.to_x[:zs].astype(low)), PAIRS_X)
        self.y_b = move(gate(self.to_y[zs:].astype(low)), PAIRS_Y)
        return [self.via_x, self.via_y, self.x_a, self.y_b]

    def second(self):
        low = jnp.bfloat16
        zs = Z_SIZE // 2
        gate = lambda value: value
        self.x_b = move(gate(plus(self.to_x[zs:], self.via_y).astype(low)), PAIRS_X)
        self.y_a = move(gate(plus(self.to_y[:zs], self.via_x).astype(low)), PAIRS_Y)
        return [self.x_b, self.y_a]

    def sum_up(self):
        zs = Z_SIZE // 2
        return jnp.concatenate(
            [
                plus(self.near[:zs], self.x_a) + self.y_a.astype(jnp.float32),
                plus(self.near[zs:], self.x_b) + self.y_b.astype(jnp.float32),
            ]
        ).astype(jnp.bfloat16)

    def result(self):
        return jnp.sum(self.parts.astype(jnp.float32), axis=0)


def plus(a, b):
    return a.astype(jnp.float32) + b.astype(jnp.float32)


def ring_total(own, first, second, h):
    x_a, y_b = first
    x_b, y_a = second
    return jnp.concatenate(
        [
            plus(own[0][h], x_a[h]) + y_a[h].astype(jnp.float32),
            plus(own[1][h], x_b[h]) + y_b[h].astype(jnp.float32),
        ]
    ).astype(jnp.bfloat16)


def body(
    tokens,
    cotangent,
    lengths,
    routes,
    slots,
    first_gain,
    qkv_weight,
    out_weight,
    second_gain,
    router_weight,
    gate_up_weight,
    down_weight,
):
    low = jnp.bfloat16
    full = jnp.float32
    dp_index = lax.axis_index("dp")
    expert_index = lax.axis_index("expert")
    z, y = dp_index // Y_SIZE, dp_index % Y_SIZE
    x, c = expert_index // C_SIZE, expert_index % C_SIZE
    sequence_length = tokens.shape[0]
    width = tokens.shape[1]
    rows = gate_up_weight.shape[1]

    chosen_by = routes[None, :, :] == jnp.arange(EXPERTS, dtype=jnp.int32)[:, None, None]
    slot_table = jnp.sum(jnp.where(chosen_by, slots[None, :, :] + 1, 0), axis=-1) - 1
    place = (z, y, x, c)
    zs = Z_SIZE // 2
    steps = range(1, Z_SIZE)
    rounds = Rounds()
    gate = rounds.gate

    small = jnp.concatenate(
        [router_weight, first_gain[:, None], second_gain[:, None]], axis=1
    )
    small = jnp.pad(small, ((0, 0), (0, 128 - small.shape[1])))
    shard = jnp.concatenate([qkv_weight, small, out_weight.T], axis=1)
    table = slot_table.astype(low)

    block = spread(shard)
    tables = spread(table)
    cuts = weight_chunks(gate_up_weight, down_weight)
    rounds.close(block, tables)

    near, far, moved = [None] * 5, [None] * 5, [None] * 5

    def send_half(q):
        moved[q] = trade(gate(cuts[q]))
        return [moved[q]]

    def send_near(q):
        near[q] = (move(moved[q], PAIRS_X), move(moved[q], PAIRS_Y))
        return near[q]

    def send_far(q):
        far[q] = move(near[q][1], PAIRS_X) if q % 2 == 0 else move(near[q][0], PAIRS_Y)
        return [far[q]]

    cosine_table, sine_table = rope_tables(sequence_length)
    cosine_table = jnp.tile(cosine_table, (1, QUERY_LANES // HEAD_SIZE))
    sine_table = jnp.tile(sine_table, (1, QUERY_LANES // HEAD_SIZE))
    from_x, from_y = move(block, PAIRS_X), move(block, PAIRS_Y)
    block_c = move(block, PAIRS_C)
    tables_c = move(tables, PAIRS_C)
    rounds.close(from_x, from_y, block_c, tables_c, cosine_table, sine_table, *send_half(0))
    far_a, far_b = move(from_y[:zs], PAIRS_X), move(from_x[zs:], PAIRS_Y)
    from_x_c, from_y_c = move(from_x, PAIRS_C), move(from_y, PAIRS_C)
    rounds.close(far_a, far_b, from_x_c, from_y_c, *send_half(1))
    far_a_c, far_b_c = move(far_a, PAIRS_C), move(far_b, PAIRS_C)
    moved[0] = gate(moved[0])
    send_half(2)
    pack = dense_assemble(
        place,
        (block, from_x, from_y, far_a, far_b),
        (block_c, from_x_c, from_y_c, far_a_c, far_b_c),
    )
    rounds.close(pack, moved[2], *send_near(0))
    out_at = qkv_weight.shape[1] + small.shape[1]
    out_t = pack[:, out_at:]
    small_full = pack[:, qkv_weight.shape[1] : out_at]
    router_full = small_full[:, :EXPERTS]
    gain_one = small_full[:, EXPERTS].astype(full)
    gain_two = small_full[:, EXPERTS + 1].astype(full)

    inputs = tokens.astype(full)
    inverse_one = rms_inverse(inputs)
    normal_one = inputs * inverse_one
    hidden_one, query_rows, keys, value_rows, mixed, log_totals = attention_forward(
        lengths, tokens, gain_one[None, :], pack, cosine_table, sine_table, rounds.after()
    )
    moved[1] = gate(moved[1])
    rounds.close(*send_half(3), *send_near(1), mixed)
    moved[2] = gate(moved[2])
    send_half(4)
    branch = multiply_transposed(mixed, out_t)
    middle = inputs + residual_scale * branch
    inverse_two = rms_inverse(middle)
    normal_two = middle * inverse_two
    hidden_two = (normal_two * gain_two).astype(low)
    grad_out = cotangent.astype(full)

    rounds.close(moved[4], *send_near(2))
    rows_own = spread(gate(hidden_two))
    moved[3] = gate(moved[3])
    rounds.close(*send_near(3))
    moved[4] = gate(moved[4])
    rounds.close(*send_near(4))
    for first, second in ((0, 1), (2, 3)):
        near[first] = (near[first][0], gate(near[first][1]))
        near[second] = (gate(near[second][0]), near[second][1])
        rounds.close(*send_far(first), *send_far(second))
    rounds.close(rows_own)
    rows_own = gate(rows_own)
    rows_other = move(rows_own, PAIRS_C)
    rounds.close(rows_other)
    rows_in = join_rows([rows_other], [rows_own])
    slots_in = jnp.concatenate([tables_c, tables], axis=0).astype(jnp.int32)
    logits_in = jnp.einsum("de,itd->iet", router_full, rows_in, preferred_element_type=full)
    chosen_in = slots_in >= 0
    peak_in = jnp.max(jnp.where(chosen_in, logits_in, -jnp.inf), axis=1, keepdims=True)
    exponent_in = jnp.where(chosen_in, jnp.exp(logits_in - peak_in), 0.0)
    gates_in = exponent_in / jnp.sum(exponent_in, axis=1, keepdims=True)

    units = range(len(UNIT_HALVES))
    even = z % 2 == 0
    ids = []
    for group in (1 - x, x):
        base = EXPERTS // (X_SIZE * C_SIZE) * (group * C_SIZE + c) + 5 * (z // 2)
        ids += [base + jnp.where(even, 0, 3), base + jnp.where(even, 1, 4), base + 2]
    unit_slots = [lax.dynamic_index_in_dim(slots_in, expert, 1, keepdims=True) for expert in ids]
    unit_gates = [lax.dynamic_index_in_dim(gates_in, expert, 1, keepdims=True) for expert in ids]
    pairs = len(UNIT_HALVES)
    sizes = [end - first for first, end in UNIT_HALVES]
    all_slots = jnp.concatenate(unit_slots, axis=1)
    infos = [jnp.stack([y, expert]).astype(jnp.int32) for expert in ids]
    buffer = None
    saved = {}

    def ring(pair, own):
        halves = range(*UNIT_HALVES[pair])
        if own:
            return [p for q in halves for p in (moved[q], near[q][1])]
        return [p for q in halves for p in (near[q][0], far[q])]

    def run_forward(pair, own):
        nonlocal buffer
        at = pair + (pairs if own else 0)
        buffer, *saved[at] = expert_forward(
            at,
            sizes[pair],
            infos[at],
            unit_slots[at],
            unit_gates[at],
            rows_in,
            ring(pair, own),
            buffer,
            rounds.after(),
        )

    dy_own = spread(gate(cotangent))
    late = [(4,), (), ()]
    for pair in range(pairs):
        sent = []
        for q in late[pair]:
            near[q] = tuple(gate(part) for part in near[q])
            sent += send_far(q)
        run_forward(pair, False)
        run_forward(pair, True)
        rounds.close(saved[pair + pairs][0], *sent, *([dy_own] if pair == 2 else []))
    dy_own = gate(dy_own)
    dy_other = move(dy_own, PAIRS_C)
    mix_other = combine(all_slots, buffer, 0, rounds.after())
    rounds.close(mix_other, dy_other)
    mix_moved = move(mix_other, PAIRS_C)
    mix_own = combine(all_slots, buffer, Z_SIZE, rounds.after())
    grads_in = join_rows([dy_other], [dy_own])
    rounds.close(mix_moved, mix_own, grads_in)

    back = None
    grads = [[None, None] for _ in units]

    def run_back(pair, own):
        nonlocal back
        at = pair + (pairs if own else 0)
        back, grads[pair][1 if own else 0] = expert_backward(
            at,
            sizes[pair],
            infos[at],
            unit_slots[at],
            unit_gates[at],
            grads_in,
            *saved[at],
            ring(pair, own),
            back,
            rounds.after(),
        )

    vias, firsts, seconds = [None] * 3, [None] * 3, [None] * 3

    def send_via(u):
        vias[u] = (move(gate(grads[u][0][2]), PAIRS_X), move(gate(grads[u][0][3]), PAIRS_Y))
        return vias[u]

    def send_first(u):
        firsts[u] = (move(gate(grads[u][0][0]), PAIRS_X), move(gate(grads[u][1][3]), PAIRS_Y))
        return firsts[u]

    def send_second(u):
        via_x, via_y = vias[u]
        seconds[u] = (
            move(gate(plus(grads[u][0][1], via_y).astype(low)), PAIRS_X),
            move(gate(plus(grads[u][1][2], via_x).astype(low)), PAIRS_Y),
        )
        return seconds[u]

    def total_of(u):
        return [ring_total(grads[u][1], firsts[u], seconds[u], h) for h in range(sizes[u])]

    terms = plus(mix_own, mix_moved).astype(low)
    mix_got = trade(gate(terms))
    run_back(0, False)
    rounds.close(grads[0][0][0])
    run_back(0, True)
    rounds.close(grads[0][1][0], *send_via(0))
    run_back(1, False)
    rounds.close(grads[1][0][0], *send_first(0))
    run_back(1, True)
    rounds.close(mix_got, grads[1][1][0], *send_second(0))
    mixture = jnp.sum(mix_got.astype(full), axis=0)
    output = (middle + residual_scale * mixture).astype(low)
    totals = total_of(0)
    backs = []

    def send_back(*parts):
        backs.append(trade(gate(parts[0] if len(parts) == 1 else jnp.concatenate(parts, axis=1))))
        return backs[-1:]

    run_back(2, False)
    rounds.close(grads[2][0][0], *send_via(1), *send_back(totals[0]))
    run_back(2, True)
    rounds.close(grads[2][1][0], *send_first(1), *send_back(totals[1]))
    copy_other = combine(all_slots, back, 0, rounds.after())
    rounds.close(copy_other)
    copy_moved = move(copy_other, PAIRS_C)
    copy_own = combine(all_slots, back, Z_SIZE, rounds.after())
    rounds.close(copy_moved, copy_own, *send_second(1), *send_via(2))
    copy_got = trade(plus(copy_own, copy_moved).astype(low))
    rounds.close(*send_first(2))
    rounds.close(*send_second(2))
    totals += total_of(1) + total_of(2)
    last_total = jnp.concatenate(totals[3:], axis=1)
    rounds.close(copy_got, output, totals[2], last_total)
    copy_got = gate(copy_got)
    chosen = (slot_table >= 0).T
    gates = dense_gates(jnp.dot(hidden_two, router_full, preferred_element_type=full), chosen)
    grad_middle, branch_gradient, out_mine, out_theirs = middle_backward(
        c,
        copy_got,
        jnp.pad(gates, ((0, 0), (0, 128 - EXPERTS))),
        pack,
        qkv_weight.shape[1],
        gain_two[None, :],
        middle,
        hidden_two,
        cotangent,
        mixed,
    )
    out_scatter = DenseScatter(out_mine, out_theirs, place)
    out_scatter.cores()
    qkv_mine, qkv_theirs, grad_hidden_one = attention_backward(
        jnp.concatenate([lengths, c[None]]),
        branch_gradient,
        query_rows,
        keys,
        value_rows,
        log_totals,
        hidden_one,
        pack,
        out_at,
        cosine_table,
        sine_table,
        tokens,
        rounds.after(),
    )
    rounds.close(grad_hidden_one, *send_back(totals[2]), *out_scatter.first())
    qkv_scatter = DenseScatter(qkv_mine, gate(qkv_theirs), place)
    sent = send_back(last_total)
    rounds.close(*qkv_scatter.cores(), *out_scatter.second())
    rounds.close(*qkv_scatter.first())
    rounds.close(*qkv_scatter.second(), *sent)
    both = jnp.concatenate([out_scatter.sum_up(), qkv_scatter.sum_up()], axis=-1)
    parts = trade(both)
    out_scatter.parts = parts[..., : width + 128]
    qkv_scatter.parts = parts[..., width + 128 :]
    gate_up_grads, down_grads = finish_grads(backs, [both])
    down_grads = down_grads.transpose(0, 2, 1)
    _, grad_norm_one = norm_backward(
        grad_hidden_one, normal_one, inverse_one, gain_one
    )
    grad_input = grad_middle + grad_norm_one

    qkv_sum = qkv_scatter.result()
    first_sum = qkv_sum[:, -128]
    qkv_sum = qkv_sum[:, :-128]
    qkv_sum = qkv_sum.reshape(qkv_sum.shape[0], -1, QUERY_LANES + 2 * KEY_LANES)
    qkv_sum = jnp.concatenate(
        [
            part.reshape(qkv_sum.shape[0], -1)
            for part in jnp.split(qkv_sum, (QUERY_LANES, QUERY_LANES + KEY_LANES), axis=2)
        ],
        axis=1,
    )
    out_sum = out_scatter.result()
    small_sum = out_sum[:, width:]
    return (
        output,
        grad_input,
        first_sum,
        qkv_sum,
        out_sum[:, :width].T,
        small_sum[:, EXPERTS],
        small_sum[:, :EXPERTS],
        gate_up_grads,
        down_grads,
    )


def solution(mesh):
    in_specs = (
        P(("dp", "expert"), None),
        P(("dp", "expert"), None),
        P(("dp", "expert")),
        P(("dp", "expert"), None),
        P(("dp", "expert"), None),
        P(("dp", "expert")),
        P(("dp", "expert"), None),
        P(None, ("dp", "expert")),
        P(("dp", "expert")),
        P(("dp", "expert"), None),
        P("expert", "dp", None),
        P("expert", None, "dp"),
    )
    out_specs = (
        P(("dp", "expert"), None),
        P(("dp", "expert"), None),
        P(("dp", "expert")),
        P(("dp", "expert"), None),
        P(None, ("dp", "expert")),
        P(("dp", "expert")),
        P(("dp", "expert"), None),
        P("expert", "dp", None),
        P("expert", None, "dp"),
    )
    fits = mesh.shape["dp"] == Z_SIZE * Y_SIZE and mesh.shape["expert"] == X_SIZE * C_SIZE
    chosen = body if fits else general_body
    return jax.shard_map(chosen, mesh=mesh, in_specs=in_specs, out_specs=out_specs, check_vma=False)
```

```python
import functools

import jax
import jax.numpy as jnp
from jax import lax
from jax.experimental import pallas as pl
from jax.experimental.pallas import tpu as pltpu
from jax.sharding import PartitionSpec as P

QUERY_HEADS = 24
KEY_VALUE_HEADS = 8
HEAD_SIZE = 64
FF = 512
EXPERTS = 40
TOP = 8
CAP = 152


epsilon = 1e-06
residual_scale = 0.22
score_scale = 0.015625
rope_base = 10000.0
masked_score = -1e30


def rope_tables(length):
    half = HEAD_SIZE // 2
    freqs = jnp.power(rope_base, -2.0 * jnp.arange(half, dtype=jnp.float32) / HEAD_SIZE)
    angles = jnp.arange(length, dtype=jnp.float32)[:, None] * freqs[None, :]
    cosine_table = jnp.concatenate([jnp.cos(angles), jnp.cos(angles)], axis=-1)
    sine_table = jnp.concatenate([jnp.sin(angles), jnp.sin(angles)], axis=-1)
    return (cosine_table, sine_table)


def rotate_half(value_rows):
    half = value_rows.shape[-1] // 2
    return jnp.concatenate([-value_rows[..., half:], value_rows[..., :half]], axis=-1)


def rotate_pairs(value_rows, cosine_table, sine_table):
    return value_rows * cosine_table[:, None, :] + rotate_half(value_rows) * sine_table[:, None, :]


def unrotate(grads, cosine_table, sine_table):
    return grads * cosine_table[:, None, :] - rotate_half(grads * sine_table[:, None, :])


def rms_inverse(value_rows):
    return lax.rsqrt(jnp.mean(value_rows * value_rows, axis=-1, keepdims=True) + epsilon)


def norm_backward(grad_normed, normal, inverse, gain):
    gain_term = jnp.sum(grad_normed * normal, axis=0)
    scaled = grad_normed * gain
    grad_input = inverse * (scaled - normal * jnp.mean(scaled * normal, axis=-1, keepdims=True))
    return (gain_term, grad_input)


def contract_rows(left, right):
    return lax.dot_general(
        left, right, (((0,), (0,)), ((), ())), preferred_element_type=jnp.float32
    )


def multiply_transposed(left, right):
    return lax.dot_general(
        left, right, (((1,), (1,)), ((), ())), preferred_element_type=jnp.float32
    )


def fetch_expert(gate_up_shard, down_shard):
    return (
        lax.all_gather(gate_up_shard, "dp", axis=0, tiled=True),
        lax.all_gather(down_shard, "dp", axis=1, tiled=True),
    )


def gate_values(hidden_rows, router_full, route_rows):
    logits = jnp.dot(hidden_rows, router_full, preferred_element_type=jnp.float32)
    chosen_mask = route_rows[:, :, None] == jnp.arange(EXPERTS)[None, None, :]
    chosen = jnp.sum(jnp.where(chosen_mask, logits[:, None, :], 0.0), axis=-1)
    return (chosen_mask, jax.nn.softmax(chosen, axis=-1))


def general_body(
    tokens,
    cotangent,
    lengths,
    routes,
    slots,
    first_gain,
    qkv_weight,
    out_weight,
    second_gain,
    router_weight,
    gate_up_weight,
    down_weight,
):
    sequence_length = tokens.shape[0]
    width = tokens.shape[1]
    query_group = QUERY_HEADS // KEY_VALUE_HEADS
    length = lengths[0]
    gathered = (
        lax.all_gather(first_gain, ("dp", "expert"), axis=0, tiled=True),
        lax.all_gather(qkv_weight, ("dp", "expert"), axis=0, tiled=True),
        lax.all_gather(out_weight, ("dp", "expert"), axis=1, tiled=True),
        lax.all_gather(second_gain, ("dp", "expert"), axis=0, tiled=True),
        lax.all_gather(router_weight, ("dp", "expert"), axis=0, tiled=True),
    )
    gain_one, qkv_full, out_full, gain_two, router_full = gathered
    inputs = tokens.astype(jnp.float32)
    inverse_one = rms_inverse(inputs)
    normal_one = inputs * inverse_one
    hidden_one = (normal_one * gain_one.astype(jnp.float32)).astype(jnp.bfloat16)
    projected_rows = jnp.dot(hidden_one, qkv_full, preferred_element_type=jnp.float32)
    cosine_table, sine_table = rope_tables(sequence_length)
    query_width_total = QUERY_HEADS * HEAD_SIZE
    key_width_total = KEY_VALUE_HEADS * HEAD_SIZE
    query_rows = rotate_pairs(
        projected_rows[:, :query_width_total].reshape(sequence_length, QUERY_HEADS, HEAD_SIZE),
        cosine_table,
        sine_table,
    ).astype(jnp.bfloat16)
    keys = rotate_pairs(
        projected_rows[:, query_width_total : query_width_total + key_width_total].reshape(
            sequence_length, KEY_VALUE_HEADS, HEAD_SIZE
        ),
        cosine_table,
        sine_table,
    ).astype(jnp.bfloat16)
    value_rows = (
        projected_rows[:, query_width_total + key_width_total :]
        .reshape(sequence_length, KEY_VALUE_HEADS, HEAD_SIZE)
        .astype(jnp.bfloat16)
    )
    row_index = jnp.arange(sequence_length)[:, None]
    column_index = jnp.arange(sequence_length)[None, :]
    allowed = (column_index <= row_index) & (column_index < length)

    def head_scores(head):
        head_query = lax.dynamic_slice_in_dim(query_rows, head * query_group, query_group, 1)
        head_key = lax.dynamic_index_in_dim(keys, head, 1, keepdims=False)
        head_value = lax.dynamic_index_in_dim(value_rows, head, 1, keepdims=False)
        scores = (
            jnp.einsum("qgd,kd->gqk", head_query, head_key, preferred_element_type=jnp.float32)
            * score_scale
        )
        return (head_query, head_key, head_value, jnp.where(allowed[None], scores, masked_score))

    def attention_head_forward(head):
        head_query, head_key, head_value, scores = head_scores(head)
        peak = jnp.max(scores, axis=-1, keepdims=True)
        exponent = jnp.exp(scores - peak)
        total = jnp.sum(exponent, axis=-1, keepdims=True)
        weights = (exponent / total).astype(jnp.bfloat16)
        head_mixed = jnp.einsum(
            "gqk,kd->qgd", weights, head_value, preferred_element_type=jnp.float32
        ).astype(jnp.bfloat16)
        return (head_mixed, (peak + jnp.log(total))[..., 0])

    mixed_head_output, log_sum_totals = lax.map(attention_head_forward, jnp.arange(KEY_VALUE_HEADS))
    mixed = mixed_head_output.transpose(1, 0, 2, 3).reshape(
        sequence_length, QUERY_HEADS * HEAD_SIZE
    )
    branch = jnp.dot(mixed, out_full, preferred_element_type=jnp.float32)
    middle = inputs + residual_scale * branch
    inverse_two = rms_inverse(middle)
    normal_two = middle * inverse_two
    hidden_two = (normal_two * gain_two.astype(jnp.float32)).astype(jnp.bfloat16)
    chosen_mask, gates = gate_values(hidden_two, router_full, routes)
    grad_out = cotangent.astype(jnp.float32)
    grad_mixture = residual_scale * grad_out

    def expert_forward(carry, pieces):
        rows, gate_up_shard, down_shard = pieces
        gate_up_full, down_full = fetch_expert(gate_up_shard, down_shard)
        gate_up = jnp.dot(rows, gate_up_full, preferred_element_type=jnp.float32)
        hidden = (jax.nn.silu(gate_up[:, :FF]) * gate_up[:, FF:]).astype(jnp.bfloat16)
        return (
            carry,
            jnp.dot(hidden, down_full, preferred_element_type=jnp.float32).astype(jnp.bfloat16),
        )

    copies = jnp.broadcast_to(hidden_two[:, None, :], (sequence_length, TOP, width))
    outgoing = jnp.zeros((EXPERTS, CAP, width), jnp.bfloat16).at[routes, slots].set(copies)
    received = lax.all_to_all(outgoing, "expert", split_axis=0, concat_axis=1, tiled=True)
    _, produced = lax.scan(expert_forward, None, (received, gate_up_weight, down_weight))
    returned = lax.all_to_all(produced, "expert", split_axis=1, concat_axis=0, tiled=True)
    expert_rows = returned[routes, slots].astype(jnp.float32)
    mixture = jnp.sum(gates[:, :, None] * expert_rows, axis=1)
    grad_gates = jnp.sum(expert_rows * grad_mixture[:, None, :], axis=-1)
    grad_rows = (gates[:, :, None] * grad_mixture[:, None, :]).astype(jnp.bfloat16)
    outgoing_grad = jnp.zeros((EXPERTS, CAP, width), jnp.bfloat16).at[routes, slots].set(grad_rows)
    grad_received = lax.all_to_all(outgoing_grad, "expert", split_axis=0, concat_axis=1, tiled=True)
    output = (middle + residual_scale * mixture).astype(jnp.bfloat16)
    again = (
        lax.all_gather(first_gain, ("dp", "expert"), axis=0, tiled=True),
        lax.all_gather(qkv_weight, ("dp", "expert"), axis=0, tiled=True),
        lax.all_gather(out_weight, ("dp", "expert"), axis=1, tiled=True),
        lax.all_gather(second_gain, ("dp", "expert"), axis=0, tiled=True),
        lax.all_gather(router_weight, ("dp", "expert"), axis=0, tiled=True),
    )
    gain_back, qkv_back, output_gradient, gain_two_back, router_back = again
    grad_chosen = gates * (grad_gates - jnp.sum(gates * grad_gates, axis=-1, keepdims=True))
    grad_logits = jnp.sum(jnp.where(chosen_mask, grad_chosen[:, :, None], 0.0), axis=1).astype(
        jnp.bfloat16
    )

    def expert_backward(carry, pieces):
        rows, grad_produced, gate_up_shard, down_shard = pieces
        gate_up_full, down_full = fetch_expert(gate_up_shard, down_shard)
        gate_up = jnp.dot(rows, gate_up_full, preferred_element_type=jnp.float32)
        gate = gate_up[:, :FF]
        upper = gate_up[:, FF:]
        sigmoid = jax.nn.sigmoid(gate)
        swish = gate * sigmoid
        hidden = (swish * upper).astype(jnp.bfloat16)
        grad_hidden = multiply_transposed(grad_produced, down_full)
        grad_gate_up = jnp.concatenate(
            [grad_hidden * upper * sigmoid * (1.0 + gate * (1.0 - sigmoid)), grad_hidden * swish],
            axis=-1,
        ).astype(jnp.bfloat16)
        grad_copy = multiply_transposed(grad_gate_up, gate_up_full).astype(jnp.bfloat16)
        gate_up_part = lax.psum_scatter(
            contract_rows(rows, grad_gate_up).astype(jnp.bfloat16),
            "dp",
            scatter_dimension=0,
            tiled=True,
        ).astype(jnp.float32)
        down_part = lax.psum_scatter(
            contract_rows(grad_produced, hidden).astype(jnp.bfloat16),
            "dp",
            scatter_dimension=0,
            tiled=True,
        ).astype(jnp.float32)
        return (carry, (grad_copy, gate_up_part, down_part.T))

    _, (grad_copies, gate_up_grads, down_grads) = lax.scan(
        expert_backward, None, (received, grad_received, gate_up_weight, down_weight)
    )
    grad_back = lax.all_to_all(grad_copies, "expert", split_axis=1, concat_axis=0, tiled=True)
    copy_sum = jnp.sum(grad_back[routes, slots].astype(jnp.float32), axis=1)
    grad_hidden_two = copy_sum + multiply_transposed(grad_logits, router_back)
    router_term = contract_rows(hidden_two, grad_logits)
    second_term, grad_norm_two = norm_backward(
        grad_hidden_two, normal_two, inverse_two, gain_two_back.astype(jnp.float32)
    )
    grad_middle = grad_out + grad_norm_two
    branch_gradient = (residual_scale * grad_middle).astype(jnp.bfloat16)
    out_term = contract_rows(mixed, branch_gradient)
    grad_mixed = (
        multiply_transposed(branch_gradient, output_gradient)
        .astype(jnp.bfloat16)
        .reshape(sequence_length, KEY_VALUE_HEADS, query_group, HEAD_SIZE)
    )

    def attention_head_backward(head):
        head_query, head_key, head_value, scores = head_scores(head)
        head_grad = lax.dynamic_index_in_dim(grad_mixed, head, 1, keepdims=False)
        head_total = lax.dynamic_index_in_dim(log_sum_totals, head, 0, keepdims=False)
        probs = jnp.exp(scores - head_total[..., None])
        grad_weights = jnp.einsum(
            "qgd,kd->gqk", head_grad, head_value, preferred_element_type=jnp.float32
        )
        grad_scores = (
            probs * (grad_weights - jnp.sum(probs * grad_weights, axis=-1, keepdims=True))
        ).astype(jnp.bfloat16)
        grad_query = (
            jnp.einsum("gqk,kd->qgd", grad_scores, head_key, preferred_element_type=jnp.float32)
            * score_scale
        )
        grad_key = (
            jnp.einsum("gqk,qgd->kd", grad_scores, head_query, preferred_element_type=jnp.float32)
            * score_scale
        )
        grad_value = jnp.einsum(
            "gqk,qgd->kd", probs.astype(jnp.bfloat16), head_grad, preferred_element_type=jnp.float32
        )
        return (grad_query, grad_key, grad_value)

    query_head_rows, key_head_rows, value_head_rows = lax.map(
        attention_head_backward, jnp.arange(KEY_VALUE_HEADS)
    )
    grad_query = unrotate(
        query_head_rows.transpose(1, 0, 2, 3).reshape(sequence_length, QUERY_HEADS, HEAD_SIZE),
        cosine_table,
        sine_table,
    )
    grad_key = unrotate(key_head_rows.transpose(1, 0, 2), cosine_table, sine_table)
    grad_value = value_head_rows.transpose(1, 0, 2)
    grad_projected = jnp.concatenate(
        [
            grad_query.reshape(sequence_length, query_width_total),
            grad_key.reshape(sequence_length, key_width_total),
            grad_value.reshape(sequence_length, key_width_total),
        ],
        axis=-1,
    ).astype(jnp.bfloat16)
    qkv_term = contract_rows(hidden_one, grad_projected)
    grad_hidden_one = multiply_transposed(grad_projected, qkv_back)
    first_term, grad_norm_one = norm_backward(
        grad_hidden_one, normal_one, inverse_one, gain_back.astype(jnp.float32)
    )
    grad_input = grad_middle + grad_norm_one
    summed = (
        lax.psum_scatter(first_term, ("dp", "expert"), scatter_dimension=0, tiled=True),
        lax.psum_scatter(qkv_term, ("dp", "expert"), scatter_dimension=0, tiled=True),
        lax.psum_scatter(out_term, ("dp", "expert"), scatter_dimension=1, tiled=True),
        lax.psum_scatter(second_term, ("dp", "expert"), scatter_dimension=0, tiled=True),
        lax.psum_scatter(router_term, ("dp", "expert"), scatter_dimension=0, tiled=True),
    )
    return (
        output,
        grad_input,
        summed[0],
        summed[1],
        summed[2],
        summed[3],
        summed[4],
        gate_up_grads,
        down_grads,
    )


WIDE = 160
Z_SIZE, Y_SIZE, X_SIZE, C_SIZE = 4, 2, 2, 2
MESH_AXES = ("dp", "expert")


def device_index(z, y, x, c):
    return ((z * Y_SIZE + y) * X_SIZE + x) * C_SIZE + c


def device_pairs(target):
    pairs = []
    for z in range(Z_SIZE):
        for y in range(Y_SIZE):
            for x in range(X_SIZE):
                for c in range(C_SIZE):
                    to = target(z, y, x, c)
                    if to is not None:
                        pairs.append((device_index(z, y, x, c), device_index(*to)))
    return pairs


PAIRS_X = device_pairs(lambda z, y, x, c: (z, y, 1 - x, c))
PAIRS_Y = device_pairs(lambda z, y, x, c: (z, 1 - y, x, c))
PAIRS_C = device_pairs(lambda z, y, x, c: (z, y, x, 1 - c))


Z_GROUPS = [[z * Y_SIZE + y for z in range(Z_SIZE)] for y in range(Y_SIZE)]


def tie_kernel(*refs):
    del refs


def tie(value, *after):
    any_spec = pl.BlockSpec(memory_space=pl.ANY)
    return pl.pallas_call(
        tie_kernel,
        in_specs=[any_spec] * (1 + len(after)),
        out_specs=any_spec,
        out_shape=jax.ShapeDtypeStruct(value.shape, value.dtype),
        input_output_aliases={0: 0},
        name="tie",
    )(value, *after)


def trade(value):
    return lax.all_to_all(
        value, "dp", split_axis=0, concat_axis=0, axis_index_groups=Z_GROUPS, tiled=True
    )


def spread(value):
    return trade(jnp.broadcast_to(value[None], (Z_SIZE, *value.shape)))


def join_kernel(*refs):
    refs[-1][...] = jnp.zeros_like(refs[-1])


class Rounds:
    def __init__(self):
        self.token = None

    def gate(self, value):
        return value if self.token is None else tie(value, self.token)

    def after(self):
        return () if self.token is None else (self.token,)

    def close(self, *arrays):
        arrays = list(arrays) + list(self.after())
        self.token = pl.pallas_call(
            join_kernel,
            in_specs=[pl.BlockSpec(memory_space=pl.ANY)] * len(arrays),
            out_specs=pl.BlockSpec(memory_space=pltpu.VMEM),
            out_shape=jax.ShapeDtypeStruct((8, 128), jnp.float32),
            name="join",
        )(*arrays)


def move(value, pairs):
    return lax.ppermute(value, MESH_AXES, pairs)


def assemble(plan, info, arrays, shape, name):
    any_spec = pl.BlockSpec(memory_space=pl.ANY)

    def kernel(info_ref, *refs):
        *parts, out, sem = refs
        copies = [
            pltpu.make_async_copy(source, target, sem.at[i])
            for i, (source, target) in enumerate(plan(info_ref, parts, out))
        ]
        for copy in copies:
            copy.start()
        for copy in copies:
            copy.wait()

    dtype = arrays[0].dtype
    size = 1
    for extent in shape:
        size *= extent
    return pl.pallas_call(
        kernel,
        grid_spec=pltpu.PrefetchScalarGridSpec(
            num_scalar_prefetch=1,
            grid=(),
            in_specs=[any_spec] * len(arrays),
            out_specs=pl.BlockSpec(memory_space=pltpu.VMEM),
            scratch_shapes=[pltpu.SemaphoreType.DMA((2 * len(arrays),))],
        ),
        out_shape=jax.ShapeDtypeStruct(shape, dtype),
        compiler_params=pltpu.CompilerParams(vmem_limit_bytes=32 * 1024 * 1024),
        cost_estimate=pl.CostEstimate(flops=0, bytes_accessed=4 * size, transcendentals=0),
        name=name,
    )(info, *arrays)


def dense_assemble(place, mine, other):
    z, y, x, c = place
    rows, n = mine[0].shape[1:]
    zs = Z_SIZE // 2

    def plan(info, parts, out):
        at_y, at_x = info[0], info[1]
        copies = []
        for k in range(2):
            at_c = info[2] if k == 0 else 1 - info[2]
            block, from_x, from_y, far_a, far_b = parts[5 * k : 5 * k + 5]
            copies += [
                (block, out.at[:, at_y, at_x, at_c]),
                (from_x, out.at[:, at_y, 1 - at_x, at_c]),
                (from_y, out.at[:, 1 - at_y, at_x, at_c]),
                (far_a, out.at[pl.ds(0, zs), 1 - at_y, 1 - at_x, at_c]),
                (far_b, out.at[pl.ds(zs, zs), 1 - at_y, 1 - at_x, at_c]),
            ]
        return copies

    shape = (Z_SIZE, Y_SIZE, X_SIZE, C_SIZE, rows, n)
    full = assemble(plan, jnp.stack([y, x, c]), (*mine, *other), shape, "dense_assemble")
    return full.reshape(-1, n)


def join_rows(other, own):
    counts = [part.shape[1] for part in own]

    def plan(info, parts, out):
        copies = []
        for k in range(2):
            at = 0
            for i, count in enumerate(counts):
                target = out.at[pl.ds(k * Z_SIZE, Z_SIZE), pl.ds(at, count)]
                copies.append((parts[k * len(counts) + i], target))
                at += count
        return copies

    shape = (2 * Z_SIZE, sum(counts), own[0].shape[2])
    return assemble(plan, jnp.zeros((1,), jnp.int32), (*other, *own), shape, "join_rows")


def half_order(z_to):
    first = 10 * (z_to // 2)
    if z_to % 2 == 0:
        return [first, first + 1, first + 2, first + 3, first + 4]
    return [first + 6, first + 7, first + 8, first + 9, first + 5]


HALF_ORDER = [half_order(z_to) for z_to in range(Z_SIZE)]
HALF_PLACE = [0] * (Z_SIZE * 5)
for order_z in range(Z_SIZE):
    for order_q in range(5):
        HALF_PLACE[HALF_ORDER[order_z][order_q]] = order_z * 5 + order_q
UNIT_HALVES = ((0, 2), (2, 4), (4, 5))


def dense_gates(logits, chosen):
    peak = jnp.max(jnp.where(chosen, logits, -jnp.inf), axis=-1, keepdims=True)
    exponent = jnp.where(chosen, jnp.exp(logits - peak), 0.0)
    return exponent / jnp.sum(exponent, axis=-1, keepdims=True)


def mm(left, right):
    return jnp.dot(left, right, preferred_element_type=jnp.float32)


def weight_loads(pieces, w_s, sem, y):
    copies = []
    for h in range(w_s.shape[0]):
        for piece, at_y in zip(pieces[2 * h : 2 * h + 2], (y, 1 - y)):
            copies.append(
                pltpu.make_async_copy(piece, w_s.at[h, :, at_y], sem.at[len(copies)])
            )
    return copies


def expert_forward_kernel(info, slots, gates, rows, *rest, count, waits):
    pieces = rest[:count]
    out, kept, gate_up_out, w_s, in_sem = rest[count + waits :]
    low = jnp.bfloat16
    step = pl.program_id(0)
    half = FF // 2
    halves = w_s.shape[0]
    loads = weight_loads(pieces, w_s, in_sem, info[0])

    @pl.when(step == 0)
    def _():
        for load in loads:
            load.start()

    group, length, width = rows.shape
    span = group * WIDE
    iota = lax.broadcasted_iota(jnp.int32, (WIDE, length), 0)
    gate_cols = []
    for j in range(group):
        pick = iota == slots[j]
        one_hot = jnp.where(pick, 1.0, 0.0).astype(low)
        gate_cols.append(jnp.sum(jnp.where(pick, gates[j], 0.0), axis=1, keepdims=True))
        kept[j * WIDE : (j + 1) * WIDE, :] = mm(one_hot, rows[j]).astype(low)
    gate_col = jnp.concatenate(gate_cols, axis=0)

    @pl.when(step == 0)
    def _():
        for load in loads:
            load.wait()

    produced = None
    for h in range(halves):
        gate_up_w = w_s[h, :, :, :, : 2 * half].reshape(width, 2 * half)
        down_t = w_s[h, :, :, :, 2 * half :].reshape(width, half)
        gate_up = mm(kept[...], gate_up_w)
        gate_up_out[:, 2 * h * half : 2 * (h + 1) * half] = gate_up
        gate = gate_up[:, :half]
        hidden = (gate * (1.0 / (1.0 + jnp.exp(-gate))) * gate_up[:, half:]).astype(low)
        term = multiply_transposed(hidden, down_t)
        produced = term if produced is None else produced + term
    out[...] = (produced * gate_col).astype(low).reshape(group, WIDE, width)


def expert_forward(place, halves, y, slots, gates, rows_in, pieces, buffer, after):
    sources, length, width = rows_in.shape
    _, rows, lanes = pieces[0].shape
    half = FF // 2
    low = jnp.bfloat16
    group = 2
    units = 2 * len(UNIT_HALVES)
    any_spec = pl.BlockSpec(memory_space=pl.ANY)
    row_spec = pl.BlockSpec((group, 1, length), lambda i, info: (i, 0, 0))
    waits = list(after)
    aliases = {}
    if buffer is not None:
        aliases = {4 + len(pieces): 0}
        waits = [buffer] + waits
    total = sources * WIDE
    span = group * WIDE
    return pl.pallas_call(
        functools.partial(expert_forward_kernel, count=len(pieces), waits=len(waits)),
        grid_spec=pltpu.PrefetchScalarGridSpec(
            num_scalar_prefetch=1,
            grid=(sources // group,),
            in_specs=[
                row_spec,
                row_spec,
                pl.BlockSpec((group, length, width), lambda i, info: (i, 0, 0)),
            ]
            + [any_spec] * (len(pieces) + len(waits)),
            out_specs=[
                pl.BlockSpec((group, WIDE, width), lambda i, info: (i, place, 0)),
                pl.BlockSpec((span, width), lambda i, info: (i, 0)),
                pl.BlockSpec((span, 2 * half * halves), lambda i, info: (i, 0)),
            ],
            scratch_shapes=[
                pltpu.VMEM((halves, Z_SIZE, Y_SIZE, rows, lanes), low),
                pltpu.SemaphoreType.DMA((4,)),
            ],
        ),
        out_shape=[
            jax.ShapeDtypeStruct((sources, units * WIDE, width), low),
            jax.ShapeDtypeStruct((total, width), low),
            jax.ShapeDtypeStruct((total, 2 * half * halves), jnp.float32),
        ],
        input_output_aliases=aliases,
        compiler_params=pltpu.CompilerParams(vmem_limit_bytes=60 * 1024 * 1024),
        cost_estimate=pl.CostEstimate(
            flops=2 * total * width * (3 * half * halves + length),
            bytes_accessed=2 * (sources * length * width + 2 * total * width)
            + 8 * total * half * halves
            + 2 * halves * width * lanes,
            transcendentals=total * half * halves,
        ),
        name="expert_forward",
    )(y, slots, gates, rows_in, *pieces, *waits)


def expert_back_kernel(info, slots, gates, dys, kept, gate_ups, *rest, count, waits):
    pieces = rest[:count]
    back, near_a_g, near_b_g, far_a_g, far_b_g = rest[count + waits : count + waits + 5]
    w_s, x_s, gd_s, dgu_s, hid_s, g_s, in_sem, out_sem = rest[count + waits + 5 :]
    low = jnp.bfloat16
    full = jnp.float32
    step = pl.program_id(0)
    y = info[0]
    expert = info[1]
    half = FF // 2
    zs = Z_SIZE // 2
    halves = w_s.shape[0]
    loads = weight_loads(pieces, w_s, in_sem, y)

    @pl.when(step == 0)
    def _():
        for load in loads:
            load.start()

    group, length, width = dys.shape
    span = group * WIDE
    here = pl.ds(pl.multiple_of(step * span, span), span)
    iota = lax.broadcasted_iota(jnp.int32, (WIDE, length), 0)
    gate_cols = []
    dy_parts = []
    for j in range(group):
        pick = iota == slots[j]
        one_hot = jnp.where(pick, 1.0, 0.0).astype(low)
        gate_col = jnp.sum(jnp.where(pick, gates[j], 0.0), axis=1, keepdims=True)
        at = pl.multiple_of(step * span + j * WIDE, WIDE)
        dy = mm(one_hot, dys[j])
        gd_s[pl.ds(at, WIDE), :] = (dy * (residual_scale * gate_col)).astype(low)
        dy_parts.append(dy.astype(low))
        gate_cols.append(gate_col)
    dy = jnp.concatenate(dy_parts, axis=0)
    gate_col = jnp.concatenate(gate_cols, axis=0)
    x_s[here, :] = kept[...]

    @pl.when(step == 0)
    def _():
        for load in loads:
            load.wait()

    grad_copy = None
    grad_gate = None
    for h in range(halves):
        gate_up_w = w_s[h, :, :, :, : 2 * half].reshape(width, 2 * half)
        down_t = w_s[h, :, :, :, 2 * half :].reshape(width, half)
        gate = gate_ups[:, 2 * h * half : (2 * h + 1) * half]
        upper = gate_ups[:, (2 * h + 1) * half : (2 * h + 2) * half]
        sigmoid = 1.0 / (1.0 + jnp.exp(-gate))
        swish = gate * sigmoid
        hidden = (swish * upper).astype(low)
        hid_s[here, h * half : (h + 1) * half] = hidden
        grad_plain = residual_scale * mm(dy, down_t)
        term = jnp.sum(hidden.astype(full) * grad_plain, axis=1, keepdims=True)
        grad_gate = term if grad_gate is None else grad_gate + term
        grad_hidden = grad_plain * gate_col
        dgu_s[here, 2 * h * half : (2 * h + 1) * half] = (
            grad_hidden * upper * sigmoid * (1.0 + gate * (1.0 - sigmoid))
        ).astype(low)
        dgu_s[here, (2 * h + 1) * half : (2 * h + 2) * half] = (grad_hidden * swish).astype(low)
        term = multiply_transposed(dgu_s[here, 2 * h * half : 2 * (h + 1) * half], gate_up_w)
        grad_copy = term if grad_copy is None else grad_copy + term
    back[:, :, :width] = grad_copy.astype(low).reshape(group, WIDE, width)
    lane = lax.broadcasted_iota(jnp.int32, (span, 128), 1)
    high = grad_gate.astype(low).astype(full)
    extra = jnp.where(lane == expert, high, 0.0) + jnp.where(
        lane == expert + 64, grad_gate - high, 0.0
    )
    back[:, :, width:] = extra.astype(low).reshape(group, WIDE, 128)

    @pl.when(step == pl.num_programs(0) - 1)
    def _():
        piece = width // Z_SIZE
        for h in range(halves):
            for zz in range(Z_SIZE):
                cols = slice(zz * piece, (zz + 1) * piece)
                got = contract_rows(x_s[:, cols], dgu_s[:, 2 * h * half : 2 * (h + 1) * half])
                g_s[h, zz, :, :, : 2 * half] = got.astype(low).reshape(2, piece // 2, 2 * half)
                got = contract_rows(gd_s[:, cols], hid_s[:, h * half : (h + 1) * half])
                g_s[h, zz, :, :, 2 * half :] = got.astype(low).reshape(2, piece // 2, half)
        stores = [
            (g_s.at[:, pl.ds(0, zs), y], near_a_g),
            (g_s.at[:, pl.ds(zs, zs), y], near_b_g),
            (g_s.at[:, pl.ds(0, zs), 1 - y], far_a_g),
            (g_s.at[:, pl.ds(zs, zs), 1 - y], far_b_g),
        ]
        stores = [pltpu.make_async_copy(a, b, out_sem.at[i]) for i, (a, b) in enumerate(stores)]
        for store in stores:
            store.start()
        for store in stores:
            store.wait()


def expert_backward(
    place, halves, info, slots, gates, grads_in, kept, gate_ups, pieces, buffer, after
):
    sources, length, width = grads_in.shape
    _, rows, lanes = pieces[0].shape
    half = FF // 2
    low = jnp.bfloat16
    group = 2
    units = 2 * len(UNIT_HALVES)
    any_spec = pl.BlockSpec(memory_space=pl.ANY)
    row_spec = pl.BlockSpec((group, 1, length), lambda i, info: (i, 0, 0))
    waits = list(after)
    aliases = {}
    if buffer is not None:
        aliases = {6 + len(pieces): 0}
        waits = [buffer] + waits
    total = sources * WIDE
    span = group * WIDE
    quarter = (halves, Z_SIZE // 2, rows, lanes)
    result = pl.pallas_call(
        functools.partial(expert_back_kernel, count=len(pieces), waits=len(waits)),
        grid_spec=pltpu.PrefetchScalarGridSpec(
            num_scalar_prefetch=1,
            grid=(sources // group,),
            in_specs=[
                row_spec,
                row_spec,
                pl.BlockSpec((group, length, width), lambda i, info: (i, 0, 0)),
                pl.BlockSpec((span, width), lambda i, info: (i, 0)),
                pl.BlockSpec((span, 2 * half * halves), lambda i, info: (i, 0)),
            ]
            + [any_spec] * (len(pieces) + len(waits)),
            out_specs=[
                pl.BlockSpec((group, WIDE, width + 128), lambda i, info: (i, place, 0)),
            ]
            + [any_spec] * 4,
            scratch_shapes=[
                pltpu.VMEM((halves, Z_SIZE, Y_SIZE, rows, lanes), low),
                pltpu.VMEM((total, width), low),
                pltpu.VMEM((total, width), low),
                pltpu.VMEM((total, 2 * half * halves), low),
                pltpu.VMEM((total, half * halves), low),
                pltpu.VMEM((halves, Z_SIZE, Y_SIZE, rows, lanes), low),
                pltpu.SemaphoreType.DMA((4,)),
                pltpu.SemaphoreType.DMA((4,)),
            ],
        ),
        out_shape=[jax.ShapeDtypeStruct((sources, units * WIDE, width + 128), low)]
        + [jax.ShapeDtypeStruct(quarter, low)] * 4,
        input_output_aliases=aliases,
        compiler_params=pltpu.CompilerParams(vmem_limit_bytes=60 * 1024 * 1024),
        cost_estimate=pl.CostEstimate(
            flops=2 * total * width * (6 * half * halves + length),
            bytes_accessed=2 * (sources * length * width + 2 * total * width)
            + 8 * total * half * halves
            + 4 * halves * width * lanes,
            transcendentals=total * half * halves,
        ),
        name="expert_backward",
    )(info, slots, gates, grads_in, kept, gate_ups, *pieces, *waits)
    return result[0], result[1:]


def middle_back_kernel(
    c_ref, got, gates, small, gain, middle, hidden, cotangent, mixed, dmiddle, dbranch, mine, theirs,
    g_s, sem,
):
    full = jnp.float32
    low = jnp.bfloat16
    c = c_ref[0]
    length, width = middle.shape
    total = got[0].astype(full)
    for z in range(1, Z_SIZE):
        total = total + got[z].astype(full)
    parts = total[:, width:]
    grad_gates = parts + pltpu.roll(parts, 64, 1)
    gate = gates[...]
    grad_logits = gate * (grad_gates - jnp.sum(gate * grad_gates, axis=1, keepdims=True))
    grad_logits = grad_logits.astype(low)
    dh2 = total[:, :width] + multiply_transposed(grad_logits, small[...])
    value = middle[...]
    inverse = rms_inverse(value)
    normal = value * inverse
    scaled = dh2 * gain[...]
    mean = jnp.mean(scaled * normal, axis=1, keepdims=True)
    grad = cotangent[...].astype(full) + inverse * (scaled - normal * mean)
    dmiddle[...] = grad
    branch = (residual_scale * grad).astype(low)
    dbranch[...] = branch
    per = g_s.shape[3]
    step = width // Z_SIZE
    rows = Y_SIZE * X_SIZE
    for z in range(Z_SIZE):
        part = slice(z * step, (z + 1) * step)
        term = contract_rows(branch[:, part], mixed[...]).astype(low)
        g_s[:, z, :, :, :width] = term.reshape(rows, C_SIZE, per, width)
        router = contract_rows(hidden[:, part], grad_logits)
        product = (dh2[:, part] * normal[:, part]).astype(low)
        second = contract_rows(product, jnp.ones((length, 128), low))
        lane = lax.broadcasted_iota(jnp.int32, router.shape, 1)
        router = jnp.where(lane == EXPERTS, second, router).astype(low)
        g_s[:, z, :, :, width:] = router.reshape(rows, C_SIZE, per, 128)
    copies = [
        pltpu.make_async_copy(g_s.at[:, :, c], mine, sem.at[0]),
        pltpu.make_async_copy(g_s.at[:, :, 1 - c], theirs, sem.at[1]),
    ]
    for copy in copies:
        copy.start()
    for copy in copies:
        copy.wait()


def middle_backward(c, got, gates, pack, small_at, gain, middle, hidden, cotangent, mixed):
    length, width = middle.shape
    low = jnp.bfloat16
    blocks = (Y_SIZE * X_SIZE, Z_SIZE)
    per = width // (Y_SIZE * X_SIZE * Z_SIZE * C_SIZE)
    any_spec = pl.BlockSpec(memory_space=pl.ANY)
    whole = lambda a: pl.BlockSpec(a.shape, lambda i, n: (0,) * a.ndim)
    split = jax.ShapeDtypeStruct((*blocks, per, width + 128), low)
    rows = pl.BlockSpec((length, width), lambda i, n: (0, 0))
    return pl.pallas_call(
        middle_back_kernel,
        grid_spec=pltpu.PrefetchScalarGridSpec(
            num_scalar_prefetch=1,
            grid=(1,),
            in_specs=[
                whole(got),
                whole(gates),
                pl.BlockSpec((width, 128), lambda i, n: (0, small_at // 128)),
                whole(gain),
                rows,
                rows,
                rows,
                rows,
            ],
            out_specs=[rows, rows, any_spec, any_spec],
            scratch_shapes=[
                pltpu.VMEM((*blocks, C_SIZE, per, width + 128), low),
                pltpu.SemaphoreType.DMA((2,)),
            ],
        ),
        out_shape=[
            jax.ShapeDtypeStruct((length, width), jnp.float32),
            jax.ShapeDtypeStruct((length, width), low),
            split,
            split,
        ],
        compiler_params=pltpu.CompilerParams(vmem_limit_bytes=56 * 1024 * 1024),
        cost_estimate=pl.CostEstimate(
            flops=2 * length * width * (width + 384),
            bytes_accessed=length * width * 24 + 4 * width * width,
            transcendentals=0,
        ),
        name="middle_backward",
    )(c[None], got, gates, pack, gain, middle, hidden, cotangent, mixed)


def turn_halves(value):
    lanes = value.shape[-1]
    lane = lax.broadcasted_iota(jnp.int32, value.shape, 1)
    ahead = pltpu.roll(value, lanes - HEAD_SIZE // 2, 1)
    behind = pltpu.roll(value, HEAD_SIZE // 2, 1)
    return jnp.where(lane % HEAD_SIZE < HEAD_SIZE // 2, -ahead, behind)


def heads_of(value, first, count):
    return jnp.concatenate(
        [value[:, (first + i) * HEAD_SIZE : (first + i + 1) * HEAD_SIZE] for i in range(count)],
        axis=0,
    )


ROW_BLOCK = 128
PAIR = 2
GROUP = QUERY_HEADS // KEY_VALUE_HEADS
QUERY_LANES = PAIR * GROUP * HEAD_SIZE
KEY_LANES = PAIR * HEAD_SIZE


def block_mask(block, length):
    shape = (ROW_BLOCK, (block + 1) * ROW_BLOCK)
    row = lax.broadcasted_iota(jnp.int32, shape, 0) + block * ROW_BLOCK
    column = lax.broadcasted_iota(jnp.int32, shape, 1)
    allowed = jnp.where((column <= row) & (column < length), 1, 0)
    return jnp.concatenate([allowed] * GROUP, axis=0) > 0


def attention_kernel(
    length, tokens, gain, wq, wk, wv, cosine, sine, *rest
):
    h1, q, k, v, mixed, lse, h_s, lse_s = rest[-8:]
    step = pl.program_id(0)
    low = jnp.bfloat16
    rows = tokens.shape[0]

    @pl.when(step == 0)
    def _():
        value = tokens[...].astype(jnp.float32)
        hidden = (value * rms_inverse(value) * gain[...]).astype(low)
        h_s[...] = hidden
        h1[...] = hidden

    lane = lax.broadcasted_iota(jnp.int32, (rows, 128), 1)
    cos = cosine[...]
    sin = sine[...]
    query = mm(h_s[...], wq[...])
    query = (query * cos + turn_halves(query) * sin).astype(low)
    key = mm(h_s[...], wk[...])
    key = (key * cos[:, :KEY_LANES] + turn_halves(key) * sin[:, :KEY_LANES]).astype(low)
    value = mm(h_s[...], wv[...]).astype(low)
    q[...] = query
    k[...] = key
    v[...] = value
    blocks = rows // ROW_BLOCK
    totals = [[] for _ in range(PAIR * GROUP)]
    masks = [block_mask(block, length[0]) for block in range(blocks)]
    outs = [[] for _ in range(PAIR * GROUP)]
    for head in range(PAIR):
        key_h = key[:, head * HEAD_SIZE : (head + 1) * HEAD_SIZE]
        value_h = value[:, head * HEAD_SIZE : (head + 1) * HEAD_SIZE]
        for block in range(blocks):
            keys = (block + 1) * ROW_BLOCK
            query_h = heads_of(
                query[block * ROW_BLOCK : (block + 1) * ROW_BLOCK], head * GROUP, GROUP
            )
            scores = multiply_transposed(query_h, key_h[:keys]) * score_scale
            scores = jnp.where(masks[block], scores, masked_score)
            peak = jnp.max(scores, axis=1, keepdims=True)
            exponent = jnp.exp(scores - peak)
            total = jnp.sum(exponent, axis=1, keepdims=True)
            weights = (exponent / total).astype(low)
            out = mm(weights, value_h[:keys]).astype(low)
            log_total = peak + jnp.log(total)
            for i in range(GROUP):
                part = slice(i * ROW_BLOCK, (i + 1) * ROW_BLOCK)
                outs[head * GROUP + i].append(out[part])
                totals[head * GROUP + i].append(log_total[part])
    mixed[...] = jnp.concatenate([jnp.concatenate(o, axis=0) for o in outs], axis=1)

    @pl.when(step == 0)
    def _():
        lse_s[...] = jnp.zeros_like(lse_s)

    kept = lse_s[...]
    for i in range(PAIR * GROUP):
        column = jnp.concatenate(totals[i], axis=0)
        kept = jnp.where(lane == step * PAIR * GROUP + i, column, kept)
    lse_s[...] = kept
    lse[...] = kept


def attention_forward(length, tokens, gain, weight, cosine, sine, after=()):
    rows, width = tokens.shape
    steps = KEY_VALUE_HEADS // PAIR
    low = jnp.bfloat16
    query_total = QUERY_HEADS * HEAD_SIZE
    key_total = KEY_VALUE_HEADS * HEAD_SIZE
    key_at = query_total // KEY_LANES
    value_at = key_at + steps
    whole = lambda shape: pl.BlockSpec(shape, lambda i, n: (0, 0))
    cols = lambda lanes, at: pl.BlockSpec((width, lanes), lambda i, n: (0, at + i))
    part = lambda lanes: pl.BlockSpec((rows, lanes), lambda i, n: (0, i))
    return pl.pallas_call(
        attention_kernel,
        grid_spec=pltpu.PrefetchScalarGridSpec(
            num_scalar_prefetch=1,
            grid=(steps,),
            in_specs=[
                whole((rows, width)),
                whole((1, width)),
                cols(QUERY_LANES, 0),
                cols(KEY_LANES, key_at),
                cols(KEY_LANES, value_at),
                whole((rows, QUERY_LANES)),
                whole((rows, QUERY_LANES)),
            ]
            + [pl.BlockSpec(memory_space=pl.ANY)] * len(after),
            out_specs=[
                whole((rows, width)),
                part(QUERY_LANES),
                part(KEY_LANES),
                part(KEY_LANES),
                part(QUERY_LANES),
                whole((rows, 128)),
            ],
            scratch_shapes=[pltpu.VMEM((rows, width), low), pltpu.VMEM((rows, 128), jnp.float32)],
        ),
        out_shape=[
            jax.ShapeDtypeStruct((rows, width), low),
            jax.ShapeDtypeStruct((rows, query_total), low),
            jax.ShapeDtypeStruct((rows, key_total), low),
            jax.ShapeDtypeStruct((rows, key_total), low),
            jax.ShapeDtypeStruct((rows, query_total), low),
            jax.ShapeDtypeStruct((rows, 128), jnp.float32),
        ],
        compiler_params=pltpu.CompilerParams(vmem_limit_bytes=48 * 1024 * 1024),
        cost_estimate=pl.CostEstimate(
            flops=2 * rows * width * (query_total + 2 * key_total)
            + 4 * QUERY_HEADS * rows * rows * HEAD_SIZE,
            bytes_accessed=2 * width * (query_total + 2 * key_total) + 10 * rows * width,
            transcendentals=QUERY_HEADS * rows * rows,
        ),
        name="attention_forward",
    )(length, tokens, gain, weight, weight, weight, cosine, sine, *after)


def attention_back_kernel(
    length, dbranch, wo, q, k, v, lse, h1, wq, wk, wv, cosine, sine, tokens, *rest
):
    mine, theirs, dh1, dh_s, g_s = rest[-5:]
    c = length[1]
    step = pl.program_id(0)
    low = jnp.bfloat16
    full = jnp.float32
    rows = dbranch.shape[0]
    span = h1.shape[1] // Z_SIZE
    split = (Y_SIZE * X_SIZE, C_SIZE, span // (Y_SIZE * X_SIZE * C_SIZE))

    @pl.when(step < pl.num_programs(0) - 1)
    def _():
        blocks = rows // ROW_BLOCK
        dmixed = mm(dbranch[...], wo[...]).astype(low)
        lane = lax.broadcasted_iota(jnp.int32, (rows, 128), 1)
        kept = lse[...]
        query, key, value = q[...], k[...], v[...]
        columns = [
            jnp.sum(jnp.where(lane == step * PAIR * GROUP + i, kept, 0.0), axis=1, keepdims=True)
            for i in range(PAIR * GROUP)
        ]
        masks = [block_mask(block, length[0]) for block in range(blocks)]
        dq = [[] for _ in range(PAIR * GROUP)]
        dks, dvs = [], []
        for head in range(PAIR):
            key_h = key[:, head * HEAD_SIZE : (head + 1) * HEAD_SIZE]
            value_h = value[:, head * HEAD_SIZE : (head + 1) * HEAD_SIZE]
            dk = [None] * blocks
            dv = [None] * blocks
            for block in range(blocks):
                keys = (block + 1) * ROW_BLOCK
                at = slice(block * ROW_BLOCK, (block + 1) * ROW_BLOCK)
                query_h = heads_of(query[at], head * GROUP, GROUP)
                dmixed_h = heads_of(dmixed[at], head * GROUP, GROUP)
                log_total = jnp.concatenate(
                    [columns[head * GROUP + i][at] for i in range(GROUP)], axis=0
                )
                scores = multiply_transposed(query_h, key_h[:keys]) * score_scale
                scores = jnp.where(masks[block], scores, masked_score)
                probs = jnp.exp(scores - log_total)
                dprobs = multiply_transposed(dmixed_h, value_h[:keys])
                delta = jnp.sum(probs * dprobs, axis=1, keepdims=True)
                dscores = (probs * (dprobs - delta)).astype(low)
                dquery = mm(dscores, key_h[:keys]) * score_scale
                dkey = contract_rows(dscores, query_h) * score_scale
                dvalue = contract_rows(probs.astype(low), dmixed_h)
                for i in range(GROUP):
                    dq[head * GROUP + i].append(dquery[i * ROW_BLOCK : (i + 1) * ROW_BLOCK])
                for b in range(block + 1):
                    part = slice(b * ROW_BLOCK, (b + 1) * ROW_BLOCK)
                    dk[b] = dkey[part] if dk[b] is None else dk[b] + dkey[part]
                    dv[b] = dvalue[part] if dv[b] is None else dv[b] + dvalue[part]
            dks.append(jnp.concatenate(dk, axis=0))
            dvs.append(jnp.concatenate(dv, axis=0))
        cos = cosine[...]
        sin = sine[...]
        dquery = jnp.concatenate([jnp.concatenate(o, axis=0) for o in dq], axis=1)
        dquery = (dquery * cos - turn_halves(dquery * sin)).astype(low)
        dkey = jnp.concatenate(dks, axis=1)
        dkey = (dkey * cos[:, :KEY_LANES] - turn_halves(dkey * sin[:, :KEY_LANES])).astype(low)
        dvalue = jnp.concatenate(dvs, axis=1).astype(low)
        hidden = h1[...]
        got = contract_rows(hidden, dquery).astype(low)
        for z in range(Z_SIZE):
            part = got[z * span : (z + 1) * span]
            g_s[:, z, :, :, :QUERY_LANES] = part.reshape(*split, QUERY_LANES)
        got = contract_rows(hidden, jnp.concatenate([dkey, dvalue], axis=1)).astype(low)
        for z in range(Z_SIZE):
            part = got[z * span : (z + 1) * span]
            g_s[:, z, :, :, QUERY_LANES:] = part.reshape(*split, 2 * KEY_LANES)
        mine[...] = g_s[:, :, c]
        theirs[...] = g_s[:, :, 1 - c]
        term = (
            multiply_transposed(dquery, wq[...])
            + multiply_transposed(dkey, wk[...])
            + multiply_transposed(dvalue, wv[...])
        )

        @pl.when(step == 0)
        def _():
            dh_s[...] = term

        @pl.when(step > 0)
        def _():
            dh_s[...] += term

    @pl.when(step == pl.num_programs(0) - 1)
    def _():
        total = dh_s[...]
        dh1[...] = total
        value = tokens[...].astype(full)
        product = (total * (value * rms_inverse(value))).astype(low)
        column = contract_rows(product, jnp.ones((rows, 128), low)).astype(low)
        for z in range(Z_SIZE):
            part = column[z * span : (z + 1) * span]
            g_s[:, z, :, :, :128] = part.reshape(*split, 128)
        mine[:, :, :, :128] = g_s[:, :, c, :, :128]
        theirs[:, :, :, :128] = g_s[:, :, 1 - c, :, :128]


def attention_backward(
    length, dbranch, q, k, v, lse, h1, weight, out_at, cosine, sine, tokens, after=()
):
    rows, width = dbranch.shape
    steps = KEY_VALUE_HEADS // PAIR
    low = jnp.bfloat16
    full = jnp.float32
    query_total = QUERY_HEADS * HEAD_SIZE
    key_total = KEY_VALUE_HEADS * HEAD_SIZE
    key_at = query_total // KEY_LANES
    value_at = key_at + steps
    whole = lambda shape: pl.BlockSpec(shape, lambda i, n: (0, 0))
    cols = lambda lanes, at: pl.BlockSpec((width, lanes), lambda i, n: (0, at + jnp.minimum(i, steps - 1)))
    part = lambda lanes: pl.BlockSpec((rows, lanes), lambda i, n: (0, jnp.minimum(i, steps - 1)))
    lanes = QUERY_LANES + 2 * KEY_LANES
    blocks = (Y_SIZE * X_SIZE, Z_SIZE)
    per = width // (Y_SIZE * X_SIZE * Z_SIZE * C_SIZE)
    return pl.pallas_call(
        attention_back_kernel,
        grid_spec=pltpu.PrefetchScalarGridSpec(
            num_scalar_prefetch=1,
            grid=(steps + 1,),
            in_specs=[
                whole((rows, width)),
                cols(QUERY_LANES, out_at // QUERY_LANES),
                part(QUERY_LANES),
                part(KEY_LANES),
                part(KEY_LANES),
                whole((rows, 128)),
                whole((rows, width)),
                cols(QUERY_LANES, 0),
                cols(KEY_LANES, key_at),
                cols(KEY_LANES, value_at),
                whole((rows, QUERY_LANES)),
                whole((rows, QUERY_LANES)),
                whole((rows, width)),
            ]
            + [pl.BlockSpec(memory_space=pl.ANY)] * len(after),
            out_specs=[
                pl.BlockSpec((*blocks, per, lanes), lambda i, n: (0, 0, 0, i)),
                pl.BlockSpec((*blocks, per, lanes), lambda i, n: (0, 0, 0, i)),
                whole((rows, width)),
            ],
            scratch_shapes=[
                pltpu.VMEM((rows, width), full),
                pltpu.VMEM((*blocks, C_SIZE, per, lanes), low),
            ],
        ),
        out_shape=[
            jax.ShapeDtypeStruct((*blocks, per, steps * lanes + 128), low),
            jax.ShapeDtypeStruct((*blocks, per, steps * lanes + 128), low),
            jax.ShapeDtypeStruct((rows, width), full),
        ],
        compiler_params=pltpu.CompilerParams(vmem_limit_bytes=48 * 1024 * 1024),
        cost_estimate=pl.CostEstimate(
            flops=4 * rows * width * (query_total + 2 * key_total)
            + 2 * rows * width * query_total
            + 10 * QUERY_HEADS * rows * rows * HEAD_SIZE,
            bytes_accessed=4 * width * (query_total + 2 * key_total) + 2 * width * width + 14 * rows * width,
            transcendentals=QUERY_HEADS * rows * rows,
        ),
        name="attention_backward",
    )(length, dbranch, weight, q, k, v, lse, h1, weight, weight, weight, cosine, sine, tokens, *after)


def combine_kernel(slots, values, *rest):
    out, p_s = rest[-2:]
    length = slots.shape[2]
    iota = lax.broadcasted_iota(jnp.int32, (WIDE, length), 0)
    for u in range(slots.shape[1]):
        pick = iota == slots[0, u : u + 1, :]
        p_s[u * WIDE : (u + 1) * WIDE, :] = jnp.where(pick, 1.0, 0.0).astype(jnp.bfloat16)
    out[0] = contract_rows(p_s[...], values[0]).astype(jnp.bfloat16)


def combine(slots, values, first, after=()):
    _, units, length = slots.shape
    n = values.shape[-1]
    low = jnp.bfloat16
    return pl.pallas_call(
        combine_kernel,
        grid=(Z_SIZE,),
        in_specs=[
            pl.BlockSpec((1, units, length), lambda i: (first + i, 0, 0)),
            pl.BlockSpec((1, units * WIDE, n), lambda i: (first + i, 0, 0)),
        ]
        + [pl.BlockSpec(memory_space=pl.ANY)] * len(after),
        out_specs=pl.BlockSpec((1, length, n), lambda i: (i, 0, 0)),
        out_shape=jax.ShapeDtypeStruct((Z_SIZE, length, n), low),
        scratch_shapes=[pltpu.VMEM((units * WIDE, length), low)],
        compiler_params=pltpu.CompilerParams(vmem_limit_bytes=60 * 1024 * 1024),
        cost_estimate=pl.CostEstimate(
            flops=2 * Z_SIZE * units * WIDE * length * n,
            bytes_accessed=Z_SIZE * (units * WIDE + length) * n * 2,
            transcendentals=0,
        ),
        name="combine",
    )(slots, values, *after)


def weight_chunks(gate_up_weight, down_weight):
    experts, rows = gate_up_weight.shape[0], gate_up_weight.shape[1]
    gate, upper = gate_up_weight[..., :FF], gate_up_weight[..., FF:]
    down_t = down_weight.transpose(0, 2, 1)
    half = FF // 2

    def one(q):
        cols = slice((q % 2) * half, (q % 2 + 1) * half)
        return jnp.concatenate([part[q // 2, :, cols] for part in (gate, upper, down_t)], axis=-1)

    return [
        jnp.stack([one(HALF_ORDER[z_to][j]) for z_to in range(Z_SIZE)]) for j in range(5)
    ]


def finish_kernel(*refs):
    gate_up, down = refs[-2:]
    rows = gate_up.shape[1]
    places = [(ref, i) for ref in refs[:4] for i in range(ref.shape[1] // rows)]
    half = FF // 2
    full = jnp.float32
    for z_from in range(Z_SIZE):
        for j in range(5):
            expert, side = divmod(HALF_ORDER[z_from][j], 2)
            part, i = places[j]
            at = slice(i * rows, (i + 1) * rows)
            cols = slice(side * half, (side + 1) * half)
            gate_up[expert, :, cols] = part[z_from, at, :half].astype(full)
            cols_up = slice(FF + side * half, FF + (side + 1) * half)
            gate_up[expert, :, cols_up] = part[z_from, at, half : 2 * half].astype(full)
            down[expert, :, cols] = part[z_from, at, 2 * half :].astype(full)


def finish_grads(backs, after):
    rows = backs[0].shape[1]
    experts = EXPERTS // (X_SIZE * C_SIZE)
    vmem = pl.BlockSpec(memory_space=pltpu.VMEM)
    return pl.pallas_call(
        finish_kernel,
        in_specs=[vmem] * len(backs) + [pl.BlockSpec(memory_space=pl.ANY)] * len(after),
        out_specs=[vmem, vmem],
        out_shape=[
            jax.ShapeDtypeStruct((experts, rows, 2 * FF), jnp.float32),
            jax.ShapeDtypeStruct((experts, rows, FF), jnp.float32),
        ],
        compiler_params=pltpu.CompilerParams(vmem_limit_bytes=40 * 1024 * 1024),
        cost_estimate=pl.CostEstimate(
            flops=0, bytes_accessed=experts * rows * FF * 18, transcendentals=0
        ),
        name="finish_grads",
    )(*backs, *after)


class DenseScatter:
    def __init__(self, mine, theirs, place):
        shape = (Y_SIZE, X_SIZE, *mine.shape[1:])
        self.mine, self.theirs, self.place = mine.reshape(shape), theirs.reshape(shape), place

    def block(self, other_y, other_x):
        y = 1 - self.place[1] if other_y else self.place[1]
        x = 1 - self.place[2] if other_x else self.place[2]
        size = (1, 1, *self.mine.shape[2:])
        got = [
            lax.dynamic_slice(a, (y, x, 0, 0, 0), size).reshape(size[2:])
            for a in (self.mine, self.got)
        ]
        return plus(*got)

    def cores(self):
        self.got = move(self.theirs, PAIRS_C)
        return [self.got]

    def first(self):
        low = jnp.bfloat16
        zs = Z_SIZE // 2
        self.near, self.to_x, self.to_y, far = [
            self.block(*at) for at in ((False, False), (False, True), (True, False), (True, True))
        ]
        gate = lambda value: value
        self.via_x = move(gate(far[:zs].astype(low)), PAIRS_X)
        self.via_y = move(gate(far[zs:].astype(low)), PAIRS_Y)
        self.x_a = move(gate(self.to_x[:zs].astype(low)), PAIRS_X)
        self.y_b = move(gate(self.to_y[zs:].astype(low)), PAIRS_Y)
        return [self.via_x, self.via_y, self.x_a, self.y_b]

    def second(self):
        low = jnp.bfloat16
        zs = Z_SIZE // 2
        gate = lambda value: value
        self.x_b = move(gate(plus(self.to_x[zs:], self.via_y).astype(low)), PAIRS_X)
        self.y_a = move(gate(plus(self.to_y[:zs], self.via_x).astype(low)), PAIRS_Y)
        return [self.x_b, self.y_a]

    def sum_up(self):
        zs = Z_SIZE // 2
        return jnp.concatenate(
            [
                plus(self.near[:zs], self.x_a) + self.y_a.astype(jnp.float32),
                plus(self.near[zs:], self.x_b) + self.y_b.astype(jnp.float32),
            ]
        ).astype(jnp.bfloat16)

    def result(self):
        return jnp.sum(self.parts.astype(jnp.float32), axis=0)


def plus(a, b):
    return a.astype(jnp.float32) + b.astype(jnp.float32)


def ring_total(own, first, second, h):
    x_a, y_b = first
    x_b, y_a = second
    return jnp.concatenate(
        [
            plus(own[0][h], x_a[h]) + y_a[h].astype(jnp.float32),
            plus(own[1][h], x_b[h]) + y_b[h].astype(jnp.float32),
        ]
    ).astype(jnp.bfloat16)


def body(
    tokens,
    cotangent,
    lengths,
    routes,
    slots,
    first_gain,
    qkv_weight,
    out_weight,
    second_gain,
    router_weight,
    gate_up_weight,
    down_weight,
):
    low = jnp.bfloat16
    full = jnp.float32
    dp_index = lax.axis_index("dp")
    expert_index = lax.axis_index("expert")
    z, y = dp_index // Y_SIZE, dp_index % Y_SIZE
    x, c = expert_index // C_SIZE, expert_index % C_SIZE
    sequence_length = tokens.shape[0]
    width = tokens.shape[1]
    rows = gate_up_weight.shape[1]

    chosen_by = routes[None, :, :] == jnp.arange(EXPERTS, dtype=jnp.int32)[:, None, None]
    slot_table = jnp.sum(jnp.where(chosen_by, slots[None, :, :] + 1, 0), axis=-1) - 1
    place = (z, y, x, c)
    zs = Z_SIZE // 2
    steps = range(1, Z_SIZE)
    rounds = Rounds()
    gate = rounds.gate

    small = jnp.concatenate(
        [router_weight, first_gain[:, None], second_gain[:, None]], axis=1
    )
    small = jnp.pad(small, ((0, 0), (0, 128 - small.shape[1])))
    shard = jnp.concatenate([qkv_weight, small, out_weight.T], axis=1)
    table = slot_table.astype(low)

    block = spread(shard)
    tables = spread(table)
    cuts = weight_chunks(gate_up_weight, down_weight)
    rounds.close(block, tables)

    near, far, moved = [None] * 5, [None] * 5, [None] * 5

    def send_half(q):
        moved[q] = trade(gate(cuts[q]))
        return [moved[q]]

    def send_near(q):
        near[q] = (move(moved[q], PAIRS_X), move(moved[q], PAIRS_Y))
        return near[q]

    def send_far(q):
        far[q] = move(near[q][1], PAIRS_X) if q % 2 == 0 else move(near[q][0], PAIRS_Y)
        return [far[q]]

    cosine_table, sine_table = rope_tables(sequence_length)
    cosine_table = jnp.tile(cosine_table, (1, QUERY_LANES // HEAD_SIZE))
    sine_table = jnp.tile(sine_table, (1, QUERY_LANES // HEAD_SIZE))
    from_x, from_y = move(block, PAIRS_X), move(block, PAIRS_Y)
    block_c = move(block, PAIRS_C)
    tables_c = move(tables, PAIRS_C)
    rounds.close(from_x, from_y, block_c, tables_c, cosine_table, sine_table, *send_half(0))
    far_a, far_b = move(from_y[:zs], PAIRS_X), move(from_x[zs:], PAIRS_Y)
    from_x_c, from_y_c = move(from_x, PAIRS_C), move(from_y, PAIRS_C)
    rounds.close(far_a, far_b, from_x_c, from_y_c, *send_half(1))
    far_a_c, far_b_c = move(far_a, PAIRS_C), move(far_b, PAIRS_C)
    moved[0] = gate(moved[0])
    send_half(2)
    pack = dense_assemble(
        place,
        (block, from_x, from_y, far_a, far_b),
        (block_c, from_x_c, from_y_c, far_a_c, far_b_c),
    )
    rounds.close(pack, moved[2], *send_near(0))
    out_at = qkv_weight.shape[1] + small.shape[1]
    out_t = pack[:, out_at:]
    small_full = pack[:, qkv_weight.shape[1] : out_at]
    router_full = small_full[:, :EXPERTS]
    gain_one = small_full[:, EXPERTS].astype(full)
    gain_two = small_full[:, EXPERTS + 1].astype(full)

    inputs = tokens.astype(full)
    inverse_one = rms_inverse(inputs)
    normal_one = inputs * inverse_one
    hidden_one, query_rows, keys, value_rows, mixed, log_totals = attention_forward(
        lengths, tokens, gain_one[None, :], pack, cosine_table, sine_table, rounds.after()
    )
    moved[1] = gate(moved[1])
    rounds.close(*send_half(3), *send_near(1), mixed)
    branch = multiply_transposed(mixed, out_t)
    middle = inputs + residual_scale * branch
    inverse_two = rms_inverse(middle)
    normal_two = middle * inverse_two
    hidden_two = (normal_two * gain_two).astype(low)
    grad_out = cotangent.astype(full)

    rows_own = spread(gate(hidden_two))
    moved[2] = gate(moved[2])
    rounds.close(*send_near(2))
    moved[3] = gate(moved[3])
    rounds.close(*send_near(3))
    for first, second in ((0, 1), (2, 3)):
        near[first] = (near[first][0], gate(near[first][1]))
        near[second] = (gate(near[second][0]), near[second][1])
        rounds.close(*send_far(first), *send_far(second))
    rounds.close(rows_own)
    rows_own = gate(rows_own)
    rows_other = move(rows_own, PAIRS_C)
    rounds.close(rows_other, *send_half(4))
    rows_in = join_rows([rows_other], [rows_own])
    slots_in = jnp.concatenate([tables_c, tables], axis=0).astype(jnp.int32)
    logits_in = jnp.einsum("de,itd->iet", router_full, rows_in, preferred_element_type=full)
    chosen_in = slots_in >= 0
    peak_in = jnp.max(jnp.where(chosen_in, logits_in, -jnp.inf), axis=1, keepdims=True)
    exponent_in = jnp.where(chosen_in, jnp.exp(logits_in - peak_in), 0.0)
    gates_in = exponent_in / jnp.sum(exponent_in, axis=1, keepdims=True)

    units = range(len(UNIT_HALVES))
    even = z % 2 == 0
    ids = []
    for group in (1 - x, x):
        base = EXPERTS // (X_SIZE * C_SIZE) * (group * C_SIZE + c) + 5 * (z // 2)
        ids += [base + jnp.where(even, 0, 3), base + jnp.where(even, 1, 4), base + 2]
    unit_slots = [lax.dynamic_index_in_dim(slots_in, expert, 1, keepdims=True) for expert in ids]
    unit_gates = [lax.dynamic_index_in_dim(gates_in, expert, 1, keepdims=True) for expert in ids]
    pairs = len(UNIT_HALVES)
    sizes = [end - first for first, end in UNIT_HALVES]
    all_slots = jnp.concatenate(unit_slots, axis=1)
    infos = [jnp.stack([y, expert]).astype(jnp.int32) for expert in ids]
    buffer = None
    saved = {}

    def ring(pair, own):
        halves = range(*UNIT_HALVES[pair])
        if own:
            return [p for q in halves for p in (moved[q], near[q][1])]
        return [p for q in halves for p in (near[q][0], far[q])]

    def run_forward(pair, own):
        nonlocal buffer
        at = pair + (pairs if own else 0)
        buffer, *saved[at] = expert_forward(
            at,
            sizes[pair],
            infos[at],
            unit_slots[at],
            unit_gates[at],
            rows_in,
            ring(pair, own),
            buffer,
            rounds.after(),
        )

    dy_own = spread(gate(cotangent))
    for pair in range(pairs):
        sent = []
        if pair == 0:
            moved[4] = gate(moved[4])
            sent += send_near(4)
        if pair == 1:
            near[4] = tuple(gate(part) for part in near[4])
            sent += send_far(4)
        run_forward(pair, False)
        run_forward(pair, True)
        rounds.close(saved[pair + pairs][0], *sent, *([dy_own] if pair == 2 else []))
    dy_own = gate(dy_own)
    dy_other = move(dy_own, PAIRS_C)
    mix_other = combine(all_slots, buffer, 0, rounds.after())
    rounds.close(mix_other, dy_other)
    mix_moved = move(mix_other, PAIRS_C)
    mix_own = combine(all_slots, buffer, Z_SIZE, rounds.after())
    grads_in = join_rows([dy_other], [dy_own])
    rounds.close(mix_moved, mix_own, grads_in)

    back = None
    grads = [[None, None] for _ in units]

    def run_back(pair, own):
        nonlocal back
        at = pair + (pairs if own else 0)
        back, grads[pair][1 if own else 0] = expert_backward(
            at,
            sizes[pair],
            infos[at],
            unit_slots[at],
            unit_gates[at],
            grads_in,
            *saved[at],
            ring(pair, own),
            back,
            rounds.after(),
        )

    vias, firsts, seconds = [None] * 3, [None] * 3, [None] * 3

    def send_via(u):
        vias[u] = (move(gate(grads[u][0][2]), PAIRS_X), move(gate(grads[u][0][3]), PAIRS_Y))
        return vias[u]

    def send_first(u):
        firsts[u] = (move(gate(grads[u][0][0]), PAIRS_X), move(gate(grads[u][1][3]), PAIRS_Y))
        return firsts[u]

    def send_second(u):
        via_x, via_y = vias[u]
        seconds[u] = (
            move(gate(plus(grads[u][0][1], via_y).astype(low)), PAIRS_X),
            move(gate(plus(grads[u][1][2], via_x).astype(low)), PAIRS_Y),
        )
        return seconds[u]

    def total_of(u):
        return [ring_total(grads[u][1], firsts[u], seconds[u], h) for h in range(sizes[u])]

    terms = plus(mix_own, mix_moved).astype(low)
    mix_got = trade(gate(terms))
    run_back(0, False)
    rounds.close(grads[0][0][0])
    run_back(0, True)
    rounds.close(grads[0][1][0], *send_via(0))
    run_back(1, False)
    rounds.close(grads[1][0][0], *send_first(0))
    run_back(1, True)
    rounds.close(mix_got, grads[1][1][0], *send_second(0))
    mixture = jnp.sum(mix_got.astype(full), axis=0)
    output = (middle + residual_scale * mixture).astype(low)
    totals = total_of(0)
    backs = []

    def send_back(*parts):
        backs.append(trade(gate(parts[0] if len(parts) == 1 else jnp.concatenate(parts, axis=1))))
        return backs[-1:]

    run_back(2, False)
    rounds.close(grads[2][0][0], *send_via(1), *send_back(totals[0]))
    run_back(2, True)
    rounds.close(grads[2][1][0], *send_first(1), *send_back(totals[1]))
    copy_other = combine(all_slots, back, 0, rounds.after())
    rounds.close(copy_other)
    copy_moved = move(copy_other, PAIRS_C)
    copy_own = combine(all_slots, back, Z_SIZE, rounds.after())
    rounds.close(copy_moved, copy_own, *send_second(1), *send_via(2))
    copy_got = trade(plus(copy_own, copy_moved).astype(low))
    rounds.close(*send_first(2))
    rounds.close(*send_second(2))
    totals += total_of(1) + total_of(2)
    last_total = jnp.concatenate(totals[3:], axis=1)
    rounds.close(copy_got, output, totals[2], last_total)
    copy_got = gate(copy_got)
    chosen = (slot_table >= 0).T
    gates = dense_gates(jnp.dot(hidden_two, router_full, preferred_element_type=full), chosen)
    grad_middle, branch_gradient, out_mine, out_theirs = middle_backward(
        c,
        copy_got,
        jnp.pad(gates, ((0, 0), (0, 128 - EXPERTS))),
        pack,
        qkv_weight.shape[1],
        gain_two[None, :],
        middle,
        hidden_two,
        cotangent,
        mixed,
    )
    out_scatter = DenseScatter(out_mine, out_theirs, place)
    out_scatter.cores()
    qkv_mine, qkv_theirs, grad_hidden_one = attention_backward(
        jnp.concatenate([lengths, c[None]]),
        branch_gradient,
        query_rows,
        keys,
        value_rows,
        log_totals,
        hidden_one,
        pack,
        out_at,
        cosine_table,
        sine_table,
        tokens,
        rounds.after(),
    )
    rounds.close(grad_hidden_one, *send_back(totals[2]), *out_scatter.first())
    qkv_scatter = DenseScatter(qkv_mine, gate(qkv_theirs), place)
    sent = send_back(last_total)
    rounds.close(*qkv_scatter.cores(), *out_scatter.second())
    rounds.close(*qkv_scatter.first())
    rounds.close(*qkv_scatter.second(), *sent)
    both = jnp.concatenate([out_scatter.sum_up(), qkv_scatter.sum_up()], axis=-1)
    parts = trade(both)
    out_scatter.parts = parts[..., : width + 128]
    qkv_scatter.parts = parts[..., width + 128 :]
    gate_up_grads, down_grads = finish_grads(backs, [both])
    down_grads = down_grads.transpose(0, 2, 1)
    _, grad_norm_one = norm_backward(
        grad_hidden_one, normal_one, inverse_one, gain_one
    )
    grad_input = grad_middle + grad_norm_one

    qkv_sum = qkv_scatter.result()
    first_sum = qkv_sum[:, -128]
    qkv_sum = qkv_sum[:, :-128]
    qkv_sum = qkv_sum.reshape(qkv_sum.shape[0], -1, QUERY_LANES + 2 * KEY_LANES)
    qkv_sum = jnp.concatenate(
        [
            part.reshape(qkv_sum.shape[0], -1)
            for part in jnp.split(qkv_sum, (QUERY_LANES, QUERY_LANES + KEY_LANES), axis=2)
        ],
        axis=1,
    )
    out_sum = out_scatter.result()
    small_sum = out_sum[:, width:]
    return (
        output,
        grad_input,
        first_sum,
        qkv_sum,
        out_sum[:, :width].T,
        small_sum[:, EXPERTS],
        small_sum[:, :EXPERTS],
        gate_up_grads,
        down_grads,
    )


def solution(mesh):
    in_specs = (
        P(("dp", "expert"), None),
        P(("dp", "expert"), None),
        P(("dp", "expert")),
        P(("dp", "expert"), None),
        P(("dp", "expert"), None),
        P(("dp", "expert")),
        P(("dp", "expert"), None),
        P(None, ("dp", "expert")),
        P(("dp", "expert")),
        P(("dp", "expert"), None),
        P("expert", "dp", None),
        P("expert", None, "dp"),
    )
    out_specs = (
        P(("dp", "expert"), None),
        P(("dp", "expert"), None),
        P(("dp", "expert")),
        P(("dp", "expert"), None),
        P(None, ("dp", "expert")),
        P(("dp", "expert")),
        P(("dp", "expert"), None),
        P("expert", "dp", None),
        P("expert", None, "dp"),
    )
    fits = mesh.shape["dp"] == Z_SIZE * Y_SIZE and mesh.shape["expert"] == X_SIZE * C_SIZE
    chosen = body if fits else general_body
    return jax.shard_map(chosen, mesh=mesh, in_specs=in_specs, out_specs=out_specs, check_vma=False)
```
